128 devices in a mesh: stream: 4 (over x_lo, core), blk: 4 (over z), uly: 8 (over y, x_hi).
Axes of the slice: x: 4 (x_hi: 2, x_lo: 2; x = x_hi * 2 + x_lo), y: 4, z: 4, core: 2. Of those that a mesh axis runs over, the one named last changes fastest.
Arguments:
- tokens: bfloat16 [4, 4096, 2048], P('stream', ('blk', 'uly')), may hold values from -6 to 6
- document_starts: int32 [4, 8], P('stream'), may hold values from 0 to 4095, as said below
- document_adapter: int32 [4, 8], P('stream'), may hold values from 0 to 7
- layernorm_gain: float32 [2, 2048], replicated, may hold values from 0.1 to 1.9
- layernorm_bias: float32 [2, 2048], replicated, may hold values from -4 to 4
- projection_weight: bfloat16 [2048, 3, 2048], P(('stream', 'blk', 'uly')), may hold values from -0.125 to 0.125
- output_weight: bfloat16 [2048, 2048], P(('stream', 'blk', 'uly')), may hold values from -1 to 1
- up_weight: bfloat16 [2048, 8192], P(('stream', 'blk', 'uly')), may hold values from -0.125 to 0.125
- down_weight: bfloat16 [8192, 2048], P(('stream', 'blk', 'uly')), may hold values from -0.0625 to 0.0625
- projection_bias: float32 [4, 2048], replicated, may hold values from -4 to 4
- upper_bias: float32 [8192], replicated, may hold values from -6 to 6
- attention_down_maps: bfloat16 [4, 2048, 128], replicated, may hold values from -0.125 to 0.125
- attention_up_maps: bfloat16 [4, 128, 2048], replicated, may hold values from -0.75 to 0.75
- upper_down_maps: bfloat16 [2048, 128], replicated, may hold values from -0.125 to 0.125
- upper_up_maps: bfloat16 [128, 8192], replicated, may hold values from -0.75 to 0.75
- lower_down_maps: bfloat16 [8192, 128], replicated, may hold values from -0.0625 to 0.0625
- lower_up_maps: bfloat16 [128, 2048], replicated, may hold values from -0.75 to 0.75
- cotangent: bfloat16 [4, 4096, 2048], P('stream', ('blk', 'uly')), may hold values from -6 to 6
Outputs:
- mixed: bfloat16 [4, 4096, 2048], P('stream', ('blk', 'uly'))
- input_grad: bfloat16 [4, 4096, 2048], P('stream', ('blk', 'uly'))
- grad_a_attn: float32 [4, 2048, 128], replicated
- grad_b_attn: float32 [4, 128, 2048], replicated
- grad_a_up: float32 [2048, 128], replicated
- grad_b_up: float32 [128, 8192], replicated
- grad_a_down: float32 [8192, 128], replicated
- grad_b_down: float32 [128, 2048], replicated
The draws below stay inside these ranges and needn't reach their ends.
Inputs may be any that keep to these rules, and one draw needn't show every extreme that they name: `document_starts`: each row starts with 0 and rises strictly; document d of a stream runs from its start to the next start, or to 4096.
All inputs are finite; a program needn't handle non-finite values.
Results may differ from the reference program's by a relative error of at most 0.015.
Values may be sent and summed in bfloat16 or wider, within the bound.
A program may use at most 384 MiB of HBM per device.

```python
import math
import jax
import jax.numpy as jnp
from jax import lax

MODEL_WIDTH = 2048
HEADS = 16
HEAD_DIM = 128
HIDDEN_UNITS = 8192
ADAPTER_RANK = 16
ADAPTER_COUNT = 8
DOCS = 8
BLOCK = 1024
SEQ = 4096
STREAMS = 4


def draw_document_starts(key, part):
    key = jax.random.fold_in(key, 11)

    def one_row(row_key):
        pick_key, left_key, right_key = jax.random.split(row_key, 3)
        longest = jax.random.randint(pick_key, (), 0, DOCS)
        left = jnp.sort(jax.random.permutation(left_key, BLOCK - 1)[:DOCS - 1]) + 1
        right = jnp.sort(jax.random.permutation(right_key, BLOCK - 1)[:DOCS - 1]) + (SEQ - BLOCK + 1)
        index = jnp.arange(1, DOCS)
        rest = jnp.where(index <= longest, left, right).astype(jnp.int32)
        return jnp.concatenate([jnp.zeros((1,), jnp.int32), rest])
    return jax.vmap(one_row)(jax.random.split(key, STREAMS)).astype(jnp.int32)


def touch_ends(values, rng, low, top_value):
    place = [jax.random.randint(jax.random.fold_in(rng, axis), (), 0, length) for axis, length in enumerate(values.shape)]
    widest = values.shape.index(max(values.shape))
    next_to = place[:widest] + [(place[widest] + 1) % values.shape[widest]] + place[widest + 1:]
    return values.at[tuple(place)].set(low).at[tuple(next_to)].set(top_value)


def block_scale(rng, extent, cuts, low, high):
    factor_of, own = 1.0, jax.random.fold_in(rng, 6)
    for position, parts in cuts:
        draws = jnp.exp(jax.random.uniform(jax.random.fold_in(own, position), (parts,), jnp.float32, low / len(cuts), high / len(cuts)))
        factor_of = factor_of * jnp.repeat(draws, extent[position] // parts).reshape([-1 if axis == position else 1 for axis in range(len(extent))])
    return factor_of


def normal_values(own_key, shape, scale, reach, cuts=(), kind=jnp.bfloat16):
    level = block_scale(own_key, shape, cuts, -0.22, 0.18) if cuts else 1.0
    values = jax.random.normal(own_key, shape, jnp.float32) * scale * level
    return jnp.minimum(jnp.maximum(values, -reach), reach).astype(kind)


def setup_inputs(seed: int = 0) -> dict:
    key_of = jax.random.split(jax.random.key(seed), 19)
    return {
        "tokens": normal_values(key_of[0], (STREAMS, SEQ, MODEL_WIDTH), 1.0, 6.0, ((0, 4), (1, 32))),
        "document_starts": draw_document_starts(jax.random.fold_in(key_of[18], 71), 0),
        "document_adapter": touch_ends(jax.random.randint(key_of[2], (STREAMS, DOCS), 0, ADAPTER_COUNT), jax.random.fold_in(key_of[2], 1), 0, ADAPTER_COUNT - 1).astype(jnp.int32),
        "layernorm_gain": jnp.clip(1.0 + 0.18 * jax.random.normal(key_of[3], (2, MODEL_WIDTH), jnp.float32), 0.1, 1.9),
        "layernorm_bias": normal_values(key_of[4], (2, MODEL_WIDTH), 0.3, 4.0, (), jnp.float32),
        "projection_weight": normal_values(key_of[5], (MODEL_WIDTH, 3, MODEL_WIDTH), MODEL_WIDTH ** -0.5, 0.125, ((0, 128),)),
        "output_weight": normal_values(key_of[6], (MODEL_WIDTH, MODEL_WIDTH), (MODEL_WIDTH // 64) ** -0.5, 1.0, ((0, 128),)),
        "up_weight": normal_values(key_of[7], (MODEL_WIDTH, HIDDEN_UNITS), MODEL_WIDTH ** -0.5, 0.125, ((0, 128),)),
        "down_weight": normal_values(key_of[8], (HIDDEN_UNITS, MODEL_WIDTH), HIDDEN_UNITS ** -0.5, 0.0625, ((0, 128),)),
        "projection_bias": normal_values(key_of[9], (4, MODEL_WIDTH), 0.3, 4.0, (), jnp.float32),
        "upper_bias": normal_values(key_of[10], (HIDDEN_UNITS,), 0.5, 6.0, (), jnp.float32),
        "attention_down_maps": normal_values(key_of[11], (4, MODEL_WIDTH, ADAPTER_COUNT * ADAPTER_RANK), MODEL_WIDTH ** -0.5, 0.125),
        "attention_up_maps": normal_values(key_of[12], (4, ADAPTER_COUNT * ADAPTER_RANK, MODEL_WIDTH), (4 * ADAPTER_RANK) ** -0.5, 0.75),
        "upper_down_maps": normal_values(key_of[13], (MODEL_WIDTH, ADAPTER_COUNT * ADAPTER_RANK), MODEL_WIDTH ** -0.5, 0.125),
        "upper_up_maps": normal_values(key_of[14], (ADAPTER_COUNT * ADAPTER_RANK, HIDDEN_UNITS), (4 * ADAPTER_RANK) ** -0.5, 0.75),
        "lower_down_maps": normal_values(key_of[15], (HIDDEN_UNITS, ADAPTER_COUNT * ADAPTER_RANK), HIDDEN_UNITS ** -0.5, 0.0625),
        "lower_up_maps": normal_values(key_of[16], (ADAPTER_COUNT * ADAPTER_RANK, MODEL_WIDTH), (4 * ADAPTER_RANK) ** -0.5, 0.75),
        "cotangent": normal_values(key_of[17], (STREAMS, SEQ, MODEL_WIDTH), 1.0, 6.0, ((0, 4), (1, 32))),
    }


@jax.custom_vjp
def low(v):
    return lax.optimization_barrier(v.astype(jnp.bfloat16)).astype(jnp.float32)

@jax.custom_vjp
def low_back(v):
    return v

def low_keep(v):
    return (low(v), None)

def low_pass(kept, grad):
    return (grad,)

def back_keep(v):
    return (v, None)

def back_low(kept, grad):
    return (low(grad),)
low.defvjp(low_keep, low_pass)
low_back.defvjp(back_keep, back_low)

def layer_norm(values, gain, shift):
    center = values - lax.optimization_barrier(jnp.mean(values, axis=-1, keepdims=True))
    spread = lax.optimization_barrier(jnp.mean(center * center, axis=-1, keepdims=True))
    return center * lax.rsqrt(spread + 1e-05) * gain + shift

def segment_of(starts, positions):
    return lax.optimization_barrier(jnp.sum((starts[None, :] <= positions[:, None]).astype(jnp.int32), axis=1)) - 1

def attention(qkv_low, segment):
    highest = lax.Precision.HIGHEST
    split = qkv_low.reshape(3, SEQ, HEADS, HEAD_DIM)
    queries, keys, values = (split[0], split[1], split[2])
    rows = math.gcd(SEQ, 512)
    positions = jnp.arange(SEQ, dtype=jnp.int32)
    scale = HEAD_DIM ** (-0.5)

    def one_block(items):
        query_rows, query_pos, query_seg = items
        raw = jnp.einsum('qhd,khd->hqk', query_rows, keys, precision=highest)
        scores = low_back(raw) * scale
        allowed = (positions[None, :] <= query_pos[:, None]) & (segment[None, :] == query_seg[:, None])
        masked = jnp.where(allowed[None], scores, -1000000000.0)
        total = jax.nn.logsumexp(masked, axis=-1, keepdims=True)
        probs = low(jnp.exp(masked - total))
        return jnp.einsum('hqk,khd->qhd', probs, values, precision=highest)
    blocks = lax.map(jax.checkpoint(one_block), (queries.reshape(SEQ // rows, rows, HEADS, HEAD_DIM), positions.reshape(SEQ // rows, rows), segment.reshape(SEQ // rows, rows)))
    return blocks.reshape(SEQ, HEADS * HEAD_DIM)

def reference(tokens, document_starts, document_adapter, layernorm_gain, layernorm_bias, projection_weight, output_weight, up_weight, down_weight, projection_bias, upper_bias, attention_down_maps, attention_up_maps, upper_down_maps, upper_up_maps, lower_down_maps, lower_up_maps, cotangent):
    highest = lax.Precision.HIGHEST
    qkv_full = projection_weight.astype(jnp.float32)
    output_projection_total = output_weight.astype(jnp.float32)
    up_projection_total = up_weight.astype(jnp.float32)
    down_projection_total = down_weight.astype(jnp.float32)
    adapter_table = (attention_down_maps.astype(jnp.float32), attention_up_maps.astype(jnp.float32), upper_down_maps.astype(jnp.float32), upper_up_maps.astype(jnp.float32), lower_down_maps.astype(jnp.float32), lower_up_maps.astype(jnp.float32))
    columns = ADAPTER_COUNT * ADAPTER_RANK
    bias_rows = jnp.stack([projection_bias[0], jnp.zeros_like(projection_bias[0]), projection_bias[1]])

    def one_stream(carry, items):
        stream_tokens, starts, chosen, stream_cot = items
        positions = jnp.arange(SEQ, dtype=jnp.int32)
        segment = segment_of(starts, positions)
        doc_ids = jnp.arange(DOCS, dtype=jnp.int32)
        token_adapter = lax.optimization_barrier(jnp.sum(jnp.where(segment[:, None] == doc_ids[None, :], chosen[None, :], 0), axis=1))
        owner = jnp.arange(columns, dtype=jnp.int32) // ADAPTER_RANK
        document_mask = (token_adapter[:, None] == owner[None, :]).astype(jnp.float32)

        def forward(inputs, la_attn, lb_attn, la_up, lb_up, la_down, lb_down):
            first_norm_input = low(layer_norm(inputs, layernorm_gain[0], layernorm_bias[0]))
            adapter_projection_delta = low(low_back(jnp.einsum('zl,xlr->xzr', first_norm_input, la_attn[:3], precision=highest) * document_mask[None]))
            qkv = jnp.einsum('td,dpe->pte', first_norm_input, qkv_full, precision=highest) + bias_rows[:, None, :] + jnp.einsum('moa,maz->moz', adapter_projection_delta, lb_attn[:3], precision=highest)
            qkv_low = low(low_back(qkv))
            attended_low = low(low_back(attention(qkv_low, segment)))
            adapter_output_delta = low(low_back(jnp.dot(attended_low, la_attn[3], precision=highest) * document_mask))
            branch = low_back(jnp.dot(attended_low, output_projection_total, precision=highest) + projection_bias[2] + jnp.dot(adapter_output_delta, lb_attn[3], precision=highest))
            residual_stream = inputs + branch
            second_norm_input = low(layer_norm(residual_stream, layernorm_gain[1], layernorm_bias[1]))
            adapter_up_delta = low(low_back(jnp.dot(second_norm_input, la_up, precision=highest) * document_mask))
            preactivation = low_back(jnp.dot(second_norm_input, up_projection_total, precision=highest) + upper_bias + jnp.dot(adapter_up_delta, lb_up, precision=highest))
            activation_reduced = low(jax.nn.gelu(preactivation, approximate=False))
            adapter_down_delta = low(low_back(jnp.dot(activation_reduced, la_down, precision=highest) * document_mask))
            return residual_stream + jnp.dot(activation_reduced, down_projection_total, precision=highest) + projection_bias[3] + jnp.dot(adapter_down_delta, lb_down, precision=highest)
        result, backward = jax.vjp(forward, stream_tokens.astype(jnp.float32), *adapter_table)
        grads = backward(stream_cot.astype(jnp.float32))
        carry = tuple((total + piece for total, piece in zip(carry, grads[1:])))
        return (carry, (result.astype(jnp.bfloat16), grads[0].astype(jnp.bfloat16)))
    start_sums = tuple((jnp.zeros(array.shape, jnp.float32) for array in adapter_table))
    sums, (mixed, input_grad) = lax.scan(one_stream, start_sums, (tokens, document_starts, document_adapter, cotangent))
    return (mixed, input_grad, sums[0], sums[1], sums[2], sums[3], sums[4], sums[5])
```

```python
import functools

import jax
import jax.numpy as jnp
import numpy as np
from jax import lax
from jax.experimental import pallas as pl
from jax.experimental.pallas import tpu as pltpu
from jax.sharding import PartitionSpec as P

HEADS = 16
ADAPTER_RANK = 16
MESH = pl.DeviceIdType.MESH
AXES = ("xl", "c", "z", "y", "xh")
SIZES = (2, 2, 4, 4, 2)
STREAM = ("xl", "c")
TOKEN = ("z", "y", "xh")
HEAD = ("z", "y")
bf16 = jnp.bfloat16
f32 = jnp.float32
LOG2E = 1.4426950408889634
MIB = 2**20
Q_TILE = 256
K_TILE = 512


def layer_norm(values, gain, shift):
    center = values - jnp.mean(values, axis=-1, keepdims=True)
    spread = jnp.mean(center * center, axis=-1, keepdims=True)
    return center * lax.rsqrt(spread + 1e-05) * gain + shift


def dot(left, right):
    return jnp.dot(left, right, preferred_element_type=f32)


def dot_nt(left, right):
    return lax.dot_general(left, right, (((1,), (1,)), ((), ())), preferred_element_type=f32)


def dot_tn(left, right):
    return lax.dot_general(left, right, (((0,), (0,)), ((), ())), preferred_element_type=f32)


def exact_gelu(values):
    return jax.nn.gelu(values, approximate=False)


class Place:
    def __init__(self):
        self.xl, self.c, self.z, self.y, self.xh = (lax.axis_index(a) for a in AXES)
        self.x = self.xh * 2 + self.xl

    def at(self, axis):
        return {"x": self.x, "y": self.y, "z": self.z, "xh": self.xh}[axis]

    def toward(self, axis, step):
        if axis == "c":
            return {"c": 1 - self.c}
        if axis == "xh":
            return {"xh": 1 - self.xh}
        to = lax.rem(self.at(axis) + (step + 4), 4)
        if axis == "x":
            return {"xl": lax.rem(to, 2), "xh": to // 2}
        return {axis: to}


class Sends:
    def __init__(self, send, recv):
        self.send, self.recv, self.used, self.open = send, recv, 0, []

    def push(self, src, dst, device):
        k = self.used
        self.used += 1
        copy = pltpu.make_async_remote_copy(
            src_ref=src,
            dst_ref=dst,
            send_sem=self.send.at[k],
            recv_sem=self.recv.at[k],
            device_id=device,
            device_id_type=MESH,
        )
        copy.start()
        self.open.append(copy)
        return copy


def greet(devices):
    barrier = pltpu.get_barrier_semaphore()
    for device in devices:
        pl.semaphore_signal(barrier, inc=1, device_id=device, device_id_type=MESH)
    pl.semaphore_wait(barrier, len(devices))


def run_all(parts):
    parts = list(parts)
    while parts:
        left = []
        for part in parts:
            try:
                next(part)
                left.append(part)
            except StopIteration:
                pass
        parts = left


ALL = slice(None)
LOWER, UPPER = pl.ds(0, 1024), pl.ds(1024, 1024)


def ring_gather(place, sends, view, order, chunk, landed, forward):
    fixed = {a: place.at(a) for a in order}
    across = place.toward("c", 1)
    later, passed = [], []
    if forward:
        passed.append(sends.push(chunk, view(fixed, ALL), across))
    for number, axis in enumerate(order):
        own = view(fixed, ALL)
        src = chunk if number == 0 else own
        here = place.at(axis)
        if axis == "xh":
            sent = sends.push(src, own, place.toward("xh", 1))
            yield
            sent.wait_recv()
            if number == 0:
                landed.wait()
            later.append(sent)
            del fixed[axis]
            continue
        up = sends.push(src, own, place.toward(axis, 1))
        down = sends.push(src, own, place.toward(axis, -1))
        yield
        before = dict(fixed) | {axis: lax.rem(here + 3, 4)}
        after = dict(fixed) | {axis: lax.rem(here + 1, 4)}
        opposite = dict(fixed) | {axis: lax.rem(here + 2, 4)}
        up.wait_recv()
        half = view(before, LOWER)
        up_two = sends.push(half, half, place.toward(axis, 1))
        down.wait_recv()
        half = view(after, UPPER)
        down_two = sends.push(half, half, place.toward(axis, -1))
        if forward:
            for block in (before, after):
                passed.append(sends.push(view(block, ALL), view(block, ALL), across))
        yield
        up_two.wait_recv()
        down_two.wait_recv()
        if number == 0:
            landed.wait()
        if forward:
            passed.append(sends.push(view(opposite, ALL), view(opposite, ALL), across))
        later += [up, down, up_two, down_two]
        del fixed[axis]
    yield
    for copy in later:
        copy.wait_send()
    for copy in passed:
        copy.wait()


def weights_kernel(wp, wo, up, dn, qkv_all, out_all, up_all, dn_all, send, recv, local):
    place = Place()
    sends = Sends(send, recv)
    partner = place.toward("c", 1)
    mates = [{"c": 1 - place.c}, {"xl": 1 - place.xl}, {"xl": 1 - place.xl, "c": 1 - place.c}]
    peers = mates + [place.toward("xh", 1)]
    peers += [place.toward(a, s) for a in ("x", "y", "z") for s in (1, -1)]
    greet(peers)
    home = (place.xl, place.c, place.z, place.y, place.xh)

    def whole(ref, lead):
        def view(fixed, columns):
            xl, xh = (ALL, ALL)
            if "x" in fixed:
                xl, xh = lax.rem(fixed["x"], 2), fixed["x"] // 2
            return ref.at[lead + (xl, place.c, fixed.get("z", ALL), fixed.get("y", ALL), xh, ALL, columns)]

        return view

    def up_view(fixed, columns):
        return up_all.at[ALL, ALL, fixed.get("z", ALL), fixed.get("y", ALL), fixed.get("xh", ALL), ALL, columns]

    def dn_view(fixed, columns):
        return dn_all.at[fixed.get("z", ALL), fixed.get("y", ALL), fixed.get("xh", ALL), ALL, columns]

    stream = place.xl * 2 + place.c

    def cols(device):
        to = device.get("xl", place.xl) * 2 + device.get("c", place.c)
        return pl.ds(pl.multiple_of(to * 2048, 2048), 2048)

    copies = [pltpu.make_async_copy(wp.at[p], qkv_all.at[(p,) + home], local.at[p]) for p in range(3)]
    copies.append(pltpu.make_async_copy(wo, out_all.at[home], local.at[3]))
    copies.append(pltpu.make_async_copy(dn, dn_all.at[home[2:]], local.at[4]))
    copies.append(pltpu.make_async_copy(up.at[:, cols({})], up_all.at[home], local.at[5]))
    for copy in copies:
        copy.start()
    spread = [sends.push(up.at[:, cols(m)], up_all.at[home], m) for m in mates]

    class Many:
        def wait(self):
            copies[5].wait()
            for s in spread:
                s.wait()

    class Nothing:
        def wait(self):
            pass

    def up_part():
        yield
        Many().wait()
        fixed = {"xh": place.xh, "y": place.y, "z": place.z}
        yield from ring_gather(place, sends, up_view, ("xh", "y", "z"), up_view(fixed, ALL), Nothing(), False)

    parts = [
        ring_gather(place, sends, whole(qkv_all, (0,)), ("y", "z", "x"), wp.at[0], copies[0], True),
        ring_gather(place, sends, whole(qkv_all, (1,)), ("z", "y", "x"), wp.at[1], copies[1], True),
        ring_gather(place, sends, whole(qkv_all, (2,)), ("x", "y", "z"), wp.at[2], copies[2], True),
        ring_gather(place, sends, whole(out_all, ()), ("x", "z", "y"), wo, copies[3], True),
        up_part(),
        ring_gather(place, sends, dn_view, ("xh", "z", "y"), dn, copies[4], False),
    ]
    run_all(parts)


def gather_weights(wp, wo, up, dn):
    n = 160
    any_ = pl.BlockSpec(memory_space=pl.ANY)
    return pl.pallas_call(
        weights_kernel,
        name="gather_weights",
        out_shape=[
            jax.ShapeDtypeStruct((3, 2, 2, 4, 4, 2, 16, 2048), bf16),
            jax.ShapeDtypeStruct((2, 2, 4, 4, 2, 16, 2048), bf16),
            jax.ShapeDtypeStruct((2, 2, 4, 4, 2, 16, 2048), bf16),
            jax.ShapeDtypeStruct((4, 4, 2, 64, 2048), bf16),
        ],
        in_specs=[any_] * 4,
        out_specs=[any_] * 4,
        scratch_shapes=[
            pltpu.SemaphoreType.DMA((n,)),
            pltpu.SemaphoreType.DMA((n,)),
            pltpu.SemaphoreType.DMA((6,)),
        ],
        compiler_params=pltpu.CompilerParams(collective_id=0, has_side_effects=True),
    )(wp, wo, up, dn)


def positions_of(local, parity):
    return (2 * (local // 128) + parity) * 128 + lax.rem(local, 128)


def flash_kernel(info, q_ref, lo_ref, ko_ref, vo_ref, kx_ref, vx_ref, o_ref, low_ref, lse_ref, *, scale):
    tile = pl.program_id(0)
    parity = info[0]
    first = info[1 + tile]
    last = (tile * Q_TILE + Q_TILE + K_TILE - 1) // K_TILE
    q = q_ref[...]
    shape = (Q_TILE, K_TILE)
    q_pos = positions_of(tile * Q_TILE + lax.broadcasted_iota(jnp.int32, (Q_TILE, 1), 0), parity)
    lo = lo_ref[...]
    ones = jnp.ones((K_TILE, 128), bf16)

    def step(kt, carry):
        top, acc = carry
        rows = pl.ds(pl.multiple_of(kt * K_TILE, K_TILE), K_TILE)
        local = kt * K_TILE + lax.broadcasted_iota(jnp.int32, (1, K_TILE), 1)
        scores = []
        for k_ref, par in ((ko_ref, parity), (kx_ref, 1 - parity)):
            k_pos = positions_of(local, par)
            s = dot_nt(q, k_ref[rows, :])
            scores.append(jnp.where((k_pos >= lo) & (k_pos <= q_pos), s, -1e30))
        new = jnp.maximum(jnp.max(scores[0], axis=1, keepdims=True), jnp.max(scores[1], axis=1, keepdims=True))
        new = jnp.maximum(top, new)
        acc = acc * jnp.exp2((top - new) * (scale * LOG2E))
        for s, v_ref in zip(scores, (vo_ref, vx_ref)):
            p = jnp.exp2((s - new) * (scale * LOG2E)).astype(bf16)
            acc = acc + dot(p, jnp.concatenate([v_ref[rows, :], ones], axis=1))
        return new, acc

    top, acc = lax.fori_loop(
        first, last, step, (jnp.full((Q_TILE, 1), -1e30, f32), jnp.zeros((Q_TILE, 256), f32))
    )
    total = acc[:, 128:]
    o = acc[:, :128] / total
    o_ref[...] = o
    low_ref[...] = o.astype(bf16)
    lse = top * (scale * LOG2E) + jnp.log2(total)
    lse_ref[...] = jnp.transpose(lse)[0:8, :]


def flash_forward(info, q, lo, ko, vo, kx, vx, scale):
    rows = q.shape[0]
    tiles = rows // Q_TILE
    whole = pl.BlockSpec((rows, 128), lambda t, s: (0, 0))
    block = pl.BlockSpec((Q_TILE, 128), lambda t, s: (t, 0))
    return pl.pallas_call(
        functools.partial(flash_kernel, scale=scale),
        name="attention_forward",
        grid_spec=pltpu.PrefetchScalarGridSpec(
            num_scalar_prefetch=1,
            grid=(tiles,),
            in_specs=[block, pl.BlockSpec((Q_TILE, 1), lambda t, s: (t, 0)), whole, whole, whole, whole],
            out_specs=[block, block, pl.BlockSpec((8, Q_TILE), lambda t, s: (t, 0))],
        ),
        out_shape=[
            jax.ShapeDtypeStruct((rows, 128), f32),
            jax.ShapeDtypeStruct((rows, 128), bf16),
            jax.ShapeDtypeStruct((tiles * 8, Q_TILE), f32),
        ],
        compiler_params=pltpu.CompilerParams(vmem_limit_bytes=40 * MIB),
    )(info, q, lo, ko, vo, kx, vx)


def flash_back_kernel(info, q_ref, do_ref, lse_ref, delta_ref, lo_ref, k_ref, v_ref, dq_ref, dk_ref, dv_ref, dq_acc, *, scale):
    other = pl.program_id(0) == 0
    kt = pl.program_id(1)
    parity = info[0]
    k_parity = jnp.where(other, 1 - parity, parity)

    @pl.when(other & (kt == 0))
    def _():
        dq_acc[...] = jnp.zeros_like(dq_acc)

    k = k_ref[0]
    v = v_ref[0]
    k_pos = positions_of(kt * K_TILE + lax.broadcasted_iota(jnp.int32, (K_TILE, 1), 0), k_parity)
    first = kt * (K_TILE // Q_TILE)
    last = info[1 + kt]

    def step(qt, carry):
        dk, dv = carry
        rows = pl.ds(pl.multiple_of(qt * Q_TILE, Q_TILE), Q_TILE)
        q = q_ref[rows, :]
        do = do_ref[rows, :]
        q_pos = positions_of(qt * Q_TILE + lax.broadcasted_iota(jnp.int32, (1, Q_TILE), 1), parity)
        lo = lo_ref[pl.ds(qt, 1), :]
        lse = lse_ref[pl.ds(qt, 1), :]
        delta = delta_ref[pl.ds(qt, 1), :]
        s = dot_nt(k, q)
        p = jnp.exp2(jnp.where((k_pos >= lo) & (k_pos <= q_pos), s * (scale * LOG2E) - lse, -1e30))
        dv = dv + dot(p.astype(bf16), do)
        dp = dot_nt(v, do)
        ds = (p * (dp - delta) * scale).astype(bf16)
        dk = dk + dot(ds, q)
        dq_acc[rows, :] += dot_tn(ds, k)
        return dk, dv

    zero = jnp.zeros((K_TILE, 128), f32)
    dk, dv = lax.fori_loop(first, last, step, (zero, zero))
    dk_ref[0] = dk.astype(dk_ref.dtype)
    dv_ref[0] = dv.astype(dv_ref.dtype)

    @pl.when(jnp.logical_not(other) & (kt == pl.num_programs(1) - 1))
    def _():
        dq_ref[...] = dq_acc[...].astype(bf16)


def flash_backward(info, q, do, lse, delta, lo, k_two, v_two, scale):
    rows = q.shape[0]
    tiles = rows // K_TILE
    whole = pl.BlockSpec((rows, 128), lambda o, t, s: (0, 0))
    line = pl.BlockSpec((rows // Q_TILE, Q_TILE), lambda o, t, s: (0, 0))
    block = pl.BlockSpec((1, K_TILE, 128), lambda o, t, s: (o, t, 0))
    return pl.pallas_call(
        functools.partial(flash_back_kernel, scale=scale),
        name="attention_backward",
        grid_spec=pltpu.PrefetchScalarGridSpec(
            num_scalar_prefetch=1,
            grid=(2, tiles),
            in_specs=[whole, whole, line, line, line, block, block],
            out_specs=[whole, block, block],
            scratch_shapes=[pltpu.VMEM((rows, 128), f32)],
        ),
        out_shape=[
            jax.ShapeDtypeStruct((rows, 128), bf16),
            jax.ShapeDtypeStruct((2, rows, 128), f32),
            jax.ShapeDtypeStruct((2, rows, 128), f32),
        ],
        compiler_params=pltpu.CompilerParams(vmem_limit_bytes=40 * MIB),
    )(info, q, do, lse, delta, lo, k_two, v_two)


def per_device(
    tokens,
    document_starts,
    document_adapter,
    layernorm_gain,
    layernorm_bias,
    projection_weight,
    output_weight,
    up_weight,
    down_weight,
    projection_bias,
    upper_bias,
    attention_down_maps,
    attention_up_maps,
    upper_down_maps,
    upper_up_maps,
    lower_down_maps,
    lower_up_maps,
    cotangent,
):
    local_rows, width = tokens.shape[1:]
    head_size = width // HEADS
    seq = local_rows * 32
    scale = head_size ** (-0.5)
    starts = document_starts[0]
    chosen = document_adapter[0]
    xl, c, z, y, xh = (lax.axis_index(a) for a in AXES)
    stream = xl * 2 + c
    first_row = ((z * 4 + y) * 2 + xh) * local_rows
    local_pos = first_row + jnp.arange(local_rows, dtype=jnp.int32)
    local_seg = jnp.sum((starts[None, :] <= local_pos[:, None]).astype(jnp.int32), axis=1) - 1
    doc_ids = jnp.arange(starts.shape[0], dtype=jnp.int32)
    token_adapter = jnp.sum(jnp.where(local_seg[:, None] == doc_ids[None, :], chosen[None, :], 0), axis=1)
    columns = jnp.arange(upper_down_maps.shape[1], dtype=jnp.int32) // ADAPTER_RANK
    mask = (token_adapter[:, None] == columns[None, :]).astype(f32)

    rows = seq // 2
    q_pos = positions_of(jnp.arange(rows, dtype=jnp.int32), xh)
    doc_lo = jnp.max(jnp.where(starts[None, :] <= q_pos[:, None], starts[None, :], 0), axis=1)
    first_tile = (doc_lo[::Q_TILE] // 256) * 128 // K_TILE
    info = jnp.concatenate([xh[None], first_tile]).astype(jnp.int32)
    last_key = (2 * ((jnp.arange(rows // K_TILE) + 1) * K_TILE // 128 - 1) + 1) * 128 + 127
    doc_end = jnp.min(jnp.where(starts[None, :] > last_key[:, None], starts[None, :], seq), axis=1)
    last_q_tile = jnp.minimum((doc_end + 255) // 256 * 128 + Q_TILE - 1, rows + Q_TILE - 1) // Q_TILE
    info_back = jnp.concatenate([xh[None], last_q_tile]).astype(jnp.int32)

    inputs = tokens[0].astype(f32)
    qkv_all, out_all, up_all, dn_all = gather_weights(
        jnp.transpose(projection_weight, (1, 0, 2)), output_weight, up_weight, down_weight
    )
    w_qkv = qkv_all.reshape(3, width, width)
    w_out = out_all.reshape(width, width)
    w_up = up_all.reshape(width, -1)
    w_down = dn_all.reshape(-1, width)
    hidden = w_up.shape[1]

    def mine(array, axis):
        return lax.dynamic_slice_in_dim(array, stream * hidden, hidden, axis)

    normed_one, norm_one_back = jax.vjp(
        lambda v: layer_norm(v, layernorm_gain[0], layernorm_bias[0]), inputs
    )
    first_in = normed_one.astype(bf16)
    adapt_qkv = (
        jnp.einsum("td,pdr->ptr", first_in, attention_down_maps[:3], preferred_element_type=f32) * mask
    ).astype(bf16)
    bias_rows = jnp.stack([projection_bias[0], jnp.zeros_like(projection_bias[0]), projection_bias[1]])
    projected = (
        jnp.einsum("td,pde->pte", first_in, w_qkv, preferred_element_type=f32)
        + bias_rows[:, None, :]
        + jnp.einsum("ptr,pre->pte", adapt_qkv, attention_up_maps[:3], preferred_element_type=f32)
    )
    by_token = projected.astype(bf16).reshape(3, local_rows, HEADS, head_size)
    by_head = lax.all_to_all(by_token, HEAD, split_axis=2, concat_axis=1, tiled=True)
    by_head = by_head.reshape(3, rows, head_size)
    across = lax.ppermute(by_head[1:], "xh", [(0, 1), (1, 0)])
    queries = by_head[0]
    attended, attended_low, lse = flash_forward(
        info, queries, doc_lo[:, None], by_head[1], by_head[2], across[0], across[1], scale
    )
    lse = lse.reshape(rows // Q_TILE, 8, Q_TILE)[:, 0]
    back = lax.all_to_all(
        attended_low.reshape(HEADS, local_rows, head_size), HEAD, split_axis=0, concat_axis=0, tiled=True
    )
    merged = jnp.transpose(back, (1, 0, 2)).reshape(local_rows, width)

    adapt_out = (dot(merged, attention_down_maps[3]) * mask).astype(bf16)
    residual = inputs + dot(merged, w_out) + projection_bias[2] + dot(adapt_out, attention_up_maps[3])
    normed_two, norm_two_back = jax.vjp(
        lambda v: layer_norm(v, layernorm_gain[1], layernorm_bias[1]), residual
    )
    second_in = normed_two.astype(bf16)
    adapt_up = (dot(second_in, upper_down_maps) * mask).astype(bf16)
    cot = cotangent[0]
    grad_adapt_down = (dot_nt(cot, lower_up_maps) * mask).astype(bf16)

    def to_all(*arrays):
        return lax.all_gather(jnp.concatenate(arrays, axis=1), STREAM, axis=0, tiled=True)

    def to_owner(*arrays):
        return lax.psum_scatter(
            jnp.concatenate(arrays, axis=1).astype(bf16), STREAM, scatter_dimension=0, tiled=True
        ).astype(f32)

    cot_all = to_all(cot, grad_adapt_down)
    cot_all, gad_all = cot_all[:, :width], cot_all[:, width:]
    second_all = to_all(second_in, adapt_up)
    second_all, up_low_all = second_all[:, :width], second_all[:, width:]
    my_up_maps = mine(upper_up_maps, 1)
    my_down_maps = mine(lower_down_maps, 0)
    grad_act = dot_nt(cot_all, w_down) + dot_nt(gad_all, my_down_maps)
    pre_act = dot(second_all, w_up) + mine(upper_bias, 0) + dot(up_low_all, my_up_maps)
    activated, gelu_back = jax.vjp(exact_gelu, pre_act)
    act_low = activated.astype(bf16)
    grad_pre = gelu_back(grad_act)[0].astype(bf16)
    back_sum = to_owner(dot_nt(grad_pre, w_up), dot_nt(grad_pre, my_up_maps))
    forth_sum = to_owner(dot(act_low, w_down), dot(act_low, my_down_maps))
    grad_b_up = dot_tn(up_low_all, grad_pre)
    grad_a_down = dot_tn(act_low, gad_all)

    adapt_down = (forth_sum[:, width:] * mask).astype(bf16)
    output = residual + forth_sum[:, :width] + projection_bias[3] + dot(adapt_down, lower_up_maps)
    grad_b_down = dot_tn(adapt_down, cot)

    grad_adapt_up = (back_sum[:, width:] * mask).astype(bf16)
    grad_a_up = dot_tn(second_in, grad_adapt_up)
    grad_second = back_sum[:, :width] + dot_nt(grad_adapt_up, upper_down_maps)
    grad_residual = cot.astype(f32) + norm_two_back(grad_second)[0]
    grad_branch = grad_residual.astype(bf16)
    grad_b_out = dot_tn(adapt_out, grad_branch)
    grad_adapt_out = (dot_nt(grad_branch, attention_up_maps[3]) * mask).astype(bf16)
    grad_a_out = dot_tn(merged, grad_adapt_out)
    grad_merged = (dot_nt(grad_branch, w_out) + dot_nt(grad_adapt_out, attention_down_maps[3])).astype(bf16)

    grad_heads = lax.all_to_all(
        jnp.transpose(grad_merged.reshape(local_rows, HEADS, head_size), (1, 0, 2)),
        HEAD, split_axis=0, concat_axis=0, tiled=True,
    ).reshape(rows, head_size)
    row_dot = jnp.sum(grad_heads.astype(f32) * attended, axis=-1).reshape(rows // Q_TILE, Q_TILE)
    dq, dk, dv = flash_backward(
        info_back, queries, grad_heads, lse, row_dot, doc_lo.reshape(rows // Q_TILE, Q_TILE),
        jnp.stack([across[0], by_head[1]]), jnp.stack([across[1], by_head[2]]), scale,
    )
    from_other = lax.ppermute(jnp.stack([dk[0], dv[0]]).astype(bf16), "xh", [(0, 1), (1, 0)])
    dk = (dk[1] + from_other[0].astype(f32)).astype(bf16)
    dv = (dv[1] + from_other[1].astype(f32)).astype(bf16)
    grad_stack = jnp.stack([dq, dk, dv]).reshape(3, HEADS, local_rows, head_size)
    grad_tokens = lax.all_to_all(grad_stack, HEAD, split_axis=1, concat_axis=1, tiled=True)
    grad_qkv = jnp.transpose(grad_tokens, (0, 2, 1, 3)).reshape(3, local_rows, width)

    grad_b_qkv = jnp.einsum("ptr,pte->pre", adapt_qkv, grad_qkv, preferred_element_type=f32)
    grad_adapt_qkv = (
        jnp.einsum("pte,pre->ptr", grad_qkv, attention_up_maps[:3], preferred_element_type=f32) * mask
    ).astype(bf16)
    grad_a_qkv = jnp.einsum("td,ptr->pdr", first_in, grad_adapt_qkv, preferred_element_type=f32)
    grad_first = jnp.einsum("pte,pde->td", grad_qkv, w_qkv, preferred_element_type=f32) + jnp.einsum(
        "ptr,pdr->td", grad_adapt_qkv, attention_down_maps[:3], preferred_element_type=f32
    )
    input_grad = grad_residual + norm_one_back(grad_first)[0]

    grad_a_attn = jnp.concatenate([grad_a_qkv, grad_a_out[None]], axis=0)
    grad_b_attn = jnp.concatenate([grad_b_qkv, grad_b_out[None]], axis=0)
    sums = lax.psum((grad_a_attn, grad_b_attn, grad_a_up, grad_b_down), AXES)
    part_b, part_a = lax.psum((grad_b_up, grad_a_down), TOKEN)
    full_b_up = lax.all_gather(part_b, STREAM, axis=1, tiled=True)
    full_a_down = lax.all_gather(part_a, STREAM, axis=0, tiled=True)
    return (
        output.astype(bf16)[None],
        input_grad.astype(bf16)[None],
        sums[0],
        sums[1],
        sums[2],
        full_b_up,
        full_a_down,
        sums[3],
    )


def solution(mesh):
    fine = jax.sharding.Mesh(mesh.devices.reshape(SIZES), AXES)
    by_token = P(STREAM, TOKEN, None)
    shard = AXES
    in_specs = (
        by_token,
        P(STREAM, None),
        P(STREAM, None),
        P(),
        P(),
        P(shard, None, None),
        P(shard, None),
        P(shard, None),
        P(shard, None),
        P(),
        P(),
        P(),
        P(),
        P(),
        P(),
        P(),
        P(),
        by_token,
    )
    out_specs = (by_token, by_token, P(), P(), P(), P(), P(), P())
    return jax.shard_map(per_device, mesh=fine, in_specs=in_specs, out_specs=out_specs, check_vma=False)
```

```python
import functools

import jax
import jax.numpy as jnp
import numpy as np
from jax import lax
from jax.experimental import pallas as pl
from jax.experimental.pallas import tpu as pltpu
from jax.sharding import PartitionSpec as P

HEADS = 16
ADAPTER_RANK = 16
MESH = pl.DeviceIdType.MESH
AXES = ("xl", "c", "z", "y", "xh")
SIZES = (2, 2, 4, 4, 2)
STREAM = ("xl", "c")
TOKEN = ("z", "y", "xh")
HEAD = ("z", "y")
bf16 = jnp.bfloat16
f32 = jnp.float32
LOG2E = 1.4426950408889634
MIB = 2**20
Q_TILE = 256
K_TILE = 512


def layer_norm(values, gain, shift):
    center = values - jnp.mean(values, axis=-1, keepdims=True)
    spread = jnp.mean(center * center, axis=-1, keepdims=True)
    return center * lax.rsqrt(spread + 1e-05) * gain + shift


def dot(left, right):
    return jnp.dot(left, right, preferred_element_type=f32)


def dot_nt(left, right):
    return lax.dot_general(left, right, (((1,), (1,)), ((), ())), preferred_element_type=f32)


def dot_tn(left, right):
    return lax.dot_general(left, right, (((0,), (0,)), ((), ())), preferred_element_type=f32)


def exact_gelu(values):
    return jax.nn.gelu(values, approximate=False)


class Place:
    def __init__(self):
        self.xl, self.c, self.z, self.y, self.xh = (lax.axis_index(a) for a in AXES)
        self.x = self.xh * 2 + self.xl

    def at(self, axis):
        return {"x": self.x, "y": self.y, "z": self.z, "xh": self.xh}[axis]

    def toward(self, axis, step):
        if axis == "c":
            return {"c": 1 - self.c}
        if axis == "xh":
            return {"xh": 1 - self.xh}
        to = lax.rem(self.at(axis) + (step + 4), 4)
        if axis == "x":
            return {"xl": lax.rem(to, 2), "xh": to // 2}
        return {axis: to}


class Sends:
    def __init__(self, send, recv):
        self.send, self.recv, self.used, self.open = send, recv, 0, []

    def push(self, src, dst, device):
        k = self.used
        self.used += 1
        copy = pltpu.make_async_remote_copy(
            src_ref=src,
            dst_ref=dst,
            send_sem=self.send.at[k],
            recv_sem=self.recv.at[k],
            device_id=device,
            device_id_type=MESH,
        )
        copy.start()
        self.open.append(copy)
        return copy


def greet(devices):
    barrier = pltpu.get_barrier_semaphore()
    for device in devices:
        pl.semaphore_signal(barrier, inc=1, device_id=device, device_id_type=MESH)
    pl.semaphore_wait(barrier, len(devices))


def run_all(parts):
    parts = list(parts)
    while parts:
        left = []
        for part in parts:
            try:
                next(part)
                left.append(part)
            except StopIteration:
                pass
        parts = left


ALL = slice(None)


def ring_gather(place, sends, view, order, chunk, landed, forward):
    fixed = {a: place.at(a) for a in order}
    across = place.toward("c", 1)
    later, passed = [], []

    def pass_on(block):
        if forward:
            passed.append(sends.push(view(block, None), view(block, None), across))

    if forward:
        passed.append(sends.push(chunk, view(fixed, None), across))
    for number, axis in enumerate(order):
        own = view(fixed, None)
        src = chunk if number == 0 else own
        here = place.at(axis)
        if axis == "xh" or number == 0:
            steps = (1,) if axis == "xh" else (2, 1, 3)
            sent = [sends.push(src, own, place.toward(axis, s)) for s in steps]
            yield
            for s, copy in zip(steps, sent):
                copy.wait_recv()
                size = 2 if axis == "xh" else 4
                pass_on(dict(fixed) | {axis: lax.rem(here + size - s, size)})
            if number == 0:
                landed.wait()
            later += sent
            del fixed[axis]
            continue
        up = sends.push(src, own, place.toward(axis, 1))
        down = sends.push(src, own, place.toward(axis, -1))
        yield
        before = dict(fixed) | {axis: lax.rem(here + 3, 4)}
        after = dict(fixed) | {axis: lax.rem(here + 1, 4)}
        opposite = dict(fixed) | {axis: lax.rem(here + 2, 4)}
        up.wait_recv()
        half = view(before, 0)
        up_two = sends.push(half, half, place.toward(axis, 1))
        down.wait_recv()
        half = view(after, 1)
        down_two = sends.push(half, half, place.toward(axis, -1))
        pass_on(before)
        pass_on(after)
        yield
        up_two.wait_recv()
        down_two.wait_recv()
        pass_on(opposite)
        later += [up, down, up_two, down_two]
        del fixed[axis]
    yield
    for copy in later:
        copy.wait_send()
    for copy in passed:
        copy.wait()


class Nothing:
    def wait(self):
        pass


def neighbours(place, axes):
    return [place.toward(a, s) for a in axes for s in ((1, 2, 3) if a in "xyz" else (1,))]


def stream_gather(place, sends, pairs, local, first_local):
    across, over = {"c": 1 - place.c}, {"xl": 1 - place.xl}
    mine = place.xl * 2 + place.c
    theirs = (1 - place.xl) * 2 + place.c
    sent, passed, kept = [], [], []
    for n, (src, dst) in enumerate(pairs):
        sent.append(sends.push(src, dst.at[mine], over))
        passed.append(sends.push(src, dst.at[mine], across))
        copy = pltpu.make_async_copy(src, dst.at[mine], local.at[first_local + n])
        copy.start()
        kept.append(copy)
    yield
    for copy, (src, dst) in zip(sent, pairs):
        copy.wait_recv()
        passed.append(sends.push(dst.at[theirs], dst.at[theirs], across))
    yield
    for copy in sent:
        copy.wait_send()
    for copy in passed + kept:
        copy.wait()


def stream_gather_kernel(a, b, a_all, b_all, send, recv, local):
    place = Place()
    greet([{"c": 1 - place.c}, {"xl": 1 - place.xl}])
    pieces = [(a.at[pl.ds(r, 32)], a_all.at[:, pl.ds(r, 32)]) for r in range(0, 128, 32)] + [(b, b_all)]
    run_all([stream_gather(place, Sends(send, recv), pieces, local, 0)])


def gather_stream(a, b):
    any_ = pl.BlockSpec(memory_space=pl.ANY)
    return pl.pallas_call(
        stream_gather_kernel,
        name="gather_stream",
        out_shape=[jax.ShapeDtypeStruct((4,) + v.shape, v.dtype) for v in (a, b)],
        in_specs=[any_] * 2,
        out_specs=[any_] * 2,
        scratch_shapes=[pltpu.SemaphoreType.DMA((n,)) for n in (15, 15, 5)],
        compiler_params=pltpu.CompilerParams(collective_id=1, has_side_effects=True),
    )(a, b)


def stream_sum(place, sends, pairs):
    across, over = {"c": 1 - place.c}, {"xl": 1 - place.xl}
    mine = place.xl * 2 + place.c
    theirs = (1 - place.xl) * 2 + place.c
    far, near = [], []
    for parts, from_core, _, _, _ in pairs:
        far.append(sends.push(parts.at[(1 - place.xl) * 2 + 1 - place.c], from_core.at[1], across))
    for parts, from_core, _, _, _ in pairs:
        near.append(sends.push(parts.at[place.xl * 2 + 1 - place.c], from_core.at[0], across))
    gone = []
    for copy, (parts, from_core, leaving, from_chip, _) in zip(far, pairs):
        copy.wait()
        leaving[...] = (parts[theirs].astype(f32) + from_core[1].astype(f32)).astype(bf16)
        gone.append(sends.push(leaving, from_chip, over))
    yield
    for copy, back, (parts, from_core, _, from_chip, result) in zip(near, gone, pairs):
        copy.wait()
        back.wait()
        result[...] = parts[mine].astype(f32) + from_core[0].astype(f32) + from_chip[...].astype(f32)


def stream_sum_scratch(arrays):
    shapes = []
    for a in arrays:
        one = a.shape[1:]
        shapes += [pltpu.VMEM((2,) + one, bf16), pltpu.VMEM(one, bf16), pltpu.VMEM(one, bf16)]
    return shapes


def stream_sum_kernel(a, b, a_sum, b_sum, a_core, a_leave, a_chip, b_core, b_leave, b_chip, send, recv):
    place = Place()
    greet([{"c": 1 - place.c}, {"xl": 1 - place.xl}])
    pairs = [(a, a_core, a_leave, a_chip, a_sum), (b, b_core, b_leave, b_chip, b_sum)]
    run_all([stream_sum(place, Sends(send, recv), pairs)])


def sum_stream(a, b):
    vmem = pl.BlockSpec(memory_space=pltpu.VMEM)
    return pl.pallas_call(
        stream_sum_kernel,
        name="sum_stream",
        out_shape=[jax.ShapeDtypeStruct(v.shape[1:], f32) for v in (a, b)],
        in_specs=[vmem] * 2,
        out_specs=[vmem] * 2,
        scratch_shapes=stream_sum_scratch((a, b)) + [pltpu.SemaphoreType.DMA((6,)), pltpu.SemaphoreType.DMA((6,))],
        compiler_params=pltpu.CompilerParams(collective_id=2, has_side_effects=True, vmem_limit_bytes=40 * MIB),
    )(a, b)


def plane(place):
    steps = [(i, j) for i in (2, 1, 3, 0) for j in (2, 1, 3, 0) if i or j]
    return [(lax.rem(place.z + i, 4), lax.rem(place.y + j, 4)) for i, j in steps]


def from_plane(place):
    steps = [(i, j) for i in (2, 1, 3, 0) for j in (2, 1, 3, 0) if i or j]
    return [(lax.rem(place.z + 4 - i, 4), lax.rem(place.y + 4 - j, 4)) for i, j in steps]


def head_columns(z, y):
    return pl.ds(pl.multiple_of((z * 4 + y) * 128, 128), 128)


def greet_plane(place, more=()):
    greet([{"z": z, "y": y} for z, y in plane(place)] + list(more))


def to_heads_kernel(qkv, mine, others, send, recv, local):
    place = Place()
    partner = {"xh": 1 - place.xh}
    greet_plane(place, [partner])
    sends = Sends(send, recv)
    here = place.z * 4 + place.y
    own = qkv.at[:, :, head_columns(place.z, place.y)]
    keep = pltpu.make_async_copy(own, mine.at[:, here], local.at[0])
    keep.start()
    kv = pl.ds(1, 2)
    swaps = [sends.push(qkv.at[kv, :, head_columns(place.z, place.y)], others.at[:, here], partner)]
    sent = []
    for z, y in plane(place):
        sent.append(sends.push(qkv.at[:, :, head_columns(z, y)], mine.at[:, here], {"z": z, "y": y}))
    for copy, (z, y) in zip(sent, from_plane(place)):
        copy.wait_recv()
        at = z * 4 + y
        swaps.append(sends.push(mine.at[kv, at], others.at[:, at], partner))
    for copy in sent:
        copy.wait_send()
    for copy in swaps:
        copy.wait()
    keep.wait()


def to_heads(qkv):
    any_ = pl.BlockSpec(memory_space=pl.ANY)
    return pl.pallas_call(
        to_heads_kernel,
        name="to_heads",
        out_shape=[jax.ShapeDtypeStruct((3, 16, 128, 128), bf16), jax.ShapeDtypeStruct((2, 16, 128, 128), bf16)],
        in_specs=[any_],
        out_specs=[any_] * 2,
        scratch_shapes=[pltpu.SemaphoreType.DMA((n,)) for n in (31, 31, 1)],
        compiler_params=pltpu.CompilerParams(collective_id=3, has_side_effects=True),
    )(qkv)


def heads_out(place, sends, blocks, merged, local):
    cols = head_columns(place.z, place.y)
    keep = pltpu.make_async_copy(blocks.at[place.z * 4 + place.y], merged.at[:, cols], local)
    keep.start()
    sent = [sends.push(blocks.at[z * 4 + y], merged.at[:, cols], {"z": z, "y": y}) for z, y in plane(place)]
    yield
    for copy in sent:
        copy.wait()
    keep.wait()


def to_tokens_kernel(blocks, merged, send, recv, local):
    place = Place()
    greet_plane(place)
    run_all([heads_out(place, Sends(send, recv), blocks, merged, local.at[0])])


def to_tokens(blocks):
    any_ = pl.BlockSpec(memory_space=pl.ANY)
    return pl.pallas_call(
        to_tokens_kernel,
        name="to_tokens",
        out_shape=jax.ShapeDtypeStruct((128, 2048), bf16),
        in_specs=[any_],
        out_specs=any_,
        scratch_shapes=[pltpu.SemaphoreType.DMA((n,)) for n in (15, 15, 1)],
        compiler_params=pltpu.CompilerParams(collective_id=4, has_side_effects=True),
    )(blocks)


def grads_in_kernel(
    grad, a, b, heads, a_sum, b_sum, a_core, a_leave, a_chip, b_core, b_leave, b_chip, send, recv, local
):
    place = Place()
    greet_plane(place, [{"c": 1 - place.c}, {"xl": 1 - place.xl}])
    sends = Sends(send, recv)

    def heads_part():
        here = place.z * 4 + place.y
        keep = pltpu.make_async_copy(grad.at[:, head_columns(place.z, place.y)], heads.at[here], local.at[0])
        keep.start()
        sent = [
            sends.push(grad.at[:, head_columns(z, y)], heads.at[here], {"z": z, "y": y}) for z, y in plane(place)
        ]
        yield
        for copy in sent:
            copy.wait()
        keep.wait()

    pairs = [(a, a_core, a_leave, a_chip, a_sum), (b, b_core, b_leave, b_chip, b_sum)]
    run_all([heads_part(), stream_sum(place, sends, pairs)])


def grads_in(grad, a, b):
    any_ = pl.BlockSpec(memory_space=pl.ANY)
    vmem = pl.BlockSpec(memory_space=pltpu.VMEM)
    return pl.pallas_call(
        grads_in_kernel,
        name="grads_in",
        out_shape=[jax.ShapeDtypeStruct((16, 128, 128), bf16)]
        + [jax.ShapeDtypeStruct(v.shape[1:], f32) for v in (a, b)],
        in_specs=[any_] + [vmem] * 2,
        out_specs=[any_] + [vmem] * 2,
        scratch_shapes=stream_sum_scratch((a, b)) + [pltpu.SemaphoreType.DMA((n,)) for n in (21, 21, 1)],
        compiler_params=pltpu.CompilerParams(collective_id=5, has_side_effects=True, vmem_limit_bytes=40 * MIB),
    )(grad, a, b)


def grads_out_kernel(dq, other, own, grads, came, sums, send, recv, local):
    place = Place()
    partner = {"xh": 1 - place.xh}
    greet_plane(place, [partner])
    sends = Sends(send, recv)
    cols = head_columns(place.z, place.y)
    here = place.z * 4 + place.y
    places = plane(place) + [(place.z, place.y)]
    swaps = [sends.push(other.at[z * 4 + y], came.at[z * 4 + y], partner) for z, y in places]
    keep = pltpu.make_async_copy(dq.at[here], grads.at[0, :, cols], local.at[0])
    keep.start()
    sent = [sends.push(dq.at[z * 4 + y], grads.at[0, :, cols], {"z": z, "y": y}) for z, y in places[:-1]]
    for n, (copy, (z, y)) in enumerate(zip(swaps, places)):
        copy.wait_recv()
        at = z * 4 + y
        sums[at] = (came[at].astype(f32) + own[at]).astype(bf16)
        if n < 15:
            sent.append(sends.push(sums.at[at], grads.at[pl.ds(1, 2), :, cols], {"z": z, "y": y}))
    last = pltpu.make_async_copy(sums.at[here], grads.at[pl.ds(1, 2), :, cols], local.at[1])
    last.start()
    for copy in swaps:
        copy.wait_send()
    for copy in sent:
        copy.wait()
    keep.wait()
    last.wait()


def grads_out(dq, other, own):
    any_ = pl.BlockSpec(memory_space=pl.ANY)
    vmem = pl.BlockSpec(memory_space=pltpu.VMEM)
    return pl.pallas_call(
        grads_out_kernel,
        name="grads_out",
        out_shape=jax.ShapeDtypeStruct((3, 128, 2048), bf16),
        in_specs=[vmem] * 3,
        out_specs=any_,
        scratch_shapes=[pltpu.VMEM((16, 2, 128, 128), bf16)] * 2
        + [pltpu.SemaphoreType.DMA((n,)) for n in (46, 46, 2)],
        compiler_params=pltpu.CompilerParams(collective_id=6, has_side_effects=True, vmem_limit_bytes=40 * MIB),
    )(dq, other, own)


ORDERS = (("x", "y", "z"), ("y", "z", "x"), ("z", "x", "y"))


def spread_sum(place, sends, order, steps, first, result_view, final, landed, across):
    if across:
        src, came, own, out = first
        copy = sends.push(src, came, place.toward("c", 1))
        yield
        copy.wait()
        out[...] = (own[...].astype(f32) + came[...].astype(f32)).astype(bf16)
    for axis, (held, slots, out) in zip(order, steps):
        size = 2 if axis == "xh" else 4
        here = place.at(axis)
        hops = (1,) if size == 2 else (2, 1, 3)
        sent = [
            sends.push(held(lax.rem(here + d, size)), slots.at[d - 1], place.toward(axis, d)) for d in hops
        ]
        yield
        for copy in sent:
            copy.wait()
        total = held(here)[...].astype(f32)
        for d in hops:
            total = total + slots[d - 1].astype(f32)
        out[...] = total.astype(bf16)
    landed.start()
    yield from ring_gather(place, sends, result_view[0], result_view[1], final, landed, True)


def rows_of(ref, size):
    return lambda p: ref.at[pl.ds(pl.multiple_of(p * size, size), size)]


def cols_of(ref, size):
    return lambda p: ref.at[:, pl.ds(pl.multiple_of(p * size, size), size)]


def sums_kernel(count, early, *refs):
    refs = list(refs)
    a, b = refs[:2]
    del refs[:2]
    if early:
        a_two, b_two = refs[:2]
        del refs[:2]
    a_res, b_res = refs[:2]
    del refs[:2]
    if early:
        a_two_res, b_two_res = refs[:2]
        del refs[:2]
    scratch, (send, recv, local) = refs[:-3], refs[-3:]
    place = Place()
    sends = Sends(send, recv)
    greet(neighbours(place, ("x", "y", "z", "c")))
    parts = []
    mine, theirs = place.c, 1 - place.c

    def line(fixed, axis):
        return fixed.get(axis, ALL)

    def a_view(i, order):
        def view(fixed, half):
            at = [line(fixed, x) for x in order]
            if half is not None:
                k = max(n for n in range(3) if order[n] not in fixed)
                at[k] = pl.ds(half * 2, 2)
            return a_res.at[(i, place.c) + tuple(at)]

        return view

    def b_view(i, order):
        def view(fixed, half):
            start, size = 0, 2048
            if order[1] in fixed:
                start, size = fixed[order[1]] * 512, 512
            if order[2] in fixed:
                start, size = start + fixed[order[2]] * 128, 128
            if half is not None:
                size = size // 2
                start = start + half * size
            cols = pl.ds(start, size) if isinstance(start, int) else pl.ds(pl.multiple_of(start, 128), size)
            return b_res.at[i, place.c, line(fixed, order[0]), :, cols]

        return view

    for i in range(count):
        order = ORDERS[i % 3]
        ca, ha, sa1, qa, sa2, ra, sa3, fa, cb, hb, sb1, qb, sb2, rb, sb3, fb = scratch[:16]
        del scratch[:16]
        half = lambda c, n: pl.ds(pl.multiple_of(c * n, n), n)
        keep = pltpu.make_async_copy(
            fa, a_view(i, order)({x: place.at(x) for x in order}, None), local.at[2 * i]
        )
        parts.append(
            spread_sum(
                place, sends, order,
                [(rows_of(ha, 256), sa1, qa), (rows_of(qa, 64), sa2, ra), (rows_of(ra, 16), sa3, fa)],
                (a.at[i, half(theirs, 1024)], ca, a.at[i, half(mine, 1024)], ha),
                (a_view(i, order), order[::-1]), fa, keep, True,
            )
        )
        keep = pltpu.make_async_copy(
            fb, b_view(i, order)({x: place.at(x) for x in order}, None), local.at[2 * i + 1]
        )
        parts.append(
            spread_sum(
                place, sends, order,
                [(rows_of(hb, 16), sb1, qb), (cols_of(qb, 512), sb2, rb), (cols_of(rb, 128), sb3, fb)],
                (b.at[i, half(theirs, 64)], cb, b.at[i, half(mine, 64)], hb),
                (b_view(i, order), order[::-1]), fb, keep, True,
            )
        )
    if early:
        sa1, qa, sa2, ra, sa3, fa, sb1, qb, sb2, rb, sb3, fb = scratch

        def two(ref):
            def view(fixed, half):
                xl, xh = (ALL, ALL)
                if "x" in fixed:
                    xl, xh = lax.rem(fixed["x"], 2), fixed["x"] // 2
                if half is not None:
                    xl = pl.ds(half, 1)
                return ref.at[xl, place.c, line(fixed, "z"), line(fixed, "y"), xh]

            return view

        home = {x: place.at(x) for x in "xyz"}
        keep = pltpu.make_async_copy(fa, two(a_two_res)(home, None), local.at[2 * count])
        parts.append(
            spread_sum(
                place, sends, ("z", "y", "xh"),
                [(rows_of(a_two, 512), sa1, qa), (rows_of(qa, 128), sa2, ra), (rows_of(ra, 64), sa3, fa)],
                None, (two(a_two_res), ("x", "z", "y")), fa, keep, False,
            )
        )
        keep = pltpu.make_async_copy(fb, two(b_two_res)(home, None), local.at[2 * count + 1])
        parts.append(
            spread_sum(
                place, sends, ("y", "z", "xh"),
                [(rows_of(b_two, 32), sb1, qb), (cols_of(qb, 512), sb2, rb), (cols_of(rb, 256), sb3, fb)],
                None, (two(b_two_res), ("x", "y", "z")), fb, keep, False,
            )
        )
    run_all(parts)


def sum_all(collective_id, a, b, a_two=None, b_two=None):
    count = a.shape[0]
    early = a_two is not None
    vm = lambda *shape: pltpu.VMEM(shape, bf16)
    scratch = []
    for _ in range(count):
        scratch += [vm(1024, 128), vm(1024, 128), vm(3, 256, 128), vm(256, 128), vm(3, 64, 128), vm(64, 128)]
        scratch += [vm(3, 16, 128), vm(16, 128)]
        scratch += [vm(64, 2048), vm(64, 2048), vm(3, 16, 2048), vm(16, 2048), vm(3, 16, 512), vm(16, 512)]
        scratch += [vm(3, 16, 128), vm(16, 128)]
    shapes = [(count, 2, 4, 4, 4, 16, 128), (count, 2, 4, 16, 2048)]
    ins = [a, b]
    if early:
        scratch += [vm(3, 512, 128), vm(512, 128), vm(3, 128, 128), vm(128, 128), vm(1, 64, 128), vm(64, 128)]
        scratch += [vm(3, 32, 2048), vm(32, 2048), vm(3, 32, 512), vm(32, 512), vm(1, 32, 256), vm(32, 256)]
        shapes += [(2, 2, 4, 4, 2, 64, 128), (2, 2, 4, 4, 2, 32, 256)]
        ins += [a_two, b_two]
    n = 62 * count + (60 if early else 0)
    out = pl.pallas_call(
        functools.partial(sums_kernel, count, early),
        name="sum_all",
        out_shape=[jax.ShapeDtypeStruct(s, bf16) for s in shapes],
        in_specs=[pl.BlockSpec(memory_space=pltpu.VMEM)] * len(ins),
        out_specs=[pl.BlockSpec(memory_space=pl.ANY)] * len(shapes),
        scratch_shapes=scratch
        + [pltpu.SemaphoreType.DMA((k,)) for k in (n, n, 2 * count + 2)],
        compiler_params=pltpu.CompilerParams(
            collective_id=collective_id, has_side_effects=True, vmem_limit_bytes=48 * MIB
        ),
    )(*ins)
    result = [out[0].reshape(count, 2048, 128), out[1].reshape(count, 128, 2048)]
    if early:
        result.append(out[2].reshape(8192, 128))
        result.append(jnp.transpose(out[3], (3, 5, 0, 1, 2, 4, 6)).reshape(128, 8192))
    return result


def weights_kernel(wp, wo, up, dn, cot, gad, qkv_all, out_all, up_all, dn_all, cot_all, gad_all, send, recv, local):
    place = Place()
    sends = Sends(send, recv)
    mates = [{"c": 1 - place.c}, {"xl": 1 - place.xl}, {"xl": 1 - place.xl, "c": 1 - place.c}]
    greet([mates[0], mates[2]] + neighbours(place, ("x", "y", "z")))
    home = (place.xl, place.c, place.z, place.y, place.xh)

    halves = {None: ALL, 0: pl.ds(0, 1024), 1: pl.ds(1024, 1024)}

    def whole(ref, lead):
        def view(fixed, half):
            columns = halves[half]
            xl, xh = (ALL, ALL)
            if "x" in fixed:
                xl, xh = lax.rem(fixed["x"], 2), fixed["x"] // 2
            return ref.at[lead + (xl, place.c, fixed.get("z", ALL), fixed.get("y", ALL), xh, ALL, columns)]

        return view

    def up_view(fixed, half):
        columns = halves[half]
        return up_all.at[ALL, ALL, fixed.get("z", ALL), fixed.get("y", ALL), fixed.get("xh", ALL), ALL, columns]

    def dn_view(fixed, half):
        columns = halves[half]
        return dn_all.at[fixed.get("z", ALL), fixed.get("y", ALL), fixed.get("xh", ALL), ALL, columns]

    stream = place.xl * 2 + place.c

    def cols(device):
        to = device.get("xl", place.xl) * 2 + device.get("c", place.c)
        return pl.ds(pl.multiple_of(to * 2048, 2048), 2048)

    copies = [pltpu.make_async_copy(wp.at[p], qkv_all.at[(p,) + home], local.at[p]) for p in range(3)]
    copies.append(pltpu.make_async_copy(wo, out_all.at[home], local.at[3]))
    copies.append(pltpu.make_async_copy(dn, dn_all.at[home[2:]], local.at[4]))
    copies.append(pltpu.make_async_copy(up.at[:, cols({})], up_all.at[home], local.at[5]))
    for copy in copies:
        copy.start()
    spread = [sends.push(up.at[:, cols(m)], up_all.at[home], m) for m in mates]

    class Many:
        def wait(self):
            copies[5].wait()
            for s in spread:
                s.wait()

    def up_part():
        yield
        Many().wait()
        fixed = {"xh": place.xh, "y": place.y, "z": place.z}
        yield from ring_gather(place, sends, up_view, ("xh", "y", "z"), up_view(fixed, None), Nothing(), False)

    parts = [
        stream_gather(place, sends, ((cot, cot_all), (gad, gad_all)), local, 6),
        ring_gather(place, sends, whole(qkv_all, (0,)), ("y", "z", "x"), wp.at[0], copies[0], True),
        ring_gather(place, sends, whole(qkv_all, (1,)), ("z", "y", "x"), wp.at[1], copies[1], True),
        ring_gather(place, sends, whole(qkv_all, (2,)), ("x", "y", "z"), wp.at[2], copies[2], True),
        ring_gather(place, sends, whole(out_all, ()), ("x", "z", "y"), wo, copies[3], True),
        up_part(),
        ring_gather(place, sends, dn_view, ("xh", "z", "y"), dn, copies[4], False),
    ]
    run_all(parts)


def gather_weights(wp, wo, up, dn, cot, gad):
    n = 180
    any_ = pl.BlockSpec(memory_space=pl.ANY)
    return pl.pallas_call(
        weights_kernel,
        name="gather_weights",
        out_shape=[
            jax.ShapeDtypeStruct((3, 2, 2, 4, 4, 2, 16, 2048), bf16),
            jax.ShapeDtypeStruct((2, 2, 4, 4, 2, 16, 2048), bf16),
            jax.ShapeDtypeStruct((2, 2, 4, 4, 2, 16, 2048), bf16),
            jax.ShapeDtypeStruct((4, 4, 2, 64, 2048), bf16),
            jax.ShapeDtypeStruct((4, 128, 2048), bf16),
            jax.ShapeDtypeStruct((4, 128, 128), bf16),
        ],
        in_specs=[any_] * 6,
        out_specs=[any_] * 6,
        scratch_shapes=[
            pltpu.SemaphoreType.DMA((n,)),
            pltpu.SemaphoreType.DMA((n,)),
            pltpu.SemaphoreType.DMA((8,)),
        ],
        compiler_params=pltpu.CompilerParams(collective_id=0, has_side_effects=True),
    )(wp, wo, up, dn, cot, gad)


def positions_of(local, parity):
    return (2 * (local // 128) + parity) * 128 + lax.rem(local, 128)


def flash_kernel(info, lo_ref, q_ref, ko_ref, vo_ref, kx_ref, vx_ref, o_ref, low_ref, lse_ref, *, scale):
    tile = pl.program_id(0)
    parity = info[0]
    first = info[1 + tile]
    last = (tile * Q_TILE + Q_TILE + K_TILE - 1) // K_TILE
    q = q_ref[0]
    q_pos = positions_of(tile * Q_TILE + lax.broadcasted_iota(jnp.int32, (Q_TILE, 1), 0), parity)
    lo = lo_ref[...]
    ones = jnp.ones((K_TILE, 128), bf16)

    def step(kt, carry):
        top, acc = carry
        rows = pl.ds(pl.multiple_of(kt * K_TILE, K_TILE), K_TILE)
        local = kt * K_TILE + lax.broadcasted_iota(jnp.int32, (1, K_TILE), 1)
        scores = []
        for k_ref, par in ((ko_ref, parity), (kx_ref, 1 - parity)):
            k_pos = positions_of(local, par)
            s = dot_nt(q, k_ref[0, rows, :])
            scores.append(jnp.where((k_pos >= lo) & (k_pos <= q_pos), s, -1e30))
        new = jnp.maximum(jnp.max(scores[0], axis=1, keepdims=True), jnp.max(scores[1], axis=1, keepdims=True))
        new = jnp.maximum(top, new)
        acc = acc * jnp.exp2((top - new) * (scale * LOG2E))
        for s, v_ref in zip(scores, (vo_ref, vx_ref)):
            p = jnp.exp2((s - new) * (scale * LOG2E)).astype(bf16)
            acc = acc + dot(p, jnp.concatenate([v_ref[0, rows, :], ones], axis=1))
        return new, acc

    top, acc = lax.fori_loop(
        first, last, step, (jnp.full((Q_TILE, 1), -1e30, f32), jnp.zeros((Q_TILE, 256), f32))
    )
    total = acc[:, 128:]
    o = acc[:, :128] / total
    o_ref[...] = o
    low_ref[...] = o.astype(bf16)
    lse = top * (scale * LOG2E) + jnp.log2(total)
    lse_ref[...] = jnp.transpose(lse)[0:8, :]


def flash_forward(info, lo, by_head, across, scale):
    rows = by_head.shape[1]
    tiles = rows // Q_TILE
    whole = lambda n: pl.BlockSpec((1, rows, 128), lambda t, s: (n, 0, 0))
    block = pl.BlockSpec((Q_TILE, 128), lambda t, s: (t, 0))
    return pl.pallas_call(
        functools.partial(flash_kernel, scale=scale),
        name="attention_forward",
        grid_spec=pltpu.PrefetchScalarGridSpec(
            num_scalar_prefetch=1,
            grid=(tiles,),
            in_specs=[
                pl.BlockSpec((Q_TILE, 1), lambda t, s: (t, 0)),
                pl.BlockSpec((1, Q_TILE, 128), lambda t, s: (0, t, 0)),
                whole(1), whole(2), whole(0), whole(1),
            ],
            out_specs=[block, block, pl.BlockSpec((8, Q_TILE), lambda t, s: (t, 0))],
        ),
        out_shape=[
            jax.ShapeDtypeStruct((rows, 128), f32),
            jax.ShapeDtypeStruct((rows, 128), bf16),
            jax.ShapeDtypeStruct((tiles * 8, Q_TILE), f32),
        ],
        compiler_params=pltpu.CompilerParams(vmem_limit_bytes=40 * MIB),
    )(info, lo, by_head, by_head, by_head, across, across)


def flash_back_kernel(
    info, q_ref, do_ref, lse_ref, delta_ref, lo_ref, ko_ref, vo_ref, kx_ref, vx_ref, dq_ref, other_ref, own_ref, dq_acc, *, scale
):
    kt = pl.program_id(0)
    parity = info[0]

    @pl.when(kt == 0)
    def _():
        dq_acc[...] = jnp.zeros_like(dq_acc)

    first = kt * (K_TILE // Q_TILE)
    last = info[1 + kt]
    blocks = K_TILE // 128
    for k_ref, v_ref, k_parity, out in ((kx_ref, vx_ref, 1 - parity, other_ref), (ko_ref, vo_ref, parity, own_ref)):
        k = k_ref[0]
        v = v_ref[0]
        k_pos = positions_of(kt * K_TILE + lax.broadcasted_iota(jnp.int32, (K_TILE, 1), 0), k_parity)

        def step(qt, carry):
            dk, dv = carry
            rows = pl.ds(pl.multiple_of(qt * Q_TILE, Q_TILE), Q_TILE)
            q = q_ref[0, rows, :]
            do = do_ref[rows, :]
            q_pos = positions_of(qt * Q_TILE + lax.broadcasted_iota(jnp.int32, (1, Q_TILE), 1), parity)
            lo = lo_ref[pl.ds(qt, 1), :]
            lse = lse_ref[pl.ds(qt, 1), :]
            delta = delta_ref[pl.ds(qt, 1), :]
            s = dot_nt(k, q)
            p = jnp.exp2(jnp.where((k_pos >= lo) & (k_pos <= q_pos), s * (scale * LOG2E) - lse, -1e30))
            dv = dv + dot(p.astype(bf16), do)
            dp = dot_nt(v, do)
            ds = (p * (dp - delta) * scale).astype(bf16)
            dk = dk + dot(ds, q)
            dq_acc[rows, :] += dot_tn(ds, k)
            return dk, dv

        zero = jnp.zeros((K_TILE, 128), f32)
        dk, dv = lax.fori_loop(first, last, step, (zero, zero))
        for b in range(blocks):
            out[b, 0] = dk[b * 128 : (b + 1) * 128].astype(out.dtype)
            out[b, 1] = dv[b * 128 : (b + 1) * 128].astype(out.dtype)

    @pl.when(kt == pl.num_programs(0) - 1)
    def _():
        dq_ref[...] = dq_acc[...].astype(bf16)


def flash_backward(info, do, lse, delta, lo, by_head, across, scale):
    rows = do.shape[0]
    tiles = rows // K_TILE
    whole = pl.BlockSpec((rows, 128), lambda t, s: (0, 0))
    line = pl.BlockSpec((rows // Q_TILE, Q_TILE), lambda t, s: (0, 0))
    block = lambda n: pl.BlockSpec((1, K_TILE, 128), lambda t, s: (n, t, 0))
    grads = pl.BlockSpec((K_TILE // 128, 2, 128, 128), lambda t, s: (t, 0, 0, 0))
    return pl.pallas_call(
        functools.partial(flash_back_kernel, scale=scale),
        name="attention_backward",
        grid_spec=pltpu.PrefetchScalarGridSpec(
            num_scalar_prefetch=1,
            grid=(tiles,),
            in_specs=[
                pl.BlockSpec((1, rows, 128), lambda t, s: (0, 0, 0)),
                whole, line, line, line, block(1), block(2), block(0), block(1),
            ],
            out_specs=[whole, grads, grads],
            scratch_shapes=[pltpu.VMEM((rows, 128), f32)],
        ),
        out_shape=[
            jax.ShapeDtypeStruct((rows, 128), bf16),
            jax.ShapeDtypeStruct((rows // 128, 2, 128, 128), bf16),
            jax.ShapeDtypeStruct((rows // 128, 2, 128, 128), f32),
        ],
        compiler_params=pltpu.CompilerParams(vmem_limit_bytes=40 * MIB),
    )(info, by_head, do, lse, delta, lo, by_head, by_head, across, across)


def per_device(
    tokens,
    document_starts,
    document_adapter,
    layernorm_gain,
    layernorm_bias,
    projection_weight,
    output_weight,
    up_weight,
    down_weight,
    projection_bias,
    upper_bias,
    attention_down_maps,
    attention_up_maps,
    upper_down_maps,
    upper_up_maps,
    lower_down_maps,
    lower_up_maps,
    cotangent,
):
    local_rows, width = tokens.shape[1:]
    head_size = width // HEADS
    seq = local_rows * 32
    scale = head_size ** (-0.5)
    starts = document_starts[0]
    chosen = document_adapter[0]
    xl, c, z, y, xh = (lax.axis_index(a) for a in AXES)
    stream = xl * 2 + c
    first_row = ((z * 4 + y) * 2 + xh) * local_rows
    local_pos = first_row + jnp.arange(local_rows, dtype=jnp.int32)
    local_seg = jnp.sum((starts[None, :] <= local_pos[:, None]).astype(jnp.int32), axis=1) - 1
    doc_ids = jnp.arange(starts.shape[0], dtype=jnp.int32)
    token_adapter = jnp.sum(jnp.where(local_seg[:, None] == doc_ids[None, :], chosen[None, :], 0), axis=1)
    columns = jnp.arange(upper_down_maps.shape[1], dtype=jnp.int32) // ADAPTER_RANK
    mask = (token_adapter[:, None] == columns[None, :]).astype(f32)

    rows = seq // 2
    q_pos = positions_of(jnp.arange(rows, dtype=jnp.int32), xh)
    doc_lo = jnp.max(jnp.where(starts[None, :] <= q_pos[:, None], starts[None, :], 0), axis=1)
    first_tile = (doc_lo[::Q_TILE] // 256) * 128 // K_TILE
    info = jnp.concatenate([xh[None], first_tile]).astype(jnp.int32)
    last_key = (2 * ((jnp.arange(rows // K_TILE) + 1) * K_TILE // 128 - 1) + 1) * 128 + 127
    doc_end = jnp.min(jnp.where(starts[None, :] > last_key[:, None], starts[None, :], seq), axis=1)
    last_q_tile = jnp.minimum((doc_end + 255) // 256 * 128 + Q_TILE - 1, rows + Q_TILE - 1) // Q_TILE
    info_back = jnp.concatenate([xh[None], last_q_tile]).astype(jnp.int32)

    inputs = tokens[0].astype(f32)
    cot = cotangent[0]
    grad_adapt_down = (dot_nt(cot, lower_up_maps) * mask).astype(bf16)
    qkv_all, out_all, up_all, dn_all, cot_all, gad_all = gather_weights(
        jnp.transpose(projection_weight, (1, 0, 2)), output_weight, up_weight, down_weight, cot, grad_adapt_down
    )
    w_qkv = qkv_all.reshape(3, width, width)
    w_out = out_all.reshape(width, width)
    w_up = up_all.reshape(width, -1)
    w_down = dn_all.reshape(-1, width)
    cot_all = cot_all.reshape(-1, width)
    gad_all = gad_all.reshape(-1, 128)
    hidden = w_up.shape[1]

    def mine(array, axis):
        return lax.dynamic_slice_in_dim(array, stream * hidden, hidden, axis)

    normed_one, norm_one_back = jax.vjp(
        lambda v: layer_norm(v, layernorm_gain[0], layernorm_bias[0]), inputs
    )
    first_in = normed_one.astype(bf16)
    adapt_qkv = (
        jnp.einsum("td,pdr->ptr", first_in, attention_down_maps[:3], preferred_element_type=f32) * mask
    ).astype(bf16)
    bias_rows = jnp.stack([projection_bias[0], jnp.zeros_like(projection_bias[0]), projection_bias[1]])
    projected = (
        jnp.einsum("td,pde->pte", first_in, w_qkv, preferred_element_type=f32)
        + bias_rows[:, None, :]
        + jnp.einsum("ptr,pre->pte", adapt_qkv, attention_up_maps[:3], preferred_element_type=f32)
    )
    by_head, across = to_heads(projected.astype(bf16))
    by_head = by_head.reshape(3, rows, head_size)
    across = across.reshape(2, rows, head_size)
    attended, attended_low, lse = flash_forward(info, doc_lo[:, None], by_head, across, scale)
    lse = lse.reshape(rows // Q_TILE, 8, Q_TILE)[:, 0]
    merged = to_tokens(attended_low.reshape(HEADS, local_rows, head_size))

    adapt_out = (dot(merged, attention_down_maps[3]) * mask).astype(bf16)
    residual = inputs + dot(merged, w_out) + projection_bias[2] + dot(adapt_out, attention_up_maps[3])
    normed_two, norm_two_back = jax.vjp(
        lambda v: layer_norm(v, layernorm_gain[1], layernorm_bias[1]), residual
    )
    second_in = normed_two.astype(bf16)
    adapt_up = (dot(second_in, upper_down_maps) * mask).astype(bf16)

    second_all, up_low_all = gather_stream(second_in, adapt_up)
    second_all = second_all.reshape(-1, width)
    up_low_all = up_low_all.reshape(-1, 128)
    my_up_maps = mine(upper_up_maps, 1)
    my_down_maps = mine(lower_down_maps, 0)
    grad_act = dot_nt(cot_all, w_down) + dot_nt(gad_all, my_down_maps)
    pre_act = dot(second_all, w_up) + mine(upper_bias, 0) + dot(up_low_all, my_up_maps)
    activated, gelu_back = jax.vjp(exact_gelu, pre_act)
    act_low = activated.astype(bf16)
    grad_pre = gelu_back(grad_act)[0].astype(bf16)

    def parts_of(value):
        return value.astype(bf16).reshape(4, local_rows, -1)

    back_sum, back_adapt = sum_stream(
        parts_of(dot_nt(grad_pre, w_up)), parts_of(dot_nt(grad_pre, my_up_maps))
    )
    grad_b_up = dot_tn(up_low_all, grad_pre)
    grad_a_down = dot_tn(act_low, gad_all)

    grad_adapt_up = (back_adapt * mask).astype(bf16)
    grad_a_up = dot_tn(second_in, grad_adapt_up)
    grad_second = back_sum + dot_nt(grad_adapt_up, upper_down_maps)
    grad_residual = cot.astype(f32) + norm_two_back(grad_second)[0]
    grad_branch = grad_residual.astype(bf16)
    grad_b_out = dot_tn(adapt_out, grad_branch)
    grad_adapt_out = (dot_nt(grad_branch, attention_up_maps[3]) * mask).astype(bf16)
    grad_a_out = dot_tn(merged, grad_adapt_out)
    grad_merged = (dot_nt(grad_branch, w_out) + dot_nt(grad_adapt_out, attention_down_maps[3])).astype(bf16)

    grad_heads, forth_sum, forth_adapt = grads_in(
        grad_merged, parts_of(dot(act_low, w_down)), parts_of(dot(act_low, my_down_maps))
    )
    adapt_down = (forth_adapt * mask).astype(bf16)
    output = residual + forth_sum + projection_bias[3] + dot(adapt_down, lower_up_maps)
    grad_b_down = dot_tn(adapt_down, cot)

    grad_heads = grad_heads.reshape(rows, head_size)
    row_dot = jnp.sum(grad_heads.astype(f32) * attended, axis=-1).reshape(rows // Q_TILE, Q_TILE)
    dq, other, own = flash_backward(
        info_back, grad_heads, lse, row_dot, doc_lo.reshape(rows // Q_TILE, Q_TILE), by_head, across, scale
    )
    grad_qkv = grads_out(dq.reshape(HEADS, local_rows, head_size), other, own)

    grad_b_qkv = jnp.einsum("ptr,pte->pre", adapt_qkv, grad_qkv, preferred_element_type=f32)
    grad_adapt_qkv = (
        jnp.einsum("pte,pre->ptr", grad_qkv, attention_up_maps[:3], preferred_element_type=f32) * mask
    ).astype(bf16)
    grad_a_qkv = jnp.einsum("td,ptr->pdr", first_in, grad_adapt_qkv, preferred_element_type=f32)
    grad_first = jnp.einsum("pte,pde->td", grad_qkv, w_qkv, preferred_element_type=f32) + jnp.einsum(
        "ptr,pdr->td", grad_adapt_qkv, attention_down_maps[:3], preferred_element_type=f32
    )
    input_grad = grad_residual + norm_one_back(grad_first)[0]

    early = sum_all(
        7,
        jnp.stack([grad_a_out, grad_a_up]).astype(bf16),
        jnp.stack([grad_b_out, grad_b_down]).astype(bf16),
        grad_a_down.astype(bf16),
        grad_b_up.astype(bf16),
    )
    late = sum_all(8, grad_a_qkv.astype(bf16), grad_b_qkv.astype(bf16))
    return (
        output.astype(bf16)[None],
        input_grad.astype(bf16)[None],
        jnp.concatenate([late[0], early[0][:1]]).astype(f32),
        jnp.concatenate([late[1], early[1][:1]]).astype(f32),
        early[0][1].astype(f32),
        early[3].astype(f32),
        early[2].astype(f32),
        early[1][1].astype(f32),
    )


def solution(mesh):
    fine = jax.sharding.Mesh(mesh.devices.reshape(SIZES), AXES)
    by_token = P(STREAM, TOKEN, None)
    shard = AXES
    in_specs = (
        by_token,
        P(STREAM, None),
        P(STREAM, None),
        P(),
        P(),
        P(shard, None, None),
        P(shard, None),
        P(shard, None),
        P(shard, None),
        P(),
        P(),
        P(),
        P(),
        P(),
        P(),
        P(),
        P(),
        by_token,
    )
    out_specs = (by_token, by_token, P(), P(), P(), P(), P(), P())
    return jax.shard_map(per_device, mesh=fine, in_specs=in_specs, out_specs=out_specs, check_vma=False)
```

```python
import functools

import jax
import jax.numpy as jnp
from jax import lax
from jax.experimental import pallas as pl
from jax.experimental.pallas import tpu as pltpu
from jax.sharding import PartitionSpec as P

HEADS = 16
ADAPTER_RANK = 16
MESH = pl.DeviceIdType.MESH
AXES = ("xl", "c", "z", "y", "xh")
SIZES = (2, 2, 4, 4, 2)
STREAM = ("xl", "c")
TOKEN = ("z", "y", "xh")
bf16 = jnp.bfloat16
f32 = jnp.float32
LOG2E = 1.4426950408889634
MIB = 2**20
Q_TILE = 256
K_TILE = 512
ALL = slice(None)


def layer_norm(values, gain, shift):
    center = values - jnp.mean(values, axis=-1, keepdims=True)
    spread = jnp.mean(center * center, axis=-1, keepdims=True)
    return center * lax.rsqrt(spread + 1e-05) * gain + shift


def layer_norm_back(values, gain, grad):
    center = values - jnp.mean(values, axis=-1, keepdims=True)
    scale = lax.rsqrt(jnp.mean(center * center, axis=-1, keepdims=True) + 1e-05)
    unit = center * scale
    grad = grad * gain
    along = jnp.mean(grad * unit, axis=-1, keepdims=True)
    return scale * (grad - jnp.mean(grad, axis=-1, keepdims=True) - unit * along)


def dot(left, right):
    return jnp.dot(left, right, preferred_element_type=f32)


def dot_nt(left, right):
    return lax.dot_general(left, right, (((1,), (1,)), ((), ())), preferred_element_type=f32)


def dot_tn(left, right):
    return lax.dot_general(left, right, (((0,), (0,)), ((), ())), preferred_element_type=f32)


def piece(n, size):
    return pl.ds(pl.multiple_of(n * size, size), size)


class Place:
    def __init__(self):
        self.xl, self.c, self.z, self.y, self.xh = (lax.axis_index(a) for a in AXES)
        self.x = self.xh * 2 + self.xl
        self.g = self.x * 2 + self.c

    def at(self, axis):
        return {"x": self.x, "y": self.y, "z": self.z}[axis]

    def step(self, axis, step):
        return lax.rem(self.at(axis) + (step + 4), 4)

    def toward(self, axis, step=1):
        if axis == "c":
            return {"c": 1 - self.c}
        to = self.step(axis, step)
        if axis == "x":
            return {"xl": lax.rem(to, 2), "xh": to // 2}
        return {axis: to}

    def member(self, dx, dc):
        to = {}
        if dx:
            to |= self.toward("x", dx)
        if dc:
            to |= {"c": 1 - self.c}
        return to


MEMBERS = [(dx, dc) for dx in (2, 1, 3, 0) for dc in (0, 1) if dx or dc]


class Sends:
    def __init__(self, send, recv):
        self.send, self.recv, self.used, self.open = send, recv, 0, []

    def push(self, src, dst, device):
        k = self.used
        self.used += 1
        copy = pltpu.make_async_remote_copy(
            src_ref=src,
            dst_ref=dst,
            send_sem=self.send.at[k],
            recv_sem=self.recv.at[k],
            device_id=device,
            device_id_type=MESH,
        )
        copy.start()
        self.open.append(copy)
        return copy


def greet(devices, perhaps=()):
    barrier = pltpu.get_barrier_semaphore()
    for device in devices:
        pl.semaphore_signal(barrier, inc=1, device_id=device, device_id_type=MESH)
    amount = len(devices) + len(perhaps)
    for device, myself in perhaps:
        amount = amount - myself.astype(jnp.int32)

        @pl.when(jnp.logical_not(myself))
        def _():
            pl.semaphore_signal(barrier, inc=1, device_id=device, device_id_type=MESH)

    pl.semaphore_wait(barrier, amount)


def run_all(parts):
    parts = list(parts)
    while parts:
        left = []
        for part in parts:
            try:
                next(part)
                left.append(part)
            except StopIteration:
                pass
        parts = left


def ring_gather(place, sends, view, order, chunk, landed, forward):
    fixed = {a: place.at(a) for a in order}
    across = place.toward("c")
    later, passed = [], []

    def pass_on(block):
        if forward:
            passed.append(sends.push(view(block, None), view(block, None), across))

    if forward:
        passed.append(sends.push(chunk, view(fixed, None), across))
    for number, axis in enumerate(order):
        own = view(fixed, None)
        src = chunk if number == 0 else own
        if number == 0:
            sent = [sends.push(src, own, place.toward(axis, s)) for s in (2, 1, 3)]
            yield
            for s, copy in zip((2, 1, 3), sent):
                copy.wait_recv()
                pass_on(fixed | {axis: place.step(axis, -s)})
            landed.wait()
            later += sent
            del fixed[axis]
            continue
        up = sends.push(src, own, place.toward(axis, 1))
        down = sends.push(src, own, place.toward(axis, -1))
        yield
        before = fixed | {axis: place.step(axis, -1)}
        after = fixed | {axis: place.step(axis, 1)}
        opposite = fixed | {axis: place.step(axis, 2)}
        up.wait_recv()
        half = view(before, 0)
        up_two = sends.push(half, half, place.toward(axis, 1))
        down.wait_recv()
        half = view(after, 1)
        down_two = sends.push(half, half, place.toward(axis, -1))
        pass_on(before)
        pass_on(after)
        yield
        up_two.wait_recv()
        down_two.wait_recv()
        pass_on(opposite)
        later += [up, down, up_two, down_two]
        del fixed[axis]
    yield
    for copy in later:
        copy.wait_send()
    for copy in passed:
        copy.wait()


class Nothing:
    def wait(self):
        pass


def neighbours(place, axes):
    return [place.toward(a, s) for a in axes for s in ((1, 2, 3) if a in "xyz" else (1,))]


def members(place):
    return [place.member(*m) for m in MEMBERS]


class GroupGather:
    def __init__(self, place, sends, buf):
        self.place, self.sends, self.buf = place, sends, buf
        self.mine = buf.at[place.x, place.c]
        self.right, self.left = place.toward("x", 1), place.toward("x", -1)
        self.up = sends.push(self.mine, self.mine, self.right)
        self.down = sends.push(self.mine, self.mine, self.left)
        self.passed = [self.pass_on(self.mine)]

    def pass_on(self, ref):
        return self.sends.push(ref, ref, self.place.toward("c"))

    def own(self):
        self.passed[0].wait_recv()

    def near(self, wait=True):
        x, c = self.place.step("x", -1), self.place.c
        self.up.wait_recv()
        half = self.buf.at[x, c, pl.ds(0, 64)]
        self.up_two = self.sends.push(half, half, self.right)
        self.passed.append(self.pass_on(self.buf.at[x, c]))
        x = self.place.step("x", 1)
        self.down.wait_recv()
        half = self.buf.at[x, c, pl.ds(64, 64)]
        self.down_two = self.sends.push(half, half, self.left)
        self.passed.append(self.pass_on(self.buf.at[x, c]))
        if wait:
            self.near_done()

    def near_done(self):
        self.passed[1].wait_recv()
        self.passed[2].wait_recv()

    def far(self):
        self.up_two.wait_recv()
        self.down_two.wait_recv()
        self.passed.append(self.pass_on(self.buf.at[self.place.step("x", 2), self.place.c]))

    def far_done(self):
        self.passed[3].wait_recv()

    def finish(self):
        for copy in [self.up, self.down, self.up_two, self.down_two] + self.passed:
            copy.wait_send()


def group_gather(place, sends, buf):
    gather = GroupGather(place, sends, buf)
    yield
    gather.own()
    gather.near()
    yield
    gather.far()
    yield
    gather.far_done()
    gather.finish()


class GroupSum:
    def __init__(self, place, sends, parts, scratch):
        self.place, self.sends, self.parts = place, sends, parts
        self.came, self.own, self.left_one, self.right_one, self.left_two, self.right_two = scratch
        self.xs = [place.step("x", s) for s in (2, 1, -1, 0)]
        self.right, self.left = place.toward("x", 1), place.toward("x", -1)
        self.crossed = {}

    @staticmethod
    def scratch(n):
        vm = lambda *s: pltpu.VMEM(s, bf16)
        return [vm(4, 128, n), vm(3, 128, n), vm(64, n), vm(64, n), vm(128, n), vm(128, n)]

    def cross(self, k):
        place = self.place
        self.crossed[k] = self.sends.push(
            self.parts.at[self.xs[k], 1 - place.c], self.came.at[k], place.toward("c")
        )

    def merge(self, k):
        self.crossed[k].wait()
        both = self.parts[self.xs[k], self.place.c].astype(f32) + self.came[k].astype(f32)
        self.own[k] = both.astype(bf16)

    def first(self):
        self.up = self.sends.push(self.own.at[0, pl.ds(0, 64)], self.left_one, self.right)
        self.down = self.sends.push(self.own.at[0, pl.ds(64, 64)], self.right_one, self.left)

    def second(self):
        self.up.wait()
        both = self.own[1, 0:64].astype(f32) + self.left_one[...].astype(f32)
        self.own[1, 0:64] = both.astype(bf16)
        self.up_two = self.sends.push(self.own.at[1], self.left_two, self.right)
        self.down.wait()
        both = self.own[2, 64:128].astype(f32) + self.right_one[...].astype(f32)
        self.own[2, 64:128] = both.astype(bf16)
        self.down_two = self.sends.push(self.own.at[2], self.right_two, self.left)

    def result(self):
        self.crossed[3].wait()
        total = self.parts[self.xs[3], self.place.c].astype(f32) + self.came[3].astype(f32)
        self.up_two.wait()
        self.down_two.wait()
        return total + self.left_two[...].astype(f32) + self.right_two[...].astype(f32)


def group_sum(place, sends, parts, scratch, out):
    total = GroupSum(place, sends, parts, scratch)
    for k in range(4):
        total.cross(k)
    yield
    total.merge(0)
    total.first()
    total.merge(1)
    total.merge(2)
    yield
    total.second()
    yield
    out[...] = total.result()


def plane(place):
    steps = [(i, j) for i in (2, 1, 3, 0) for j in (2, 1, 3, 0) if i or j]
    return [(lax.rem(place.z + i, 4), lax.rem(place.y + j, 4)) for i, j in steps]


def from_plane(place):
    steps = [(i, j) for i in (2, 1, 3, 0) for j in (2, 1, 3, 0) if i or j]
    return [(lax.rem(place.z + 4 - i, 4), lax.rem(place.y + 4 - j, 4)) for i, j in steps]


def projectors(place):
    x, c = place.z, place.y // 2
    member = {"xl": lax.rem(x, 2), "xh": x // 2, "c": c}
    mine = (place.x == x) & (place.c == c)
    return [(member | {"z": z, "y": y}, None) for z, y in plane(place)] + [
        (member | {"z": place.z, "y": place.y}, mine)
    ]


def attenders(place):
    found = []
    for dx, dc in MEMBERS + [(0, 0)]:
        for j in range(2):
            z, y = place.x, 2 * place.c + j
            device = place.member(dx, dc) | {"z": z, "y": y}
            mine = None if dx or dc else (place.z == z) & (place.y == y)
            found.append((dx, dc, j, device, mine))
    return found


def head_columns(z, y):
    return pl.ds(pl.multiple_of((z * 4 + y) * 128, 128), 128)


def split_greeting(pairs):
    return [d for d, m in pairs if m is None], [(d, m) for d, m in pairs if m is not None]


def plane_devices(place):
    return [{"z": z, "y": y} for z, y in plane(place)]


class Post:
    def __init__(self, src, dst, device, myself, send_sem, recv_sem):
        self.remote = pltpu.make_async_remote_copy(
            src_ref=src, dst_ref=dst, send_sem=send_sem, recv_sem=recv_sem, device_id=device, device_id_type=MESH
        )
        self.myself = myself
        if myself is None:
            self.remote.start()
        else:
            pl.when(myself)(pltpu.make_async_copy(src, dst, recv_sem).start)
            pl.when(jnp.logical_not(myself))(self.remote.start)

    def wait_send(self):
        if self.myself is None:
            self.remote.wait_send()
        else:
            pl.when(jnp.logical_not(self.myself))(self.remote.wait_send)


def heads_out(place, sends, blocks, merged, local):
    cols = head_columns(place.z, place.y)
    keep = pltpu.make_async_copy(blocks.at[place.z * 4 + place.y], merged.at[:, cols], local)
    keep.start()
    sent = [sends.push(blocks.at[z * 4 + y], merged.at[:, cols], {"z": z, "y": y}) for z, y in plane(place)]
    yield
    for copy in sent:
        copy.wait()
    keep.wait()


def grads_in_kernel(grad, parts, heads, total, *refs):
    scratch, (send, recv, local) = refs[:-3], refs[-3:]
    place = Place()
    greet(plane_devices(place) + members(place))
    sends = Sends(send, recv)

    def heads_part():
        here = place.z * 4 + place.y
        keep = pltpu.make_async_copy(grad.at[:, head_columns(place.z, place.y)], heads.at[here], local.at[0])
        keep.start()
        sent = [
            sends.push(grad.at[:, head_columns(z, y)], heads.at[here], {"z": z, "y": y}) for z, y in plane(place)
        ]
        yield
        for copy in sent:
            copy.wait()
        keep.wait()

    run_all([heads_part(), group_sum(place, sends, parts, scratch, total)])


def grads_in(grad, parts):
    any_ = pl.BlockSpec(memory_space=pl.ANY)
    vmem = pl.BlockSpec(memory_space=pltpu.VMEM)
    n = parts.shape[-1]
    return pl.pallas_call(
        grads_in_kernel,
        name="grads_in",
        out_shape=[jax.ShapeDtypeStruct((16, 128, 128), bf16), jax.ShapeDtypeStruct((128, n), f32)],
        in_specs=[any_, vmem],
        out_specs=[any_, vmem],
        scratch_shapes=GroupSum.scratch(n) + [pltpu.SemaphoreType.DMA((k,)) for k in (23, 23, 1)],
        compiler_params=pltpu.CompilerParams(collective_id=2, has_side_effects=True, vmem_limit_bytes=40 * MIB),
    )(grad, parts)


def grads_out_kernel(dq, other, own, grads, came, sums, by_head, send, recv, a_recv, local):
    place = Place()
    partner = {"xh": 1 - place.xh}
    greet(plane_devices(place) + members(place))
    sends = Sends(send, recv)
    here = place.z * 4 + place.y
    places = plane(place) + [(place.z, place.y)]
    kv = pl.ds(1, 2)
    swaps = [sends.push(other.at[z * 4 + y], came.at[z * 4 + y], partner) for z, y in places]
    gone = []

    def send_block(k, src, part, z, y, last):
        dst = by_head.at[part, here]
        if last:
            pltpu.make_async_copy(src, dst, a_recv.at[k, here]).start()
            return
        copy = pltpu.make_async_remote_copy(
            src_ref=src, dst_ref=dst, send_sem=local.at[len(gone)], recv_sem=a_recv.at[k, here],
            device_id={"z": z, "y": y}, device_id_type=MESH,
        )
        copy.start()
        gone.append(copy)

    for n, (z, y) in enumerate(places):
        send_block(0, dq.at[z * 4 + y], 0, z, y, n == 15)
    for n, (copy, (z, y)) in enumerate(zip(swaps, places)):
        copy.wait_recv()
        at = z * 4 + y
        sums[at] = (came[at].astype(f32) + own[at]).astype(bf16)
        send_block(1, sums.at[at], kv, z, y, n == 15)

    mine = None
    shared = []
    for dx, dc in MEMBERS + [(0, 0)]:
        g = place.step("x", dx) * 2 + (1 - place.c if dc else place.c)
        for k, part in ((0, 0), (1, kv)):
            for j in range(2):
                dst = by_head.at[part, g * 2 + j]
                pltpu.make_async_copy(dst, dst, a_recv.at[k, g * 2 + j]).wait()
        src, dst = by_head.at[:, piece(g, 2)], grads.at[:, place.x, place.c]
        if dx or dc:
            shared.append(sends.push(src, dst, place.member(dx, dc)))
        else:
            mine = pltpu.make_async_copy(src, dst, local.at[30])
            mine.start()
    for copy in swaps + gone:
        copy.wait_send()
    for copy in shared:
        copy.wait()
    mine.wait()


def grads_out(dq, other, own):
    any_ = pl.BlockSpec(memory_space=pl.ANY)
    vmem = pl.BlockSpec(memory_space=pltpu.VMEM)
    return pl.pallas_call(
        grads_out_kernel,
        name="grads_out",
        out_shape=jax.ShapeDtypeStruct((3, 4, 2, 2, 128, 128), bf16),
        in_specs=[vmem] * 3,
        out_specs=any_,
        scratch_shapes=[pltpu.VMEM((16, 2, 128, 128), bf16)] * 2
        + [pltpu.VMEM((3, 16, 128, 128), bf16)]
        + [pltpu.SemaphoreType.DMA(k) for k in ((23,), (23,), (2, 16), (31,))],
        compiler_params=pltpu.CompilerParams(collective_id=3, has_side_effects=True, vmem_limit_bytes=40 * MIB),
    )(dq, other, own)


ORDERS = (("x", "y", "z"), ("y", "z", "x"), ("z", "x", "y"))


def spread_sum(place, sends, order, steps, result_view, final, landed, across=None):
    if across:
        src, came, own, out = across
        copy = sends.push(src, came, place.toward("c"))
        yield
        copy.wait()
        out[...] = (own[...].astype(f32) + came[...].astype(f32)).astype(bf16)
    for axis, (held, slots, out) in zip(order, steps):
        sent = [
            sends.push(held(place.step(axis, d)), slots.at[d - 1], place.toward(axis, d)) for d in (2, 1, 3)
        ]
        yield
        for copy in sent:
            copy.wait()
        total = held(place.at(axis))[...].astype(f32)
        for d in range(3):
            total = total + slots[d].astype(f32)
        out[...] = total.astype(bf16)
    landed.start()
    yield from ring_gather(place, sends, result_view[0], result_view[1], final, landed, True)


def rows_of(ref, size):
    return lambda p: ref.at[piece(p, size)]


def cols_of(ref, size):
    return lambda p: ref.at[:, piece(p, size)]


def mid_rows_of(ref, size):
    return lambda p: ref.at[:, piece(p, size)]


def sums_kernel(count, a, b, two, a_res, b_res, two_res, *refs):
    scratch, (send, recv, local) = list(refs[:-3]), refs[-3:]
    place = Place()
    sends = Sends(send, recv)
    greet(neighbours(place, ("x", "y", "z", "c")))
    parts = []
    mine, theirs = place.c, 1 - place.c
    here = {x: place.at(x) for x in "xyz"}

    def a_view(i, order):
        def view(fixed, half):
            at = [fixed.get(x, ALL) for x in order]
            if half is not None:
                at[max(n for n in range(3) if order[n] not in fixed)] = pl.ds(half * 2, 2)
            return a_res.at[(i, place.c) + tuple(at)]

        return view

    def b_view(i, order):
        def view(fixed, half):
            start, size = 0, 2048
            if order[1] in fixed:
                start, size = fixed[order[1]] * 512, 512
            if order[2] in fixed:
                start, size = start + fixed[order[2]] * 128, 128
            if half is not None:
                size = size // 2
                start = start + half * size
            cols = pl.ds(start, size) if isinstance(start, int) else pl.ds(pl.multiple_of(start, 128), size)
            return b_res.at[i, place.c, fixed.get(order[0], ALL), :, cols]

        return view

    for i in range(count):
        order = ORDERS[i % 3]
        ca, ha, sa1, qa, sa2, ra, sa3, fa, cb, hb, sb1, qb, sb2, rb, sb3, fb = scratch[:16]
        del scratch[:16]
        keep = pltpu.make_async_copy(fa, a_view(i, order)(here, None), local.at[2 * i])
        parts.append(
            spread_sum(
                place, sends, order,
                [(rows_of(ha, 256), sa1, qa), (rows_of(qa, 64), sa2, ra), (rows_of(ra, 16), sa3, fa)],
                (a_view(i, order), order[::-1]), fa, keep,
                (a.at[i, piece(theirs, 1024)], ca, a.at[i, piece(mine, 1024)], ha),
            )
        )
        keep = pltpu.make_async_copy(fb, b_view(i, order)(here, None), local.at[2 * i + 1])
        parts.append(
            spread_sum(
                place, sends, order,
                [(rows_of(hb, 16), sb1, qb), (cols_of(qb, 512), sb2, rb), (cols_of(rb, 128), sb3, fb)],
                (b_view(i, order), order[::-1]), fb, keep,
                (b.at[i, piece(theirs, 64)], cb, b.at[i, piece(mine, 64)], hb),
            )
        )
    s1, q1, s2, f2 = scratch

    def two_view(n):
        def view(fixed, half):
            xl, xh = (ALL, ALL)
            if "x" in fixed:
                xl, xh = lax.rem(fixed["x"], 2), fixed["x"] // 2
            if half is not None:
                xl = pl.ds(half, 1)
            return two_res.at[n, xl, place.c, fixed.get("z", ALL), fixed.get("y", ALL), xh]

        return view

    for n, axes in enumerate((("z", "y"), ("y", "z"))):
        if n == 0:
            steps = [
                (lambda p: two.at[0, p], s1.at[0], q1.at[0]),
                (lambda p: q1.at[0, p], s2.at[0], f2.at[0]),
            ]
        else:
            steps = [
                (lambda p: two.at[1, :, p], s1.at[1], q1.at[1]),
                (lambda p: q1.at[1, p], s2.at[1], f2.at[1]),
            ]
        keep = pltpu.make_async_copy(f2.at[n], two_view(n)(here, None), local.at[2 * count + n])
        order = (("x", "z", "y"), ("x", "y", "z"))[n]
        parts.append(spread_sum(place, sends, axes, steps, (two_view(n), order), f2.at[n], keep))
    run_all(parts)
    assert sends.used <= send.shape[0], sends.used


def sum_all(a, b, two):
    count = a.shape[0]
    vm = lambda *shape: pltpu.VMEM(shape, bf16)
    scratch = []
    for _ in range(count):
        scratch += [vm(1024, 128), vm(1024, 128), vm(3, 256, 128), vm(256, 128), vm(3, 64, 128), vm(64, 128)]
        scratch += [vm(3, 16, 128), vm(16, 128)]
        scratch += [vm(64, 2048), vm(64, 2048), vm(3, 16, 2048), vm(16, 2048), vm(3, 16, 512), vm(16, 512)]
        scratch += [vm(3, 16, 128), vm(16, 128)]
    scratch += [vm(2, 3, 4, 64, 128), vm(2, 4, 64, 128), vm(2, 3, 64, 128), vm(2, 64, 128)]
    shapes = [(count, 2, 4, 4, 4, 16, 128), (count, 2, 4, 16, 2048), (2, 2, 2, 4, 4, 2, 64, 128)]
    n = 62 * count + 60
    a_all, b_all, two_all = pl.pallas_call(
        functools.partial(sums_kernel, count),
        name="sum_all",
        out_shape=[jax.ShapeDtypeStruct(s, bf16) for s in shapes],
        in_specs=[pl.BlockSpec(memory_space=pltpu.VMEM)] * 3,
        out_specs=[pl.BlockSpec(memory_space=pl.ANY)] * 3,
        scratch_shapes=scratch + [pltpu.SemaphoreType.DMA((k,)) for k in (n, n, 2 * count + 2)],
        compiler_params=pltpu.CompilerParams(collective_id=4, has_side_effects=True, vmem_limit_bytes=48 * MIB),
    )(a, b, two.reshape(2, 4, 4, 64, 128))
    return a_all.reshape(count, 2048, 128), b_all.reshape(count, 128, 2048), two_all.reshape(2, 8192, 128)


def positions_of(local, parity):
    return (2 * (local // 128) + parity) * 128 + lax.rem(local, 128)


def flash_back_kernel(
    info, q_ref, do_ref, lse_ref, delta_ref, lo_ref, ko_ref, vo_ref, kx_ref, vx_ref, dq_ref, other_ref, own_ref, dq_acc, *, scale
):
    kt = pl.program_id(0)
    parity = info[0]

    @pl.when(kt == 0)
    def _():
        dq_acc[...] = jnp.zeros_like(dq_acc)

    first = kt * (K_TILE // Q_TILE)
    last = info[1 + kt]
    blocks = K_TILE // 128
    for k_ref, v_ref, k_parity, out in ((kx_ref, vx_ref, 1 - parity, other_ref), (ko_ref, vo_ref, parity, own_ref)):
        k = k_ref[0]
        v = v_ref[0]
        k_pos = positions_of(kt * K_TILE + lax.broadcasted_iota(jnp.int32, (K_TILE, 1), 0), k_parity)

        def step(qt, carry):
            dk, dv = carry
            rows = pl.ds(pl.multiple_of(qt * Q_TILE, Q_TILE), Q_TILE)
            q = q_ref[0, rows, :]
            do = do_ref[rows, :]
            q_pos = positions_of(qt * Q_TILE + lax.broadcasted_iota(jnp.int32, (1, Q_TILE), 1), parity)
            lo = lo_ref[pl.ds(qt, 1), :]
            lse = lse_ref[pl.ds(qt, 1), :]
            delta = delta_ref[pl.ds(qt, 1), :]
            s = dot_nt(k, q)
            p = jnp.exp2(jnp.where((k_pos >= lo) & (k_pos <= q_pos), s * (scale * LOG2E) - lse, -1e30))
            dv = dv + dot(p.astype(bf16), do)
            dp = dot_nt(v, do)
            ds = (p * (dp - delta) * scale).astype(bf16)
            dk = dk + dot(ds, q)
            dq_acc[rows, :] += dot_tn(ds, k)
            return dk, dv

        zero = jnp.zeros((K_TILE, 128), f32)
        dk, dv = lax.fori_loop(first, last, step, (zero, zero))
        for b in range(blocks):
            out[b, 0] = dk[b * 128 : (b + 1) * 128].astype(out.dtype)
            out[b, 1] = dv[b * 128 : (b + 1) * 128].astype(out.dtype)

    @pl.when(kt == pl.num_programs(0) - 1)
    def _():
        dq_ref[...] = dq_acc[...].astype(bf16)


def flash_backward(info, do, lse, delta, lo, by_head, across, scale):
    rows = do.shape[0]
    tiles = rows // K_TILE
    whole = pl.BlockSpec((rows, 128), lambda t, s: (0, 0))
    line = pl.BlockSpec((rows // Q_TILE, Q_TILE), lambda t, s: (0, 0))
    block = lambda n: pl.BlockSpec((1, K_TILE, 128), lambda t, s: (n, t, 0))
    grads = pl.BlockSpec((K_TILE // 128, 2, 128, 128), lambda t, s: (t, 0, 0, 0))
    return pl.pallas_call(
        functools.partial(flash_back_kernel, scale=scale),
        name="attention_backward",
        grid_spec=pltpu.PrefetchScalarGridSpec(
            num_scalar_prefetch=1,
            grid=(tiles,),
            in_specs=[
                pl.BlockSpec((1, rows, 128), lambda t, s: (0, 0, 0)),
                whole, line, line, line, block(1), block(2), block(0), block(1),
            ],
            out_specs=[whole, grads, grads],
            scratch_shapes=[pltpu.VMEM((rows, 128), f32)],
        ),
        out_shape=[
            jax.ShapeDtypeStruct((rows, 128), bf16),
            jax.ShapeDtypeStruct((rows // 128, 2, 128, 128), bf16),
            jax.ShapeDtypeStruct((rows // 128, 2, 128, 128), f32),
        ],
        compiler_params=pltpu.CompilerParams(vmem_limit_bytes=40 * MIB),
    )(info, by_head, do, lse, delta, lo, by_head, by_head, across, across)


def attend(t, mine, others, lo_ref, att, low, lse_ref, parity, scale):
    at = pl.ds(pl.multiple_of(t * Q_TILE, Q_TILE), Q_TILE)
    q = mine[0, at, :]
    q_pos = positions_of(t * Q_TILE + lax.broadcasted_iota(jnp.int32, (Q_TILE, 1), 0), parity)
    lo = lo_ref[at, :]
    ones = jnp.ones((K_TILE, 128), bf16)

    def step(kt, carry):
        top, acc = carry
        rows = pl.ds(pl.multiple_of(kt * K_TILE, K_TILE), K_TILE)
        local = kt * K_TILE + lax.broadcasted_iota(jnp.int32, (1, K_TILE), 1)
        scores = []
        for k, par in ((mine[1, rows, :], parity), (others[0, rows, :], 1 - parity)):
            k_pos = positions_of(local, par)
            scores.append(jnp.where((k_pos >= lo) & (k_pos <= q_pos), dot_nt(q, k), -1e30))
        new = jnp.maximum(jnp.max(scores[0], axis=1, keepdims=True), jnp.max(scores[1], axis=1, keepdims=True))
        new = jnp.maximum(top, new)
        acc = acc * jnp.exp2((top - new) * (scale * LOG2E))
        for s, v in zip(scores, (mine[2, rows, :], others[1, rows, :])):
            p = jnp.exp2((s - new) * (scale * LOG2E)).astype(bf16)
            acc = acc + dot(p, jnp.concatenate([v, ones], axis=1))
        return new, acc

    start = (jnp.full((Q_TILE, 1), -1e30, f32), jnp.zeros((Q_TILE, 256), f32))
    top, acc = lax.fori_loop(0, (t * Q_TILE + Q_TILE + K_TILE - 1) // K_TILE, step, start)
    total = acc[:, 128:]
    o = acc[:, :128] / total
    att[at, :] = o
    for b in range(Q_TILE // 128):
        low[t * (Q_TILE // 128) + b] = o[b * 128 : (b + 1) * 128].astype(bf16)
    lse = top * (scale * LOG2E) + jnp.log2(total)
    lse_ref[pl.ds(pl.multiple_of(t * 8, 8), 8), :] = jnp.transpose(lse)[0:8, :]


def front_kernel(
    tok, gain, shift, bias, dmaps, umaps, mask, cot, lum, lo, wp, wo, up, dn,
    act_all, qkv_w, out_all, up_all, dn_all, cot_all, heads, across, merged, att, lse,
    act, cotbuf, wq, rows, mine, others, low, send, recv, a_send, a_recv, local, *, scale,
):
    place = Place()
    sends = Sends(send, recv)
    partner = {"xh": 1 - place.xh}
    always, perhaps = split_greeting(projectors(place))
    greet(plane_devices(place) + members(place) + always, perhaps)
    home = (place.xl, place.c, place.z, place.y, place.xh)

    def out_view(halfs):
        def view(fixed, half):
            xl, xh = (ALL, ALL)
            if "x" in fixed:
                xl, xh = lax.rem(fixed["x"], 2), fixed["x"] // 2
            cols = pl.ds(halfs * 1024, 1024) if half is None else pl.ds(halfs * 1024 + half * 512, 512)
            return out_all.at[xl, place.c, fixed.get("z", ALL), fixed.get("y", ALL), xh, ALL, cols]

        return view

    def up_view(fixed, half):
        xl = ALL if half is None else pl.ds(half, 1)
        return up_all.at[xl, ALL, fixed.get("z", ALL), fixed.get("y", ALL)]

    def dn_view(fixed, half):
        cols = ALL if half is None else pl.ds(half * 1024, 1024)
        return dn_all.at[fixed.get("z", ALL), fixed.get("y", ALL), :, cols]

    def wq_view(p, cols):
        def view(fixed, half):
            xl = ALL if half is None else pl.ds(half, 1)
            return wq.at[p, xl, ALL, fixed.get("z", ALL), fixed.get("y", ALL), ALL, ALL, cols]

        return view

    def index(dx, dc):
        return place.step("x", dx) * 2 + (1 - place.c if dc else place.c)

    copies = [
        pltpu.make_async_copy(
            wp.at[:, :, piece(place.g, 256)], wq.at[:, place.xl, place.c, place.z, place.y, place.xh], local.at[0]
        ),
        pltpu.make_async_copy(up.at[:, piece(place.g, 1024)], up_all.at[home], local.at[1]),
        pltpu.make_async_copy(dn, dn_all.at[place.z, place.y], local.at[2]),
    ]
    copies += [
        pltpu.make_async_copy(
            wo.at[:, pl.ds(h * 1024, 1024)],
            out_view(h)({a: place.at(a) for a in "xyz"}, None),
            local.at[3 + h],
        )
        for h in range(2)
    ]
    for copy in copies:
        copy.start()
    wq_spread = [
        sends.push(
            wp.at[:, :, piece(index(*m), 256)],
            wq.at[:, place.xl, place.c, place.z, place.y, place.xh],
            place.member(*m),
        )
        for m in MEMBERS
    ]
    up_spread = [
        sends.push(up.at[:, piece(index(*m), 1024)], up_all.at[home], place.member(*m)) for m in MEMBERS
    ]

    values = tok[...].astype(f32)
    normed = layer_norm(values, gain[...], shift[...]).astype(bf16)
    own = act.at[place.x, place.c]
    own[:, 0:2048] = normed
    for p in range(3):
        own[:, 2048 + p * 128 : 2176 + p * 128] = (dot(normed, dmaps[p]) * mask[...]).astype(bf16)
    act_gather = GroupGather(place, sends, act)
    own = cotbuf.at[place.x, place.c]
    own[:, 0:2048] = cot[...]
    own[:, 2048:2176] = (dot_nt(cot[...], lum[...]) * mask[...]).astype(bf16)

    copies[0].wait()
    for copy in wq_spread:
        copy.wait()
    fixed = {"z": place.z, "y": place.y}
    qkv_parts = []
    for p, cols, order in (
        (0, ALL, ("y", "z")), (1, ALL, ("z", "y")), (2, pl.ds(0, 128), ("y", "z")), (2, pl.ds(128, 128), ("z", "y"))
    ):
        view = wq_view(p, cols)
        qkv_parts.append(ring_gather(place, sends, view, order, view(fixed, None), Nothing(), False))
    up_gather = ring_gather(place, sends, up_view, ("y", "z"), up_view(fixed, None), Nothing(), False)
    dn_gather = ring_gather(place, sends, dn_view, ("z", "y"), dn, copies[2], False)
    out_gathers = [
        ring_gather(place, sends, out_view(h), order, wo.at[:, pl.ds(h * 1024, 1024)], copies[3 + h], True)
        for h, order in enumerate((("y", "z", "x"), ("x", "z", "y")))
    ]

    def tick(*parts):
        for part in parts:
            next(part)

    tick(*qkv_parts)
    act_gather.own()
    tick(*qkv_parts)
    act_gather.near()
    tick(*qkv_parts)
    copies[1].wait()
    for copy in up_spread:
        copy.wait()
    act_gather.far()
    act_gather.far_done()
    cot_gather = group_gather(place, sends, cotbuf)
    run_all(qkv_parts)
    tick(up_gather, dn_gather, cot_gather)
    kept = [
        pltpu.make_async_copy(wq, qkv_w, local.at[5]),
        pltpu.make_async_copy(act, act_all, local.at[6]),
    ]
    for copy in kept:
        copy.start()

    def project(x, _):
        left = act[x, :, :, 0:2048].reshape(256, 2048)
        for p in range(3):
            low_rank = act[x, :, :, 2048 + p * 128 : 2176 + p * 128].reshape(256, 128)
            value = dot(left, wq[p].reshape(2048, 256)) + bias[p] + dot(low_rank, umaps[p])
            rows[p, x] = value.astype(bf16).reshape(2, 128, 256)
        return 0

    lax.fori_loop(0, 4, project, 0)

    here = place.z * 4 + place.y
    kv = pl.ds(1, 2)
    posts = []
    for n, (dx, dc, j, device, myself) in enumerate(attenders(place)):
        src = rows.at[:, place.step("x", dx), 1 - place.c if dc else place.c, :, pl.ds(j * 128, 128)]
        posts.append(
            Post(src, mine.at[:, piece(here, 128)], device, myself, a_send.at[n], a_recv.at[here])
        )
    swaps = []
    for z, y in plane(place) + [(place.z, place.y)]:
        n = z * 4 + y
        dst = mine.at[:, piece(n, 128)]
        pltpu.make_async_copy(dst, dst, a_recv.at[n]).wait()
        swaps.append(sends.push(mine.at[kv, piece(n, 128)], others.at[:, piece(n, 128)], partner))
    tick(up_gather, dn_gather, cot_gather, *out_gathers)
    for copy in swaps:
        copy.wait()
    kept += [
        pltpu.make_async_copy(mine, heads, local.at[7]),
        pltpu.make_async_copy(others, across, local.at[8]),
    ]
    for copy in kept[2:]:
        copy.start()
    tick(*out_gathers, cot_gather)

    def tile(t, _):
        attend(t, mine, others, lo, att, low, lse, place.xh, scale)
        return 0

    tiles = mine.shape[1] // Q_TILE
    lax.fori_loop(0, tiles - 2, tile, 0)
    tick(up_gather, dn_gather, *out_gathers)
    lax.fori_loop(tiles - 2, tiles, tile, 0)
    back = heads_out(place, sends, low, merged, local.at[9])
    tick(back, *out_gathers)
    for copy in posts:
        copy.wait_send()
    for copy in kept:
        copy.wait()
    act_gather.finish()
    run_all([back, up_gather, dn_gather, cot_gather, *out_gathers])
    last = pltpu.make_async_copy(cotbuf, cot_all, local.at[10])
    last.start()
    last.wait()
    assert sends.used <= send.shape[0], sends.used


def front(tok, gain, shift, bias, dmaps, umaps, mask, cot, lum, lo, wp, wo, up, dn, scale):
    any_ = pl.BlockSpec(memory_space=pl.ANY)
    vmem = pl.BlockSpec(memory_space=pltpu.VMEM)
    shape = lambda *s: jax.ShapeDtypeStruct(s, bf16)
    vm = lambda *s: pltpu.VMEM(s, bf16)
    return pl.pallas_call(
        functools.partial(front_kernel, scale=scale),
        name="front",
        out_shape=[
            shape(4, 2, 128, 2432),
            shape(3, 2, 2, 4, 4, 2, 16, 256),
            shape(2, 2, 4, 4, 2, 16, 2048),
            shape(2, 2, 4, 4, 2, 16, 1024),
            shape(4, 4, 64, 2048),
            shape(4, 2, 128, 2176),
            shape(3, 2048, 128),
            shape(2, 2048, 128),
            shape(128, 2048),
            jax.ShapeDtypeStruct((2048, 128), f32),
            jax.ShapeDtypeStruct((64, 256), f32),
        ],
        in_specs=[vmem] * 14,
        out_specs=[any_] * 9 + [vmem] * 2,
        scratch_shapes=[
            vm(4, 2, 128, 2432),
            vm(4, 2, 128, 2176),
            vm(3, 2, 2, 4, 4, 2, 16, 256),
            vm(3, 4, 2, 128, 256),
            vm(3, 2048, 128),
            vm(2, 2048, 128),
            vm(16, 128, 128),
        ]
        + [pltpu.SemaphoreType.DMA((n,)) for n in (160, 160, 16, 16, 11)],
        compiler_params=pltpu.CompilerParams(
            collective_id=0, has_side_effects=True, vmem_limit_bytes=56 * MIB
        ),
    )(tok, gain, shift, bias, dmaps, umaps, mask, cot, lum, lo, wp, wo, up, dn)


def feed_forward_kernel(
    second, cot_all, up, dn, umap, dmap, bias, back, forth, two,
    sa, cot, up_v, dn_v, grad_act, act, pre, parts, total, *refs,
):
    scratch, (send, recv, local) = refs[:-3], refs[-3:]
    place = Place()
    greet(members(place))
    sends = Sends(send, recv)
    sa[place.x, place.c] = second[...]
    gather = GroupGather(place, sends, sa)
    loads = [
        pltpu.make_async_copy(src, dst, local.at[n])
        for n, (src, dst) in enumerate(((dn, dn_v), (cot_all, cot), (up, up_v)))
    ]
    for copy in loads:
        copy.start()

    def rows(ref, x, start, size):
        return ref[x, :, :, pl.ds(start, size)].reshape(256, size)

    loads[0].wait()
    loads[1].wait()

    def grad_tile(n, _):
        x, cols = n // 4, piece(lax.rem(n, 4), 256)
        value = dot_nt(rows(cot, x, 0, 2048), dn_v[cols, :])
        grad_act[x, :, cols] = value + dot_nt(rows(cot, x, 2048, 128), dmap[cols, :])
        return 0

    lax.fori_loop(0, 16, grad_tile, 0)
    loads[2].wait()

    def hidden(x):
        def tile(n, _):
            cols = piece(n, 256)
            value = dot(rows(sa, x, 0, 2048), up_v[:, cols]) + bias[:, cols]
            value = value + dot(rows(sa, x, 2048, 128), umap[:, cols])
            phi = 0.5 * (1.0 + lax.erf(value * 0.7071067811865476))
            slope = phi + value * (0.3989422804014327 * jnp.exp2(value * value * (-0.5 * LOG2E)))
            act[x, :, cols] = (value * phi).astype(bf16)
            pre[x, :, cols] = (grad_act[x, :, cols] * slope).astype(bf16)
            return 0

        lax.fori_loop(0, 4, tile, 0)

    def backward(x):
        def tile(n, _):
            cols = piece(n, 256)
            parts[x, :, :, cols] = dot_nt(pre[x], up_v[cols, :]).astype(bf16).reshape(2, 128, 256)
            return 0

        lax.fori_loop(0, 8, tile, 0)
        parts[x, :, :, pl.ds(2048, 128)] = dot_nt(pre[x], umap[...]).astype(bf16).reshape(2, 128, 128)

    gather.own()
    hidden(place.x)
    gather.near()
    hidden(place.step("x", -1))
    hidden(place.step("x", 1))
    gather.far()
    gather.far_done()
    hidden(place.step("x", 2))

    sums = GroupSum(place, sends, parts, scratch)
    backward(sums.xs[0])
    sums.cross(0)
    backward(sums.xs[1])
    sums.cross(1)
    sums.merge(0)
    sums.first()
    backward(sums.xs[2])
    sums.cross(2)
    backward(sums.xs[3])
    sums.cross(3)
    sums.merge(1)
    sums.merge(2)
    sums.second()

    def forward(n, _):
        x, cols = n // 4, piece(lax.rem(n, 4), 512)
        value = dot(act[x], dn_v[:, cols])
        forth[x, :, :, cols] = value.astype(bf16).reshape(2, 128, 512)
        return 0

    lax.fori_loop(0, 16, forward, 0)

    def small(x, _):
        forth[x, :, :, pl.ds(2048, 128)] = dot(act[x], dmap[...]).astype(bf16).reshape(2, 128, 128)
        one = dot_tn(act[x], rows(cot, x, 2048, 128))
        other = dot_tn(pre[x], rows(sa, x, 2048, 128))

        @pl.when(x == 0)
        def _():
            total[0] = one
            total[1] = other

        @pl.when(x > 0)
        def _():
            total[0] += one
            total[1] += other

        return 0

    lax.fori_loop(0, 4, small, 0)
    two[...] = total[...].astype(bf16)
    back[...] = sums.result()
    gather.finish()


def feed_forward(second, cot_all, up, dn, umap, dmap, bias):
    any_ = pl.BlockSpec(memory_space=pl.ANY)
    vmem = pl.BlockSpec(memory_space=pltpu.VMEM)
    vm = lambda *s: pltpu.VMEM(s, bf16)
    return pl.pallas_call(
        feed_forward_kernel,
        name="feed_forward",
        out_shape=[
            jax.ShapeDtypeStruct((128, 2176), f32),
            jax.ShapeDtypeStruct((4, 2, 128, 2176), bf16),
            jax.ShapeDtypeStruct((2, 1024, 128), bf16),
        ],
        in_specs=[vmem] + [any_] * 3 + [vmem] * 3,
        out_specs=[vmem] * 3,
        scratch_shapes=[
            vm(4, 2, 128, 2176),
            vm(4, 2, 128, 2176),
            vm(2048, 1024),
            vm(1024, 2048),
            pltpu.VMEM((4, 256, 1024), f32),
            vm(4, 256, 1024),
            vm(4, 256, 1024),
            vm(4, 2, 128, 2176),
            pltpu.VMEM((2, 1024, 128), f32),
        ]
        + GroupSum.scratch(2176)
        + [pltpu.SemaphoreType.DMA((k,)) for k in (16, 16, 3)],
        compiler_params=pltpu.CompilerParams(collective_id=1, has_side_effects=True, vmem_limit_bytes=60 * MIB),
    )(second, cot_all, up, dn, umap, dmap, bias)


def both_heads(gq, p, x):
    heads = [gq[p, x, :, j].reshape(256, 128) for j in range(2)]
    return jnp.concatenate(heads, axis=1)


def tail_kernel(
    grads, qkv_w, act_all, umaps, dmaps, mask, tok, gain, grad_res,
    input_grad, a_final, b_final,
    a_res, b_res, gq, wq, act, parts, gaq, a_sum, b_sum, a_s1, a_q1, a_s2, a_f, b_s1, b_q1, b_s2, b_f, *refs,
):
    scratch, (send, recv, local) = refs[:-3], refs[-3:]
    place = Place()
    greet(members(place) + neighbours(place, ("y", "z")))
    sends = Sends(send, recv)
    loads = [
        pltpu.make_async_copy(src, dst, local.at[n])
        for n, (src, dst) in enumerate(((grads, gq), (qkv_w, wq), (act_all, act)))
    ]
    for copy in loads:
        copy.start()
    loads[0].wait()
    loads[1].wait()

    def partial(x):
        left = [both_heads(gq, p, x) for p in range(3)]

        def tile(n, _):
            xl, c, z = n // 4, lax.rem(n // 2, 2), piece(lax.rem(n, 2), 2)
            value = dot_nt(left[0], wq[0, xl, c, z].reshape(256, 256))
            for p in (1, 2):
                value = value + dot_nt(left[p], wq[p, xl, c, z].reshape(256, 256))
            parts[x, :, :, piece(n, 256)] = value.astype(bf16).reshape(2, 128, 256)
            return 0

        lax.fori_loop(0, 8, tile, 0)
        for p in range(3):
            value = dot_nt(left[p], umaps[p]).astype(bf16)
            parts[x, :, :, 2048 + p * 128 : 2176 + p * 128] = value.reshape(2, 128, 128)

    sums = GroupSum(place, sends, parts, scratch)
    partial(sums.xs[0])
    sums.cross(0)
    partial(sums.xs[1])
    sums.cross(1)
    sums.merge(0)
    sums.first()
    partial(sums.xs[2])
    sums.cross(2)
    partial(sums.xs[3])
    sums.cross(3)
    sums.merge(1)
    sums.merge(2)
    sums.second()

    loads[2].wait()
    for p in range(3):
        total = jnp.zeros((128, 256), f32)
        for x in range(4):
            low_rank = act[x, :, :, 2048 + p * 128 : 2176 + p * 128].reshape(256, 128)
            total = total + dot_tn(low_rank, both_heads(gq, p, x))
        b_sum[p] = total.astype(bf16)

    here = {a: place.at(a) for a in "xyz"}

    def b_view(fixed, half):
        y = fixed.get("y")
        yr, yc = (ALL, ALL) if y is None else (y // 2, lax.rem(y, 2))
        if half is not None:
            yr = pl.ds(half, 1)
        return b_res.at[:, fixed.get("x", ALL), place.c, fixed.get("z", ALL), yr, yc]

    keep = pltpu.make_async_copy(b_f, b_view(here, None), local.at[3])
    b_part = spread_sum(
        place, sends, ("z", "y"),
        [
            (lambda p: b_sum.at[:, piece(p, 32)], b_s1, b_q1),
            (lambda p: b_q1.at[:, piece(p // 2, 16), piece(lax.rem(p, 2), 128)], b_s2, b_f),
        ],
        (b_view, ("y", "z", "x")), b_f, keep,
    )
    next(b_part)
    total = sums.result()
    own = gaq.at[place.x, place.c]
    grad_first = total[:, 0:2048]
    for p in range(3):
        low_rank = (total[:, 2048 + p * 128 : 2176 + p * 128] * mask[...]).astype(bf16)
        own[:, p * 128 : p * 128 + 128] = low_rank
        grad_first = grad_first + dot_nt(low_rank, dmaps[p])
    gather = GroupGather(place, sends, gaq)
    next(b_part)
    result = grad_res[...] + layer_norm_back(tok[...].astype(f32), gain[...], grad_first)
    input_grad[...] = result.astype(bf16)
    gather.own()
    gather.near()
    next(b_part)
    gather.far()
    gather.far_done()

    cols = piece(place.g, 256)
    left = act[:, :, :, cols].reshape(1024, 256)
    for p in range(3):
        right = gaq[:, :, :, p * 128 : p * 128 + 128].reshape(1024, 128)
        a_sum[p] = dot_tn(left, right).astype(bf16)

    def a_view(fixed, half):
        y = fixed.get("y", ALL)
        if half is not None:
            y = pl.ds(half * 2, 2)
        return a_res.at[:, fixed.get("x", ALL), place.c, fixed.get("z", ALL), y]

    keep = pltpu.make_async_copy(a_f, a_view(here, None), local.at[4])
    a_part = spread_sum(
        place, sends, ("z", "y"),
        [
            (lambda p: a_sum.at[:, piece(p, 64)], a_s1, a_q1),
            (lambda p: a_q1.at[:, piece(p, 16)], a_s2, a_f),
        ],
        (a_view, ("y", "x", "z")), a_f, keep,
    )
    run_all([a_part, b_part])
    gather.finish()
    moves = [pltpu.make_async_copy(a_res, a_final, local.at[5])]
    for g in range(8):
        for yc in range(2):
            src = b_res.at[:, g // 2, g % 2, :, :, yc]
            dst = b_final.at[:, :, :, :, pl.ds(g * 256 + yc * 128, 128)]
            moves.append(pltpu.make_async_copy(src, dst, local.at[6 + g * 2 + yc]))
    for copy in moves:
        copy.start()
    for copy in moves:
        copy.wait()
    assert sends.used <= send.shape[0], sends.used


def tail(grads, qkv_w, act_all, umaps, dmaps, mask, tok, gain, grad_res):
    any_ = pl.BlockSpec(memory_space=pl.ANY)
    vmem = pl.BlockSpec(memory_space=pltpu.VMEM)
    vm = lambda *s: pltpu.VMEM(s, bf16)
    shape = lambda *s: jax.ShapeDtypeStruct(s, bf16)
    a_shape, b_shape = (3, 4, 2, 4, 4, 16, 128), (3, 4, 2, 4, 2, 2, 16, 128)
    return pl.pallas_call(
        tail_kernel,
        name="tail",
        out_shape=[shape(128, 2048), shape(*a_shape), shape(3, 4, 2, 16, 2048)],
        in_specs=[any_] * 3 + [vmem] * 6,
        out_specs=[vmem] + [any_] * 2,
        scratch_shapes=[
            vm(*a_shape),
            vm(*b_shape),
            vm(3, 4, 2, 2, 128, 128),
            vm(3, 2, 2, 4, 4, 2, 16, 256),
            vm(4, 2, 128, 2432),
            vm(4, 2, 128, 2432),
            vm(4, 2, 128, 384),
            vm(3, 256, 128),
            vm(3, 128, 256),
            vm(3, 3, 64, 128),
            vm(3, 64, 128),
            vm(3, 3, 16, 128),
            vm(3, 16, 128),
            vm(3, 3, 32, 256),
            vm(3, 32, 256),
            vm(3, 3, 16, 128),
            vm(3, 16, 128),
        ]
        + GroupSum.scratch(2432)
        + [pltpu.SemaphoreType.DMA((k,)) for k in (100, 100, 22)],
        compiler_params=pltpu.CompilerParams(collective_id=5, has_side_effects=True, vmem_limit_bytes=56 * MIB),
    )(grads, qkv_w, act_all, umaps, dmaps, mask, tok, gain, grad_res)


def per_device(
    tokens,
    document_starts,
    document_adapter,
    layernorm_gain,
    layernorm_bias,
    projection_weight,
    output_weight,
    up_weight,
    down_weight,
    projection_bias,
    upper_bias,
    attention_down_maps,
    attention_up_maps,
    upper_down_maps,
    upper_up_maps,
    lower_down_maps,
    lower_up_maps,
    cotangent,
):
    local_rows, width = tokens.shape[1:]
    head_size = width // HEADS
    seq = local_rows * 32
    scale = head_size ** (-0.5)
    starts = document_starts[0]
    chosen = document_adapter[0]
    xl, c, z, y, xh = (lax.axis_index(a) for a in AXES)
    group = (xh * 2 + xl) * 2 + c
    first_row = ((z * 4 + y) * 2 + xh) * local_rows
    local_pos = first_row + jnp.arange(local_rows, dtype=jnp.int32)
    local_seg = jnp.sum((starts[None, :] <= local_pos[:, None]).astype(jnp.int32), axis=1) - 1
    doc_ids = jnp.arange(starts.shape[0], dtype=jnp.int32)
    token_adapter = jnp.sum(jnp.where(local_seg[:, None] == doc_ids[None, :], chosen[None, :], 0), axis=1)
    columns = jnp.arange(upper_down_maps.shape[1], dtype=jnp.int32) // ADAPTER_RANK
    mask = (token_adapter[:, None] == columns[None, :]).astype(f32)

    rows = seq // 2
    q_pos = positions_of(jnp.arange(rows, dtype=jnp.int32), xh)
    doc_lo = jnp.max(jnp.where(starts[None, :] <= q_pos[:, None], starts[None, :], 0), axis=1)
    last_key = (2 * ((jnp.arange(rows // K_TILE) + 1) * K_TILE // 128 - 1) + 1) * 128 + 127
    doc_end = jnp.min(jnp.where(starts[None, :] > last_key[:, None], starts[None, :], seq), axis=1)
    last_q_tile = jnp.minimum((doc_end + 255) // 256 * 128 + Q_TILE - 1, rows + Q_TILE - 1) // Q_TILE
    info_back = jnp.concatenate([xh[None], last_q_tile]).astype(jnp.int32)

    inputs = tokens[0].astype(f32)
    cot = cotangent[0]
    bias_rows = jnp.stack([projection_bias[0], jnp.zeros_like(projection_bias[0]), projection_bias[1]])

    def my_columns(array):
        return lax.dynamic_slice_in_dim(array, group * 256, 256, array.ndim - 1)

    def my_hidden(array):
        lead = array.shape[:-1]
        part = lax.dynamic_slice_in_dim(array, (xl * 2 + c) * 2048, 2048, array.ndim - 1)
        part = part.reshape(lead + (16, 2, 64))
        return lax.dynamic_index_in_dim(part, xh, len(lead) + 1, False).reshape(lead + (1024,))

    up_members = jnp.transpose(up_weight.reshape(16, 2, 2, 16, 2, 64), (0, 4, 1, 2, 3, 5)).reshape(16, 8192)
    my_up_maps = my_columns(attention_up_maps[:3])
    (
        act_all, qkv_w, out_all, up_all, dn_all, cot_all, by_head, across, merged, attended, lse
    ) = front(
        tokens[0], layernorm_gain[:1], layernorm_bias[:1], my_columns(bias_rows)[:, None, :],
        attention_down_maps[:3], my_up_maps, mask, cot, lower_up_maps, doc_lo[:, None],
        jnp.transpose(projection_weight, (1, 0, 2)), output_weight, up_members, down_weight, scale,
    )
    w_out = out_all.reshape(width, width)
    lse = lse.reshape(rows // Q_TILE, 8, Q_TILE)[:, 0]

    adapt_out = (dot(merged, attention_down_maps[3]) * mask).astype(bf16)
    residual = inputs + dot(merged, w_out) + projection_bias[2] + dot(adapt_out, attention_up_maps[3])
    second_in = layer_norm(residual, layernorm_gain[1], layernorm_bias[1]).astype(bf16)
    adapt_up = (dot(second_in, upper_down_maps) * mask).astype(bf16)

    down_maps = lax.dynamic_slice_in_dim(lower_down_maps, (xl * 2 + c) * 2048, 2048, 0)
    down_maps = lax.dynamic_index_in_dim(down_maps.reshape(16, 2, 64, 128), xh, 1, False).reshape(1024, 128)
    back, forth, two = feed_forward(
        jnp.concatenate([second_in, adapt_up], axis=1), cot_all, up_all.reshape(width, 1024),
        dn_all.reshape(1024, width), my_hidden(upper_up_maps), down_maps, my_hidden(upper_bias)[None],
    )

    grad_adapt_up = (back[:, width:] * mask).astype(bf16)
    grad_a_up = dot_tn(second_in, grad_adapt_up)
    grad_second = back[:, :width] + dot_nt(grad_adapt_up, upper_down_maps)
    grad_residual = cot.astype(f32) + layer_norm_back(residual, layernorm_gain[1], grad_second)
    grad_branch = grad_residual.astype(bf16)
    grad_b_out = dot_tn(adapt_out, grad_branch)
    grad_adapt_out = (dot_nt(grad_branch, attention_up_maps[3]) * mask).astype(bf16)
    grad_a_out = dot_tn(merged, grad_adapt_out)
    grad_merged = (dot_nt(grad_branch, w_out) + dot_nt(grad_adapt_out, attention_down_maps[3])).astype(bf16)

    grad_heads, forth_sum = grads_in(grad_merged, forth)
    adapt_down = (forth_sum[:, width:] * mask).astype(bf16)
    output = residual + forth_sum[:, :width] + projection_bias[3] + dot(adapt_down, lower_up_maps)
    grad_b_down = dot_tn(adapt_down, cot)

    grad_heads = grad_heads.reshape(rows, head_size)
    row_dot = jnp.sum(grad_heads.astype(f32) * attended, axis=-1).reshape(rows // Q_TILE, Q_TILE)
    dq, other, own = flash_backward(
        info_back, grad_heads, lse, row_dot, doc_lo.reshape(rows // Q_TILE, Q_TILE), by_head, across, scale
    )
    grad_qkv = grads_out(dq.reshape(HEADS, local_rows, head_size), other, own)
    early = sum_all(
        jnp.stack([grad_a_out, grad_a_up]).astype(bf16), jnp.stack([grad_b_out, grad_b_down]).astype(bf16), two
    )
    input_grad, late_a, late_b = tail(
        grad_qkv, qkv_w, act_all, my_up_maps, attention_down_maps[:3], mask, tokens[0], layernorm_gain[:1],
        grad_residual,
    )
    late_a = late_a.reshape(3, width, 128)
    late_b = late_b.reshape(3, 128, width)
    return (
        output.astype(bf16)[None],
        input_grad[None],
        jnp.concatenate([late_a, early[0][:1]]).astype(f32),
        jnp.concatenate([late_b, early[1][:1]]).astype(f32),
        early[0][1].astype(f32),
        jnp.transpose(early[2][1]).astype(f32),
        early[2][0].astype(f32),
        early[1][1].astype(f32),
    )


def solution(mesh):
    fine = jax.sharding.Mesh(mesh.devices.reshape(SIZES), AXES)
    by_token = P(STREAM, TOKEN, None)
    shard = AXES
    in_specs = (
        by_token,
        P(STREAM, None),
        P(STREAM, None),
        P(),
        P(),
        P(shard, None, None),
        P(shard, None),
        P(shard, None),
        P(shard, None),
        P(),
        P(),
        P(),
        P(),
        P(),
        P(),
        P(),
        P(),
        by_token,
    )
    out_specs = (by_token, by_token, P(), P(), P(), P(), P(), P())
    return jax.shard_map(per_device, mesh=fine, in_specs=in_specs, out_specs=out_specs, check_vma=False)
```

```python
import functools

import jax
import jax.numpy as jnp
from jax import lax
from jax.experimental import pallas as pl
from jax.experimental.pallas import tpu as pltpu
from jax.sharding import PartitionSpec as P

HEADS = 16
ADAPTER_RANK = 16
MESH = pl.DeviceIdType.MESH
AXES = ("xl", "c", "z", "y", "xh")
SIZES = (2, 2, 4, 4, 2)
STREAM = ("xl", "c")
TOKEN = ("z", "y", "xh")
bf16 = jnp.bfloat16
f32 = jnp.float32
LOG2E = 1.4426950408889634
MIB = 2**20
Q_TILE = 256
K_TILE = 512
F_TILE = 256
ALL = slice(None)


def layer_norm(values, gain, shift):
    center = values - jnp.mean(values, axis=-1, keepdims=True)
    spread = jnp.mean(center * center, axis=-1, keepdims=True)
    return center * lax.rsqrt(spread + 1e-05) * gain + shift


def layer_norm_back(values, gain, grad):
    center = values - jnp.mean(values, axis=-1, keepdims=True)
    scale = lax.rsqrt(jnp.mean(center * center, axis=-1, keepdims=True) + 1e-05)
    unit = center * scale
    grad = grad * gain
    along = jnp.mean(grad * unit, axis=-1, keepdims=True)
    return scale * (grad - jnp.mean(grad, axis=-1, keepdims=True) - unit * along)


def dot(left, right):
    return jnp.dot(left, right, preferred_element_type=f32)


def dot_nt(left, right):
    return lax.dot_general(left, right, (((1,), (1,)), ((), ())), preferred_element_type=f32)


def dot_tn(left, right):
    return lax.dot_general(left, right, (((0,), (0,)), ((), ())), preferred_element_type=f32)


def piece(n, size):
    return pl.ds(pl.multiple_of(n * size, size), size)


class Place:
    def __init__(self):
        self.xl, self.c, self.z, self.y, self.xh = (lax.axis_index(a) for a in AXES)
        self.x = self.xh * 2 + self.xl
        self.g = self.x * 2 + self.c

    def at(self, axis):
        return {"x": self.x, "y": self.y, "z": self.z}[axis]

    def step(self, axis, step):
        return lax.rem(self.at(axis) + (step + 4), 4)

    def toward(self, axis, step=1):
        if axis == "c":
            return {"c": 1 - self.c}
        to = self.step(axis, step)
        if axis == "x":
            return {"xl": lax.rem(to, 2), "xh": to // 2}
        return {axis: to}

    def member(self, dx, dc):
        to = {}
        if dx:
            to |= self.toward("x", dx)
        if dc:
            to |= {"c": 1 - self.c}
        return to


MEMBERS = [(dx, dc) for dx in (2, 1, 3, 0) for dc in (0, 1) if dx or dc]


class Sends:
    def __init__(self, send, recv):
        self.send, self.recv, self.used, self.open = send, recv, 0, []

    def push(self, src, dst, device):
        k = self.used
        self.used += 1
        copy = pltpu.make_async_remote_copy(
            src_ref=src,
            dst_ref=dst,
            send_sem=self.send.at[k],
            recv_sem=self.recv.at[k],
            device_id=device,
            device_id_type=MESH,
        )
        copy.start()
        self.open.append(copy)
        return copy


def greet(devices, perhaps=()):
    barrier = pltpu.get_barrier_semaphore()
    for device in devices:
        pl.semaphore_signal(barrier, inc=1, device_id=device, device_id_type=MESH)
    amount = len(devices) + len(perhaps)
    for device, myself in perhaps:
        amount = amount - myself.astype(jnp.int32)

        @pl.when(jnp.logical_not(myself))
        def _():
            pl.semaphore_signal(barrier, inc=1, device_id=device, device_id_type=MESH)

    pl.semaphore_wait(barrier, amount)


def run_all(parts):
    parts = list(parts)
    while parts:
        left = []
        for part in parts:
            try:
                next(part)
                left.append(part)
            except StopIteration:
                pass
        parts = left


def ring_gather(place, sends, view, order, chunk, landed, forward):
    fixed = {a: place.at(a) for a in order}
    across = place.toward("c")
    later, passed = [], []

    def pass_on(block):
        if forward:
            passed.append(sends.push(view(block, None), view(block, None), across))

    if forward:
        passed.append(sends.push(chunk, view(fixed, None), across))
    for number, axis in enumerate(order):
        own = view(fixed, None)
        src = chunk if number == 0 else own
        if number == 0:
            sent = [sends.push(src, own, place.toward(axis, s)) for s in (2, 1, 3)]
            yield
            for s, copy in zip((2, 1, 3), sent):
                copy.wait_recv()
                pass_on(fixed | {axis: place.step(axis, -s)})
            landed.wait()
            later += sent
            del fixed[axis]
            continue
        up = sends.push(src, own, place.toward(axis, 1))
        down = sends.push(src, own, place.toward(axis, -1))
        yield
        before = fixed | {axis: place.step(axis, -1)}
        after = fixed | {axis: place.step(axis, 1)}
        opposite = fixed | {axis: place.step(axis, 2)}
        up.wait_recv()
        half = view(before, 0)
        up_two = sends.push(half, half, place.toward(axis, 1))
        down.wait_recv()
        half = view(after, 1)
        down_two = sends.push(half, half, place.toward(axis, -1))
        pass_on(before)
        pass_on(after)
        yield
        up_two.wait_recv()
        down_two.wait_recv()
        pass_on(opposite)
        later += [up, down, up_two, down_two]
        del fixed[axis]
    yield
    for copy in later:
        copy.wait_send()
    for copy in passed:
        copy.wait()


class Nothing:
    def wait(self):
        pass


def neighbours(place, axes):
    return [place.toward(a, s) for a in axes for s in ((1, 2, 3) if a in "xyz" else (1,))]


def members(place):
    return [place.member(*m) for m in MEMBERS]


class GroupGather:
    def __init__(self, place, sends, buf):
        self.place, self.sends, self.buf = place, sends, buf
        self.mine = buf.at[place.x, place.c]
        self.right, self.left = place.toward("x", 1), place.toward("x", -1)
        self.up = sends.push(self.mine, self.mine, self.right)
        self.down = sends.push(self.mine, self.mine, self.left)
        self.passed = [self.pass_on(self.mine)]

    def pass_on(self, ref):
        return self.sends.push(ref, ref, self.place.toward("c"))

    def own(self):
        self.passed[0].wait_recv()

    def near(self, wait=True):
        x, c = self.place.step("x", -1), self.place.c
        self.up.wait_recv()
        half = self.buf.at[x, c, pl.ds(0, 64)]
        self.up_two = self.sends.push(half, half, self.right)
        self.passed.append(self.pass_on(self.buf.at[x, c]))
        x = self.place.step("x", 1)
        self.down.wait_recv()
        half = self.buf.at[x, c, pl.ds(64, 64)]
        self.down_two = self.sends.push(half, half, self.left)
        self.passed.append(self.pass_on(self.buf.at[x, c]))
        if wait:
            self.near_done()

    def near_done(self):
        self.passed[1].wait_recv()
        self.passed[2].wait_recv()

    def far(self):
        self.up_two.wait_recv()
        self.down_two.wait_recv()
        self.passed.append(self.pass_on(self.buf.at[self.place.step("x", 2), self.place.c]))

    def far_done(self):
        self.passed[3].wait_recv()

    def finish(self):
        for copy in [self.up, self.down, self.up_two, self.down_two] + self.passed:
            copy.wait_send()


def group_gather(place, sends, buf):
    gather = GroupGather(place, sends, buf)
    yield
    gather.own()
    gather.near()
    yield
    gather.far()
    yield
    gather.far_done()
    gather.finish()


def places_in_turn(place):
    return [place.step("x", s) for s in (2, 1, -1, 0)]


class GroupSum:
    def __init__(self, place, sends, parts, scratch):
        self.place, self.sends, self.parts = place, sends, parts
        self.came, self.own, self.left_one, self.right_one, self.left_two, self.right_two = scratch
        self.right, self.left = place.toward("x", 1), place.toward("x", -1)
        self.crossed = {}

    @staticmethod
    def scratch(n):
        vm = lambda *s: pltpu.VMEM(s, bf16)
        return [vm(4, 128, n), vm(3, 128, n), vm(64, n), vm(64, n), vm(128, n), vm(128, n)]

    def cross(self, k):
        place = self.place
        self.crossed[k] = self.sends.push(
            self.parts.at[k, 1 - place.c], self.came.at[k], place.toward("c")
        )

    def merge(self, k):
        self.crossed[k].wait()
        both = self.parts[k, self.place.c].astype(f32) + self.came[k].astype(f32)
        self.own[k] = both.astype(bf16)

    def first(self):
        self.up = self.sends.push(self.own.at[0, pl.ds(0, 64)], self.left_one, self.right)
        self.down = self.sends.push(self.own.at[0, pl.ds(64, 64)], self.right_one, self.left)

    def second(self):
        self.up.wait()
        both = self.own[1, 0:64].astype(f32) + self.left_one[...].astype(f32)
        self.own[1, 0:64] = both.astype(bf16)
        self.up_two = self.sends.push(self.own.at[1], self.left_two, self.right)
        self.down.wait()
        both = self.own[2, 64:128].astype(f32) + self.right_one[...].astype(f32)
        self.own[2, 64:128] = both.astype(bf16)
        self.down_two = self.sends.push(self.own.at[2], self.right_two, self.left)

    def result(self):
        self.crossed[3].wait()
        total = self.parts[3, self.place.c].astype(f32) + self.came[3].astype(f32)
        self.up_two.wait()
        self.down_two.wait()
        return total + self.left_two[...].astype(f32) + self.right_two[...].astype(f32)


def group_sum(place, sends, parts, scratch, out):
    total = GroupSum(place, sends, parts, scratch)
    for k in range(4):
        total.cross(k)
    yield
    total.merge(0)
    total.first()
    total.merge(1)
    total.merge(2)
    yield
    total.second()
    yield
    out[...] = total.result()


def plane(place):
    steps = [(i, j) for i in (2, 1, 3, 0) for j in (2, 1, 3, 0) if i or j]
    return [(lax.rem(place.z + i, 4), lax.rem(place.y + j, 4)) for i, j in steps]


def from_plane(place):
    steps = [(i, j) for i in (2, 1, 3, 0) for j in (2, 1, 3, 0) if i or j]
    return [(lax.rem(place.z + 4 - i, 4), lax.rem(place.y + 4 - j, 4)) for i, j in steps]


def projectors(place):
    x, c = place.z, place.y // 2
    member = {"xl": lax.rem(x, 2), "xh": x // 2, "c": c}
    mine = (place.x == x) & (place.c == c)
    return [(member | {"z": z, "y": y}, None) for z, y in plane(place)] + [
        (member | {"z": place.z, "y": place.y}, mine)
    ]


def attenders(place):
    found = []
    for dx, dc in MEMBERS + [(0, 0)]:
        for j in range(2):
            z, y = place.x, 2 * place.c + j
            device = place.member(dx, dc) | {"z": z, "y": y}
            mine = None if dx or dc else (place.z == z) & (place.y == y)
            found.append((dx, dc, j, device, mine))
    return found


def head_columns(z, y):
    return pl.ds(pl.multiple_of((z * 4 + y) * 128, 128), 128)


def split_greeting(pairs):
    return [d for d, m in pairs if m is None], [(d, m) for d, m in pairs if m is not None]


def plane_devices(place):
    return [{"z": z, "y": y} for z, y in plane(place)]


class Post:
    def __init__(self, src, dst, device, myself, send_sem, recv_sem):
        self.remote = pltpu.make_async_remote_copy(
            src_ref=src, dst_ref=dst, send_sem=send_sem, recv_sem=recv_sem, device_id=device, device_id_type=MESH
        )
        self.myself = myself
        if myself is None:
            self.remote.start()
        else:
            pl.when(myself)(pltpu.make_async_copy(src, dst, recv_sem).start)
            pl.when(jnp.logical_not(myself))(self.remote.start)

    def wait_send(self):
        if self.myself is None:
            self.remote.wait_send()
        else:
            pl.when(jnp.logical_not(self.myself))(self.remote.wait_send)


def heads_out(place, sends, blocks, merged, local):
    cols = head_columns(place.z, place.y)
    keep = pltpu.make_async_copy(blocks.at[place.z * 4 + place.y], merged.at[:, cols], local)
    keep.start()
    sent = [sends.push(blocks.at[z * 4 + y], merged.at[:, cols], {"z": z, "y": y}) for z, y in plane(place)]
    yield
    for copy in sent:
        copy.wait()
    keep.wait()


def reduce_piece(place, sends, final, across, plane_step, along):
    if across:
        src, came, own, out = across
        copy = sends.push(src, came, place.toward("c"))
        yield
        copy.wait()
        out[...] = (own[...].astype(f32) + came[...].astype(f32)).astype(bf16)
    held, slots, out = plane_step
    sent = [sends.push(held(z, y), slots.at[n], {"z": z, "y": y}) for n, (z, y) in enumerate(plane(place))]
    yield
    for copy in sent:
        copy.wait()
    total = held(place.z, place.y)[...].astype(f32)
    for n in range(15):
        total = total + slots[n].astype(f32)
    out[...] = total.astype(bf16)
    if along:
        held, slots, out = along
        sent = [sends.push(held(place.step("x", d)), slots.at[d - 1], place.toward("x", d)) for d in (2, 1, 3)]
        yield
        for copy in sent:
            copy.wait()
        total = held(place.x)[...].astype(f32)
        for d in range(3):
            total = total + slots[d].astype(f32)
        out[...] = total.astype(bf16)


def give_all(place, sends, order, final, view, local):
    here = {a: place.at(a) for a in "xyz"}
    keep = pltpu.make_async_copy(final, view(here), local)
    keep.start()

    def fixed_view(fixed, half):
        at = {a: fixed.get(a, ALL) for a in "xyz"}
        if half is not None:
            at[order[0]] = pl.ds(half * 2, 2)
        return view(at)

    return ring_gather(place, sends, fixed_view, order, final, keep, True)


def a_sum_scratch():
    vm = lambda *shape: pltpu.VMEM(shape, bf16)
    return [vm(1024, 128), vm(1024, 128), vm(15, 64, 128), vm(64, 128), vm(3, 16, 128)]


def b_sum_scratch():
    vm = lambda *shape: pltpu.VMEM(shape, bf16)
    return [vm(64, 2048), vm(64, 2048), vm(15, 64, 128), vm(64, 128), vm(3, 16, 128)]


def a_sum(place, sends, a, final, scratch):
    came, half, s1, quarter, s2 = scratch
    return reduce_piece(
        place, sends, final,
        (a.at[piece(1 - place.c, 1024)], came, a.at[piece(place.c, 1024)], half),
        (lambda z, y: half.at[piece(z * 4 + y, 64)], s1, quarter),
        (lambda x: quarter.at[piece(x, 16)], s2, final),
    )


def b_sum(place, sends, b, final, scratch):
    came, half, s1, quarter, s2 = scratch
    return reduce_piece(
        place, sends, final,
        (b.at[piece(1 - place.c, 64)], came, b.at[piece(place.c, 64)], half),
        (lambda z, y: half.at[:, piece(z * 4 + y, 128)], s1, quarter),
        (lambda x: quarter.at[piece(x, 16)], s2, final),
    )


def two_parts(at):
    x = at["x"]
    if x is ALL:
        return ALL, ALL
    if isinstance(x, pl.Slice):
        return pl.ds(x.start // 2, 1), ALL
    return lax.rem(x, 2), x // 2


def positions_of(local, parity):
    return (2 * (local // 128) + parity) * 128 + lax.rem(local, 128)


def document_start(starts, positions):
    found = jnp.zeros_like(positions)
    for d in range(8):
        found = jnp.where(positions >= starts[0, d], starts[0, d], found)
    return found


def attend(t, mine, others, starts, parity, scale):
    q = mine[0, piece(t, F_TILE), :]
    q_pos = positions_of(t * F_TILE + lax.broadcasted_iota(jnp.int32, (F_TILE, 1), 0), parity)
    lo = document_start(starts, q_pos)
    ones = jnp.ones((K_TILE, 128), bf16)

    def step(kt, carry):
        top, acc = carry
        rows = piece(kt, K_TILE)
        local = kt * K_TILE + lax.broadcasted_iota(jnp.int32, (1, K_TILE), 1)
        scores = []
        for k, k_parity in ((mine[1, rows, :], parity), (others[0, rows, :], 1 - parity)):
            k_pos = positions_of(local, k_parity)
            scores.append(jnp.where((k_pos >= lo) & (k_pos <= q_pos), dot_nt(q, k), -1e30))
        new = jnp.maximum(jnp.max(scores[0], axis=1, keepdims=True), jnp.max(scores[1], axis=1, keepdims=True))
        new = jnp.maximum(top, new)
        acc = acc * jnp.exp2((top - new) * (scale * LOG2E))
        for s, v in zip(scores, (mine[2, rows, :], others[1, rows, :])):
            p = jnp.exp2((s - new) * (scale * LOG2E)).astype(bf16)
            acc = acc + dot(p, jnp.concatenate([v, ones], axis=1))
        return new, acc

    start = (jnp.full((F_TILE, 1), -1e30, f32), jnp.zeros((F_TILE, 256), f32))
    return lax.fori_loop(0, (t * F_TILE + F_TILE + K_TILE - 1) // K_TILE, step, start)


def front_kernel(
    starts, chosen, tok, gain, shift, bias, dmaps, umaps, cot, lum, wp, wo, up, dn,
    act_all, qkv_w, out_all, up_all, dn_all, cot_all, heads, across, merged, att, lse, mask,
    act, cotbuf, wq, up_own, rows, mine, others, low, wq_t, send, recv, a_send, a_recv, local, *, scale,
):
    place = Place()
    sends = Sends(send, recv)
    always, perhaps = split_greeting(projectors(place))
    greet(plane_devices(place) + members(place) + always, perhaps)
    home = (place.xl, place.c, place.z, place.y, place.xh)

    def out_view(h):
        def view(fixed, half):
            xl, xh = (ALL, ALL)
            if "x" in fixed:
                xl, xh = lax.rem(fixed["x"], 2), fixed["x"] // 2
            cols = pl.ds(h * 1024, 1024) if half is None else pl.ds(h * 1024 + half * 512, 512)
            return out_all.at[xl, place.c, fixed.get("z", ALL), fixed.get("y", ALL), xh, ALL, cols]

        return view

    def up_view(fixed, half):
        xl = ALL if half is None else pl.ds(half, 1)
        return up_all.at[xl, ALL, fixed.get("z", ALL), fixed.get("y", ALL)]

    def dn_view(fixed, half):
        cols = ALL if half is None else pl.ds(half * 1024, 1024)
        return dn_all.at[fixed.get("z", ALL), fixed.get("y", ALL), :, cols]

    def wq_view(p, cols):
        def view(fixed, half):
            xl = ALL if half is None else pl.ds(half, 1)
            return wq.at[p, xl, ALL, fixed.get("z", ALL), fixed.get("y", ALL), ALL, ALL, cols]

        return view

    def index(dx, dc):
        return place.step("x", dx) * 2 + (1 - place.c if dc else place.c)

    copies = [
        pltpu.make_async_copy(
            wp.at[:, :, piece(place.g, 256)], wq.at[:, place.xl, place.c, place.z, place.y, place.xh], local.at[0]
        ),
        pltpu.make_async_copy(dn, dn_all.at[place.z, place.y], local.at[2]),
    ]
    copies += [
        pltpu.make_async_copy(
            wo.at[:, pl.ds(h * 1024, 1024)],
            out_view(h)({a: place.at(a) for a in "xyz"}, None),
            local.at[3 + h],
        )
        for h in range(2)
    ]
    for copy in copies:
        copy.start()
    wq_spread = [
        sends.push(
            wp.at[:, :, piece(index(*m), 256)],
            wq.at[:, place.xl, place.c, place.z, place.y, place.xh],
            place.member(*m),
        )
        for m in MEMBERS
    ]

    values = tok[...].astype(f32)
    normed = layer_norm(values, gain[...], shift[...]).astype(bf16)
    position = ((place.z * 4 + place.y) * 2 + place.xh) * 128 + lax.broadcasted_iota(jnp.int32, (128, 1), 0)
    adapter = jnp.zeros_like(position)
    for d in range(8):
        adapter = jnp.where(position >= starts[0, d], chosen[0, d], adapter)
    column = lax.broadcasted_iota(jnp.int32, (128, 128), 1) // ADAPTER_RANK
    keep = (column == adapter).astype(f32)
    mask[...] = keep
    own = act.at[place.x, place.c]
    own[:, 0:2048] = normed
    for p in range(3):
        own[:, 2048 + p * 128 : 2176 + p * 128] = (dot(normed, dmaps[p]) * keep).astype(bf16)
    act_gather = GroupGather(place, sends, act)

    for lead in range(4):
        for pair in range(8):
            at = lead * 2048 + pair * 256
            one, two = up[:, at : at + 128], up[:, at + 128 : at + 256]
            for h in range(2):
                to = (h * 4 + lead) * 1024 + pair * 128
                sides = [v[:, h * 64 : h * 64 + 64] for v in (one, two)]
                up_own[:, to : to + 128] = jnp.concatenate(sides, axis=1)
    up_keep = pltpu.make_async_copy(up_own.at[:, piece(place.g, 1024)], up_all.at[home], local.at[1])
    up_keep.start()
    up_spread = [
        sends.push(up_own.at[:, piece(index(*m), 1024)], up_all.at[home], place.member(*m)) for m in MEMBERS
    ]

    copies[0].wait()
    for copy in wq_spread:
        copy.wait()
    fixed = {"z": place.z, "y": place.y}
    qkv_parts = []
    for p, cols, order in (
        (0, ALL, ("y", "z")), (1, ALL, ("z", "y")), (2, pl.ds(0, 128), ("y", "z")), (2, pl.ds(128, 128), ("z", "y"))
    ):
        view = wq_view(p, cols)
        qkv_parts.append(ring_gather(place, sends, view, order, view(fixed, None), Nothing(), False))
    up_gather = ring_gather(place, sends, up_view, ("y", "z"), up_view(fixed, None), Nothing(), False)
    dn_gather = ring_gather(place, sends, dn_view, ("z", "y"), dn, copies[1], False)
    out_gathers = [
        ring_gather(place, sends, out_view(h), order, wo.at[:, pl.ds(h * 1024, 1024)], copies[2 + h], True)
        for h, order in enumerate((("y", "z", "x"), ("z", "y", "x")))
    ]

    def tick(*parts):
        for part in parts:
            next(part)

    tick(*qkv_parts, dn_gather, *out_gathers)
    own = cotbuf.at[place.x, place.c]
    own[:, 0:2048] = cot[...]
    own[:, 2048:2176] = (dot_nt(cot[...], lum[...]) * keep).astype(bf16)
    act_gather.own()
    tick(*qkv_parts)
    act_gather.near(False)
    tick(*qkv_parts, *out_gathers)
    run_all(qkv_parts)
    tick(*out_gathers)
    up_keep.wait()
    for copy in up_spread:
        copy.wait()
    tick(up_gather)
    kept = []

    def project(x):
        left = act[x, :, :, 0:2048].reshape(256, 2048)
        for p in range(3):
            low_rank = act[x, :, :, 2048 + p * 128 : 2176 + p * 128].reshape(256, 128)
            value = dot(left, wq[p].reshape(2048, 256)) + bias[p] + dot(low_rank, umaps[p])
            rows[p, x] = value.astype(bf16).reshape(2, 128, 256)

    here = place.z * 4 + place.y
    kv = pl.ds(1, 2)
    posts = []

    def post(dx):
        x = place.step("x", dx)
        for n, (to, dc, j, device, myself) in enumerate(attenders(place)):
            if to == dx:
                src = rows.at[:, x, 1 - place.c if dc else place.c, :, pl.ds(j * 128, 128)]
                posts.append(
                    Post(src, mine.at[:, piece(here, 128)], device, myself, a_send.at[0, n], a_recv.at[0, here])
                )
        for n, (to, dc, j, device, _) in enumerate(attenders(place)):
            if to == dx:
                src = rows.at[kv, x, 1 - place.c if dc else place.c, :, pl.ds(j * 128, 128)]
                device = place.member((dx + 2) % 4, dc) | {"z": device["z"], "y": device["y"]}
                myself = None if dc or dx != 2 else (place.z == device["z"]) & (place.y == device["y"])
                posts.append(
                    Post(src, others.at[:, piece(here, 128)], device, myself, a_send.at[1, n], a_recv.at[1, here])
                )

    project(place.x)
    post(0)
    act_gather.near_done()
    project(place.step("x", -1))
    project(place.step("x", 1))
    post(1)
    post(3)
    act_gather.far()
    act_gather.far_done()
    project(place.step("x", 2))
    post(2)
    tick(dn_gather, up_gather, *out_gathers)
    kept.append(pltpu.make_async_copy(act, act_all, local.at[6]))
    kept[-1].start()
    for p in range(3):
        for n in range(4):
            wq_t[p, :, n * 512 : n * 512 + 512] = jnp.transpose(wq[p, n // 2, n % 2].reshape(512, 256))
    kept.append(pltpu.make_async_copy(wq_t, qkv_w, local.at[5]))
    kept[-1].start()
    for n in range(16):
        dst = mine.at[:, piece(n, 128)]
        pltpu.make_async_copy(dst, dst, a_recv.at[0, n]).wait()
    kept.append(pltpu.make_async_copy(mine, heads, local.at[7]))
    kept[-1].start()
    for n in range(16):
        dst = others.at[:, piece(n, 128)]
        pltpu.make_async_copy(dst, dst, a_recv.at[1, n]).wait()
    kept.append(pltpu.make_async_copy(others, across, local.at[8]))
    kept[-1].start()
    cot_gather = group_gather(place, sends, cotbuf)
    tick(cot_gather)

    def tile(t, _):
        peak, total = attend(t, mine, others, starts, place.xh, scale)
        weight = total[:, 128:]
        o = total[:, :128] / weight
        att[piece(t, F_TILE), :] = o
        for b in range(F_TILE // 128):
            low[t * (F_TILE // 128) + b] = o[b * 128 : (b + 1) * 128].astype(bf16)
        line = jnp.transpose(peak * (scale * LOG2E) + jnp.log2(weight))
        for n in range(F_TILE // Q_TILE):
            lse[pl.ds(t * (F_TILE // Q_TILE) + n, 1), :] = line[0:1, n * Q_TILE : n * Q_TILE + Q_TILE]
        return 0

    tiles = mine.shape[1] // F_TILE
    lax.fori_loop(0, tiles // 2, tile, 0)
    tick(dn_gather, up_gather)
    lax.fori_loop(tiles // 2, tiles * 3 // 4, tile, 0)
    tick(cot_gather, *out_gathers)
    lax.fori_loop(tiles * 3 // 4, tiles, tile, 0)
    back = heads_out(place, sends, low, merged, local.at[9])
    tick(back)
    for copy in posts:
        copy.wait_send()
    for copy in kept:
        copy.wait()
    act_gather.finish()
    run_all([back, up_gather, dn_gather, cot_gather, *out_gathers])
    last = pltpu.make_async_copy(cotbuf, cot_all, local.at[10])
    last.start()
    last.wait()
    assert sends.used <= send.shape[0], sends.used


def front(starts, chosen, tok, gain, shift, bias, dmaps, umaps, cot, lum, wp, wo, up, dn, scale):
    any_ = pl.BlockSpec(memory_space=pl.ANY)
    vmem = pl.BlockSpec(memory_space=pltpu.VMEM)
    smem = pl.BlockSpec(memory_space=pltpu.SMEM)
    shape = lambda *s: jax.ShapeDtypeStruct(s, bf16)
    vm = lambda *s: pltpu.VMEM(s, bf16)
    return pl.pallas_call(
        functools.partial(front_kernel, scale=scale),
        name="front",
        out_shape=[
            shape(4, 2, 128, 2432),
            shape(3, 256, 2048),
            shape(2, 2, 4, 4, 2, 16, 2048),
            shape(2, 2, 4, 4, 2, 16, 1024),
            shape(4, 4, 64, 2048),
            shape(4, 2, 128, 2176),
            shape(3, 2048, 128),
            shape(2, 2048, 128),
            shape(128, 2048),
            jax.ShapeDtypeStruct((2048, 128), f32),
            jax.ShapeDtypeStruct((8, 256), f32),
            jax.ShapeDtypeStruct((128, 128), f32),
        ],
        in_specs=[smem] * 2 + [vmem] * 12,
        out_specs=[any_] * 9 + [vmem] * 3,
        scratch_shapes=[
            vm(4, 2, 128, 2432),
            vm(4, 2, 128, 2176),
            vm(3, 2, 2, 4, 4, 2, 16, 256),
            vm(16, 8192),
            vm(3, 4, 2, 128, 256),
            vm(3, 2048, 128),
            vm(2, 2048, 128),
            vm(16, 128, 128),
            vm(3, 256, 2048),
        ]
        + [pltpu.SemaphoreType.DMA(n) for n in ((150,), (150,), (2, 16), (2, 16), (11,))],
        compiler_params=pltpu.CompilerParams(
            collective_id=0, has_side_effects=True, vmem_limit_bytes=56 * MIB
        ),
    )(starts, chosen, tok, gain, shift, bias, dmaps, umaps, cot, lum, wp, wo, up, dn)


def middle_kernel(
    starts, grad, queries, others, att, lse, umaps, mask, parts, a_own, b_own, two,
    by_member, low_rank, total, a_final, b_final, two_final,
    do, delta, dq_acc, dq, own_low, other_low, by_head, from_other, *refs, scale,
):
    scratch, (send, recv, a_send, a_recv, local) = list(refs[:-5]), refs[-5:]
    place = Place()
    across = [{"xh": 1 - place.xh, "z": z, "y": y} for z, y in plane(place)]
    greet(plane_devices(place) + members(place) + across)
    sends = Sends(send, recv)
    here = place.z * 4 + place.y
    parity = place.xh
    kv = pl.ds(1, 2)

    keep = pltpu.make_async_copy(grad.at[:, head_columns(place.z, place.y)], do.at[piece(here, 128)], local.at[0])
    keep.start()
    grads_sent = [
        sends.push(grad.at[:, head_columns(z, y)], do.at[piece(here, 128)], {"z": z, "y": y})
        for z, y in plane(place)
    ]

    def take(n):
        got = scratch[:n]
        del scratch[:n]
        return got

    forth = group_sum(place, sends, parts, take(6), total)
    early = [
        a_sum(place, sends, a_own, a_final, take(5)),
        b_sum(place, sends, b_own, b_final, take(5)),
    ]
    early += [
        reduce_piece(
            place, sends, two_final.at[n], None,
            (lambda z, y, n=n: two.at[n, z, y], scratch[n], two_final.at[n]), None,
        )
        for n in range(2)
    ]

    def tick(*parts):
        for part in parts:
            try:
                next(part)
            except StopIteration:
                pass

    tick(forth, *early)
    dq_acc[...] = jnp.zeros_like(dq_acc)
    keep.wait()
    for copy in grads_sent:
        copy.wait_recv()
    ones = jnp.ones((8, 128), bf16)
    tiles, key_tiles = do.shape[0] // Q_TILE, do.shape[0] // K_TILE

    def row_dots(t, _):
        rows = piece(t, Q_TILE)
        value = do[rows, :].astype(f32) * att[rows, :]
        high = value.astype(bf16)
        low = (value - high.astype(f32)).astype(bf16)
        delta[t] = dot_nt(ones, high) + dot_nt(ones, low)
        return 0

    lax.fori_loop(0, tiles, row_dots, 0)
    tick(forth, *early[:2])

    def keys(kt):
        rows = piece(kt, K_TILE)
        sides = ((others[0, rows, :], others[1, rows, :], 1 - parity), (queries[1, rows, :], queries[2, rows, :], parity))
        local = kt * K_TILE + lax.broadcasted_iota(jnp.int32, (K_TILE, 1), 0)

        def step(qt, carry):
            rows = piece(qt, Q_TILE)
            q = queries[0, rows, :]
            d = do[rows, :]
            q_pos = positions_of(qt * Q_TILE + lax.broadcasted_iota(jnp.int32, (1, Q_TILE), 1), parity)
            lo = document_start(starts, q_pos)
            found, dq_part = [], None
            for (k, v, k_parity), (dk, dv) in zip(sides, carry):
                k_pos = positions_of(local, k_parity)
                s = dot_nt(k, q)
                allowed = (k_pos >= lo) & (k_pos <= q_pos)
                p = jnp.exp2(jnp.where(allowed, s * (scale * LOG2E) - lse[pl.ds(qt, 1), :], -1e30))
                dv = dv + dot(p.astype(bf16), d)
                ds = (p * (dot_nt(v, d) - delta[qt, 0:1, :]) * scale).astype(bf16)
                dk = dk + dot(ds, q)
                part = dot_tn(ds, k)
                dq_part = part if dq_part is None else dq_part + part
                found.append((dk, dv))
            dq_acc[rows, :] += dq_part
            return tuple(found)

        zero = jnp.zeros((K_TILE, 128), f32)
        return lax.fori_loop(kt * (K_TILE // Q_TILE), tiles, step, ((zero, zero),) * 2)

    blocks = K_TILE // 128
    gone = []

    def to_token(k, n, src, dst, other, away):
        z, y = n // 4, lax.rem(n, 4)
        myself = None if other or away else (place.z == z) & (place.y == y)
        device = {"z": z, "y": y} | ({"xh": 1 - place.xh} if other else {})
        gone.append(Post(src, dst, device, myself, a_send.at[k, n], a_recv.at[k, here]))

    for turn in (2, 1, 3, 0):
        kt = lax.rem(place.z + turn, key_tiles)
        for k, low, (dk, dv) in zip((2, 1), (other_low, own_low), keys(kt)):
            for b in range(blocks):
                n = kt * blocks + b
                low[n, 0] = dk[b * 128 : (b + 1) * 128].astype(bf16)
                low[n, 1] = dv[b * 128 : (b + 1) * 128].astype(bf16)
                dst = from_other.at[:, here] if k == 2 else by_head.at[kv, here]
                to_token(k, n, low.at[n], dst, k == 2, turn != 0)
        if turn == 1:
            tick(forth, *early)
    for n in range(16):
        dq[n] = dq_acc[n * 128 : (n + 1) * 128].astype(bf16)
    for turn in (2, 1, 3, 0):
        for b in range(blocks):
            n = lax.rem(place.z + turn, 4) * 4 + b
            to_token(0, n, dq.at[n], by_head.at[0, here], False, turn != 0)
    tick(*early)

    mine = None
    shared = []
    for dx, dc in MEMBERS + [(0, 0)]:
        g = place.step("x", dx) * 2 + (1 - place.c if dc else place.c)
        for j in range(2):
            for k, dst in ((2, from_other.at[:, 0]), (1, by_head.at[kv, 0]), (0, by_head.at[0, 0])):
                pltpu.make_async_copy(dst, dst, a_recv.at[k, g * 2 + j]).wait()
        pair = piece(g, 2)
        by_head[1:3, pair] = (by_head[1:3, pair].astype(f32) + from_other[:, pair].astype(f32)).astype(bf16)
        src, dst = by_head.at[:, pair], by_member.at[:, place.x, place.c]
        if dx or dc:
            shared.append(sends.push(src, dst, place.member(dx, dc)))
        else:
            mine = pltpu.make_async_copy(src, dst, local.at[7])
            mine.start()
    for p in range(3):
        whole = jnp.concatenate([by_head[p, n] for n in range(16)], axis=1)
        low_rank[:, p * 128 : p * 128 + 128] = (dot_nt(whole, umaps[p]) * mask[...]).astype(bf16)
    run_all([forth] + early)
    for copy in gone + grads_sent:
        copy.wait_send()
    for copy in shared:
        copy.wait()
    mine.wait()
    assert sends.used <= send.shape[0], sends.used


def middle(starts, grad, queries, others, att, lse, umaps, mask, parts, a_own, b_own, two, scale):
    any_ = pl.BlockSpec(memory_space=pl.ANY)
    vmem = pl.BlockSpec(memory_space=pltpu.VMEM)
    smem = pl.BlockSpec(memory_space=pltpu.SMEM)
    vm = lambda *s: pltpu.VMEM(s, bf16)
    shape = lambda *s: jax.ShapeDtypeStruct(s, bf16)
    return pl.pallas_call(
        functools.partial(middle_kernel, scale=scale),
        name="attention_backward",
        out_shape=[
            shape(3, 4, 2, 2, 128, 128),
            shape(128, 384),
            jax.ShapeDtypeStruct((128, 2048), f32),
            shape(16, 128),
            shape(16, 128),
            shape(2, 64, 128),
        ],
        in_specs=[smem] + [vmem] * 11,
        out_specs=[any_] + [vmem] * 5,
        scratch_shapes=[
            vm(2048, 128),
            pltpu.VMEM((8, 8, 256), f32),
            pltpu.VMEM((2048, 128), f32),
            vm(16, 128, 128),
            vm(16, 2, 128, 128),
            vm(16, 2, 128, 128),
            vm(3, 16, 128, 128),
            vm(2, 16, 128, 128),
        ]
        + GroupSum.scratch(2048)
        + a_sum_scratch()
        + b_sum_scratch()
        + [vm(15, 64, 128)] * 2
        + [pltpu.SemaphoreType.DMA(k) for k in ((100,), (100,), (3, 16), (3, 16), (8,))],
        compiler_params=pltpu.CompilerParams(collective_id=2, has_side_effects=True, vmem_limit_bytes=58 * MIB),
    )(starts, grad, queries, others, att, lse, umaps, mask, parts, a_own, b_own, two.reshape(2, 4, 4, 64, 128))


def feed_forward_kernel(
    second, cot_all, up, dn, umap, dmap, bias, back, forth, two, mine_in, mine_cot,
    sa, cot, up_v, dn_v, grad_act, act, pre, parts, total, *refs,
):
    scratch, (send, recv, local) = refs[:-3], refs[-3:]
    place = Place()
    greet(members(place))
    sends = Sends(send, recv)
    sa[place.x, place.c] = second[...]
    gather = GroupGather(place, sends, sa)
    loads = [
        pltpu.make_async_copy(src, dst, local.at[n])
        for n, (src, dst) in enumerate(((dn, dn_v), (cot_all, cot), (up, up_v)))
    ]
    for copy in loads:
        copy.start()

    def rows(ref, x, start, size):
        return ref[x, :, :, pl.ds(start, size)].reshape(256, size)

    loads[0].wait()
    loads[1].wait()

    def grad_tile(n, _):
        xs, cols = piece(n // 4, 2), piece(lax.rem(n, 4), 256)
        value = dot_nt(cot[xs, :, :, 0:2048].reshape(512, 2048), dn_v[cols, :])
        value = value + dot_nt(cot[xs, :, :, 2048:2176].reshape(512, 128), dmap[cols, :])
        grad_act[xs, :, cols] = value.reshape(2, 256, 256)
        return 0

    lax.fori_loop(0, 8, grad_tile, 0)
    loads[2].wait()
    xs = places_in_turn(place)

    def hidden(k):
        x = xs[k]

        def tile(n, _):
            cols = piece(n, 256)
            value = dot(rows(sa, x, 0, 2048), up_v[:, cols]) + bias[:, cols]
            value = value + dot(rows(sa, x, 2048, 128), umap[:, cols])
            phi = 0.5 * (1.0 + lax.erf(value * 0.7071067811865476))
            slope = phi + value * (0.3989422804014327 * jnp.exp2(value * value * (-0.5 * LOG2E)))
            act[k, :, cols] = (value * phi).astype(bf16)
            pre[k, :, cols] = (grad_act[x, :, cols] * slope).astype(bf16)
            return 0

        lax.fori_loop(0, 4, tile, 0)

    def backward(k, n):
        ks = pl.ds(k, n)

        def tile(t, _):
            cols = piece(t, 256)
            value = dot_nt(pre[ks].reshape(n * 256, 1024), up_v[cols, :]).astype(bf16)
            parts[ks, :, :, cols] = value.reshape(n, 2, 128, 256)
            return 0

        lax.fori_loop(0, 8, tile, 0)
        value = dot_nt(pre[ks].reshape(n * 256, 1024), umap[...]).astype(bf16)
        parts[ks, :, :, 2048:2176] = value.reshape(n, 2, 128, 128)
        value = dot(act[ks].reshape(n * 256, 1024), dmap[...]).astype(bf16)
        parts[ks, :, :, 2176:2304] = value.reshape(n, 2, 128, 128)

    gather.own()
    hidden(3)
    gather.near()
    hidden(2)
    hidden(1)
    gather.far()
    gather.far_done()
    hidden(0)

    sums = GroupSum(place, sends, parts, scratch)
    backward(0, 1)
    sums.cross(0)
    backward(1, 1)
    sums.cross(1)
    sums.merge(0)
    sums.first()
    backward(2, 2)
    sums.cross(2)
    sums.cross(3)
    sums.merge(1)
    sums.merge(2)
    sums.second()

    def forward(n, _):
        ks, cols = piece(n // 4, 2), piece(lax.rem(n, 4), 512)
        value = dot(act[ks].reshape(512, 1024), dn_v[:, cols]).astype(bf16)
        forth[ks, :, :, cols] = value.reshape(2, 2, 128, 512)
        return 0

    lax.fori_loop(0, 8, forward, 0)

    def small(k, _):
        x = lax.rem(place.x + jnp.where(k == 3, 0, jnp.where(k == 2, 3, 2 - k)), 4)
        one = dot_tn(act[k], rows(cot, x, 2048, 128))
        other = dot_tn(pre[k], rows(sa, x, 2048, 128))

        @pl.when(k == 0)
        def _():
            total[0] = one
            total[1] = other

        @pl.when(k > 0)
        def _():
            total[0] += one
            total[1] += other

        return 0

    lax.fori_loop(0, 4, small, 0)
    cols = piece(place.g, 256)
    mine_in[...] = sa[:, :, :, cols].reshape(1024, 256)
    mine_cot[...] = cot[:, :, :, cols].reshape(1024, 256)
    two[...] = total[...].astype(bf16)
    back[...] = sums.result()
    gather.finish()


def feed_forward(second, cot_all, up, dn, umap, dmap, bias):
    any_ = pl.BlockSpec(memory_space=pl.ANY)
    vmem = pl.BlockSpec(memory_space=pltpu.VMEM)
    vm = lambda *s: pltpu.VMEM(s, bf16)
    return pl.pallas_call(
        feed_forward_kernel,
        name="feed_forward",
        out_shape=[
            jax.ShapeDtypeStruct((128, 2304), f32),
            jax.ShapeDtypeStruct((4, 2, 128, 2048), bf16),
            jax.ShapeDtypeStruct((2, 1024, 128), bf16),
            jax.ShapeDtypeStruct((1024, 256), bf16),
            jax.ShapeDtypeStruct((1024, 256), bf16),
        ],
        in_specs=[vmem] + [any_] * 3 + [vmem] * 3,
        out_specs=[vmem] * 5,
        scratch_shapes=[
            vm(4, 2, 128, 2176),
            vm(4, 2, 128, 2176),
            vm(2048, 1024),
            vm(1024, 2048),
            pltpu.VMEM((4, 256, 1024), f32),
            vm(4, 256, 1024),
            vm(4, 256, 1024),
            vm(4, 2, 128, 2304),
            pltpu.VMEM((2, 1024, 128), f32),
        ]
        + GroupSum.scratch(2304)
        + [pltpu.SemaphoreType.DMA((k,)) for k in (16, 16, 3)],
        compiler_params=pltpu.CompilerParams(collective_id=1, has_side_effects=True, vmem_limit_bytes=60 * MIB),
    )(second, cot_all, up, dn, umap, dmap, bias)


def both_heads(gq, p, x):
    heads = [gq[p, x, :, j].reshape(256, 128) for j in range(2)]
    return jnp.concatenate(heads, axis=1)


def tail_kernel(
    grads, qkv_w, act_all, dmaps, low_rank, small, tok, gain, grad_res, mine_in, mine_cot, a_piece, b_piece, two_piece,
    input_grad, a_final, b_final, a_early, b_early, two_res,
    a_res, b_res, gq, wq, act, left, parts, lows, a_sums, b_sums, a_s, a_f, b_s, b_f, *refs,
):
    scratch, (send, recv, local) = refs[:-3], refs[-3:]
    place = Place()
    greet(members(place) + plane_devices(place))
    sends = Sends(send, recv)
    loads = [
        pltpu.make_async_copy(src, dst, local.at[n])
        for n, (src, dst) in enumerate(((grads, gq), (qkv_w, wq), (act_all, act)))
    ]
    for copy in loads:
        copy.start()
    own = lows.at[place.x, place.c]
    own[:, 0:384] = low_rank[...]
    own[:, 384:640] = small[...]
    spread = [sends.push(own, own, place.member(*m)) for m in MEMBERS]

    def two_view(n):
        def view(at):
            xl, xh = two_parts(at)
            return two_res.at[n, xl, place.c, at["z"], at["y"], xh]

        return view

    def b_early_view(at):
        z, y = at["z"], at["y"]
        if isinstance(y, pl.Slice):
            cols = pl.ds(y.start * 128 if z is ALL else pl.multiple_of(z * 512 + y.start * 128, 128), 256)
        elif z is ALL:
            cols = ALL
        else:
            cols = piece(z, 512) if y is ALL else piece(z * 4 + y, 128)
        return b_early.at[place.c, at["x"], :, cols]

    early = [
        give_all(place, sends, ("z", "y", "x"), two_piece.at[0], two_view(0), local.at[3]),
        give_all(place, sends, ("z", "x", "y"), two_piece.at[1], two_view(1), local.at[4]),
        give_all(
            place, sends, ("y", "z", "x"), a_piece,
            lambda at: a_early.at[place.c, at["z"], at["y"], at["x"]], local.at[5],
        ),
        give_all(place, sends, ("x", "y", "z"), b_piece, b_early_view, local.at[6]),
    ]

    def tick(*parts):
        for part in parts:
            next(part)

    tick(*early)
    loads[0].wait()
    loads[1].wait()
    xs = places_in_turn(place)
    for k in range(4):
        left[k] = jnp.concatenate([both_heads(gq, p, xs[k]) for p in range(3)], axis=1)

    def partial(k, n):
        ks = pl.ds(k, n)

        def tile(t, _):
            cols = piece(t, 512)
            value = dot(left[ks].reshape(n * 256, 768), wq[:, :, cols].reshape(768, 512)).astype(bf16)
            parts[ks, :, :, cols] = value.reshape(n, 2, 128, 512)
            return 0

        lax.fori_loop(0, 4, tile, 0)

    sums = GroupSum(place, sends, parts, scratch)
    partial(0, 1)
    sums.cross(0)
    partial(1, 1)
    sums.cross(1)
    sums.merge(0)
    sums.first()
    partial(2, 2)
    sums.cross(2)
    sums.cross(3)

    loads[2].wait()
    for p in range(3):
        total = jnp.zeros((128, 256), f32)
        for x in range(4):
            left_rows = act[x, :, :, 2048 + p * 128 : 2176 + p * 128].reshape(256, 128)
            total = total + dot_tn(left_rows, both_heads(gq, p, x))
        b_sums[p] = total.astype(bf16)
    for copy in spread:
        copy.wait()
    b_sums[3] = dot_tn(lows[:, :, :, 512:640].reshape(1024, 128), mine_cot[...]).astype(bf16)
    rows = act[:, :, :, piece(place.g, 256)].reshape(1024, 256)
    for p in range(4):
        right = lows[:, :, :, p * 128 : p * 128 + 128].reshape(1024, 128)
        a_sums[p] = dot_tn(rows if p < 3 else mine_in[...], right).astype(bf16)

    def a_view(at):
        return a_res.at[:, at["x"], place.c, at["z"], at["y"]]

    def a_held(z, y):
        return a_sums.at[:, piece(z * 4 + y, 16)]

    def b_view(at):
        y = at["y"]
        if y is ALL:
            yr, yc = ALL, ALL
        elif isinstance(y, pl.Slice):
            yr, yc = pl.ds(y.start // 2, 1), ALL
        else:
            yr, yc = y // 2, lax.rem(y, 2)
        return b_res.at[:, at["x"], place.c, at["z"], yr, yc]

    def b_held(z, y):
        return b_sums.at[:, pl.ds(pl.multiple_of(z * 32 + y // 2 * 16, 16), 16), piece(lax.rem(y, 2), 128)]

    def late_part(final, held, slots, order, view, sem):
        yield from reduce_piece(place, sends, final, None, (held, slots, final), None)
        yield from give_all(place, sends, order, final, view, sem)

    late = [
        late_part(a_f, a_held, a_s, ("z", "x", "y"), a_view, local.at[7]),
        late_part(b_f, b_held, b_s, ("y", "x", "z"), b_view, local.at[8]),
    ]
    tick(*late)
    tick(*early)
    sums.merge(1)
    sums.merge(2)
    sums.second()
    tick(*late, *early)
    tick(*late, *early)
    grad_first = sums.result()
    for p in range(3):
        grad_first = grad_first + dot_nt(low_rank[:, p * 128 : p * 128 + 128], dmaps[p])
    result = grad_res[...] + layer_norm_back(tok[...].astype(f32), gain[...], grad_first)
    input_grad[...] = result.astype(bf16)
    run_all(late + early)
    moves = [pltpu.make_async_copy(a_res, a_final, local.at[9])]
    for g in range(8):
        for yc in range(2):
            src = b_res.at[:, g // 2, g % 2, :, :, yc]
            dst = b_final.at[:, :, :, :, pl.ds(g * 256 + yc * 128, 128)]
            moves.append(pltpu.make_async_copy(src, dst, local.at[10 + g * 2 + yc]))
    for copy in moves:
        copy.start()
    for copy in moves:
        copy.wait()
    assert sends.used <= send.shape[0], sends.used


def tail(grads, qkv_w, act_all, dmaps, low_rank, small, tok, gain, grad_res, mine_in, mine_cot, a_piece, b_piece, two_piece):
    any_ = pl.BlockSpec(memory_space=pl.ANY)
    vmem = pl.BlockSpec(memory_space=pltpu.VMEM)
    vm = lambda *s: pltpu.VMEM(s, bf16)
    shape = lambda *s: jax.ShapeDtypeStruct(s, bf16)
    a_shape, b_shape = (4, 4, 2, 4, 4, 16, 128), (4, 4, 2, 4, 2, 2, 16, 128)
    input_grad, late_a, late_b, early_a, early_b, early_two = pl.pallas_call(
        tail_kernel,
        name="tail",
        out_shape=[
            shape(128, 2048),
            shape(*a_shape),
            shape(4, 4, 2, 16, 2048),
            shape(2, 4, 4, 4, 16, 128),
            shape(2, 4, 16, 2048),
            shape(2, 2, 2, 4, 4, 2, 64, 128),
        ],
        in_specs=[any_] * 3 + [vmem] * 11,
        out_specs=[vmem] + [any_] * 5,
        scratch_shapes=[
            vm(*a_shape),
            vm(*b_shape),
            vm(3, 4, 2, 2, 128, 128),
            vm(3, 256, 2048),
            vm(4, 2, 128, 2432),
            vm(4, 256, 768),
            vm(4, 2, 128, 2048),
            vm(4, 2, 128, 640),
            vm(4, 256, 128),
            vm(4, 128, 256),
            vm(15, 4, 16, 128),
            vm(4, 16, 128),
            vm(15, 4, 16, 128),
            vm(4, 16, 128),
        ]
        + GroupSum.scratch(2048)
        + [pltpu.SemaphoreType.DMA((k,)) for k in (200, 200, 26)],
        compiler_params=pltpu.CompilerParams(collective_id=3, has_side_effects=True, vmem_limit_bytes=60 * MIB),
    )(
        grads, qkv_w, act_all, dmaps, low_rank, small, tok, gain, grad_res, mine_in, mine_cot, a_piece, b_piece, two_piece
    )
    return (
        input_grad,
        late_a.reshape(4, 2048, 128),
        late_b.reshape(4, 128, 2048),
        early_a.reshape(2048, 128),
        early_b.reshape(128, 2048),
        early_two.reshape(2, 8192, 128),
    )


def per_device(
    tokens,
    document_starts,
    document_adapter,
    layernorm_gain,
    layernorm_bias,
    projection_weight,
    output_weight,
    up_weight,
    down_weight,
    projection_bias,
    upper_bias,
    attention_down_maps,
    attention_up_maps,
    upper_down_maps,
    upper_up_maps,
    lower_down_maps,
    lower_up_maps,
    cotangent,
):
    local_rows, width = tokens.shape[1:]
    head_size = width // HEADS
    seq = local_rows * 32
    scale = head_size ** (-0.5)
    xl, c, z, y, xh = (lax.axis_index(a) for a in AXES)
    group = (xh * 2 + xl) * 2 + c
    inputs = tokens[0].astype(f32)
    cot = cotangent[0]
    bias_rows = jnp.stack([projection_bias[0], jnp.zeros_like(projection_bias[0]), projection_bias[1]])

    def my_columns(array):
        return lax.dynamic_slice_in_dim(array, group * 256, 256, array.ndim - 1)

    def my_hidden(array):
        lead = array.shape[:-1]
        part = lax.dynamic_slice_in_dim(array, (xl * 2 + c) * 2048, 2048, array.ndim - 1)
        part = part.reshape(lead + (16, 2, 64))
        return lax.dynamic_index_in_dim(part, xh, len(lead) + 1, False).reshape(lead + (1024,))

    my_up_maps = my_columns(attention_up_maps[:3])
    (
        act_all, qkv_w, out_all, up_all, dn_all, cot_all, by_head, across, merged, attended, lse, mask
    ) = front(
        document_starts, document_adapter, tokens[0], layernorm_gain[:1], layernorm_bias[:1],
        my_columns(bias_rows)[:, None, :], attention_down_maps, my_up_maps, cot, lower_up_maps,
        jnp.transpose(projection_weight, (1, 0, 2)), output_weight, up_weight, down_weight, scale,
    )
    w_out = out_all.reshape(width, width)

    adapt_out = (dot(merged, attention_down_maps[3]) * mask).astype(bf16)
    residual = inputs + dot(merged, w_out) + projection_bias[2] + dot(adapt_out, attention_up_maps[3])
    second_in = layer_norm(residual, layernorm_gain[1], layernorm_bias[1]).astype(bf16)
    adapt_up = (dot(second_in, upper_down_maps) * mask).astype(bf16)

    down_maps = lax.dynamic_slice_in_dim(lower_down_maps, (xl * 2 + c) * 2048, 2048, 0)
    down_maps = lax.dynamic_index_in_dim(down_maps.reshape(16, 2, 64, 128), xh, 1, False).reshape(1024, 128)
    back, forth, two, mine_in, mine_cot = feed_forward(
        jnp.concatenate([second_in, adapt_up], axis=1), cot_all, up_all.reshape(width, 1024),
        dn_all.reshape(1024, width), my_hidden(upper_up_maps), down_maps, my_hidden(upper_bias)[None],
    )

    grad_adapt_up = (back[:, width : width + 128] * mask).astype(bf16)
    grad_second = back[:, :width] + dot_nt(grad_adapt_up, upper_down_maps)
    grad_residual = cot.astype(f32) + layer_norm_back(residual, layernorm_gain[1], grad_second)
    grad_branch = grad_residual.astype(bf16)
    grad_b_out = dot_tn(adapt_out, grad_branch)
    grad_adapt_out = (dot_nt(grad_branch, attention_up_maps[3]) * mask).astype(bf16)
    grad_a_out = dot_tn(merged, grad_adapt_out)
    grad_merged = (dot_nt(grad_branch, w_out) + dot_nt(grad_adapt_out, attention_down_maps[3])).astype(bf16)

    adapt_down = (back[:, width + 128 :] * mask).astype(bf16)
    grad_qkv, grad_adapt_qkv, forth_sum, a_piece, b_piece, two_piece = middle(
        document_starts, grad_merged, by_head, across, attended, lse, attention_up_maps, mask, forth,
        grad_a_out.astype(bf16), grad_b_out.astype(bf16), two, scale,
    )
    input_grad, late_a, late_b, early_a, early_b, early_two = tail(
        grad_qkv, qkv_w, act_all, attention_down_maps, grad_adapt_qkv,
        jnp.concatenate([grad_adapt_up, adapt_down], axis=1), tokens[0], layernorm_gain[:1], grad_residual,
        mine_in, mine_cot, a_piece, b_piece, two_piece,
    )
    output = residual + forth_sum + projection_bias[3] + dot(adapt_down, lower_up_maps)
    return (
        output.astype(bf16)[None],
        input_grad[None],
        jnp.concatenate([late_a[:3], early_a[None]]).astype(f32),
        jnp.concatenate([late_b[:3], early_b[None]]).astype(f32),
        late_a[3].astype(f32),
        jnp.transpose(early_two[1]).astype(f32),
        early_two[0].astype(f32),
        late_b[3].astype(f32),
    )


def solution(mesh):
    fine = jax.sharding.Mesh(mesh.devices.reshape(SIZES), AXES)
    by_token = P(STREAM, TOKEN, None)
    shard = AXES
    in_specs = (
        by_token,
        P(STREAM, None),
        P(STREAM, None),
        P(),
        P(),
        P(shard, None, None),
        P(shard, None),
        P(shard, None),
        P(shard, None),
        P(),
        P(),
        P(),
        P(),
        P(),
        P(),
        P(),
        P(),
        by_token,
    )
    out_specs = (by_token, by_token, P(), P(), P(), P(), P(), P())
    return jax.shard_map(per_device, mesh=fine, in_specs=in_specs, out_specs=out_specs, check_vma=False)
```

```python
import functools

import jax
import jax.numpy as jnp
from jax import lax
from jax.experimental import pallas as pl
from jax.experimental.pallas import tpu as pltpu
from jax.sharding import PartitionSpec as P

HEADS = 16
ADAPTER_RANK = 16
MESH = pl.DeviceIdType.MESH
AXES = ("xl", "c", "z", "y", "xh")
SIZES = (2, 2, 4, 4, 2)
STREAM = ("xl", "c")
TOKEN = ("z", "y", "xh")
bf16 = jnp.bfloat16
f32 = jnp.float32
LOG2E = 1.4426950408889634
MIB = 2**20
Q_TILE = 256
K_TILE = 512
F_TILE = 256
ALL = slice(None)


def layer_norm(values, gain, shift):
    center = values - jnp.mean(values, axis=-1, keepdims=True)
    spread = jnp.mean(center * center, axis=-1, keepdims=True)
    return center * lax.rsqrt(spread + 1e-05) * gain + shift


def layer_norm_back(values, gain, grad):
    center = values - jnp.mean(values, axis=-1, keepdims=True)
    scale = lax.rsqrt(jnp.mean(center * center, axis=-1, keepdims=True) + 1e-05)
    unit = center * scale
    grad = grad * gain
    along = jnp.mean(grad * unit, axis=-1, keepdims=True)
    return scale * (grad - jnp.mean(grad, axis=-1, keepdims=True) - unit * along)


def dot(left, right):
    return jnp.dot(left, right, preferred_element_type=f32)


def dot_nt(left, right):
    return lax.dot_general(left, right, (((1,), (1,)), ((), ())), preferred_element_type=f32)


def dot_tn(left, right):
    return lax.dot_general(left, right, (((0,), (0,)), ((), ())), preferred_element_type=f32)


def piece(n, size):
    return pl.ds(pl.multiple_of(n * size, size), size)


class Place:
    def __init__(self):
        self.xl, self.c, self.z, self.y, self.xh = (lax.axis_index(a) for a in AXES)
        self.x = self.xh * 2 + self.xl
        self.g = self.x * 2 + self.c

    def at(self, axis):
        return {"x": self.x, "y": self.y, "z": self.z}[axis]

    def step(self, axis, step):
        return lax.rem(self.at(axis) + (step + 4), 4)

    def toward(self, axis, step=1):
        if axis == "c":
            return {"c": 1 - self.c}
        to = self.step(axis, step)
        if axis == "x":
            return {"xl": lax.rem(to, 2), "xh": to // 2}
        return {axis: to}

    def member(self, dx, dc):
        to = {}
        if dx:
            to |= self.toward("x", dx)
        if dc:
            to |= {"c": 1 - self.c}
        return to


MEMBERS = [(dx, dc) for dx in (2, 1, 3, 0) for dc in (0, 1) if dx or dc]


class Sends:
    def __init__(self, send, recv):
        self.send, self.recv, self.used, self.open = send, recv, 0, []

    def push(self, src, dst, device):
        k = self.used
        self.used += 1
        copy = pltpu.make_async_remote_copy(
            src_ref=src,
            dst_ref=dst,
            send_sem=self.send.at[k],
            recv_sem=self.recv.at[k],
            device_id=device,
            device_id_type=MESH,
        )
        copy.start()
        self.open.append(copy)
        return copy


def greet(devices, perhaps=()):
    barrier = pltpu.get_barrier_semaphore()
    for device in devices:
        pl.semaphore_signal(barrier, inc=1, device_id=device, device_id_type=MESH)
    amount = len(devices) + len(perhaps)
    for device, myself in perhaps:
        amount = amount - myself.astype(jnp.int32)

        @pl.when(jnp.logical_not(myself))
        def _():
            pl.semaphore_signal(barrier, inc=1, device_id=device, device_id_type=MESH)

    pl.semaphore_wait(barrier, amount)


def run_all(parts):
    parts = list(parts)
    while parts:
        left = []
        for part in parts:
            try:
                next(part)
                left.append(part)
            except StopIteration:
                pass
        parts = left


def ring_gather(place, sends, view, order, chunk, landed, forward, direct=False):
    fixed = {a: place.at(a) for a in order}
    across = place.toward("c")
    later, passed = [], []

    def pass_on(block):
        if forward:
            passed.append(sends.push(view(block, None), view(block, None), across))

    if forward:
        passed.append(sends.push(chunk, view(fixed, None), across))
    for number, axis in enumerate(order):
        own = view(fixed, None)
        src = chunk if number == 0 else own
        if number == 0 or direct:
            sent = [sends.push(src, own, place.toward(axis, s)) for s in (2, 1, 3)]
            yield
            for s, copy in zip((2, 1, 3), sent):
                copy.wait_recv()
                pass_on(fixed | {axis: place.step(axis, -s)})
            if number == 0:
                landed.wait()
            later += sent
            del fixed[axis]
            continue
        up = sends.push(src, own, place.toward(axis, 1))
        down = sends.push(src, own, place.toward(axis, -1))
        yield
        before = fixed | {axis: place.step(axis, -1)}
        after = fixed | {axis: place.step(axis, 1)}
        opposite = fixed | {axis: place.step(axis, 2)}
        up.wait_recv()
        half = view(before, 0)
        up_two = sends.push(half, half, place.toward(axis, 1))
        down.wait_recv()
        half = view(after, 1)
        down_two = sends.push(half, half, place.toward(axis, -1))
        pass_on(before)
        pass_on(after)
        yield
        up_two.wait_recv()
        down_two.wait_recv()
        pass_on(opposite)
        later += [up, down, up_two, down_two]
        del fixed[axis]
    yield
    for copy in later:
        copy.wait_send()
    for copy in passed:
        copy.wait()


class Nothing:
    def wait(self):
        pass


def neighbours(place, axes):
    return [place.toward(a, s) for a in axes for s in ((1, 2, 3) if a in "xyz" else (1,))]


def members(place):
    return [place.member(*m) for m in MEMBERS]


class GroupGather:
    def __init__(self, place, sends, buf):
        self.place, self.sends, self.buf = place, sends, buf
        self.mine = buf.at[place.x, place.c]
        self.right, self.left = place.toward("x", 1), place.toward("x", -1)
        self.up = sends.push(self.mine, self.mine, self.right)
        self.down = sends.push(self.mine, self.mine, self.left)
        self.passed = [self.pass_on(self.mine)]

    def pass_on(self, ref):
        return self.sends.push(ref, ref, self.place.toward("c"))

    def own(self):
        self.passed[0].wait_recv()

    def near(self, wait=True):
        x, c = self.place.step("x", -1), self.place.c
        self.up.wait_recv()
        half = self.buf.at[x, c, pl.ds(0, 64)]
        self.up_two = self.sends.push(half, half, self.right)
        self.passed.append(self.pass_on(self.buf.at[x, c]))
        x = self.place.step("x", 1)
        self.down.wait_recv()
        half = self.buf.at[x, c, pl.ds(64, 64)]
        self.down_two = self.sends.push(half, half, self.left)
        self.passed.append(self.pass_on(self.buf.at[x, c]))
        if wait:
            self.near_done()

    def near_done(self):
        self.passed[1].wait_recv()
        self.passed[2].wait_recv()

    def far(self):
        self.up_two.wait_recv()
        self.down_two.wait_recv()
        self.passed.append(self.pass_on(self.buf.at[self.place.step("x", 2), self.place.c]))

    def far_done(self):
        self.passed[3].wait_recv()

    def finish(self):
        for copy in [self.up, self.down, self.up_two, self.down_two] + self.passed:
            copy.wait_send()


def group_gather(place, sends, buf):
    gather = GroupGather(place, sends, buf)
    yield
    gather.own()
    gather.near()
    yield
    gather.far()
    yield
    gather.far_done()
    gather.finish()


def places_in_turn(place):
    return [place.step("x", s) for s in (2, 1, -1, 0)]


class GroupSum:
    def __init__(self, place, sends, parts, scratch):
        self.place, self.sends, self.parts = place, sends, parts
        self.came, self.own, self.left_one, self.right_one, self.left_two, self.right_two = scratch
        self.right, self.left = place.toward("x", 1), place.toward("x", -1)
        self.crossed = {}

    @staticmethod
    def scratch(n):
        vm = lambda *s: pltpu.VMEM(s, bf16)
        return [vm(4, 128, n), vm(3, 128, n), vm(64, n), vm(64, n), vm(128, n), vm(128, n)]

    def cross(self, k):
        place = self.place
        self.crossed[k] = self.sends.push(
            self.parts.at[k, 1 - place.c], self.came.at[k], place.toward("c")
        )

    def merge(self, k):
        self.crossed[k].wait()
        both = self.parts[k, self.place.c].astype(f32) + self.came[k].astype(f32)
        self.own[k] = both.astype(bf16)

    def first(self):
        self.up = self.sends.push(self.own.at[0, pl.ds(0, 64)], self.left_one, self.right)
        self.down = self.sends.push(self.own.at[0, pl.ds(64, 64)], self.right_one, self.left)

    def second(self):
        self.up.wait()
        both = self.own[1, 0:64].astype(f32) + self.left_one[...].astype(f32)
        self.own[1, 0:64] = both.astype(bf16)
        self.up_two = self.sends.push(self.own.at[1], self.left_two, self.right)
        self.down.wait()
        both = self.own[2, 64:128].astype(f32) + self.right_one[...].astype(f32)
        self.own[2, 64:128] = both.astype(bf16)
        self.down_two = self.sends.push(self.own.at[2], self.right_two, self.left)

    def result(self):
        self.crossed[3].wait()
        total = self.parts[3, self.place.c].astype(f32) + self.came[3].astype(f32)
        self.up_two.wait()
        self.down_two.wait()
        return total + self.left_two[...].astype(f32) + self.right_two[...].astype(f32)


def group_sum(place, sends, parts, scratch, out):
    total = GroupSum(place, sends, parts, scratch)
    for k in range(4):
        total.cross(k)
    yield
    total.merge(0)
    total.first()
    total.merge(1)
    total.merge(2)
    yield
    total.second()
    yield
    out[...] = total.result()


def plane(place):
    steps = [(i, j) for i in (2, 1, 3, 0) for j in (2, 1, 3, 0) if i or j]
    return [(lax.rem(place.z + i, 4), lax.rem(place.y + j, 4)) for i, j in steps]


def from_plane(place):
    steps = [(i, j) for i in (2, 1, 3, 0) for j in (2, 1, 3, 0) if i or j]
    return [(lax.rem(place.z + 4 - i, 4), lax.rem(place.y + 4 - j, 4)) for i, j in steps]


def projectors(place):
    x, c = place.z, place.y // 2
    member = {"xl": lax.rem(x, 2), "xh": x // 2, "c": c}
    mine = (place.x == x) & (place.c == c)
    return [(member | {"z": z, "y": y}, None) for z, y in plane(place)] + [
        (member | {"z": place.z, "y": place.y}, mine)
    ]


def attenders(place):
    found = []
    for dx, dc in MEMBERS + [(0, 0)]:
        for j in range(2):
            z, y = place.x, 2 * place.c + j
            device = place.member(dx, dc) | {"z": z, "y": y}
            mine = None if dx or dc else (place.z == z) & (place.y == y)
            found.append((dx, dc, j, device, mine))
    return found


def head_columns(z, y):
    return pl.ds(pl.multiple_of((z * 4 + y) * 128, 128), 128)


def split_greeting(pairs):
    return [d for d, m in pairs if m is None], [(d, m) for d, m in pairs if m is not None]


def plane_devices(place):
    return [{"z": z, "y": y} for z, y in plane(place)]


class Post:
    def __init__(self, src, dst, device, myself, send_sem, recv_sem):
        self.remote = pltpu.make_async_remote_copy(
            src_ref=src, dst_ref=dst, send_sem=send_sem, recv_sem=recv_sem, device_id=device, device_id_type=MESH
        )
        self.myself = myself
        if myself is None:
            self.remote.start()
        else:
            pl.when(myself)(pltpu.make_async_copy(src, dst, recv_sem).start)
            pl.when(jnp.logical_not(myself))(self.remote.start)

    def wait_send(self):
        if self.myself is None:
            self.remote.wait_send()
        else:
            pl.when(jnp.logical_not(self.myself))(self.remote.wait_send)


def heads_out(place, sends, blocks, merged, local):
    cols = head_columns(place.z, place.y)
    keep = pltpu.make_async_copy(blocks.at[place.z * 4 + place.y], merged.at[:, cols], local)
    keep.start()
    sent = [sends.push(blocks.at[z * 4 + y], merged.at[:, cols], {"z": z, "y": y}) for z, y in plane(place)]
    yield
    for copy in sent:
        copy.wait()
    keep.wait()


def reduce_piece(place, sends, final, across, plane_step, along):
    if across:
        src, came, own, out = across
        copy = sends.push(src, came, place.toward("c"))
        yield
        copy.wait()
        out[...] = (own[...].astype(f32) + came[...].astype(f32)).astype(bf16)
    held, slots, out = plane_step
    sent = [sends.push(held(z, y), slots.at[n], {"z": z, "y": y}) for n, (z, y) in enumerate(plane(place))]
    yield
    for copy in sent:
        copy.wait()
    total = held(place.z, place.y)[...].astype(f32)
    for n in range(15):
        total = total + slots[n].astype(f32)
    out[...] = total.astype(bf16)
    if along:
        held, slots, out = along
        sent = [sends.push(held(place.step("x", d)), slots.at[d - 1], place.toward("x", d)) for d in (2, 1, 3)]
        yield
        for copy in sent:
            copy.wait()
        total = held(place.x)[...].astype(f32)
        for d in range(3):
            total = total + slots[d].astype(f32)
        out[...] = total.astype(bf16)


def give_all(place, sends, order, final, view, local, direct=False):
    here = {a: place.at(a) for a in "xyz"}
    keep = pltpu.make_async_copy(final, view(here), local)
    keep.start()

    def fixed_view(fixed, half):
        at = {a: fixed.get(a, ALL) for a in "xyz"}
        if half is not None:
            at[order[0]] = pl.ds(half * 2, 2)
        return view(at)

    return ring_gather(place, sends, fixed_view, order, final, keep, True, direct)


def a_sum_scratch():
    vm = lambda *shape: pltpu.VMEM(shape, bf16)
    return [vm(1024, 128), vm(1024, 128), vm(15, 64, 128), vm(64, 128), vm(3, 16, 128)]


def b_sum_scratch():
    vm = lambda *shape: pltpu.VMEM(shape, bf16)
    return [vm(64, 2048), vm(64, 2048), vm(15, 64, 128), vm(64, 128), vm(3, 16, 128)]


def a_sum(place, sends, a, final, scratch):
    came, half, s1, quarter, s2 = scratch
    return reduce_piece(
        place, sends, final,
        (a.at[piece(1 - place.c, 1024)], came, a.at[piece(place.c, 1024)], half),
        (lambda z, y: half.at[piece(z * 4 + y, 64)], s1, quarter),
        (lambda x: quarter.at[piece(x, 16)], s2, final),
    )


def b_sum(place, sends, b, final, scratch):
    came, half, s1, quarter, s2 = scratch
    return reduce_piece(
        place, sends, final,
        (b.at[piece(1 - place.c, 64)], came, b.at[piece(place.c, 64)], half),
        (lambda z, y: half.at[:, piece(z * 4 + y, 128)], s1, quarter),
        (lambda x: quarter.at[piece(x, 16)], s2, final),
    )


def two_parts(at):
    x = at["x"]
    if x is ALL:
        return ALL, ALL
    if isinstance(x, pl.Slice):
        return pl.ds(x.start // 2, 1), ALL
    return lax.rem(x, 2), x // 2


def positions_of(local, parity):
    return (2 * (local // 128) + parity) * 128 + lax.rem(local, 128)


def document_start(starts, positions):
    found = jnp.zeros_like(positions)
    for d in range(8):
        found = jnp.where(positions >= starts[0, d], starts[0, d], found)
    return found


def attend(t, mine, others, starts, parity, scale):
    q = mine[0, piece(t, F_TILE), :]
    q_pos = positions_of(t * F_TILE + lax.broadcasted_iota(jnp.int32, (F_TILE, 1), 0), parity)
    lo = document_start(starts, q_pos)
    ones = jnp.ones((K_TILE, 128), bf16)

    def step(kt, carry):
        top, acc = carry
        rows = piece(kt, K_TILE)
        local = kt * K_TILE + lax.broadcasted_iota(jnp.int32, (1, K_TILE), 1)
        scores = []
        for k, k_parity in ((mine[1, rows, :], parity), (others[0, rows, :], 1 - parity)):
            k_pos = positions_of(local, k_parity)
            scores.append(jnp.where((k_pos >= lo) & (k_pos <= q_pos), dot_nt(q, k), -1e30))
        new = jnp.maximum(jnp.max(scores[0], axis=1, keepdims=True), jnp.max(scores[1], axis=1, keepdims=True))
        new = jnp.maximum(top, new)
        acc = acc * jnp.exp2((top - new) * (scale * LOG2E))
        for s, v in zip(scores, (mine[2, rows, :], others[1, rows, :])):
            p = jnp.exp2((s - new) * (scale * LOG2E)).astype(bf16)
            acc = acc + dot(p, jnp.concatenate([v, ones], axis=1))
        return new, acc

    start = (jnp.full((F_TILE, 1), -1e30, f32), jnp.zeros((F_TILE, 256), f32))
    return lax.fori_loop(0, (t * F_TILE + F_TILE + K_TILE - 1) // K_TILE, step, start)


def front_kernel(
    starts, chosen, tok, gain, shift, bias, dmaps, umaps, cot, lum, wp, wo, up,
    act_all, qkv_w, out_all, up_all, cot_all, heads, across, merged, att, lse, mask,
    act, cotbuf, wq, up_own, rows, mine, others, low, wq_t, send, recv, a_send, a_recv, local, *, scale,
):
    place = Place()
    sends = Sends(send, recv)
    always, perhaps = split_greeting(projectors(place))
    greet(plane_devices(place) + members(place) + always, perhaps)
    home = (place.xl, place.c, place.z, place.y, place.xh)

    def out_view(h):
        def view(fixed, half):
            xl, xh = (ALL, ALL)
            if "x" in fixed:
                xl, xh = lax.rem(fixed["x"], 2), fixed["x"] // 2
            cols = pl.ds(h * 1024, 1024) if half is None else pl.ds(h * 1024 + half * 512, 512)
            return out_all.at[xl, place.c, fixed.get("z", ALL), fixed.get("y", ALL), xh, ALL, cols]

        return view

    def up_view(xl):
        def view(fixed, half):
            c = ALL if half is None else pl.ds(half, 1)
            return up_all.at[pl.ds(xl, 1), c, fixed.get("z", ALL), fixed.get("y", ALL)]

        return view

    def wq_view(p, xl):
        def view(fixed, half):
            c = ALL if half is None else pl.ds(half, 1)
            return wq.at[p, xl, c, fixed.get("z", ALL), fixed.get("y", ALL)]

        return view

    def index(dx, dc):
        return place.step("x", dx) * 2 + (1 - place.c if dc else place.c)

    copies = [
        pltpu.make_async_copy(
            wp.at[:, :, piece(place.g, 256)], wq.at[:, place.xl, place.c, place.z, place.y, place.xh], local.at[0]
        ),
    ]
    copies += [
        pltpu.make_async_copy(
            wo.at[:, pl.ds(h * 1024, 1024)],
            out_view(h)({a: place.at(a) for a in "xyz"}, None),
            local.at[3 + h],
        )
        for h in range(2)
    ]
    for copy in copies:
        copy.start()
    wq_spread = [
        sends.push(
            wp.at[:, :, piece(index(*m), 256)],
            wq.at[:, place.xl, place.c, place.z, place.y, place.xh],
            place.member(*m),
        )
        for m in MEMBERS
    ]

    values = tok[...].astype(f32)
    normed = layer_norm(values, gain[...], shift[...]).astype(bf16)
    position = ((place.z * 4 + place.y) * 2 + place.xh) * 128 + lax.broadcasted_iota(jnp.int32, (128, 1), 0)
    adapter = jnp.zeros_like(position)
    for d in range(8):
        adapter = jnp.where(position >= starts[0, d], chosen[0, d], adapter)
    column = lax.broadcasted_iota(jnp.int32, (128, 128), 1) // ADAPTER_RANK
    keep = (column == adapter).astype(f32)
    mask[...] = keep
    own = act.at[place.x, place.c]
    own[:, 0:2048] = normed
    for p in range(3):
        own[:, 2048 + p * 128 : 2176 + p * 128] = (dot(normed, dmaps[p]) * keep).astype(bf16)
    act_gather = GroupGather(place, sends, act)

    for lead in range(4):
        for pair in range(8):
            at = lead * 2048 + pair * 256
            one, two = up[:, at : at + 128], up[:, at + 128 : at + 256]
            for h in range(2):
                to = (h * 4 + lead) * 1024 + pair * 128
                sides = [v[:, h * 64 : h * 64 + 64] for v in (one, two)]
                up_own[:, to : to + 128] = jnp.concatenate(sides, axis=1)
    up_keep = pltpu.make_async_copy(up_own.at[:, piece(place.g, 1024)], up_all.at[home], local.at[1])
    up_keep.start()
    up_spread = [
        sends.push(up_own.at[:, piece(index(*m), 1024)], up_all.at[home], place.member(*m)) for m in MEMBERS
    ]

    copies[0].wait()
    for copy in wq_spread:
        copy.wait()
    fixed = {"z": place.z, "y": place.y}
    qkv_parts = []
    for p, xl, order in (
        (0, ALL, ("y", "z")), (1, ALL, ("z", "y")), (2, pl.ds(0, 1), ("y", "z")), (2, pl.ds(1, 1), ("z", "y"))
    ):
        view = wq_view(p, xl)
        qkv_parts.append(ring_gather(place, sends, view, order, view(fixed, None), Nothing(), False))
    up_gathers = [
        ring_gather(place, sends, up_view(n), order, up_view(n)(fixed, None), Nothing(), False)
        for n, order in enumerate((("y", "z"), ("z", "y")))
    ]
    out_gathers = [
        ring_gather(place, sends, out_view(h), order, wo.at[:, pl.ds(h * 1024, 1024)], copies[1 + h], True)
        for h, order in enumerate((("x", "y", "z"), ("z", "y", "x")))
    ]

    def tick(*parts):
        for part in parts:
            next(part)

    tick(*qkv_parts, *out_gathers)
    own = cotbuf.at[place.x, place.c]
    own[:, 0:2048] = cot[...]
    own[:, 2048:2176] = (dot_nt(cot[...], lum[...]) * keep).astype(bf16)
    act_gather.own()
    tick(*qkv_parts)
    act_gather.near(False)
    tick(*qkv_parts, *out_gathers)
    run_all(qkv_parts)
    tick(*out_gathers)
    up_keep.wait()
    for copy in up_spread:
        copy.wait()
    tick(*up_gathers)
    kept = []

    def project(x):
        left = act[x, :, :, 0:2048].reshape(256, 2048)
        for p in range(3):
            low_rank = act[x, :, :, 2048 + p * 128 : 2176 + p * 128].reshape(256, 128)
            value = dot(left, wq[p].reshape(2048, 256)) + bias[p] + dot(low_rank, umaps[p])
            for j in range(2):
                rows[p, x, :, j] = value[:, j * 128 : j * 128 + 128].astype(bf16).reshape(2, 128, 128)

    here = place.z * 4 + place.y
    kv = pl.ds(1, 2)
    posts = []

    def post(dx):
        x = place.step("x", dx)
        for n, (to, dc, j, device, myself) in enumerate(attenders(place)):
            if to == dx:
                src = rows.at[:, x, 1 - place.c if dc else place.c, j]
                posts.append(
                    Post(src, mine.at[:, piece(here, 128)], device, myself, a_send.at[0, n], a_recv.at[0, here])
                )
        for n, (to, dc, j, device, _) in enumerate(attenders(place)):
            if to == dx:
                src = rows.at[kv, x, 1 - place.c if dc else place.c, j]
                device = place.member((dx + 2) % 4, dc) | {"z": device["z"], "y": device["y"]}
                myself = None if dc or dx != 2 else (place.z == device["z"]) & (place.y == device["y"])
                posts.append(
                    Post(src, others.at[:, piece(here, 128)], device, myself, a_send.at[1, n], a_recv.at[1, here])
                )

    project(place.x)
    post(0)
    act_gather.near_done()
    project(place.step("x", -1))
    project(place.step("x", 1))
    post(1)
    post(3)
    act_gather.far()
    act_gather.far_done()
    project(place.step("x", 2))
    post(2)
    tick(*up_gathers, *out_gathers)
    kept.append(pltpu.make_async_copy(act, act_all, local.at[6]))
    kept[-1].start()
    for p in range(3):
        for n in range(4):
            wq_t[p, :, n * 512 : n * 512 + 512] = jnp.transpose(wq[p, n // 2, n % 2].reshape(512, 256))
    kept.append(pltpu.make_async_copy(wq_t, qkv_w, local.at[5]))
    kept[-1].start()
    for n in range(16):
        dst = mine.at[:, piece(n, 128)]
        pltpu.make_async_copy(dst, dst, a_recv.at[0, n]).wait()
    kept.append(pltpu.make_async_copy(mine, heads, local.at[7]))
    kept[-1].start()
    for n in range(16):
        dst = others.at[:, piece(n, 128)]
        pltpu.make_async_copy(dst, dst, a_recv.at[1, n]).wait()
    kept.append(pltpu.make_async_copy(others, across, local.at[8]))
    kept[-1].start()
    cot_gather = group_gather(place, sends, cotbuf)
    tick(cot_gather)

    def tile(t, _):
        peak, total = attend(t, mine, others, starts, place.xh, scale)
        weight = total[:, 128:]
        o = total[:, :128] / weight
        att[piece(t, F_TILE), :] = o
        for b in range(F_TILE // 128):
            low[t * (F_TILE // 128) + b] = o[b * 128 : (b + 1) * 128].astype(bf16)
        line = jnp.transpose(peak * (scale * LOG2E) + jnp.log2(weight))
        for n in range(F_TILE // Q_TILE):
            lse[pl.ds(t * (F_TILE // Q_TILE) + n, 1), :] = line[0:1, n * Q_TILE : n * Q_TILE + Q_TILE]
        return 0

    tiles = mine.shape[1] // F_TILE
    lax.fori_loop(0, tiles // 2, tile, 0)
    tick(*up_gathers)
    lax.fori_loop(tiles // 2, tiles * 3 // 4, tile, 0)
    tick(cot_gather, *out_gathers)
    lax.fori_loop(tiles * 3 // 4, tiles, tile, 0)
    back = heads_out(place, sends, low, merged, local.at[9])
    tick(back)
    for copy in posts:
        copy.wait_send()
    for copy in kept:
        copy.wait()
    act_gather.finish()
    run_all([back, *up_gathers, cot_gather, *out_gathers])
    last = pltpu.make_async_copy(cotbuf, cot_all, local.at[10])
    last.start()
    last.wait()
    assert sends.used <= send.shape[0], sends.used


def front(starts, chosen, tok, gain, shift, bias, dmaps, umaps, cot, lum, wp, wo, up, scale):
    any_ = pl.BlockSpec(memory_space=pl.ANY)
    vmem = pl.BlockSpec(memory_space=pltpu.VMEM)
    smem = pl.BlockSpec(memory_space=pltpu.SMEM)
    shape = lambda *s: jax.ShapeDtypeStruct(s, bf16)
    vm = lambda *s: pltpu.VMEM(s, bf16)
    return pl.pallas_call(
        functools.partial(front_kernel, scale=scale),
        name="front",
        out_shape=[
            shape(4, 2, 128, 2432),
            shape(3, 256, 2048),
            shape(2, 2, 4, 4, 2, 16, 2048),
            shape(2, 2, 4, 4, 2, 16, 1024),
            shape(4, 2, 128, 2176),
            shape(3, 2048, 128),
            shape(2, 2048, 128),
            shape(128, 2048),
            jax.ShapeDtypeStruct((2048, 128), f32),
            jax.ShapeDtypeStruct((8, 256), f32),
            jax.ShapeDtypeStruct((128, 128), f32),
        ],
        in_specs=[smem] * 2 + [vmem] * 11,
        out_specs=[any_] * 8 + [vmem] * 3,
        scratch_shapes=[
            vm(4, 2, 128, 2432),
            vm(4, 2, 128, 2176),
            vm(3, 2, 2, 4, 4, 2, 16, 256),
            vm(16, 8192),
            vm(3, 4, 2, 2, 128, 128),
            vm(3, 2048, 128),
            vm(2, 2048, 128),
            vm(16, 128, 128),
            vm(3, 256, 2048),
        ]
        + [pltpu.SemaphoreType.DMA(n) for n in ((150,), (150,), (2, 16), (2, 16), (11,))],
        compiler_params=pltpu.CompilerParams(
            collective_id=0, has_side_effects=True, vmem_limit_bytes=56 * MIB
        ),
    )(starts, chosen, tok, gain, shift, bias, dmaps, umaps, cot, lum, wp, wo, up)


def middle_kernel(
    starts, grad, queries_in, others_in, att_in, lse, umaps_in, mask, a_own, b_own, two,
    by_member, low_rank, a_final, b_final, two_final,
    queries, others, att, umaps, do, delta, dq_acc, dq, own_low, other_low, by_head, from_other, *refs, scale,
):
    scratch, (send, recv, a_send, a_recv, s_send, s_recv, local) = list(refs[:-7]), refs[-7:]
    place = Place()
    across = [{"xh": 1 - place.xh, "z": z, "y": y} for z, y in plane(place)]
    greet(plane_devices(place) + members(place) + across)
    sends = Sends(send, recv)
    here = place.z * 4 + place.y
    parity = place.xh
    kv = pl.ds(1, 2)

    keep = pltpu.make_async_copy(grad.at[:, head_columns(place.z, place.y)], do.at[piece(here, 128)], local.at[0])
    keep.start()
    loads = [
        pltpu.make_async_copy(src, dst, local.at[1 + n])
        for n, (src, dst) in enumerate(
            ((att_in, att), (queries_in, queries), (others_in, others), (umaps_in, umaps))
        )
    ]
    for copy in loads:
        copy.start()
    grads_sent = [
        sends.push(grad.at[:, head_columns(z, y)], do.at[piece(here, 128)], {"z": z, "y": y})
        for z, y in plane(place)
    ]

    def take(n):
        got = scratch[:n]
        del scratch[:n]
        return got

    early = [
        a_sum(place, sends, a_own, a_final, take(5)),
        b_sum(place, sends, b_own, b_final, take(5)),
    ]
    early += [
        reduce_piece(
            place, sends, two_final.at[n], None,
            (lambda z, y, n=n: two.at[n, z, y], scratch[n], two_final.at[n]), None,
        )
        for n in range(2)
    ]

    def tick(*parts):
        for part in parts:
            try:
                next(part)
            except StopIteration:
                pass

    tick(*early)
    dq_acc[...] = jnp.zeros_like(dq_acc)
    keep.wait()
    for copy in grads_sent:
        copy.wait_recv()
    for copy in loads:
        copy.wait()
    ones = jnp.ones((8, 128), bf16)
    tiles, key_tiles = do.shape[0] // Q_TILE, do.shape[0] // K_TILE

    def row_dots(t, _):
        rows = piece(t, Q_TILE)
        value = do[rows, :].astype(f32) * att[rows, :]
        high = value.astype(bf16)
        low = (value - high.astype(f32)).astype(bf16)
        delta[t] = dot_nt(ones, high) + dot_nt(ones, low)
        return 0

    lax.fori_loop(0, tiles, row_dots, 0)
    tick(*early[:2])

    def keys(kt):
        rows = piece(kt, K_TILE)
        sides = ((others[0, rows, :], others[1, rows, :], 1 - parity), (queries[1, rows, :], queries[2, rows, :], parity))
        local = kt * K_TILE + lax.broadcasted_iota(jnp.int32, (K_TILE, 1), 0)

        def step(qt, carry):
            rows = piece(qt, Q_TILE)
            q = queries[0, rows, :]
            d = do[rows, :]
            q_pos = positions_of(qt * Q_TILE + lax.broadcasted_iota(jnp.int32, (1, Q_TILE), 1), parity)
            lo = document_start(starts, q_pos)
            found, dq_part = [], None
            for (k, v, k_parity), (dk, dv) in zip(sides, carry):
                k_pos = positions_of(local, k_parity)
                s = dot_nt(k, q)
                allowed = (k_pos >= lo) & (k_pos <= q_pos)
                p = jnp.exp2(jnp.where(allowed, s * (scale * LOG2E) - lse[pl.ds(qt, 1), :], -1e30))
                dv = dv + dot(p.astype(bf16), d)
                ds = (p * (dot_nt(v, d) - delta[qt, 0:1, :]) * scale).astype(bf16)
                dk = dk + dot(ds, q)
                part = dot_tn(ds, k)
                dq_part = part if dq_part is None else dq_part + part
                found.append((dk, dv))
            dq_acc[rows, :] += dq_part
            return tuple(found)

        zero = jnp.zeros((K_TILE, 128), f32)
        return lax.fori_loop(kt * (K_TILE // Q_TILE), tiles, step, ((zero, zero),) * 2)

    blocks = K_TILE // 128
    gone = []

    def to_token(k, n, src, dst, other, away):
        z, y = n // 4, lax.rem(n, 4)
        myself = None if other or away else (place.z == z) & (place.y == y)
        device = {"z": z, "y": y} | ({"xh": 1 - place.xh} if other else {})
        gone.append(Post(src, dst, device, myself, a_send.at[k, n], a_recv.at[k, here]))

    shared = []

    def share(turn, k, part):
        x = lax.rem(place.z + (4 - turn), 4)
        for c in range(2):
            g = x * 2 + c
            pair = piece(g, 2)
            if k:
                both = by_head[1:3, pair].astype(f32) + from_other[:, pair].astype(f32)
                by_head[1:3, pair] = both.astype(bf16)
            device = {"xl": lax.rem(x, 2), "xh": x // 2, "c": c}
            myself = (place.x == x) & (place.c == c)
            src, dst = by_head.at[part, pair], by_member.at[part, place.x, place.c]
            n = turn * 2 + c
            shared.append(Post(src, dst, device, myself, s_send.at[k, n], s_recv.at[k, place.g]))

    def heads_of(turn):
        x = lax.rem(place.z + (4 - turn), 4)
        return [x * 4 + y for y in range(4)]

    def share_keys(turn):
        for head in heads_of(turn):
            for k, dst in ((2, from_other.at[:, 0]), (1, by_head.at[kv, 0])):
                pltpu.make_async_copy(dst, dst, a_recv.at[k, head]).wait()
        share(turn, 1, kv)

    def share_queries(turn):
        for head in heads_of(turn):
            dst = by_head.at[0, 0]
            pltpu.make_async_copy(dst, dst, a_recv.at[0, head]).wait()
        share(turn, 0, 0)

    for turn in (2, 1, 3, 0):
        kt = lax.rem(place.z + turn, key_tiles)
        for k, low, (dk, dv) in zip((2, 1), (other_low, own_low), keys(kt)):
            for b in range(blocks):
                n = kt * blocks + b
                low[n, 0] = dk[b * 128 : (b + 1) * 128].astype(bf16)
                low[n, 1] = dv[b * 128 : (b + 1) * 128].astype(bf16)
                dst = from_other.at[:, here] if k == 2 else by_head.at[kv, here]
                to_token(k, n, low.at[n], dst, k == 2, turn != 0)
    for n in range(16):
        dq[n] = dq_acc[n * 128 : (n + 1) * 128].astype(bf16)
    for turn in (2, 1, 3, 0):
        for b in range(blocks):
            n = lax.rem(place.z + turn, 4) * 4 + b
            to_token(0, n, dq.at[n], by_head.at[0, here], False, turn != 0)
    tick(*early)
    for turn in (2, 1, 3, 0):
        share_keys(turn)
    tick(*early)
    for turn in (2, 1, 3, 0):
        share_queries(turn)
    for p in range(3):
        whole = jnp.concatenate([by_head[p, n] for n in range(16)], axis=1)
        low_rank[:, p * 128 : p * 128 + 128] = (dot_nt(whole, umaps[p]) * mask[...]).astype(bf16)
    for n in range(8):
        for k, dst in ((0, by_member.at[0, 0, 0]), (1, by_member.at[kv, 0, 0])):
            pltpu.make_async_copy(dst, dst, s_recv.at[k, n]).wait()
    run_all(early)
    for copy in gone + grads_sent + shared:
        copy.wait_send()
    assert sends.used <= send.shape[0], sends.used


def middle(starts, grad, queries, others, att, lse, umaps, mask, a_own, b_own, two, scale):
    any_ = pl.BlockSpec(memory_space=pl.ANY)
    vmem = pl.BlockSpec(memory_space=pltpu.VMEM)
    smem = pl.BlockSpec(memory_space=pltpu.SMEM)
    vm = lambda *s: pltpu.VMEM(s, bf16)
    shape = lambda *s: jax.ShapeDtypeStruct(s, bf16)
    return pl.pallas_call(
        functools.partial(middle_kernel, scale=scale),
        name="attention_backward",
        out_shape=[
            shape(3, 4, 2, 2, 128, 128),
            shape(128, 384),
            shape(16, 128),
            shape(16, 128),
            shape(2, 64, 128),
        ],
        in_specs=[smem, vmem, any_, any_, any_, vmem, any_, vmem] + [vmem] * 3,
        out_specs=[any_] + [vmem] * 4,
        scratch_shapes=[
            vm(3, 2048, 128),
            vm(2, 2048, 128),
            pltpu.VMEM((2048, 128), f32),
            vm(4, 128, 2048),
            vm(2048, 128),
            pltpu.VMEM((8, 8, 256), f32),
            pltpu.VMEM((2048, 128), f32),
            vm(16, 128, 128),
            vm(16, 2, 128, 128),
            vm(16, 2, 128, 128),
            vm(3, 16, 128, 128),
            vm(2, 16, 128, 128),
        ]
        + a_sum_scratch()
        + b_sum_scratch()
        + [vm(15, 64, 128)] * 2
        + [pltpu.SemaphoreType.DMA(k) for k in ((100,), (100,), (3, 16), (3, 16), (2, 8), (2, 8), (8,))],
        compiler_params=pltpu.CompilerParams(collective_id=2, has_side_effects=True, vmem_limit_bytes=58 * MIB),
    )(starts, grad, queries, others, att, lse, umaps, mask, a_own, b_own, two.reshape(2, 4, 4, 64, 128))


def feed_forward_kernel(
    merged, tok, gain, shift, bias_out, bias_end, out_down, out_up, up_down, low_up, mask, umap, dmap, bias, dn, cot_own,
    w_out_in, cot_all, up,
    grad_merged, grad_res, mixed, small_out, a_out, b_out, two, mine_in, mine_cot,
    w_out, residual, low_out, sa, cot, up_v, dn_v, slope, act, pre, parts, total, *refs,
):
    scratch, (send, recv, local) = refs[:-3], refs[-3:]
    scratch, forth_scratch = scratch[:6], scratch[6:]
    place = Place()
    greet(members(place) + plane_devices(place))
    sends = Sends(send, recv)
    loads = [
        pltpu.make_async_copy(src, dst, local.at[n]) for n, (src, dst) in enumerate(((w_out_in, w_out), (up, up_v), (cot_all, cot)))
    ]
    for copy in loads:
        copy.start()

    def dn_view(h):
        def view(fixed, half):
            cols = pl.ds(h * 1024, 1024) if half is None else pl.ds(h * 1024 + half * 512, 512)
            return dn_v.at[fixed.get("z", ALL), fixed.get("y", ALL), :, cols]

        return view

    here = {"z": place.z, "y": place.y}
    dn_v[place.z, place.y] = dn[...]
    dn_gathers = [
        ring_gather(place, sends, dn_view(h), order, dn_view(h)(here, None), Nothing(), False)
        for h, order in enumerate((("y", "z"), ("z", "y")))
    ]

    def tick(*parts):
        for part in parts:
            next(part)

    tick(*dn_gathers)
    low_out[...] = (dot(merged[...], out_down[...]) * mask[...]).astype(bf16)
    loads[0].wait()

    def out_tile(n, _):
        cols = piece(n, 256)
        value = tok[:, cols].astype(f32) + dot(merged[...], w_out[:, cols]) + bias_out[:, cols]
        residual[:, cols] = value + dot(low_out[...], out_up[:, cols])
        return 0

    lax.fori_loop(0, 6, out_tile, 0)
    tick(*dn_gathers)
    lax.fori_loop(6, 8, out_tile, 0)
    second = layer_norm(residual[...], gain[...], shift[...]).astype(bf16)
    own = sa.at[place.x, place.c]
    own[:, 0:2048] = second
    own[:, 2048:2176] = (dot(second, up_down[...]) * mask[...]).astype(bf16)
    gather = GroupGather(place, sends, sa)

    def rows(ref, x, start, size):
        return ref[x, :, :, pl.ds(start, size)].reshape(256, size)

    xs = places_in_turn(place)

    def hidden(k):
        x = xs[k]

        def tile(n, _):
            cols = piece(n, 256)
            value = dot(rows(sa, x, 0, 2048), up_v[:, cols]) + bias[:, cols]
            value = value + dot(rows(sa, x, 2048, 128), umap[:, cols])
            phi = 0.5 * (1.0 + lax.erf(value * 0.7071067811865476))
            act[k, :, cols] = (value * phi).astype(bf16)
            slope[k, :, cols] = phi + value * (0.3989422804014327 * jnp.exp2(value * value * (-0.5 * LOG2E)))
            return 0

        lax.fori_loop(0, 4, tile, 0)

    def grad_hidden(k):
        x = xs[k]

        def tile(n, _):
            cols = piece(n, 256)
            value = dot_nt(rows(cot, x, 0, 2048), dn_v[n].reshape(256, 2048))
            value = value + dot_nt(rows(cot, x, 2048, 128), dmap[cols, :])
            pre[k, :, cols] = (value * slope[k, :, cols]).astype(bf16)
            return 0

        lax.fori_loop(0, 4, tile, 0)

    def backward(k, n):
        ks = pl.ds(k, n)

        def tile(t, _):
            cols = piece(t, 256)
            value = dot_nt(pre[ks].reshape(n * 256, 1024), up_v[cols, :]).astype(bf16)
            parts[ks, :, :, cols] = value.reshape(n, 2, 128, 256)
            return 0

        lax.fori_loop(0, 8, tile, 0)
        value = dot_nt(pre[ks].reshape(n * 256, 1024), umap[...]).astype(bf16)
        parts[ks, :, :, 2048:2176] = value.reshape(n, 2, 128, 128)
        value = dot(act[ks].reshape(n * 256, 1024), dmap[...]).astype(bf16)
        parts[ks, :, :, 2176:2304] = value.reshape(n, 2, 128, 128)

    loads[1].wait()
    gather.own()
    hidden(3)
    tick(*dn_gathers)
    gather.near()
    hidden(2)
    hidden(1)
    run_all(dn_gathers)
    loads[2].wait()
    grad_hidden(3)
    gather.far()
    grad_hidden(2)
    gather.far_done()
    hidden(0)
    grad_hidden(0)

    sums = GroupSum(place, sends, parts, scratch)
    backward(0, 1)
    sums.cross(0)
    grad_hidden(1)
    sums.merge(0)
    sums.first()
    backward(1, 1)
    sums.cross(1)
    backward(2, 2)
    sums.cross(2)
    sums.cross(3)
    sums.merge(1)
    sums.merge(2)
    sums.second()

    def small(k, _):
        x = lax.rem(place.x + jnp.where(k == 3, 0, jnp.where(k == 2, 3, 2 - k)), 4)
        one = dot_tn(act[k], rows(cot, x, 2048, 128))
        other = dot_tn(pre[k], rows(sa, x, 2048, 128))

        @pl.when(k == 0)
        def _():
            total[0] = one
            total[1] = other

        @pl.when(k > 0)
        def _():
            total[0] += one
            total[1] += other

        return 0

    lax.fori_loop(0, 4, small, 0)
    cols = piece(place.g, 256)
    mine_in[...] = sa[:, :, :, cols].reshape(1024, 256)
    mine_cot[...] = cot[:, :, :, cols].reshape(1024, 256)
    def forward(n, _):
        ks, cols = piece(n // 4, 2), piece(lax.rem(n, 4), 512)
        value = dot(act[ks].reshape(512, 1024), dn_v[:, :, :, cols].reshape(1024, 512)).astype(bf16)
        cot[ks, :, :, cols] = value.reshape(2, 2, 128, 512)
        return 0

    lax.fori_loop(0, 8, forward, 0)

    two[...] = total[...].astype(bf16)
    forth = GroupSum(place, sends, cot.at[:, :, :, pl.ds(0, 2048)], forth_scratch)
    for k in range(4):
        forth.cross(k)
    summed = sums.result()
    forth.merge(0)
    forth.first()
    low_up_grad = (summed[:, 2048:2176] * mask[...]).astype(bf16)
    low_down = (summed[:, 2176:2304] * mask[...]).astype(bf16)
    small_out[:, 0:128] = low_up_grad
    small_out[:, 128:256] = low_down
    grad_second = summed[:, 0:2048] + dot_nt(low_up_grad, up_down[...])
    value = cot_own[...].astype(f32) + layer_norm_back(residual[...], gain[...], grad_second)
    grad_res[...] = value
    branch = value.astype(bf16)
    low_grad = (dot_nt(branch, out_up[...]) * mask[...]).astype(bf16)

    def merged_tile(n, _):
        cols = piece(n, 256)
        value = dot_nt(branch, w_out[cols, :]) + dot_nt(low_grad, out_down[cols, :])
        grad_merged[:, cols] = value.astype(bf16)
        return 0

    lax.fori_loop(0, 4, merged_tile, 0)
    forth.merge(1)
    forth.merge(2)
    forth.second()
    lax.fori_loop(4, 8, merged_tile, 0)
    b_out[...] = dot_tn(low_out[...], branch).astype(bf16)
    a_out[...] = dot_tn(merged[...], low_grad).astype(bf16)
    value = residual[...] + bias_end[...] + dot(low_down, low_up[...])
    mixed[...] = (value + forth.result()).astype(bf16)
    gather.finish()
    assert sends.used <= send.shape[0], sends.used


def feed_forward(*args):
    any_ = pl.BlockSpec(memory_space=pl.ANY)
    vmem = pl.BlockSpec(memory_space=pltpu.VMEM)
    vm = lambda *s: pltpu.VMEM(s, bf16)
    shape = lambda *s: jax.ShapeDtypeStruct(s, bf16)
    return pl.pallas_call(
        feed_forward_kernel,
        name="feed_forward",
        out_shape=[
            shape(128, 2048),
            jax.ShapeDtypeStruct((128, 2048), f32),
            shape(128, 2048),
            shape(128, 256),
            shape(2048, 128),
            shape(128, 2048),
            shape(2, 1024, 128),
            shape(1024, 256),
            shape(1024, 256),
        ],
        in_specs=[vmem] * 16 + [any_] * 3,
        out_specs=[vmem] * 9,
        scratch_shapes=[
            vm(2048, 2048),
            pltpu.VMEM((128, 2048), f32),
            vm(128, 128),
            vm(4, 2, 128, 2176),
            vm(4, 2, 128, 2176),
            vm(2048, 1024),
            vm(4, 4, 64, 2048),
            pltpu.VMEM((4, 256, 1024), f32),
            vm(4, 256, 1024),
            vm(4, 256, 1024),
            vm(4, 2, 128, 2304),
            pltpu.VMEM((2, 1024, 128), f32),
        ]
        + GroupSum.scratch(2304)
        + GroupSum.scratch(2048)
        + [pltpu.SemaphoreType.DMA((k,)) for k in (40, 40, 3)],
        compiler_params=pltpu.CompilerParams(collective_id=1, has_side_effects=True, vmem_limit_bytes=63 * MIB),
    )(*args)


def both_heads(gq, p, x):
    heads = [gq[p, x, :, j].reshape(256, 128) for j in range(2)]
    return jnp.concatenate(heads, axis=1)


def tail_kernel(
    grads, qkv_w, act_all, dmaps, low_rank, small, tok, gain, grad_res, mine_in, mine_cot, a_piece, b_piece, two_piece,
    input_grad, a_final, b_final, a_up, b_down, two_a, two_b, a_early, b_early,
    a_res, b_res, gq, wq, act, left, parts, lows, a_sums, b_sums, a_s, a_f, b_s, b_f, *refs,
):
    scratch, (send, recv, local) = refs[:-3], refs[-3:]
    place = Place()
    greet(members(place) + plane_devices(place))
    sends = Sends(send, recv)
    loads = [
        pltpu.make_async_copy(src, dst, local.at[n])
        for n, (src, dst) in enumerate(((grads, gq), (qkv_w, wq), (act_all, act)))
    ]
    for copy in loads:
        copy.start()
    own = lows.at[place.x, place.c]
    own[:, 0:384] = low_rank[...]
    own[:, 384:640] = small[...]
    spread = [sends.push(own, own, place.member(dx, 0)) for dx in (2, 1, 3)]
    passed = [sends.push(own, own, place.member(0, 1))]

    def two_view(res):
        def view(at):
            xl, xh = two_parts(at)
            return res.at[xl, place.c, at["z"], at["y"], xh]

        return view

    def b_early_view(at):
        z, y = at["z"], at["y"]
        if isinstance(y, pl.Slice):
            cols = pl.ds(y.start * 128 if z is ALL else pl.multiple_of(z * 512 + y.start * 128, 128), 256)
        elif z is ALL:
            cols = ALL
        else:
            cols = piece(z, 512) if y is ALL else piece(z * 4 + y, 128)
        return b_early.at[place.c, at["x"], :, cols]

    early = [
        give_all(place, sends, ("x", "z", "y"), two_piece.at[0], two_view(two_a), local.at[3]),
        give_all(place, sends, ("x", "y", "z"), two_piece.at[1], two_view(two_b), local.at[4]),
        give_all(
            place, sends, ("x", "y", "z"), a_piece,
            lambda at: a_early.at[place.c, at["z"], at["y"], at["x"]], local.at[5],
        ),
        give_all(place, sends, ("x", "y", "z"), b_piece, b_early_view, local.at[6]),
    ]

    def tick(*parts):
        for part in parts:
            next(part)

    tick(*early)
    loads[0].wait()
    loads[2].wait()
    for p in range(3):
        total = jnp.zeros((128, 256), f32)
        for x in range(4):
            left_rows = act[x, :, :, 2048 + p * 128 : 2176 + p * 128].reshape(256, 128)
            total = total + dot_tn(left_rows, both_heads(gq, p, x))
        b_sums[p] = total.astype(bf16)
    def a_view(at):
        return a_res.at[:, at["x"], place.c, at["z"], at["y"]]

    def a_held(z, y):
        return a_sums.at[:, piece(z * 4 + y, 16)]

    def b_view(at):
        y = at["y"]
        if y is ALL:
            yr, yc = ALL, ALL
        elif isinstance(y, pl.Slice):
            yr, yc = pl.ds(y.start // 2, 1), ALL
        else:
            yr, yc = y // 2, lax.rem(y, 2)
        return b_res.at[:, at["x"], place.c, at["z"], yr, yc]

    def b_held(z, y):
        return b_sums.at[:, pl.ds(pl.multiple_of(z * 32 + y // 2 * 16, 16), 16), piece(lax.rem(y, 2), 128)]

    def late_part(final, held, slots, order, view, sem):
        yield from reduce_piece(place, sends, final, None, (held, slots, final), None)
        yield from give_all(place, sends, order, final, view, sem, True)

    late = [
        late_part(a_f, a_held, a_s, ("z", "y", "x"), a_view, local.at[7]),
        late_part(b_f, b_held, b_s, ("x", "z", "y"), b_view, local.at[8]),
    ]
    loads[1].wait()
    xs = places_in_turn(place)
    for k in range(4):
        left[k] = jnp.concatenate([both_heads(gq, p, xs[k]) for p in range(3)], axis=1)

    def partial(k, n):
        ks = pl.ds(k, n)

        def tile(t, _):
            cols = piece(t, 512)
            value = dot(left[ks].reshape(n * 256, 768), wq[:, :, cols].reshape(768, 512)).astype(bf16)
            parts[ks, :, :, cols] = value.reshape(n, 2, 128, 512)
            return 0

        lax.fori_loop(0, 4, tile, 0)

    sums = GroupSum(place, sends, parts, scratch)
    partial(0, 1)
    sums.cross(0)
    partial(1, 1)
    sums.cross(1)
    sums.merge(0)
    sums.first()
    partial(2, 2)
    sums.cross(2)
    sums.cross(3)
    for dx, copy in zip((2, 1, 3), spread):
        copy.wait()
        came = lows.at[place.step("x", -dx), place.c]
        passed.append(sends.push(came, came, place.member(0, 1)))
    for copy in passed:
        copy.wait()
    b_sums[3] = dot_tn(lows[:, :, :, 512:640].reshape(1024, 128), mine_cot[...]).astype(bf16)
    rows = act[:, :, :, piece(place.g, 256)].reshape(1024, 256)
    for p in range(4):
        right = lows[:, :, :, p * 128 : p * 128 + 128].reshape(1024, 128)
        a_sums[p] = dot_tn(rows if p < 3 else mine_in[...], right).astype(bf16)

    tick(*late)
    sums.merge(1)
    sums.merge(2)
    sums.second()
    tick(*early)
    tick(*late)
    tick(*early)
    tick(*late)
    grad_first = sums.result()
    for p in range(3):
        grad_first = grad_first + dot_nt(low_rank[:, p * 128 : p * 128 + 128], dmaps[p])
    result = grad_res[...] + layer_norm_back(tok[...].astype(f32), gain[...], grad_first)
    input_grad[...] = result.astype(bf16)
    run_all(late + early)
    moves = [
        pltpu.make_async_copy(a_res.at[pl.ds(0, 3)], a_final, local.at[9]),
        pltpu.make_async_copy(a_res.at[3], a_up, local.at[10]),
    ]
    for part, whole, n in ((pl.ds(0, 3), b_final, 12), (3, b_down, 28)):
        for g in range(8):
            for yc in range(2):
                src = b_res.at[part, g // 2, g % 2, :, :, yc]
                cols = pl.ds(g * 256 + yc * 128, 128)
                dst = whole.at[:, :, :, :, cols] if n == 12 else whole.at[:, :, :, cols]
                moves.append(pltpu.make_async_copy(src, dst, local.at[n + g * 2 + yc]))
    for copy in moves:
        copy.start()
    for copy in moves:
        copy.wait()
    assert sends.used <= send.shape[0], sends.used


def tail(grads, qkv_w, act_all, dmaps, low_rank, small, tok, gain, grad_res, mine_in, mine_cot, a_piece, b_piece, two_piece):
    any_ = pl.BlockSpec(memory_space=pl.ANY)
    vmem = pl.BlockSpec(memory_space=pltpu.VMEM)
    vm = lambda *s: pltpu.VMEM(s, bf16)
    shape = lambda *s: jax.ShapeDtypeStruct(s, bf16)
    a_shape, b_shape = (4, 4, 2, 4, 4, 16, 128), (4, 4, 2, 4, 2, 2, 16, 128)
    input_grad, a_all, b_all, a_up, b_down, two_a, two_b, a_out, b_out = pl.pallas_call(
        tail_kernel,
        name="tail",
        out_shape=[
            shape(128, 2048),
            shape(3, *a_shape[1:]),
            shape(3, 4, 2, 16, 2048),
            shape(*a_shape[1:]),
            shape(4, 2, 16, 2048),
            shape(2, 2, 4, 4, 2, 64, 128),
            shape(2, 2, 4, 4, 2, 64, 128),
            shape(2, 4, 4, 4, 16, 128),
            shape(2, 4, 16, 2048),
        ],
        in_specs=[any_] * 3 + [vmem] * 11,
        out_specs=[vmem] + [any_] * 8,
        scratch_shapes=[
            vm(*a_shape),
            vm(*b_shape),
            vm(3, 4, 2, 2, 128, 128),
            vm(3, 256, 2048),
            vm(4, 2, 128, 2432),
            vm(4, 256, 768),
            vm(4, 2, 128, 2048),
            vm(4, 2, 128, 640),
            vm(4, 256, 128),
            vm(4, 128, 256),
            vm(15, 4, 16, 128),
            vm(4, 16, 128),
            vm(15, 4, 16, 128),
            vm(4, 16, 128),
        ]
        + GroupSum.scratch(2048)
        + [pltpu.SemaphoreType.DMA((k,)) for k in (200, 200, 45)],
        compiler_params=pltpu.CompilerParams(collective_id=3, has_side_effects=True, vmem_limit_bytes=60 * MIB),
    )(
        grads, qkv_w, act_all, dmaps, low_rank, small, tok, gain, grad_res, mine_in, mine_cot, a_piece, b_piece, two_piece
    )
    return (
        input_grad,
        jnp.concatenate([a_all.reshape(3, 2048, 128), a_out.reshape(1, 2048, 128)]),
        jnp.concatenate([b_all.reshape(3, 128, 2048), b_out.reshape(1, 128, 2048)]),
        a_up.reshape(2048, 128),
        b_down.reshape(128, 2048),
        two_a.reshape(8192, 128),
        two_b.reshape(8192, 128),
    )


def per_device(
    tokens,
    document_starts,
    document_adapter,
    layernorm_gain,
    layernorm_bias,
    projection_weight,
    output_weight,
    up_weight,
    down_weight,
    projection_bias,
    upper_bias,
    attention_down_maps,
    attention_up_maps,
    upper_down_maps,
    upper_up_maps,
    lower_down_maps,
    lower_up_maps,
    cotangent,
):
    local_rows, width = tokens.shape[1:]
    head_size = width // HEADS
    seq = local_rows * 32
    scale = head_size ** (-0.5)
    xl, c, z, y, xh = (lax.axis_index(a) for a in AXES)
    group = (xh * 2 + xl) * 2 + c
    cot = cotangent[0]
    bias_rows = jnp.stack([projection_bias[0], jnp.zeros_like(projection_bias[0]), projection_bias[1]])

    def my_columns(array):
        return lax.dynamic_slice_in_dim(array, group * 256, 256, array.ndim - 1)

    def my_hidden(array):
        lead = array.shape[:-1]
        part = lax.dynamic_slice_in_dim(array, (xl * 2 + c) * 2048, 2048, array.ndim - 1)
        part = part.reshape(lead + (16, 2, 64))
        return lax.dynamic_index_in_dim(part, xh, len(lead) + 1, False).reshape(lead + (1024,))

    my_up_maps = my_columns(attention_up_maps[:3])
    (
        act_all, qkv_w, out_all, up_all, cot_all, by_head, across, merged, attended, lse, mask
    ) = front(
        document_starts, document_adapter, tokens[0], layernorm_gain[:1], layernorm_bias[:1],
        my_columns(bias_rows)[:, None, :], attention_down_maps, my_up_maps, cot, lower_up_maps,
        jnp.transpose(projection_weight, (1, 0, 2)), output_weight, up_weight, scale,
    )
    down_maps = lax.dynamic_slice_in_dim(lower_down_maps, (xl * 2 + c) * 2048, 2048, 0)
    down_maps = lax.dynamic_index_in_dim(down_maps.reshape(16, 2, 64, 128), xh, 1, False).reshape(1024, 128)
    grad_merged, grad_residual, mixed, small, a_out, b_out, two, mine_in, mine_cot = feed_forward(
        merged, tokens[0], layernorm_gain[1:], layernorm_bias[1:], projection_bias[2:3], projection_bias[3:4],
        attention_down_maps[3], attention_up_maps[3], upper_down_maps, lower_up_maps, mask, my_hidden(upper_up_maps),
        down_maps, my_hidden(upper_bias)[None], down_weight, cot,
        out_all.reshape(width, width), cot_all, up_all.reshape(width, 1024),
    )
    grad_qkv, grad_adapt_qkv, a_piece, b_piece, two_piece = middle(
        document_starts, grad_merged, by_head, across, attended, lse, attention_up_maps, mask, a_out, b_out, two, scale
    )
    input_grad, a_all, b_all, a_up, b_down, hidden_a, hidden_b = tail(
        grad_qkv, qkv_w, act_all, attention_down_maps, grad_adapt_qkv,
        small, tokens[0], layernorm_gain[:1], grad_residual,
        mine_in, mine_cot, a_piece, b_piece, two_piece,
    )
    return (
        mixed[None],
        input_grad[None],
        a_all.astype(f32),
        b_all.astype(f32),
        a_up.astype(f32),
        jnp.transpose(hidden_b).astype(f32),
        hidden_a.astype(f32),
        b_down.astype(f32),
    )


def solution(mesh):
    fine = jax.sharding.Mesh(mesh.devices.reshape(SIZES), AXES)
    by_token = P(STREAM, TOKEN, None)
    shard = AXES
    in_specs = (
        by_token,
        P(STREAM, None),
        P(STREAM, None),
        P(),
        P(),
        P(shard, None, None),
        P(shard, None),
        P(shard, None),
        P(shard, None),
        P(),
        P(),
        P(),
        P(),
        P(),
        P(),
        P(),
        P(),
        by_token,
    )
    out_specs = (by_token, by_token, P(), P(), P(), P(), P(), P())
    return jax.shard_map(per_device, mesh=fine, in_specs=in_specs, out_specs=out_specs, check_vma=False)
```

```python
import functools

import jax
import jax.numpy as jnp
from jax import lax
from jax.experimental import pallas as pl
from jax.experimental.pallas import tpu as pltpu
from jax.sharding import PartitionSpec as P

HEADS = 16
ADAPTER_RANK = 16
MESH = pl.DeviceIdType.MESH
AXES = ("xl", "c", "z", "y", "xh")
SIZES = (2, 2, 4, 4, 2)
STREAM = ("xl", "c")
TOKEN = ("z", "y", "xh")
bf16 = jnp.bfloat16
f32 = jnp.float32
LOG2E = 1.4426950408889634
MIB = 2**20
Q_TILE = 256
K_TILE = 512
F_TILE = 256
ALL = slice(None)


def layer_norm(values, gain, shift):
    center = values - jnp.mean(values, axis=-1, keepdims=True)
    spread = jnp.mean(center * center, axis=-1, keepdims=True)
    return center * lax.rsqrt(spread + 1e-05) * gain + shift


def layer_norm_back(values, gain, grad):
    center = values - jnp.mean(values, axis=-1, keepdims=True)
    scale = lax.rsqrt(jnp.mean(center * center, axis=-1, keepdims=True) + 1e-05)
    unit = center * scale
    grad = grad * gain
    along = jnp.mean(grad * unit, axis=-1, keepdims=True)
    return scale * (grad - jnp.mean(grad, axis=-1, keepdims=True) - unit * along)


def dot(left, right):
    return jnp.dot(left, right, preferred_element_type=f32)


def dot_nt(left, right):
    return lax.dot_general(left, right, (((1,), (1,)), ((), ())), preferred_element_type=f32)


def dot_tn(left, right):
    return lax.dot_general(left, right, (((0,), (0,)), ((), ())), preferred_element_type=f32)


def piece(n, size):
    return pl.ds(pl.multiple_of(n * size, size), size)


class Place:
    def __init__(self):
        self.xl, self.c, self.z, self.y, self.xh = (lax.axis_index(a) for a in AXES)
        self.x = self.xh * 2 + self.xl
        self.g = self.x * 2 + self.c

    def at(self, axis):
        return {"x": self.x, "y": self.y, "z": self.z}[axis]

    def step(self, axis, step):
        return lax.rem(self.at(axis) + (step + 4), 4)

    def toward(self, axis, step=1):
        if axis == "c":
            return {"c": 1 - self.c}
        to = self.step(axis, step)
        if axis == "x":
            return {"xl": lax.rem(to, 2), "xh": to // 2}
        return {axis: to}

    def member(self, dx, dc):
        to = {}
        if dx:
            to |= self.toward("x", dx)
        if dc:
            to |= {"c": 1 - self.c}
        return to


MEMBERS = [(dx, dc) for dx in (2, 1, 3, 0) for dc in (0, 1) if dx or dc]


class Sends:
    def __init__(self, send, recv):
        self.send, self.recv, self.used, self.open = send, recv, 0, []

    def push(self, src, dst, device):
        k = self.used
        self.used += 1
        copy = pltpu.make_async_remote_copy(
            src_ref=src,
            dst_ref=dst,
            send_sem=self.send.at[k],
            recv_sem=self.recv.at[k],
            device_id=device,
            device_id_type=MESH,
        )
        copy.start()
        self.open.append(copy)
        return copy


def greet(devices, perhaps=()):
    barrier = pltpu.get_barrier_semaphore()
    for device in devices:
        pl.semaphore_signal(barrier, inc=1, device_id=device, device_id_type=MESH)
    amount = len(devices) + len(perhaps)
    for device, myself in perhaps:
        amount = amount - myself.astype(jnp.int32)

        @pl.when(jnp.logical_not(myself))
        def _():
            pl.semaphore_signal(barrier, inc=1, device_id=device, device_id_type=MESH)

    pl.semaphore_wait(barrier, amount)


def run_all(parts):
    parts = list(parts)
    while parts:
        left = []
        for part in parts:
            try:
                next(part)
                left.append(part)
            except StopIteration:
                pass
        parts = left


def ring_gather(place, sends, view, order, chunk, landed, forward, direct=False):
    fixed = {a: place.at(a) for a in order}
    across = place.toward("c")
    later, passed = [], []

    def pass_on(block):
        if forward:
            passed.append(sends.push(view(block, None), view(block, None), across))

    if forward:
        passed.append(sends.push(chunk, view(fixed, None), across))
    for number, axis in enumerate(order):
        own = view(fixed, None)
        src = chunk if number == 0 else own
        if number == 0 or direct:
            sent = [sends.push(src, own, place.toward(axis, s)) for s in (2, 1, 3)]
            yield
            for s, copy in zip((2, 1, 3), sent):
                copy.wait_recv()
                pass_on(fixed | {axis: place.step(axis, -s)})
            if number == 0:
                landed.wait()
            later += sent
            del fixed[axis]
            continue
        up = sends.push(src, own, place.toward(axis, 1))
        down = sends.push(src, own, place.toward(axis, -1))
        yield
        before = fixed | {axis: place.step(axis, -1)}
        after = fixed | {axis: place.step(axis, 1)}
        opposite = fixed | {axis: place.step(axis, 2)}
        up.wait_recv()
        half = view(before, 0)
        up_two = sends.push(half, half, place.toward(axis, 1))
        down.wait_recv()
        half = view(after, 1)
        down_two = sends.push(half, half, place.toward(axis, -1))
        pass_on(before)
        pass_on(after)
        yield
        up_two.wait_recv()
        down_two.wait_recv()
        pass_on(opposite)
        later += [up, down, up_two, down_two]
        del fixed[axis]
    yield
    for copy in later:
        copy.wait_send()
    for copy in passed:
        copy.wait()


class Nothing:
    def wait(self):
        pass


def neighbours(place, axes):
    return [place.toward(a, s) for a in axes for s in ((1, 2, 3) if a in "xyz" else (1,))]


def members(place):
    return [place.member(*m) for m in MEMBERS]


class GroupGather:
    def __init__(self, place, sends, buf):
        self.place, self.sends, self.buf = place, sends, buf
        self.mine = buf.at[place.x, place.c]
        self.right, self.left = place.toward("x", 1), place.toward("x", -1)
        self.up = sends.push(self.mine, self.mine, self.right)
        self.down = sends.push(self.mine, self.mine, self.left)
        self.passed = [self.pass_on(self.mine)]

    def pass_on(self, ref):
        return self.sends.push(ref, ref, self.place.toward("c"))

    def own(self):
        self.passed[0].wait_recv()

    def near(self, wait=True):
        x, c = self.place.step("x", -1), self.place.c
        self.up.wait_recv()
        half = self.buf.at[x, c, pl.ds(0, 64)]
        self.up_two = self.sends.push(half, half, self.right)
        self.passed.append(self.pass_on(self.buf.at[x, c]))
        x = self.place.step("x", 1)
        self.down.wait_recv()
        half = self.buf.at[x, c, pl.ds(64, 64)]
        self.down_two = self.sends.push(half, half, self.left)
        self.passed.append(self.pass_on(self.buf.at[x, c]))
        if wait:
            self.near_done()

    def near_done(self):
        self.passed[1].wait_recv()
        self.passed[2].wait_recv()

    def far(self):
        self.up_two.wait_recv()
        self.down_two.wait_recv()
        self.passed.append(self.pass_on(self.buf.at[self.place.step("x", 2), self.place.c]))

    def far_done(self):
        self.passed[3].wait_recv()

    def finish(self):
        for copy in [self.up, self.down, self.up_two, self.down_two] + self.passed:
            copy.wait_send()


def group_gather(place, sends, buf):
    gather = GroupGather(place, sends, buf)
    yield
    gather.own()
    gather.near()
    yield
    gather.far()
    yield
    gather.far_done()
    gather.finish()


def places_in_turn(place):
    return [place.step("x", s) for s in (2, 1, -1, 0)]


class GroupSum:
    def __init__(self, place, sends, parts, scratch):
        self.place, self.sends, self.parts = place, sends, parts
        self.came, self.own, self.left_one, self.right_one, self.left_two, self.right_two = scratch
        self.right, self.left = place.toward("x", 1), place.toward("x", -1)
        self.crossed = {}

    @staticmethod
    def scratch(n):
        vm = lambda *s: pltpu.VMEM(s, bf16)
        return [vm(4, 128, n), vm(3, 128, n), vm(64, n), vm(64, n), vm(128, n), vm(128, n)]

    def cross(self, k):
        place = self.place
        self.crossed[k] = self.sends.push(
            self.parts.at[k, 1 - place.c], self.came.at[k], place.toward("c")
        )

    def merge(self, k):
        self.crossed[k].wait()
        both = self.parts[k, self.place.c].astype(f32) + self.came[k].astype(f32)
        self.own[k] = both.astype(bf16)

    def first(self):
        self.up = self.sends.push(self.own.at[0, pl.ds(0, 64)], self.left_one, self.right)
        self.down = self.sends.push(self.own.at[0, pl.ds(64, 64)], self.right_one, self.left)

    def second(self):
        self.up.wait()
        both = self.own[1, 0:64].astype(f32) + self.left_one[...].astype(f32)
        self.own[1, 0:64] = both.astype(bf16)
        self.up_two = self.sends.push(self.own.at[1], self.left_two, self.right)
        self.down.wait()
        both = self.own[2, 64:128].astype(f32) + self.right_one[...].astype(f32)
        self.own[2, 64:128] = both.astype(bf16)
        self.down_two = self.sends.push(self.own.at[2], self.right_two, self.left)

    def result(self):
        self.crossed[3].wait()
        total = self.parts[3, self.place.c].astype(f32) + self.came[3].astype(f32)
        self.up_two.wait()
        self.down_two.wait()
        return total + self.left_two[...].astype(f32) + self.right_two[...].astype(f32)


def group_sum(place, sends, parts, scratch, out):
    total = GroupSum(place, sends, parts, scratch)
    for k in range(4):
        total.cross(k)
    yield
    total.merge(0)
    total.first()
    total.merge(1)
    total.merge(2)
    yield
    total.second()
    yield
    out[...] = total.result()


def plane(place):
    steps = [(i, j) for i in (2, 1, 3, 0) for j in (2, 1, 3, 0) if i or j]
    return [(lax.rem(place.z + i, 4), lax.rem(place.y + j, 4)) for i, j in steps]


def from_plane(place):
    steps = [(i, j) for i in (2, 1, 3, 0) for j in (2, 1, 3, 0) if i or j]
    return [(lax.rem(place.z + 4 - i, 4), lax.rem(place.y + 4 - j, 4)) for i, j in steps]


def projectors(place):
    x, c = place.z, place.y // 2
    member = {"xl": lax.rem(x, 2), "xh": x // 2, "c": c}
    mine = (place.x == x) & (place.c == c)
    return [(member | {"z": z, "y": y}, None) for z, y in plane(place)] + [
        (member | {"z": place.z, "y": place.y}, mine)
    ]


def attenders(place):
    found = []
    for dx, dc in MEMBERS + [(0, 0)]:
        for j in range(2):
            z, y = place.x, 2 * place.c + j
            device = place.member(dx, dc) | {"z": z, "y": y}
            mine = None if dx or dc else (place.z == z) & (place.y == y)
            found.append((dx, dc, j, device, mine))
    return found


def head_columns(z, y):
    return pl.ds(pl.multiple_of((z * 4 + y) * 128, 128), 128)


def split_greeting(pairs):
    return [d for d, m in pairs if m is None], [(d, m) for d, m in pairs if m is not None]


def plane_devices(place):
    return [{"z": z, "y": y} for z, y in plane(place)]


class Post:
    def __init__(self, src, dst, device, myself, send_sem, recv_sem):
        self.remote = pltpu.make_async_remote_copy(
            src_ref=src, dst_ref=dst, send_sem=send_sem, recv_sem=recv_sem, device_id=device, device_id_type=MESH
        )
        self.myself = myself
        if myself is None:
            self.remote.start()
        else:
            pl.when(myself)(pltpu.make_async_copy(src, dst, recv_sem).start)
            pl.when(jnp.logical_not(myself))(self.remote.start)

    def wait_send(self):
        if self.myself is None:
            self.remote.wait_send()
        else:
            pl.when(jnp.logical_not(self.myself))(self.remote.wait_send)


def heads_out(place, sends, blocks, merged, local):
    cols = head_columns(place.z, place.y)
    keep = pltpu.make_async_copy(blocks.at[place.z * 4 + place.y], merged.at[:, cols], local)
    keep.start()
    sent = [sends.push(blocks.at[z * 4 + y], merged.at[:, cols], {"z": z, "y": y}) for z, y in plane(place)]
    yield
    for copy in sent:
        copy.wait()
    keep.wait()


def reduce_piece(place, sends, final, across, plane_step, along):
    if across:
        src, came, own, out = across
        copy = sends.push(src, came, place.toward("c"))
        yield
        copy.wait()
        out[...] = (own[...].astype(f32) + came[...].astype(f32)).astype(bf16)
    held, slots, out = plane_step
    sent = [sends.push(held(z, y), slots.at[n], {"z": z, "y": y}) for n, (z, y) in enumerate(plane(place))]
    yield
    for copy in sent:
        copy.wait()
    total = held(place.z, place.y)[...].astype(f32)
    for n in range(15):
        total = total + slots[n].astype(f32)
    out[...] = total.astype(bf16)
    if along:
        held, slots, out = along
        sent = [sends.push(held(place.step("x", d)), slots.at[d - 1], place.toward("x", d)) for d in (2, 1, 3)]
        yield
        for copy in sent:
            copy.wait()
        total = held(place.x)[...].astype(f32)
        for d in range(3):
            total = total + slots[d].astype(f32)
        out[...] = total.astype(bf16)


def give_all(place, sends, order, final, view, local, direct=False):
    here = {a: place.at(a) for a in "xyz"}
    keep = pltpu.make_async_copy(final, view(here), local)
    keep.start()

    def fixed_view(fixed, half):
        at = {a: fixed.get(a, ALL) for a in "xyz"}
        if half is not None:
            at[order[0]] = pl.ds(half * 2, 2)
        return view(at)

    return ring_gather(place, sends, fixed_view, order, final, keep, True, direct)


def a_sum_scratch():
    vm = lambda *shape: pltpu.VMEM(shape, bf16)
    return [vm(1024, 128), vm(1024, 128), vm(15, 64, 128), vm(64, 128), vm(3, 16, 128)]


def b_sum_scratch():
    vm = lambda *shape: pltpu.VMEM(shape, bf16)
    return [vm(64, 2048), vm(64, 2048), vm(15, 64, 128), vm(64, 128), vm(3, 16, 128)]


def a_sum(place, sends, a, final, scratch):
    came, half, s1, quarter, s2 = scratch
    return reduce_piece(
        place, sends, final,
        (a.at[piece(1 - place.c, 1024)], came, a.at[piece(place.c, 1024)], half),
        (lambda z, y: half.at[piece(z * 4 + y, 64)], s1, quarter),
        (lambda x: quarter.at[piece(x, 16)], s2, final),
    )


def b_sum(place, sends, b, final, scratch):
    came, half, s1, quarter, s2 = scratch
    return reduce_piece(
        place, sends, final,
        (b.at[piece(1 - place.c, 64)], came, b.at[piece(place.c, 64)], half),
        (lambda z, y: half.at[:, piece(z * 4 + y, 128)], s1, quarter),
        (lambda x: quarter.at[piece(x, 16)], s2, final),
    )


def two_parts(at):
    x = at["x"]
    if x is ALL:
        return ALL, ALL
    if isinstance(x, pl.Slice):
        return pl.ds(x.start // 2, 1), ALL
    return lax.rem(x, 2), x // 2


def positions_of(local, parity):
    return (2 * (local // 128) + parity) * 128 + lax.rem(local, 128)


def document_start(starts, positions):
    found = jnp.zeros_like(positions)
    for d in range(8):
        found = jnp.where(positions >= starts[0, d], starts[0, d], found)
    return found


def attend(t, mine, others, starts, parity, scale):
    q = mine[0, piece(t, F_TILE), :]
    q_pos = positions_of(t * F_TILE + lax.broadcasted_iota(jnp.int32, (F_TILE, 1), 0), parity)
    lo = document_start(starts, q_pos)
    ones = jnp.ones((K_TILE, 128), bf16)

    def step(kt, carry):
        top, acc = carry
        rows = piece(kt, K_TILE)
        local = kt * K_TILE + lax.broadcasted_iota(jnp.int32, (1, K_TILE), 1)
        scores = []
        for k, k_parity in ((mine[1, rows, :], parity), (others[0, rows, :], 1 - parity)):
            k_pos = positions_of(local, k_parity)
            scores.append(jnp.where((k_pos >= lo) & (k_pos <= q_pos), dot_nt(q, k), -1e30))
        new = jnp.maximum(jnp.max(scores[0], axis=1, keepdims=True), jnp.max(scores[1], axis=1, keepdims=True))
        new = jnp.maximum(top, new)
        acc = acc * jnp.exp2((top - new) * (scale * LOG2E))
        for s, v in zip(scores, (mine[2, rows, :], others[1, rows, :])):
            p = jnp.exp2((s - new) * (scale * LOG2E)).astype(bf16)
            acc = acc + dot(p, jnp.concatenate([v, ones], axis=1))
        return new, acc

    start = (jnp.full((F_TILE, 1), -1e30, f32), jnp.zeros((F_TILE, 256), f32))
    return lax.fori_loop(0, (t * F_TILE + F_TILE + K_TILE - 1) // K_TILE, step, start)


def front_kernel(
    starts, chosen, tok, gain, shift, bias, cot, wp, wo, up, umaps_in, dmaps_in, lum_in,
    act_all, qkv_w, out_all, up_all, cot_all, heads, across, merged, att, lse, mask,
    umaps, dmaps, lum, act, cotbuf, wq, up_own, rows, mine, others, low, wq_t, send, recv, a_send, a_recv, local, *, scale,
):
    place = Place()
    sends = Sends(send, recv)
    loads = [
        pltpu.make_async_copy(dmaps_in.at[pl.ds(0, 3)], dmaps, local.at[14]),
        pltpu.make_async_copy(lum_in, lum, local.at[15]),
    ]
    for copy in loads:
        copy.start()
    always, perhaps = split_greeting(projectors(place))
    greet(plane_devices(place) + members(place) + always, perhaps)
    home = (place.xl, place.c, place.z, place.y, place.xh)

    def out_view(h):
        def view(fixed, half):
            xl, xh = (ALL, ALL)
            if "x" in fixed:
                xl, xh = lax.rem(fixed["x"], 2), fixed["x"] // 2
            cols = pl.ds(h * 1024, 1024) if half is None else pl.ds(h * 1024 + half * 512, 512)
            return out_all.at[xl, place.c, fixed.get("z", ALL), fixed.get("y", ALL), xh, ALL, cols]

        return view

    def up_view(xl):
        def view(fixed, half):
            c = ALL if half is None else pl.ds(half, 1)
            return up_all.at[pl.ds(xl, 1), c, fixed.get("z", ALL), fixed.get("y", ALL)]

        return view

    def wq_view(p, xl):
        def view(fixed, half):
            c = ALL if half is None else pl.ds(half, 1)
            return wq.at[p, xl, c, fixed.get("z", ALL), fixed.get("y", ALL)]

        return view

    def index(dx, dc):
        return place.step("x", dx) * 2 + (1 - place.c if dc else place.c)

    copies = [
        pltpu.make_async_copy(
            wp.at[:, :, piece(place.g, 256)], wq.at[:, place.xl, place.c, place.z, place.y, place.xh], local.at[0]
        ),
    ]
    copies += [
        pltpu.make_async_copy(
            wo.at[:, pl.ds(h * 1024, 1024)],
            out_view(h)({a: place.at(a) for a in "xyz"}, None),
            local.at[3 + h],
        )
        for h in range(2)
    ]
    copies.append(pltpu.make_async_copy(umaps_in.at[pl.ds(0, 3), :, piece(place.g, 256)], umaps, local.at[2]))
    for copy in copies:
        copy.start()
    wq_spread = [
        sends.push(
            wp.at[:, :, piece(index(*m), 256)],
            wq.at[:, place.xl, place.c, place.z, place.y, place.xh],
            place.member(*m),
        )
        for m in MEMBERS
    ]

    values = tok[...].astype(f32)
    normed = layer_norm(values, gain[0:1, :], shift[0:1, :]).astype(bf16)
    position = ((place.z * 4 + place.y) * 2 + place.xh) * 128 + lax.broadcasted_iota(jnp.int32, (128, 1), 0)
    adapter = jnp.zeros_like(position)
    for d in range(8):
        adapter = jnp.where(position >= starts[0, d], chosen[0, d], adapter)
    column = lax.broadcasted_iota(jnp.int32, (128, 128), 1) // ADAPTER_RANK
    keep = (column == adapter).astype(f32)
    mask[...] = keep
    own = act.at[place.x, place.c]
    own[:, 0:2048] = normed
    loads[0].wait()
    for p in range(3):
        own[:, 2048 + p * 128 : 2176 + p * 128] = (dot(normed, dmaps[p]) * keep).astype(bf16)
    act_gather = GroupGather(place, sends, act)

    for lead in range(4):
        for pair in range(8):
            at = lead * 2048 + pair * 256
            one, two = up[:, at : at + 128], up[:, at + 128 : at + 256]
            for h in range(2):
                to = (h * 4 + lead) * 1024 + pair * 128
                sides = [v[:, h * 64 : h * 64 + 64] for v in (one, two)]
                up_own[:, to : to + 128] = jnp.concatenate(sides, axis=1)
    up_keep = pltpu.make_async_copy(up_own.at[:, piece(place.g, 1024)], up_all.at[home], local.at[1])
    up_keep.start()
    up_spread = [
        sends.push(up_own.at[:, piece(index(*m), 1024)], up_all.at[home], place.member(*m)) for m in MEMBERS
    ]

    copies[0].wait()
    for copy in wq_spread:
        copy.wait()
    fixed = {"z": place.z, "y": place.y}
    qkv_parts = []
    for p, xl, order in (
        (0, ALL, ("y", "z")), (1, ALL, ("z", "y")), (2, pl.ds(0, 1), ("y", "z")), (2, pl.ds(1, 1), ("z", "y"))
    ):
        view = wq_view(p, xl)
        qkv_parts.append(ring_gather(place, sends, view, order, view(fixed, None), Nothing(), False))
    up_gathers = [
        ring_gather(place, sends, up_view(n), order, up_view(n)(fixed, None), Nothing(), False)
        for n, order in enumerate((("y", "z"), ("z", "y")))
    ]
    out_gathers = [
        ring_gather(place, sends, out_view(h), order, wo.at[:, pl.ds(h * 1024, 1024)], copies[1 + h], True)
        for h, order in enumerate((("x", "y", "z"), ("z", "y", "x")))
    ]

    def tick(*parts):
        for part in parts:
            next(part)

    tick(*qkv_parts, *out_gathers)
    own = cotbuf.at[place.x, place.c]
    own[:, 0:2048] = cot[...]
    loads[1].wait()
    own[:, 2048:2176] = (dot_nt(cot[...], lum[...]) * keep).astype(bf16)
    act_gather.own()
    tick(*qkv_parts)
    act_gather.near(False)
    tick(*qkv_parts, *out_gathers)
    run_all(qkv_parts)
    kept = []
    copies[3].wait()

    def project(x):
        left = act[x, :, :, 0:2048].reshape(256, 2048)
        for p in range(3):
            low_rank = act[x, :, :, 2048 + p * 128 : 2176 + p * 128].reshape(256, 128)
            value = dot(left, wq[p].reshape(2048, 256)) + dot(low_rank, umaps[p])
            if p != 1:
                value = value + bias[p // 2 : p // 2 + 1, piece(place.g, 256)]
            for j in range(2):
                rows[p, x, :, j] = value[:, j * 128 : j * 128 + 128].astype(bf16).reshape(2, 128, 128)

    here = place.z * 4 + place.y
    kv = pl.ds(1, 2)
    posts = []

    def post(dx):
        x = place.step("x", dx)
        for n, (to, dc, j, device, myself) in enumerate(attenders(place)):
            if to == dx:
                src = rows.at[:, x, 1 - place.c if dc else place.c, j]
                posts.append(
                    Post(src, mine.at[:, piece(here, 128)], device, myself, a_send.at[0, n], a_recv.at[0, here])
                )
        for n, (to, dc, j, device, _) in enumerate(attenders(place)):
            if to == dx:
                src = rows.at[kv, x, 1 - place.c if dc else place.c, j]
                device = place.member((dx + 2) % 4, dc) | {"z": device["z"], "y": device["y"]}
                myself = None if dc or dx != 2 else (place.z == device["z"]) & (place.y == device["y"])
                posts.append(
                    Post(src, others.at[:, piece(here, 128)], device, myself, a_send.at[1, n], a_recv.at[1, here])
                )

    project(place.x)
    post(0)
    act_gather.near_done()
    project(place.step("x", -1))
    project(place.step("x", 1))
    post(1)
    post(3)
    up_keep.wait()
    for copy in up_spread:
        copy.wait()
    tick(*up_gathers, *out_gathers)
    act_gather.far()
    act_gather.far_done()
    project(place.step("x", 2))
    post(2)
    tick(*up_gathers, *out_gathers)
    kept.append(pltpu.make_async_copy(act, act_all, local.at[6]))
    kept[-1].start()
    for p in range(3):
        for n in range(4):
            wq_t[p, :, n * 512 : n * 512 + 512] = jnp.transpose(wq[p, n // 2, n % 2].reshape(512, 256))
    kept.append(pltpu.make_async_copy(wq_t, qkv_w, local.at[5]))
    kept[-1].start()
    for n in range(16):
        dst = mine.at[:, piece(n, 128)]
        pltpu.make_async_copy(dst, dst, a_recv.at[0, n]).wait()
    kept.append(pltpu.make_async_copy(mine, heads, local.at[7]))
    kept[-1].start()
    for n in range(16):
        dst = others.at[:, piece(n, 128)]
        pltpu.make_async_copy(dst, dst, a_recv.at[1, n]).wait()
    kept.append(pltpu.make_async_copy(others, across, local.at[8]))
    kept[-1].start()
    cot_gather = group_gather(place, sends, cotbuf)

    def keep_cot(n, steps):
        copies = []
        for step in steps:
            x = place.step("x", step)
            copies.append(pltpu.make_async_copy(cotbuf.at[x], cot_all.at[x], local.at[n + len(copies)]))
            copies[-1].start()
        return copies

    tick(cot_gather)

    def tile(t, _):
        peak, total = attend(t, mine, others, starts, place.xh, scale)
        weight = total[:, 128:]
        o = total[:, :128] / weight
        att[piece(t, F_TILE), :] = o
        for b in range(F_TILE // 128):
            low[t * (F_TILE // 128) + b] = o[b * 128 : (b + 1) * 128].astype(bf16)
        line = jnp.transpose(peak * (scale * LOG2E) + jnp.log2(weight))
        for n in range(F_TILE // Q_TILE):
            lse[pl.ds(t * (F_TILE // Q_TILE) + n, 1), :] = line[0:1, n * Q_TILE : n * Q_TILE + Q_TILE]
        return 0

    tiles = mine.shape[1] // F_TILE
    lax.fori_loop(0, tiles // 2, tile, 0)
    tick(*up_gathers, *out_gathers)
    lax.fori_loop(tiles // 2, tiles * 3 // 4, tile, 0)
    tick(cot_gather, *out_gathers)
    kept += keep_cot(11, (0, 1, 3))
    lax.fori_loop(tiles * 3 // 4, tiles, tile, 0)
    back = heads_out(place, sends, low, merged, local.at[9])
    tick(back)
    for copy in posts:
        copy.wait_send()
    for copy in kept:
        copy.wait()
    act_gather.finish()
    run_all([back, *up_gathers, cot_gather, *out_gathers])
    for copy in keep_cot(10, (2,)):
        copy.wait()
    assert sends.used <= send.shape[0], sends.used


def front(starts, chosen, tok, gain, shift, bias, cot, wp, wo, up, umaps, dmaps, lum, scale):
    any_ = pl.BlockSpec(memory_space=pl.ANY)
    vmem = pl.BlockSpec(memory_space=pltpu.VMEM)
    smem = pl.BlockSpec(memory_space=pltpu.SMEM)
    shape = lambda *s: jax.ShapeDtypeStruct(s, bf16)
    vm = lambda *s: pltpu.VMEM(s, bf16)
    return pl.pallas_call(
        functools.partial(front_kernel, scale=scale),
        name="front",
        out_shape=[
            shape(4, 2, 128, 2432),
            shape(3, 256, 2048),
            shape(2, 2, 4, 4, 2, 16, 2048),
            shape(2, 2, 4, 4, 2, 16, 1024),
            shape(4, 2, 128, 2176),
            shape(3, 2048, 128),
            shape(2, 2048, 128),
            shape(128, 2048),
            jax.ShapeDtypeStruct((2048, 128), f32),
            jax.ShapeDtypeStruct((8, 256), f32),
            jax.ShapeDtypeStruct((128, 128), f32),
        ],
        in_specs=[smem] * 2 + [vmem] * 8 + [any_] * 3,
        out_specs=[any_] * 8 + [vmem] * 3,
        scratch_shapes=[
            vm(3, 128, 256),
            vm(3, 2048, 128),
            vm(128, 2048),
            vm(4, 2, 128, 2432),
            vm(4, 2, 128, 2176),
            vm(3, 2, 2, 4, 4, 2, 16, 256),
            vm(16, 8192),
            vm(3, 4, 2, 2, 128, 128),
            vm(3, 2048, 128),
            vm(2, 2048, 128),
            vm(16, 128, 128),
            vm(3, 256, 2048),
        ]
        + [pltpu.SemaphoreType.DMA(n) for n in ((150,), (150,), (2, 16), (2, 16), (16,))],
        compiler_params=pltpu.CompilerParams(
            collective_id=0, has_side_effects=True, vmem_limit_bytes=56 * MIB
        ),
    )(starts, chosen, tok, gain, shift, bias, cot, wp, wo, up, umaps, dmaps, lum)


def middle_kernel(
    starts, grad, queries_in, others_in, att_in, lse, umaps_in, mask, a_own, b_own, two,
    by_member, low_rank, a_final, b_final, two_final,
    queries, others, att, umaps, do, delta, dq_acc, dq, own_low, other_low, by_head, from_other, *refs, scale,
):
    scratch, (send, recv, a_send, a_recv, s_send, s_recv, local) = list(refs[:-7]), refs[-7:]
    place = Place()
    across = [{"xh": 1 - place.xh, "z": z, "y": y} for z, y in plane(place)]
    greet(plane_devices(place) + members(place) + across)
    sends = Sends(send, recv)
    here = place.z * 4 + place.y
    parity = place.xh
    kv = pl.ds(1, 2)

    keep = pltpu.make_async_copy(grad.at[:, head_columns(place.z, place.y)], do.at[piece(here, 128)], local.at[0])
    keep.start()
    loads = [
        pltpu.make_async_copy(src, dst, local.at[1 + n])
        for n, (src, dst) in enumerate(
            ((att_in, att), (queries_in, queries), (others_in, others), (umaps_in, umaps))
        )
    ]
    for copy in loads:
        copy.start()
    grads_sent = [
        sends.push(grad.at[:, head_columns(z, y)], do.at[piece(here, 128)], {"z": z, "y": y})
        for z, y in plane(place)
    ]

    def take(n):
        got = scratch[:n]
        del scratch[:n]
        return got

    early = [
        a_sum(place, sends, a_own, a_final, take(5)),
        b_sum(place, sends, b_own, b_final, take(5)),
    ]
    early += [
        reduce_piece(
            place, sends, two_final.at[n], None,
            (lambda z, y, n=n: two.at[n, z, y], scratch[n], two_final.at[n]), None,
        )
        for n in range(2)
    ]

    def tick(*parts):
        for part in parts:
            try:
                next(part)
            except StopIteration:
                pass

    tick(*early)
    dq_acc[...] = jnp.zeros_like(dq_acc)
    keep.wait()
    for copy in grads_sent:
        copy.wait_recv()
    for copy in loads:
        copy.wait()
    ones = jnp.ones((8, 128), bf16)
    tiles, key_tiles = do.shape[0] // Q_TILE, do.shape[0] // K_TILE

    def row_dots(t, _):
        rows = piece(t, Q_TILE)
        value = do[rows, :].astype(f32) * att[rows, :]
        high = value.astype(bf16)
        low = (value - high.astype(f32)).astype(bf16)
        delta[t] = dot_nt(ones, high) + dot_nt(ones, low)
        return 0

    lax.fori_loop(0, tiles, row_dots, 0)
    tick(*early[:2])

    def keys(kt):
        rows = piece(kt, K_TILE)
        sides = ((others[0, rows, :], others[1, rows, :], 1 - parity), (queries[1, rows, :], queries[2, rows, :], parity))
        local = kt * K_TILE + lax.broadcasted_iota(jnp.int32, (K_TILE, 1), 0)

        def step(qt, carry):
            rows = piece(qt, Q_TILE)
            q = queries[0, rows, :]
            d = do[rows, :]
            q_pos = positions_of(qt * Q_TILE + lax.broadcasted_iota(jnp.int32, (1, Q_TILE), 1), parity)
            lo = document_start(starts, q_pos)
            found, dq_part = [], None
            for (k, v, k_parity), (dk, dv) in zip(sides, carry):
                k_pos = positions_of(local, k_parity)
                s = dot_nt(k, q)
                allowed = (k_pos >= lo) & (k_pos <= q_pos)
                p = jnp.exp2(jnp.where(allowed, s * (scale * LOG2E) - lse[pl.ds(qt, 1), :], -1e30))
                dv = dv + dot(p.astype(bf16), d)
                ds = (p * (dot_nt(v, d) - delta[qt, 0:1, :]) * scale).astype(bf16)
                dk = dk + dot(ds, q)
                part = dot_tn(ds, k)
                dq_part = part if dq_part is None else dq_part + part
                found.append((dk, dv))
            dq_acc[rows, :] += dq_part
            return tuple(found)

        zero = jnp.zeros((K_TILE, 128), f32)
        return lax.fori_loop(kt * (K_TILE // Q_TILE), tiles, step, ((zero, zero),) * 2)

    blocks = K_TILE // 128
    gone = []

    def to_token(k, n, src, dst, other, away):
        z, y = n // 4, lax.rem(n, 4)
        myself = None if other or away else (place.z == z) & (place.y == y)
        device = {"z": z, "y": y} | ({"xh": 1 - place.xh} if other else {})
        gone.append(Post(src, dst, device, myself, a_send.at[k, n], a_recv.at[k, here]))

    shared = []

    def share(turn, k, part):
        x = lax.rem(place.z + (4 - turn), 4)
        for c in range(2):
            g = x * 2 + c
            pair = piece(g, 2)
            if k:
                both = by_head[1:3, pair].astype(f32) + from_other[:, pair].astype(f32)
                by_head[1:3, pair] = both.astype(bf16)
            device = {"xl": lax.rem(x, 2), "xh": x // 2, "c": c}
            myself = (place.x == x) & (place.c == c)
            src, dst = by_head.at[part, pair], by_member.at[part, place.x, place.c]
            n = turn * 2 + c
            shared.append(Post(src, dst, device, myself, s_send.at[k, n], s_recv.at[k, place.g]))

    def heads_of(turn):
        x = lax.rem(place.z + (4 - turn), 4)
        return [x * 4 + y for y in range(4)]

    def share_keys(turn):
        for head in heads_of(turn):
            for k, dst in ((2, from_other.at[:, 0]), (1, by_head.at[kv, 0])):
                pltpu.make_async_copy(dst, dst, a_recv.at[k, head]).wait()
        share(turn, 1, kv)

    def share_queries(turn):
        for head in heads_of(turn):
            dst = by_head.at[0, 0]
            pltpu.make_async_copy(dst, dst, a_recv.at[0, head]).wait()
        share(turn, 0, 0)

    for turn in (2, 1, 3, 0):
        kt = lax.rem(place.z + turn, key_tiles)
        for k, low, (dk, dv) in zip((2, 1), (other_low, own_low), keys(kt)):
            for b in range(blocks):
                n = kt * blocks + b
                low[n, 0] = dk[b * 128 : (b + 1) * 128].astype(bf16)
                low[n, 1] = dv[b * 128 : (b + 1) * 128].astype(bf16)
                dst = from_other.at[:, here] if k == 2 else by_head.at[kv, here]
                to_token(k, n, low.at[n], dst, k == 2, turn != 0)
    for n in range(16):
        dq[n] = dq_acc[n * 128 : (n + 1) * 128].astype(bf16)
    for turn in (2, 1, 3, 0):
        for b in range(blocks):
            n = lax.rem(place.z + turn, 4) * 4 + b
            to_token(0, n, dq.at[n], by_head.at[0, here], False, turn != 0)
    tick(*early)
    for turn in (2, 1, 3, 0):
        share_keys(turn)
    tick(*early)
    for turn in (2, 1, 3, 0):
        share_queries(turn)
    for p in range(3):
        whole = jnp.concatenate([by_head[p, n] for n in range(16)], axis=1)
        low_rank[:, p * 128 : p * 128 + 128] = (dot_nt(whole, umaps[p]) * mask[...]).astype(bf16)
    for n in range(8):
        for k, dst in ((0, by_member.at[0, 0, 0]), (1, by_member.at[kv, 0, 0])):
            pltpu.make_async_copy(dst, dst, s_recv.at[k, n]).wait()
    run_all(early)
    for copy in gone + grads_sent + shared:
        copy.wait_send()
    assert sends.used <= send.shape[0], sends.used


def middle(starts, grad, queries, others, att, lse, umaps, mask, a_own, b_own, two, scale):
    any_ = pl.BlockSpec(memory_space=pl.ANY)
    vmem = pl.BlockSpec(memory_space=pltpu.VMEM)
    smem = pl.BlockSpec(memory_space=pltpu.SMEM)
    vm = lambda *s: pltpu.VMEM(s, bf16)
    shape = lambda *s: jax.ShapeDtypeStruct(s, bf16)
    return pl.pallas_call(
        functools.partial(middle_kernel, scale=scale),
        name="attention_backward",
        out_shape=[
            shape(3, 4, 2, 2, 128, 128),
            shape(128, 384),
            shape(16, 128),
            shape(16, 128),
            shape(2, 64, 128),
        ],
        in_specs=[smem, vmem, any_, any_, any_, vmem, any_, vmem] + [vmem] * 3,
        out_specs=[any_] + [vmem] * 4,
        scratch_shapes=[
            vm(3, 2048, 128),
            vm(2, 2048, 128),
            pltpu.VMEM((2048, 128), f32),
            vm(4, 128, 2048),
            vm(2048, 128),
            pltpu.VMEM((8, 8, 256), f32),
            pltpu.VMEM((2048, 128), f32),
            vm(16, 128, 128),
            vm(16, 2, 128, 128),
            vm(16, 2, 128, 128),
            vm(3, 16, 128, 128),
            vm(2, 16, 128, 128),
        ]
        + a_sum_scratch()
        + b_sum_scratch()
        + [vm(15, 64, 128)] * 2
        + [pltpu.SemaphoreType.DMA(k) for k in ((100,), (100,), (3, 16), (3, 16), (2, 8), (2, 8), (8,))],
        compiler_params=pltpu.CompilerParams(collective_id=2, has_side_effects=True, vmem_limit_bytes=58 * MIB),
    )(starts, grad, queries, others, att, lse, umaps, mask, a_own, b_own, two.reshape(2, 4, 4, 64, 128))


def feed_forward_kernel(
    merged, tok, gains, shifts, biases, up_down, low_up, mask, bias_all, dn, cot_own,
    w_out_in, cot_all, up, out_down_in, out_up_in, umap_in, dmap_in,
    grad_merged, grad_res, mixed, small_out, a_out, b_out, two, mine_in, mine_cot,
    out_down, out_up, umap_all, umap, dmap, bias, w_out, residual, low_out, sa, cot, up_v, dn_v, slope, act, pre, parts, total, *refs,
):
    scratch, (send, recv, local) = refs[:-3], refs[-3:]
    scratch, forth_scratch = scratch[:6], scratch[6:]
    place = Place()
    greet(members(place) + plane_devices(place))
    sends = Sends(send, recv)
    loads = [
        pltpu.make_async_copy(src, dst, local.at[n]) for n, (src, dst) in enumerate(
            (
                (out_down_in.at[3], out_down), (w_out_in, w_out), (out_up_in.at[3], out_up),
                (umap_in.at[:, piece(place.xl * 2 + place.c, 2048)], umap_all),
                (dmap_in.at[place.xl * 2 + place.c, :, place.xh], dmap), (up, up_v), (cot_all, cot),
            )
        )
    ]
    for copy in loads:
        copy.start()

    def dn_view(h):
        def view(fixed, half):
            cols = pl.ds(h * 1024, 1024) if half is None else pl.ds(h * 1024 + half * 512, 512)
            return dn_v.at[fixed.get("z", ALL), fixed.get("y", ALL), :, cols]

        return view

    here = {"z": place.z, "y": place.y}
    dn_v[place.z, place.y] = dn[...]
    dn_gathers = [
        ring_gather(place, sends, dn_view(h), order, dn_view(h)(here, None), Nothing(), False)
        for h, order in enumerate((("y", "z"), ("z", "y")))
    ]

    def tick(*parts):
        for part in parts:
            next(part)

    tick(*dn_gathers)
    gain, shift = gains[1:2, :], shifts[1:2, :]
    bias_out, bias_end = biases[2:3, :], biases[3:4, :]
    loads[0].wait()
    low_out[...] = (dot(merged[...], out_down[...]) * mask[...]).astype(bf16)
    loads[1].wait()
    loads[2].wait()

    def out_tile(n, _):
        cols = piece(n, 256)
        value = tok[:, cols].astype(f32) + dot(merged[...], w_out[:, cols]) + biases[2:3, cols]
        residual[:, cols] = value + dot(low_out[...], out_up[:, cols])
        return 0

    lax.fori_loop(0, 6, out_tile, 0)
    tick(*dn_gathers)
    lax.fori_loop(6, 8, out_tile, 0)
    second = layer_norm(residual[...], gain, shift).astype(bf16)
    own = sa.at[place.x, place.c]
    own[:, 0:2048] = second
    own[:, 2048:2176] = (dot(second, up_down[...]) * mask[...]).astype(bf16)
    gather = GroupGather(place, sends, sa)

    loads[3].wait()
    loads[4].wait()
    whole_bias = bias_all[:, piece(place.xl * 2 + place.c, 2048)]
    for n in range(8):
        for whole, out in ((umap_all[:, n * 256 : n * 256 + 256], umap), (whole_bias[:, n * 256 : n * 256 + 256], bias)):
            sides = [jnp.concatenate([whole[:, h : h + 64], whole[:, 128 + h : 192 + h]], axis=1) for h in (0, 64)]
            out[:, n * 128 : n * 128 + 128] = jnp.where(place.xh == 0, sides[0], sides[1])

    def rows(ref, x, start, size):
        return ref[x, :, :, pl.ds(start, size)].reshape(256, size)

    xs = places_in_turn(place)

    def hidden(k):
        x = xs[k]

        def tile(n, _):
            cols = piece(n, 256)
            value = dot(rows(sa, x, 0, 2048), up_v[:, cols]) + bias[:, cols]
            value = value + dot(rows(sa, x, 2048, 128), umap[:, cols])
            phi = 0.5 * (1.0 + lax.erf(value * 0.7071067811865476))
            act[k, :, cols] = (value * phi).astype(bf16)
            slope[k, :, cols] = phi + value * (0.3989422804014327 * jnp.exp2(value * value * (-0.5 * LOG2E)))
            return 0

        lax.fori_loop(0, 4, tile, 0)

    def grad_hidden(k):
        x = xs[k]

        def tile(n, _):
            cols = piece(n, 256)
            value = dot_nt(rows(cot, x, 0, 2048), dn_v[n].reshape(256, 2048))
            value = value + dot_nt(rows(cot, x, 2048, 128), dmap[piece(n, 4)].reshape(256, 128))
            pre[k, :, cols] = (value * slope[k, :, cols]).astype(bf16)
            return 0

        lax.fori_loop(0, 4, tile, 0)

    def backward(k, n):
        ks = pl.ds(k, n)

        def tile(t, _):
            cols = piece(t, 256)
            value = dot_nt(pre[ks].reshape(n * 256, 1024), up_v[cols, :]).astype(bf16)
            parts[ks, :, :, cols] = value.reshape(n, 2, 128, 256)
            return 0

        lax.fori_loop(0, 8, tile, 0)
        value = dot_nt(pre[ks].reshape(n * 256, 1024), umap[...]).astype(bf16)
        parts[ks, :, :, 2048:2176] = value.reshape(n, 2, 128, 128)
        value = dot(act[ks].reshape(n * 256, 1024), dmap[...].reshape(1024, 128)).astype(bf16)
        parts[ks, :, :, 2176:2304] = value.reshape(n, 2, 128, 128)

    loads[5].wait()
    gather.own()
    hidden(3)
    tick(*dn_gathers)
    gather.near()
    hidden(2)
    hidden(1)
    run_all(dn_gathers)
    loads[6].wait()
    grad_hidden(3)
    gather.far()
    grad_hidden(2)
    gather.far_done()
    hidden(0)
    grad_hidden(0)

    sums = GroupSum(place, sends, parts, scratch)
    backward(0, 1)
    sums.cross(0)
    grad_hidden(1)
    sums.merge(0)
    sums.first()
    backward(1, 1)
    sums.cross(1)
    backward(2, 2)
    sums.cross(2)
    sums.cross(3)
    sums.merge(1)
    sums.merge(2)
    sums.second()

    def small(k, _):
        x = lax.rem(place.x + jnp.where(k == 3, 0, jnp.where(k == 2, 3, 2 - k)), 4)
        one = dot_tn(act[k], rows(cot, x, 2048, 128))
        other = dot_tn(pre[k], rows(sa, x, 2048, 128))

        @pl.when(k == 0)
        def _():
            total[0] = one
            total[1] = other

        @pl.when(k > 0)
        def _():
            total[0] += one
            total[1] += other

        return 0

    lax.fori_loop(0, 4, small, 0)
    cols = piece(place.g, 256)
    mine_in[...] = sa[:, :, :, cols].reshape(1024, 256)
    mine_cot[...] = cot[:, :, :, cols].reshape(1024, 256)
    def forward(n, _):
        ks, cols = piece(n // 4, 2), piece(lax.rem(n, 4), 512)
        value = dot(act[ks].reshape(512, 1024), dn_v[:, :, :, cols].reshape(1024, 512)).astype(bf16)
        cot[ks, :, :, cols] = value.reshape(2, 2, 128, 512)
        return 0

    lax.fori_loop(0, 8, forward, 0)

    two[...] = total[...].astype(bf16)
    forth = GroupSum(place, sends, cot.at[:, :, :, pl.ds(0, 2048)], forth_scratch)
    for k in range(4):
        forth.cross(k)
    forth.merge(0)
    forth.first()
    summed = sums.result()
    low_up_grad = (summed[:, 2048:2176] * mask[...]).astype(bf16)
    low_down = (summed[:, 2176:2304] * mask[...]).astype(bf16)
    small_out[:, 0:128] = low_up_grad
    small_out[:, 128:256] = low_down
    grad_second = summed[:, 0:2048] + dot_nt(low_up_grad, up_down[...])
    value = cot_own[...].astype(f32) + layer_norm_back(residual[...], gain, grad_second)
    grad_res[...] = value
    branch = value.astype(bf16)
    low_grad = (dot_nt(branch, out_up[...]) * mask[...]).astype(bf16)

    def merged_tile(n, _):
        cols = piece(n, 256)
        value = dot_nt(branch, w_out[cols, :]) + dot_nt(low_grad, out_down[cols, :])
        grad_merged[:, cols] = value.astype(bf16)
        return 0

    lax.fori_loop(0, 4, merged_tile, 0)
    forth.merge(1)
    forth.merge(2)
    forth.second()
    lax.fori_loop(4, 8, merged_tile, 0)
    b_out[...] = dot_tn(low_out[...], branch).astype(bf16)
    a_out[...] = dot_tn(merged[...], low_grad).astype(bf16)
    value = residual[...] + bias_end + dot(low_down, low_up[...])
    mixed[...] = (value + forth.result()).astype(bf16)
    gather.finish()
    assert sends.used <= send.shape[0], sends.used


def feed_forward(*args):
    any_ = pl.BlockSpec(memory_space=pl.ANY)
    vmem = pl.BlockSpec(memory_space=pltpu.VMEM)
    vm = lambda *s: pltpu.VMEM(s, bf16)
    shape = lambda *s: jax.ShapeDtypeStruct(s, bf16)
    return pl.pallas_call(
        feed_forward_kernel,
        name="feed_forward",
        out_shape=[
            shape(128, 2048),
            jax.ShapeDtypeStruct((128, 2048), f32),
            shape(128, 2048),
            shape(128, 256),
            shape(2048, 128),
            shape(128, 2048),
            shape(2, 1024, 128),
            shape(1024, 256),
            shape(1024, 256),
        ],
        in_specs=[vmem] * 11 + [any_] * 7,
        out_specs=[vmem] * 9,
        scratch_shapes=[
            vm(2048, 128),
            vm(128, 2048),
            vm(128, 2048),
            vm(128, 1024),
            vm(16, 64, 128),
            pltpu.VMEM((1, 1024), f32),
            vm(2048, 2048),
            pltpu.VMEM((128, 2048), f32),
            vm(128, 128),
            vm(4, 2, 128, 2176),
            vm(4, 2, 128, 2176),
            vm(2048, 1024),
            vm(4, 4, 64, 2048),
            pltpu.VMEM((4, 256, 1024), f32),
            vm(4, 256, 1024),
            vm(4, 256, 1024),
            vm(4, 2, 128, 2304),
            pltpu.VMEM((2, 1024, 128), f32),
        ]
        + GroupSum.scratch(2304)
        + GroupSum.scratch(2048)
        + [pltpu.SemaphoreType.DMA((k,)) for k in (40, 40, 7)],
        compiler_params=pltpu.CompilerParams(collective_id=1, has_side_effects=True, vmem_limit_bytes=63 * MIB),
    )(*args)


def both_heads(gq, p, x):
    heads = [gq[p, x, :, j].reshape(256, 128) for j in range(2)]
    return jnp.concatenate(heads, axis=1)


def tail_kernel(
    grads, qkv_w, act_all, dmaps_in, grad_res_in, low_rank, small, tok, gain, mine_in, mine_cot, a_piece, b_piece, two_piece,
    input_grad, a_res, b_res, two_a, two_b, a_early, b_early,
    dmaps, grad_res, gq, wq, act, left, parts, lows, a_sums, b_sums, a_s, a_f, b_s, b_f, *refs,
):
    scratch, (send, recv, local) = refs[:-3], refs[-3:]
    place = Place()
    greet(members(place) + plane_devices(place))
    sends = Sends(send, recv)
    loads = [
        pltpu.make_async_copy(src, dst, local.at[n])
        for n, (src, dst) in enumerate(((grads, gq), (qkv_w, wq), (act_all, act)))
    ]
    loads.append(pltpu.make_async_copy(dmaps_in.at[pl.ds(0, 3)], dmaps, local.at[44]))
    loads.append(pltpu.make_async_copy(grad_res_in, grad_res, local.at[45]))
    for copy in loads:
        copy.start()
    own = lows.at[place.x, place.c]
    own[:, 0:384] = low_rank[...]
    own[:, 384:640] = small[...]
    spread = [sends.push(own, own, place.member(dx, 0)) for dx in (2, 1, 3)]
    passed = [sends.push(own, own, place.member(0, 1))]

    def two_view(res):
        def view(at):
            xl, xh = two_parts(at)
            return res.at[xl, place.c, at["z"], at["y"], xh]

        return view

    def b_early_view(at):
        z, y = at["z"], at["y"]
        if isinstance(y, pl.Slice):
            cols = pl.ds(y.start * 128 if z is ALL else pl.multiple_of(z * 512 + y.start * 128, 128), 256)
        elif z is ALL:
            cols = ALL
        else:
            cols = piece(z, 512) if y is ALL else piece(z * 4 + y, 128)
        return b_early.at[place.c, at["x"], :, cols]

    early = [
        give_all(place, sends, ("x", "z", "y"), two_piece.at[0], two_view(two_a), local.at[3]),
        give_all(place, sends, ("x", "y", "z"), two_piece.at[1], two_view(two_b), local.at[4]),
        give_all(
            place, sends, ("x", "y", "z"), a_piece,
            lambda at: a_early.at[place.c, at["z"], at["y"], at["x"]], local.at[5],
        ),
        give_all(place, sends, ("x", "y", "z"), b_piece, b_early_view, local.at[6]),
    ]

    def tick(*parts):
        for part in parts:
            next(part)

    tick(*early)
    def a_view(at):
        return a_res.at[:, at["x"], place.c, at["z"], at["y"]]

    def a_held(z, y):
        return a_sums.at[:, piece(z * 4 + y, 16)]

    def b_view(at):
        y = at["y"]
        if y is ALL:
            yr, yc = ALL, ALL
        elif isinstance(y, pl.Slice):
            yr, yc = pl.ds(y.start // 2, 1), ALL
        else:
            yr, yc = y // 2, lax.rem(y, 2)
        return b_res.at[:, at["x"], place.c, at["z"], yr, yc]

    def b_held(z, y):
        return b_sums.at[:, pl.ds(pl.multiple_of(z * 32 + y // 2 * 16, 16), 16), piece(lax.rem(y, 2), 128)]

    def late_part(final, held, slots, order, view, sem):
        yield from reduce_piece(place, sends, final, None, (held, slots, final), None)
        yield from give_all(place, sends, order, final, view, sem, True)

    late = [
        late_part(a_f, a_held, a_s, ("z", "y", "x"), a_view, local.at[7]),
        late_part(b_f, b_held, b_s, ("y", "x", "z"), b_view, local.at[8]),
    ]
    loads[0].wait()
    loads[1].wait()
    xs = places_in_turn(place)
    for k in range(4):
        left[k] = jnp.concatenate([both_heads(gq, p, xs[k]) for p in range(3)], axis=1)

    def partial(k, n):
        ks = pl.ds(k, n)

        def tile(t, _):
            cols = piece(t, 512)
            value = dot(left[ks].reshape(n * 256, 768), wq[:, :, cols].reshape(768, 512)).astype(bf16)
            parts[ks, :, :, cols] = value.reshape(n, 2, 128, 512)
            return 0

        lax.fori_loop(0, 4, tile, 0)

    sums = GroupSum(place, sends, parts, scratch)
    partial(0, 1)
    sums.cross(0)
    partial(1, 1)
    sums.cross(1)
    sums.merge(0)
    sums.first()
    tick(*early)
    partial(2, 2)
    sums.cross(2)
    sums.cross(3)
    tick(*early)
    loads[2].wait()
    for p in range(3):
        total = jnp.zeros((128, 256), f32)
        for x in range(4):
            left_rows = act[x, :, :, 2048 + p * 128 : 2176 + p * 128].reshape(256, 128)
            total = total + dot_tn(left_rows, both_heads(gq, p, x))
        b_sums[p] = total.astype(bf16)
    for dx, copy in zip((2, 1, 3), spread):
        copy.wait()
        came = lows.at[place.step("x", -dx), place.c]
        passed.append(sends.push(came, came, place.member(0, 1)))
    for copy in passed:
        copy.wait()
    b_sums[3] = dot_tn(lows[:, :, :, 512:640].reshape(1024, 128), mine_cot[...]).astype(bf16)
    rows = act[:, :, :, piece(place.g, 256)].reshape(1024, 256)
    for p in range(4):
        right = lows[:, :, :, p * 128 : p * 128 + 128].reshape(1024, 128)
        a_sums[p] = dot_tn(rows if p < 3 else mine_in[...], right).astype(bf16)

    tick(*late)
    sums.merge(1)
    sums.merge(2)
    sums.second()
    tick(*late)
    tick(*early)
    tick(*late)
    loads[3].wait()
    loads[4].wait()
    grad_first = sums.result()
    for p in range(3):
        grad_first = grad_first + dot_nt(low_rank[:, p * 128 : p * 128 + 128], dmaps[p])
    result = grad_res[...] + layer_norm_back(tok[...].astype(f32), gain[0:1, :], grad_first)
    input_grad[...] = result.astype(bf16)
    tick(*late)
    run_all(early + late)
    assert sends.used <= send.shape[0], sends.used


def tail(grads, qkv_w, act_all, dmaps, grad_res, low_rank, small, tok, gain, mine_in, mine_cot, a_piece, b_piece, two_piece):
    any_ = pl.BlockSpec(memory_space=pl.ANY)
    vmem = pl.BlockSpec(memory_space=pltpu.VMEM)
    vm = lambda *s: pltpu.VMEM(s, bf16)
    shape = lambda *s: jax.ShapeDtypeStruct(s, bf16)
    a_shape, b_shape = (4, 4, 2, 4, 4, 16, 128), (4, 4, 2, 4, 2, 2, 16, 128)
    return pl.pallas_call(
        tail_kernel,
        name="tail",
        out_shape=[
            shape(128, 2048),
            shape(*a_shape),
            shape(*b_shape),
            shape(2, 2, 4, 4, 2, 64, 128),
            shape(2, 2, 4, 4, 2, 64, 128),
            shape(2, 4, 4, 4, 16, 128),
            shape(2, 4, 16, 2048),
        ],
        in_specs=[any_] * 5 + [vmem] * 9,
        out_specs=[vmem] + [any_] * 6,
        scratch_shapes=[
            vm(3, 2048, 128),
            pltpu.VMEM((128, 2048), f32),
            vm(3, 4, 2, 2, 128, 128),
            vm(3, 256, 2048),
            vm(4, 2, 128, 2432),
            vm(4, 256, 768),
            vm(4, 2, 128, 2048),
            vm(4, 2, 128, 640),
            vm(4, 256, 128),
            vm(4, 128, 256),
            vm(15, 4, 16, 128),
            vm(4, 16, 128),
            vm(15, 4, 16, 128),
            vm(4, 16, 128),
        ]
        + GroupSum.scratch(2048)
        + [pltpu.SemaphoreType.DMA((k,)) for k in (200, 200, 46)],
        compiler_params=pltpu.CompilerParams(collective_id=3, has_side_effects=True, vmem_limit_bytes=60 * MIB),
    )(
        grads, qkv_w, act_all, dmaps, grad_res, low_rank, small, tok, gain, mine_in, mine_cot, a_piece, b_piece, two_piece
    )
def widen_kernel(a, a_one, b, b_one, hid_a, hid_b, a_out, b_out, up_out, hid_b_out, hid_a_out, down_out):
    for n in range(3):
        a_out[n] = a[n].reshape(256, 128).astype(f32)
        for yc in range(2):
            cols = pl.ds(yc * 128, 128)
            b_out[n, :, cols] = b[n, 0, 0, :, :, yc].reshape(128, 128).astype(f32)
    for yc in range(2):
        cols = pl.ds(yc * 128, 128)
        down_out[:, cols] = b[3, 0, 0, :, :, yc].reshape(128, 128).astype(f32)
    a_out[3] = a_one[...].astype(f32)
    up_out[...] = a[3].reshape(256, 128).astype(f32)
    b_out[3] = b_one[...].astype(f32)
    hid_a_out[...] = hid_a[...].astype(f32)
    hid_b_out[...] = jnp.transpose(hid_b[...].astype(f32))


def widen(a, b, hid_a, hid_b, a_one, b_one):
    out = lambda *s: jax.ShapeDtypeStruct(s, f32)
    spec = pl.BlockSpec
    return pl.pallas_call(
        widen_kernel,
        name="widen",
        grid=(8,),
        out_shape=[
            out(4, 2048, 128), out(4, 128, 2048), out(2048, 128), out(128, 8192), out(8192, 128), out(128, 2048)
        ],
        in_specs=[
            spec((4, 256, 128), lambda g: (0, g, 0)),
            spec((256, 128), lambda g: (g, 0)),
            spec((4, 1, 1, 4, 2, 2, 16, 128), lambda g: (0, g // 2, g % 2, 0, 0, 0, 0, 0)),
            spec((128, 256), lambda g: (0, g)),
            spec((1024, 128), lambda g: (g, 0)),
            spec((1024, 128), lambda g: (g, 0)),
        ],
        out_specs=[
            spec((4, 256, 128), lambda g: (0, g, 0)),
            spec((4, 128, 256), lambda g: (0, 0, g)),
            spec((256, 128), lambda g: (g, 0)),
            spec((128, 1024), lambda g: (0, g)),
            spec((1024, 128), lambda g: (g, 0)),
            spec((128, 256), lambda g: (0, g)),
        ],
        compiler_params=pltpu.CompilerParams(vmem_limit_bytes=62 * MIB),
    )(
        a.reshape(4, 2048, 128), a_one.reshape(2048, 128), b, b_one.reshape(128, 2048), hid_a.reshape(8192, 128),
        hid_b.reshape(8192, 128),
    )


def per_device(
    tokens,
    document_starts,
    document_adapter,
    layernorm_gain,
    layernorm_bias,
    projection_weight,
    output_weight,
    up_weight,
    down_weight,
    projection_bias,
    upper_bias,
    attention_down_maps,
    attention_up_maps,
    upper_down_maps,
    upper_up_maps,
    lower_down_maps,
    lower_up_maps,
    cotangent,
):
    local_rows, width = tokens.shape[1:]
    head_size = width // HEADS
    seq = local_rows * 32
    scale = head_size ** (-0.5)
    xl, c, z, y, xh = (lax.axis_index(a) for a in AXES)
    group = (xh * 2 + xl) * 2 + c
    cot = cotangent[0]
    (
        act_all, qkv_w, out_all, up_all, cot_all, by_head, across, merged, attended, lse, mask
    ) = front(
        document_starts, document_adapter, tokens[0], layernorm_gain, layernorm_bias, projection_bias, cot,
        jnp.transpose(projection_weight, (1, 0, 2)), output_weight, up_weight, attention_up_maps, attention_down_maps,
        lower_up_maps, scale,
    )
    grad_merged, grad_residual, mixed, small, a_out, b_out, two, mine_in, mine_cot = feed_forward(
        merged, tokens[0], layernorm_gain, layernorm_bias, projection_bias, upper_down_maps, lower_up_maps, mask,
        upper_bias[None], down_weight, cot, out_all.reshape(width, width), cot_all, up_all.reshape(width, 1024),
        attention_down_maps, attention_up_maps, upper_up_maps, lower_down_maps.reshape(4, 16, 2, 64, 128),
    )
    grad_qkv, grad_adapt_qkv, a_piece, b_piece, two_piece = middle(
        document_starts, grad_merged, by_head, across, attended, lse, attention_up_maps, mask, a_out, b_out, two, scale
    )
    input_grad, *sums = tail(
        grad_qkv, qkv_w, act_all, attention_down_maps, grad_residual, grad_adapt_qkv, small, tokens[0], layernorm_gain,
        mine_in, mine_cot, a_piece, b_piece, two_piece,
    )
    return (mixed[None], input_grad[None], *widen(*sums))


def solution(mesh):
    fine = jax.sharding.Mesh(mesh.devices.reshape(SIZES), AXES)
    by_token = P(STREAM, TOKEN, None)
    shard = AXES
    in_specs = (
        by_token,
        P(STREAM, None),
        P(STREAM, None),
        P(),
        P(),
        P(shard, None, None),
        P(shard, None),
        P(shard, None),
        P(shard, None),
        P(),
        P(),
        P(),
        P(),
        P(),
        P(),
        P(),
        P(),
        by_token,
    )
    out_specs = (by_token, by_token, P(), P(), P(), P(), P(), P())
    return jax.shard_map(per_device, mesh=fine, in_specs=in_specs, out_specs=out_specs, check_vma=False)
```

```python
import functools

import jax
import jax.numpy as jnp
from jax import lax
from jax.experimental import pallas as pl
from jax.experimental.pallas import tpu as pltpu
from jax.sharding import PartitionSpec as P

HEADS = 16
ADAPTER_RANK = 16
MESH = pl.DeviceIdType.MESH
AXES = ("xl", "c", "z", "y", "xh")
SIZES = (2, 2, 4, 4, 2)
STREAM = ("xl", "c")
TOKEN = ("z", "y", "xh")
bf16 = jnp.bfloat16
f32 = jnp.float32
LOG2E = 1.4426950408889634
MIB = 2**20
Q_TILE = 256
K_TILE = 512
F_TILE = 256
ALL = slice(None)


def layer_norm(values, gain, shift):
    center = values - jnp.mean(values, axis=-1, keepdims=True)
    spread = jnp.mean(center * center, axis=-1, keepdims=True)
    return center * lax.rsqrt(spread + 1e-05) * gain + shift


def layer_norm_back(values, gain, grad):
    center = values - jnp.mean(values, axis=-1, keepdims=True)
    scale = lax.rsqrt(jnp.mean(center * center, axis=-1, keepdims=True) + 1e-05)
    unit = center * scale
    grad = grad * gain
    along = jnp.mean(grad * unit, axis=-1, keepdims=True)
    return scale * (grad - jnp.mean(grad, axis=-1, keepdims=True) - unit * along)


def dot(left, right):
    return jnp.dot(left, right, preferred_element_type=f32)


def dot_nt(left, right):
    return lax.dot_general(left, right, (((1,), (1,)), ((), ())), preferred_element_type=f32)


def dot_tn(left, right):
    return lax.dot_general(left, right, (((0,), (0,)), ((), ())), preferred_element_type=f32)


def piece(n, size):
    return pl.ds(pl.multiple_of(n * size, size), size)


class Place:
    def __init__(self):
        self.xl, self.c, self.z, self.y, self.xh = (lax.axis_index(a) for a in AXES)
        self.x = self.xh * 2 + self.xl
        self.g = self.x * 2 + self.c

    def at(self, axis):
        return {"x": self.x, "y": self.y, "z": self.z}[axis]

    def step(self, axis, step):
        return lax.rem(self.at(axis) + (step + 4), 4)

    def toward(self, axis, step=1):
        if axis == "c":
            return {"c": 1 - self.c}
        to = self.step(axis, step)
        if axis == "x":
            return {"xl": lax.rem(to, 2), "xh": to // 2}
        return {axis: to}

    def member(self, dx, dc):
        to = {}
        if dx:
            to |= self.toward("x", dx)
        if dc:
            to |= {"c": 1 - self.c}
        return to


MEMBERS = [(dx, dc) for dx in (2, 1, 3, 0) for dc in (0, 1) if dx or dc]


class Sends:
    def __init__(self, send, recv):
        self.send, self.recv, self.used, self.open = send, recv, 0, []

    def push(self, src, dst, device):
        k = self.used
        self.used += 1
        copy = pltpu.make_async_remote_copy(
            src_ref=src,
            dst_ref=dst,
            send_sem=self.send.at[k],
            recv_sem=self.recv.at[k],
            device_id=device,
            device_id_type=MESH,
        )
        copy.start()
        self.open.append(copy)
        return copy


def greet(devices, perhaps=()):
    barrier = pltpu.get_barrier_semaphore()
    for device in devices:
        pl.semaphore_signal(barrier, inc=1, device_id=device, device_id_type=MESH)
    amount = len(devices) + len(perhaps)
    for device, myself in perhaps:
        amount = amount - myself.astype(jnp.int32)

        @pl.when(jnp.logical_not(myself))
        def _():
            pl.semaphore_signal(barrier, inc=1, device_id=device, device_id_type=MESH)

    pl.semaphore_wait(barrier, amount)


def run_all(parts):
    parts = list(parts)
    while parts:
        left = []
        for part in parts:
            try:
                next(part)
                left.append(part)
            except StopIteration:
                pass
        parts = left


def ring_gather(place, sends, view, order, chunk, landed, forward, direct=False):
    fixed = {a: place.at(a) for a in order}
    across = place.toward("c")
    later, passed = [], []

    def pass_on(block):
        if forward:
            passed.append(sends.push(view(block, None), view(block, None), across))

    if forward:
        passed.append(sends.push(chunk, view(fixed, None), across))
    for number, axis in enumerate(order):
        own = view(fixed, None)
        src = chunk if number == 0 else own
        if number == 0 or direct:
            sent = [sends.push(src, own, place.toward(axis, s)) for s in (2, 1, 3)]
            yield
            for s, copy in zip((2, 1, 3), sent):
                copy.wait_recv()
                pass_on(fixed | {axis: place.step(axis, -s)})
            if number == 0:
                landed.wait()
            later += sent
            del fixed[axis]
            continue
        up = sends.push(src, own, place.toward(axis, 1))
        down = sends.push(src, own, place.toward(axis, -1))
        yield
        before = fixed | {axis: place.step(axis, -1)}
        after = fixed | {axis: place.step(axis, 1)}
        opposite = fixed | {axis: place.step(axis, 2)}
        up.wait_recv()
        half = view(before, 0)
        up_two = sends.push(half, half, place.toward(axis, 1))
        down.wait_recv()
        half = view(after, 1)
        down_two = sends.push(half, half, place.toward(axis, -1))
        pass_on(before)
        pass_on(after)
        yield
        up_two.wait_recv()
        down_two.wait_recv()
        pass_on(opposite)
        later += [up, down, up_two, down_two]
        del fixed[axis]
    yield
    for copy in later:
        copy.wait_send()
    for copy in passed:
        copy.wait()


class Nothing:
    def wait(self):
        pass


def neighbours(place, axes):
    return [place.toward(a, s) for a in axes for s in ((1, 2, 3) if a in "xyz" else (1,))]


def members(place):
    return [place.member(*m) for m in MEMBERS]


class GroupGather:
    def __init__(self, place, sends, buf):
        self.place, self.sends, self.buf = place, sends, buf
        self.mine = buf.at[place.x, place.c]
        self.right, self.left = place.toward("x", 1), place.toward("x", -1)
        self.up = sends.push(self.mine, self.mine, self.right)
        self.down = sends.push(self.mine, self.mine, self.left)
        self.passed = [self.pass_on(self.mine)]

    def pass_on(self, ref):
        return self.sends.push(ref, ref, self.place.toward("c"))

    def own(self):
        self.passed[0].wait_recv()

    def near(self, wait=True):
        x, c = self.place.step("x", -1), self.place.c
        self.up.wait_recv()
        half = self.buf.at[x, c, pl.ds(0, 64)]
        self.up_two = self.sends.push(half, half, self.right)
        self.passed.append(self.pass_on(self.buf.at[x, c]))
        x = self.place.step("x", 1)
        self.down.wait_recv()
        half = self.buf.at[x, c, pl.ds(64, 64)]
        self.down_two = self.sends.push(half, half, self.left)
        self.passed.append(self.pass_on(self.buf.at[x, c]))
        if wait:
            self.near_done()

    def near_done(self):
        self.passed[1].wait_recv()
        self.passed[2].wait_recv()

    def far(self):
        self.up_two.wait_recv()
        self.down_two.wait_recv()
        self.passed.append(self.pass_on(self.buf.at[self.place.step("x", 2), self.place.c]))

    def far_done(self):
        self.passed[3].wait_recv()

    def finish(self):
        for copy in [self.up, self.down, self.up_two, self.down_two] + self.passed:
            copy.wait_send()


def group_gather(place, sends, buf):
    gather = GroupGather(place, sends, buf)
    yield
    gather.own()
    gather.near()
    yield
    gather.far()
    yield
    gather.far_done()
    gather.finish()


def places_in_turn(place):
    return [place.step("x", s) for s in (2, 1, -1, 0)]


class GroupSum:
    def __init__(self, place, sends, parts, scratch):
        self.place, self.sends, self.parts = place, sends, parts
        self.came, self.own, self.left_one, self.right_one, self.left_two, self.right_two = scratch
        self.right, self.left = place.toward("x", 1), place.toward("x", -1)
        self.crossed = {}

    @staticmethod
    def scratch(n):
        vm = lambda *s: pltpu.VMEM(s, bf16)
        return [vm(4, 128, n), vm(3, 128, n), vm(64, n), vm(64, n), vm(128, n), vm(128, n)]

    def cross(self, k):
        place = self.place
        self.crossed[k] = self.sends.push(
            self.parts.at[k, 1 - place.c], self.came.at[k], place.toward("c")
        )

    def merge(self, k):
        self.crossed[k].wait()
        both = self.parts[k, self.place.c].astype(f32) + self.came[k].astype(f32)
        self.own[k] = both.astype(bf16)

    def first(self):
        self.up = self.sends.push(self.own.at[0, pl.ds(0, 64)], self.left_one, self.right)
        self.down = self.sends.push(self.own.at[0, pl.ds(64, 64)], self.right_one, self.left)

    def second(self):
        self.up.wait()
        both = self.own[1, 0:64].astype(f32) + self.left_one[...].astype(f32)
        self.own[1, 0:64] = both.astype(bf16)
        self.up_two = self.sends.push(self.own.at[1], self.left_two, self.right)
        self.down.wait()
        both = self.own[2, 64:128].astype(f32) + self.right_one[...].astype(f32)
        self.own[2, 64:128] = both.astype(bf16)
        self.down_two = self.sends.push(self.own.at[2], self.right_two, self.left)

    def result(self):
        self.crossed[3].wait()
        total = self.parts[3, self.place.c].astype(f32) + self.came[3].astype(f32)
        self.up_two.wait()
        self.down_two.wait()
        return total + self.left_two[...].astype(f32) + self.right_two[...].astype(f32)


def group_sum(place, sends, parts, scratch, out):
    total = GroupSum(place, sends, parts, scratch)
    for k in range(4):
        total.cross(k)
    yield
    total.merge(0)
    total.first()
    total.merge(1)
    total.merge(2)
    yield
    total.second()
    yield
    out[...] = total.result()


def plane(place):
    steps = [(i, j) for i in (2, 1, 3, 0) for j in (2, 1, 3, 0) if i or j]
    return [(lax.rem(place.z + i, 4), lax.rem(place.y + j, 4)) for i, j in steps]


def from_plane(place):
    steps = [(i, j) for i in (2, 1, 3, 0) for j in (2, 1, 3, 0) if i or j]
    return [(lax.rem(place.z + 4 - i, 4), lax.rem(place.y + 4 - j, 4)) for i, j in steps]


def projectors(place):
    x, c = place.z, place.y // 2
    member = {"xl": lax.rem(x, 2), "xh": x // 2, "c": c}
    mine = (place.x == x) & (place.c == c)
    return [(member | {"z": z, "y": y}, None) for z, y in plane(place)] + [
        (member | {"z": place.z, "y": place.y}, mine)
    ]


def attenders(place):
    found = []
    for dx, dc in MEMBERS + [(0, 0)]:
        for j in range(2):
            z, y = place.x, 2 * place.c + j
            device = place.member(dx, dc) | {"z": z, "y": y}
            mine = None if dx or dc else (place.z == z) & (place.y == y)
            found.append((dx, dc, j, device, mine))
    return found


def head_columns(z, y):
    return pl.ds(pl.multiple_of((z * 4 + y) * 128, 128), 128)


def split_greeting(pairs):
    return [d for d, m in pairs if m is None], [(d, m) for d, m in pairs if m is not None]


def plane_devices(place):
    return [{"z": z, "y": y} for z, y in plane(place)]


class Post:
    def __init__(self, src, dst, device, myself, send_sem, recv_sem):
        self.remote = pltpu.make_async_remote_copy(
            src_ref=src, dst_ref=dst, send_sem=send_sem, recv_sem=recv_sem, device_id=device, device_id_type=MESH
        )
        self.myself = myself
        if myself is None:
            self.remote.start()
        else:
            pl.when(myself)(pltpu.make_async_copy(src, dst, recv_sem).start)
            pl.when(jnp.logical_not(myself))(self.remote.start)

    def wait_send(self):
        if self.myself is None:
            self.remote.wait_send()
        else:
            pl.when(jnp.logical_not(self.myself))(self.remote.wait_send)


def heads_out(place, sends, blocks, merged, local):
    cols = head_columns(place.z, place.y)
    keep = pltpu.make_async_copy(blocks.at[place.z * 4 + place.y], merged.at[:, cols], local)
    keep.start()
    sent = [sends.push(blocks.at[z * 4 + y], merged.at[:, cols], {"z": z, "y": y}) for z, y in plane(place)]
    yield
    for copy in sent:
        copy.wait()
    keep.wait()


def reduce_piece(place, sends, final, across, plane_step, along):
    if across:
        src, came, own, out = across
        copy = sends.push(src, came, place.toward("c"))
        yield
        copy.wait()
        out[...] = (own[...].astype(f32) + came[...].astype(f32)).astype(bf16)
    held, slots, out = plane_step
    sent = [sends.push(held(z, y), slots.at[n], {"z": z, "y": y}) for n, (z, y) in enumerate(plane(place))]
    yield
    for copy in sent:
        copy.wait()
    total = held(place.z, place.y)[...].astype(f32)
    for n in range(15):
        total = total + slots[n].astype(f32)
    out[...] = total.astype(bf16)
    if along:
        held, slots, out = along
        sent = [sends.push(held(place.step("x", d)), slots.at[d - 1], place.toward("x", d)) for d in (2, 1, 3)]
        yield
        for copy in sent:
            copy.wait()
        total = held(place.x)[...].astype(f32)
        for d in range(3):
            total = total + slots[d].astype(f32)
        out[...] = total.astype(bf16)


def give_all(place, sends, order, final, view, local, direct=False):
    here = {a: place.at(a) for a in "xyz"}
    keep = pltpu.make_async_copy(final, view(here), local)
    keep.start()

    def fixed_view(fixed, half):
        at = {a: fixed.get(a, ALL) for a in "xyz"}
        if half is not None:
            at[order[0]] = pl.ds(half * 2, 2)
        return view(at)

    return ring_gather(place, sends, fixed_view, order, final, keep, True, direct)


def a_sum_scratch():
    vm = lambda *shape: pltpu.VMEM(shape, bf16)
    return [vm(1024, 128), vm(1024, 128), vm(15, 64, 128), vm(64, 128), vm(3, 16, 128)]


def b_sum_scratch():
    vm = lambda *shape: pltpu.VMEM(shape, bf16)
    return [vm(64, 2048), vm(64, 2048), vm(15, 64, 128), vm(64, 128), vm(3, 16, 128)]


def a_sum(place, sends, a, final, scratch):
    came, half, s1, quarter, s2 = scratch
    return reduce_piece(
        place, sends, final,
        (a.at[piece(1 - place.c, 1024)], came, a.at[piece(place.c, 1024)], half),
        (lambda z, y: half.at[piece(z * 4 + y, 64)], s1, quarter),
        (lambda x: quarter.at[piece(x, 16)], s2, final),
    )


def b_sum(place, sends, b, final, scratch):
    came, half, s1, quarter, s2 = scratch
    return reduce_piece(
        place, sends, final,
        (b.at[piece(1 - place.c, 64)], came, b.at[piece(place.c, 64)], half),
        (lambda z, y: half.at[:, piece(z * 4 + y, 128)], s1, quarter),
        (lambda x: quarter.at[piece(x, 16)], s2, final),
    )


def two_parts(at):
    x = at["x"]
    if x is ALL:
        return ALL, ALL
    if isinstance(x, pl.Slice):
        return pl.ds(x.start // 2, 1), ALL
    return lax.rem(x, 2), x // 2


def positions_of(local, parity):
    return (2 * (local // 128) + parity) * 128 + lax.rem(local, 128)


def document_start(starts, positions):
    found = jnp.zeros_like(positions)
    for d in range(8):
        found = jnp.where(positions >= starts[0, d], starts[0, d], found)
    return found


def attend(t, mine, others, starts, parity, scale):
    q = mine[0, piece(t, F_TILE), :]
    q_pos = positions_of(t * F_TILE + lax.broadcasted_iota(jnp.int32, (F_TILE, 1), 0), parity)
    lo = document_start(starts, q_pos)
    ones = jnp.ones((K_TILE, 128), bf16)

    def step(kt, carry):
        top, acc = carry
        rows = piece(kt, K_TILE)
        local = kt * K_TILE + lax.broadcasted_iota(jnp.int32, (1, K_TILE), 1)
        scores = []
        for k, k_parity in ((mine[1, rows, :], parity), (others[0, rows, :], 1 - parity)):
            k_pos = positions_of(local, k_parity)
            scores.append(jnp.where((k_pos >= lo) & (k_pos <= q_pos), dot_nt(q, k), -1e30))
        new = jnp.maximum(jnp.max(scores[0], axis=1, keepdims=True), jnp.max(scores[1], axis=1, keepdims=True))
        new = jnp.maximum(top, new)
        acc = acc * jnp.exp2((top - new) * (scale * LOG2E))
        for s, v in zip(scores, (mine[2, rows, :], others[1, rows, :])):
            p = jnp.exp2((s - new) * (scale * LOG2E)).astype(bf16)
            acc = acc + dot(p, jnp.concatenate([v, ones], axis=1))
        return new, acc

    start = (jnp.full((F_TILE, 1), -1e30, f32), jnp.zeros((F_TILE, 256), f32))
    return lax.fori_loop(0, (t * F_TILE + F_TILE + K_TILE - 1) // K_TILE, step, start)


def front_kernel(
    starts, chosen, tok, gain, shift, bias, cot, wp, wo, up, umaps_in, dmaps_in, lum_in,
    act_all, qkv_w, out_all, up_all, cot_all, heads, across, merged, att, lse, mask,
    umaps, dmaps, lum, act, cotbuf, wq, up_own, rows, mine, others, low, wq_t, send, recv, a_send, a_recv, local, *, scale,
):
    place = Place()
    sends = Sends(send, recv)
    loads = [
        pltpu.make_async_copy(dmaps_in.at[pl.ds(0, 3)], dmaps, local.at[14]),
        pltpu.make_async_copy(lum_in, lum, local.at[15]),
    ]
    for copy in loads:
        copy.start()
    always, perhaps = split_greeting(projectors(place))
    greet(plane_devices(place) + members(place) + always, perhaps)
    home = (place.xl, place.c, place.z, place.y, place.xh)

    def out_view(h):
        def view(fixed, half):
            xl, xh = (ALL, ALL)
            if "x" in fixed:
                xl, xh = lax.rem(fixed["x"], 2), fixed["x"] // 2
            cols = pl.ds(h * 1024, 1024) if half is None else pl.ds(h * 1024 + half * 512, 512)
            return out_all.at[xl, place.c, fixed.get("z", ALL), fixed.get("y", ALL), xh, ALL, cols]

        return view

    def up_view(xl):
        def view(fixed, half):
            c = ALL if half is None else pl.ds(half, 1)
            return up_all.at[pl.ds(xl, 1), c, fixed.get("z", ALL), fixed.get("y", ALL)]

        return view

    def wq_view(p, xl):
        def view(fixed, half):
            c = ALL if half is None else pl.ds(half, 1)
            return wq.at[p, xl, c, fixed.get("z", ALL), fixed.get("y", ALL)]

        return view

    def index(dx, dc):
        return place.step("x", dx) * 2 + (1 - place.c if dc else place.c)

    copies = [
        pltpu.make_async_copy(
            wp.at[:, :, piece(place.g, 256)], wq.at[:, place.xl, place.c, place.z, place.y, place.xh], local.at[0]
        ),
    ]
    copies += [
        pltpu.make_async_copy(
            wo.at[:, pl.ds(h * 1024, 1024)],
            out_view(h)({a: place.at(a) for a in "xyz"}, None),
            local.at[3 + h],
        )
        for h in range(2)
    ]
    copies.append(pltpu.make_async_copy(umaps_in.at[pl.ds(0, 3), :, piece(place.g, 256)], umaps, local.at[2]))
    for copy in copies:
        copy.start()
    wq_spread = [
        sends.push(
            wp.at[:, :, piece(index(*m), 256)],
            wq.at[:, place.xl, place.c, place.z, place.y, place.xh],
            place.member(*m),
        )
        for m in MEMBERS
    ]

    values = tok[...].astype(f32)
    normed = layer_norm(values, gain[0:1, :], shift[0:1, :]).astype(bf16)
    position = ((place.z * 4 + place.y) * 2 + place.xh) * 128 + lax.broadcasted_iota(jnp.int32, (128, 1), 0)
    adapter = jnp.zeros_like(position)
    for d in range(8):
        adapter = jnp.where(position >= starts[0, d], chosen[0, d], adapter)
    column = lax.broadcasted_iota(jnp.int32, (128, 128), 1) // ADAPTER_RANK
    keep = (column == adapter).astype(f32)
    mask[...] = keep
    own = act.at[place.x, place.c]
    own[:, 0:2048] = normed
    loads[0].wait()
    for p in range(3):
        own[:, 2048 + p * 128 : 2176 + p * 128] = (dot(normed, dmaps[p]) * keep).astype(bf16)
    act_gather = GroupGather(place, sends, act)

    for lead in range(4):
        for pair in range(8):
            at = lead * 2048 + pair * 256
            one, two = up[:, at : at + 128], up[:, at + 128 : at + 256]
            for h in range(2):
                to = (h * 4 + lead) * 1024 + pair * 128
                sides = [v[:, h * 64 : h * 64 + 64] for v in (one, two)]
                up_own[:, to : to + 128] = jnp.concatenate(sides, axis=1)
    up_keep = pltpu.make_async_copy(up_own.at[:, piece(place.g, 1024)], up_all.at[home], local.at[1])
    up_keep.start()
    up_spread = [
        sends.push(up_own.at[:, piece(index(*m), 1024)], up_all.at[home], place.member(*m)) for m in MEMBERS
    ]

    copies[0].wait()
    for copy in wq_spread:
        copy.wait()
    fixed = {"z": place.z, "y": place.y}
    qkv_parts = []
    for p, xl, order in (
        (0, ALL, ("y", "z")), (1, ALL, ("z", "y")), (2, pl.ds(0, 1), ("y", "z")), (2, pl.ds(1, 1), ("z", "y"))
    ):
        view = wq_view(p, xl)
        qkv_parts.append(ring_gather(place, sends, view, order, view(fixed, None), Nothing(), False))
    up_gathers = [
        ring_gather(place, sends, up_view(n), order, up_view(n)(fixed, None), Nothing(), False)
        for n, order in enumerate((("y", "z"), ("z", "y")))
    ]
    out_gathers = [
        ring_gather(place, sends, out_view(h), order, wo.at[:, pl.ds(h * 1024, 1024)], copies[1 + h], True)
        for h, order in enumerate((("x", "y", "z"), ("z", "y", "x")))
    ]

    def tick(*parts):
        for part in parts:
            next(part)

    tick(*qkv_parts, *out_gathers)
    own = cotbuf.at[place.x, place.c]
    own[:, 0:2048] = cot[...]
    loads[1].wait()
    own[:, 2048:2176] = (dot_nt(cot[...], lum[...]) * keep).astype(bf16)
    act_gather.own()
    tick(*qkv_parts)
    act_gather.near(False)
    tick(*qkv_parts, *out_gathers)
    run_all(qkv_parts)
    kept = []
    copies[3].wait()

    def project(x):
        left = act[x, :, :, 0:2048].reshape(256, 2048)
        for p in range(3):
            low_rank = act[x, :, :, 2048 + p * 128 : 2176 + p * 128].reshape(256, 128)
            value = dot(left, wq[p].reshape(2048, 256)) + dot(low_rank, umaps[p])
            if p != 1:
                value = value + bias[p // 2 : p // 2 + 1, piece(place.g, 256)]
            for j in range(2):
                rows[p, x, :, j] = value[:, j * 128 : j * 128 + 128].astype(bf16).reshape(2, 128, 128)

    here = place.z * 4 + place.y
    kv = pl.ds(1, 2)
    posts = []

    def post(dx):
        x = place.step("x", dx)
        for n, (to, dc, j, device, myself) in enumerate(attenders(place)):
            if to == dx:
                src = rows.at[:, x, 1 - place.c if dc else place.c, j]
                posts.append(
                    Post(src, mine.at[:, piece(here, 128)], device, myself, a_send.at[0, n], a_recv.at[0, here])
                )
        for n, (to, dc, j, device, _) in enumerate(attenders(place)):
            if to == dx:
                src = rows.at[kv, x, 1 - place.c if dc else place.c, j]
                device = place.member((dx + 2) % 4, dc) | {"z": device["z"], "y": device["y"]}
                myself = None if dc or dx != 2 else (place.z == device["z"]) & (place.y == device["y"])
                posts.append(
                    Post(src, others.at[:, piece(here, 128)], device, myself, a_send.at[1, n], a_recv.at[1, here])
                )

    project(place.x)
    post(0)
    act_gather.near_done()
    project(place.step("x", -1))
    project(place.step("x", 1))
    post(1)
    post(3)
    up_keep.wait()
    for copy in up_spread:
        copy.wait()
    tick(*up_gathers, *out_gathers)
    act_gather.far()
    act_gather.far_done()
    project(place.step("x", 2))
    post(2)
    tick(*up_gathers, *out_gathers)
    kept.append(pltpu.make_async_copy(act, act_all, local.at[6]))
    kept[-1].start()
    for p in range(3):
        for n in range(4):
            wq_t[p, :, n * 512 : n * 512 + 512] = jnp.transpose(wq[p, n // 2, n % 2].reshape(512, 256))
    kept.append(pltpu.make_async_copy(wq_t, qkv_w, local.at[5]))
    kept[-1].start()
    for n in range(16):
        dst = mine.at[:, piece(n, 128)]
        pltpu.make_async_copy(dst, dst, a_recv.at[0, n]).wait()
    kept.append(pltpu.make_async_copy(mine, heads, local.at[7]))
    kept[-1].start()
    for n in range(16):
        dst = others.at[:, piece(n, 128)]
        pltpu.make_async_copy(dst, dst, a_recv.at[1, n]).wait()
    kept.append(pltpu.make_async_copy(others, across, local.at[8]))
    kept[-1].start()
    cot_gather = group_gather(place, sends, cotbuf)

    def keep_cot(n, steps):
        copies = []
        for step in steps:
            x = place.step("x", step)
            copies.append(pltpu.make_async_copy(cotbuf.at[x], cot_all.at[x], local.at[n + len(copies)]))
            copies[-1].start()
        return copies

    tick(cot_gather)

    def tile(t, _):
        peak, total = attend(t, mine, others, starts, place.xh, scale)
        weight = total[:, 128:]
        o = total[:, :128] / weight
        att[piece(t, F_TILE), :] = o
        for b in range(F_TILE // 128):
            low[t * (F_TILE // 128) + b] = o[b * 128 : (b + 1) * 128].astype(bf16)
        line = jnp.transpose(peak * (scale * LOG2E) + jnp.log2(weight))
        for n in range(F_TILE // Q_TILE):
            lse[pl.ds(t * (F_TILE // Q_TILE) + n, 1), :] = line[0:1, n * Q_TILE : n * Q_TILE + Q_TILE]
        return 0

    tiles = mine.shape[1] // F_TILE
    lax.fori_loop(0, tiles // 2, tile, 0)
    tick(*up_gathers, *out_gathers)
    lax.fori_loop(tiles // 2, tiles * 3 // 4, tile, 0)
    tick(cot_gather, *out_gathers)
    kept += keep_cot(11, (0, 1, 3))
    lax.fori_loop(tiles * 3 // 4, tiles, tile, 0)
    back = heads_out(place, sends, low, merged, local.at[9])
    tick(back)
    for copy in posts:
        copy.wait_send()
    for copy in kept:
        copy.wait()
    act_gather.finish()
    run_all([back, *up_gathers, cot_gather, *out_gathers])
    for copy in keep_cot(10, (2,)):
        copy.wait()
    assert sends.used <= send.shape[0], sends.used


def front(starts, chosen, tok, gain, shift, bias, cot, wp, wo, up, umaps, dmaps, lum, scale):
    any_ = pl.BlockSpec(memory_space=pl.ANY)
    vmem = pl.BlockSpec(memory_space=pltpu.VMEM)
    smem = pl.BlockSpec(memory_space=pltpu.SMEM)
    shape = lambda *s: jax.ShapeDtypeStruct(s, bf16)
    vm = lambda *s: pltpu.VMEM(s, bf16)
    return pl.pallas_call(
        functools.partial(front_kernel, scale=scale),
        name="front",
        out_shape=[
            shape(4, 2, 128, 2432),
            shape(3, 256, 2048),
            shape(2, 2, 4, 4, 2, 16, 2048),
            shape(2, 2, 4, 4, 2, 16, 1024),
            shape(4, 2, 128, 2176),
            shape(3, 2048, 128),
            shape(2, 2048, 128),
            shape(128, 2048),
            jax.ShapeDtypeStruct((2048, 128), f32),
            jax.ShapeDtypeStruct((8, 256), f32),
            jax.ShapeDtypeStruct((128, 128), f32),
        ],
        in_specs=[smem] * 2 + [vmem] * 8 + [any_] * 3,
        out_specs=[any_] * 8 + [vmem] * 3,
        scratch_shapes=[
            vm(3, 128, 256),
            vm(3, 2048, 128),
            vm(128, 2048),
            vm(4, 2, 128, 2432),
            vm(4, 2, 128, 2176),
            vm(3, 2, 2, 4, 4, 2, 16, 256),
            vm(16, 8192),
            vm(3, 4, 2, 2, 128, 128),
            vm(3, 2048, 128),
            vm(2, 2048, 128),
            vm(16, 128, 128),
            vm(3, 256, 2048),
        ]
        + [pltpu.SemaphoreType.DMA(n) for n in ((150,), (150,), (2, 16), (2, 16), (16,))],
        compiler_params=pltpu.CompilerParams(
            collective_id=0, has_side_effects=True, vmem_limit_bytes=56 * MIB
        ),
    )(starts, chosen, tok, gain, shift, bias, cot, wp, wo, up, umaps, dmaps, lum)


def middle_kernel(
    starts, grad, queries_in, others_in, att_in, lse, umaps_in, mask, a_own, b_own, two,
    by_member, low_rank, a_final, b_final, two_final,
    queries, others, att, umaps, do, delta, dq_acc, dq, own_low, other_low, by_head, from_other, *refs, scale,
):
    scratch, (send, recv, a_send, a_recv, s_send, s_recv, local) = list(refs[:-7]), refs[-7:]
    place = Place()
    across = [{"xh": 1 - place.xh, "z": z, "y": y} for z, y in plane(place)]
    greet(plane_devices(place) + members(place) + across)
    sends = Sends(send, recv)
    here = place.z * 4 + place.y
    parity = place.xh
    kv = pl.ds(1, 2)

    keep = pltpu.make_async_copy(grad.at[:, head_columns(place.z, place.y)], do.at[piece(here, 128)], local.at[0])
    keep.start()
    loads = [
        pltpu.make_async_copy(src, dst, local.at[1 + n])
        for n, (src, dst) in enumerate(
            ((att_in, att), (queries_in, queries), (others_in, others), (umaps_in, umaps))
        )
    ]
    for copy in loads:
        copy.start()
    grads_sent = [
        sends.push(grad.at[:, head_columns(z, y)], do.at[piece(here, 128)], {"z": z, "y": y})
        for z, y in plane(place)
    ]

    def take(n):
        got = scratch[:n]
        del scratch[:n]
        return got

    early = [
        a_sum(place, sends, a_own, a_final, take(5)),
        b_sum(place, sends, b_own, b_final, take(5)),
    ]
    early += [
        reduce_piece(
            place, sends, two_final.at[n], None,
            (lambda z, y, n=n: two.at[n, z, y], scratch[n], two_final.at[n]), None,
        )
        for n in range(2)
    ]

    def tick(*parts):
        for part in parts:
            try:
                next(part)
            except StopIteration:
                pass

    tick(*early)
    dq_acc[...] = jnp.zeros_like(dq_acc)
    keep.wait()
    for copy in grads_sent:
        copy.wait_recv()
    for copy in loads:
        copy.wait()
    ones = jnp.ones((8, 128), bf16)
    tiles, key_tiles = do.shape[0] // Q_TILE, do.shape[0] // K_TILE

    def row_dots(t, _):
        rows = piece(t, Q_TILE)
        value = do[rows, :].astype(f32) * att[rows, :]
        high = value.astype(bf16)
        low = (value - high.astype(f32)).astype(bf16)
        delta[t] = dot_nt(ones, high) + dot_nt(ones, low)
        return 0

    lax.fori_loop(0, tiles, row_dots, 0)
    tick(*early[:2])

    def keys(kt):
        rows = piece(kt, K_TILE)
        sides = ((others[0, rows, :], others[1, rows, :], 1 - parity), (queries[1, rows, :], queries[2, rows, :], parity))
        local = kt * K_TILE + lax.broadcasted_iota(jnp.int32, (K_TILE, 1), 0)

        def step(qt, carry):
            rows = piece(qt, Q_TILE)
            q = queries[0, rows, :]
            d = do[rows, :]
            q_pos = positions_of(qt * Q_TILE + lax.broadcasted_iota(jnp.int32, (1, Q_TILE), 1), parity)
            lo = document_start(starts, q_pos)
            found, dq_part = [], None
            for (k, v, k_parity), (dk, dv) in zip(sides, carry):
                k_pos = positions_of(local, k_parity)
                s = dot_nt(k, q)
                allowed = (k_pos >= lo) & (k_pos <= q_pos)
                p = jnp.exp2(jnp.where(allowed, s * (scale * LOG2E) - lse[pl.ds(qt, 1), :], -1e30))
                dv = dv + dot(p.astype(bf16), d)
                ds = (p * (dot_nt(v, d) - delta[qt, 0:1, :]) * scale).astype(bf16)
                dk = dk + dot(ds, q)
                part = dot_tn(ds, k)
                dq_part = part if dq_part is None else dq_part + part
                found.append((dk, dv))
            dq_acc[rows, :] += dq_part
            return tuple(found)

        zero = jnp.zeros((K_TILE, 128), f32)
        return lax.fori_loop(kt * (K_TILE // Q_TILE), tiles, step, ((zero, zero),) * 2)

    blocks = K_TILE // 128
    gone = []

    def to_token(k, n, src, dst, other, away):
        z, y = n // 4, lax.rem(n, 4)
        myself = None if other or away else (place.z == z) & (place.y == y)
        device = {"z": z, "y": y} | ({"xh": 1 - place.xh} if other else {})
        gone.append(Post(src, dst, device, myself, a_send.at[k, n], a_recv.at[k, here]))

    shared = []

    def share(turn, k, part):
        x = lax.rem(place.z + (4 - turn), 4)
        for c in range(2):
            g = x * 2 + c
            pair = piece(g, 2)
            if k:
                both = by_head[1:3, pair].astype(f32) + from_other[:, pair].astype(f32)
                by_head[1:3, pair] = both.astype(bf16)
            device = {"xl": lax.rem(x, 2), "xh": x // 2, "c": c}
            myself = (place.x == x) & (place.c == c)
            src, dst = by_head.at[part, pair], by_member.at[part, place.x, place.c]
            n = turn * 2 + c
            shared.append(Post(src, dst, device, myself, s_send.at[k, n], s_recv.at[k, place.g]))

    def heads_of(turn):
        x = lax.rem(place.z + (4 - turn), 4)
        return [x * 4 + y for y in range(4)]

    def share_keys(turn):
        for head in heads_of(turn):
            for k, dst in ((2, from_other.at[:, 0]), (1, by_head.at[kv, 0])):
                pltpu.make_async_copy(dst, dst, a_recv.at[k, head]).wait()
        share(turn, 1, kv)

    def share_queries(turn):
        for head in heads_of(turn):
            dst = by_head.at[0, 0]
            pltpu.make_async_copy(dst, dst, a_recv.at[0, head]).wait()
        share(turn, 0, 0)

    for turn in (2, 1, 3, 0):
        kt = lax.rem(place.z + turn, key_tiles)
        for k, low, (dk, dv) in zip((2, 1), (other_low, own_low), keys(kt)):
            for b in range(blocks):
                n = kt * blocks + b
                low[n, 0] = dk[b * 128 : (b + 1) * 128].astype(bf16)
                low[n, 1] = dv[b * 128 : (b + 1) * 128].astype(bf16)
                dst = from_other.at[:, here] if k == 2 else by_head.at[kv, here]
                to_token(k, n, low.at[n], dst, k == 2, turn != 0)
    for n in range(16):
        dq[n] = dq_acc[n * 128 : (n + 1) * 128].astype(bf16)
    for turn in (2, 1, 3, 0):
        for b in range(blocks):
            n = lax.rem(place.z + turn, 4) * 4 + b
            to_token(0, n, dq.at[n], by_head.at[0, here], False, turn != 0)
    tick(*early)
    for turn in (2, 1, 3, 0):
        share_keys(turn)
    tick(*early)
    for turn in (2, 1, 3, 0):
        share_queries(turn)
    for p in range(3):
        whole = jnp.concatenate([by_head[p, n] for n in range(16)], axis=1)
        low_rank[:, p * 128 : p * 128 + 128] = (dot_nt(whole, umaps[p]) * mask[...]).astype(bf16)
    for n in range(8):
        for k, dst in ((0, by_member.at[0, 0, 0]), (1, by_member.at[kv, 0, 0])):
            pltpu.make_async_copy(dst, dst, s_recv.at[k, n]).wait()
    run_all(early)
    for copy in gone + grads_sent + shared:
        copy.wait_send()
    assert sends.used <= send.shape[0], sends.used


def middle(starts, grad, queries, others, att, lse, umaps, mask, a_own, b_own, two, scale):
    any_ = pl.BlockSpec(memory_space=pl.ANY)
    vmem = pl.BlockSpec(memory_space=pltpu.VMEM)
    smem = pl.BlockSpec(memory_space=pltpu.SMEM)
    vm = lambda *s: pltpu.VMEM(s, bf16)
    shape = lambda *s: jax.ShapeDtypeStruct(s, bf16)
    return pl.pallas_call(
        functools.partial(middle_kernel, scale=scale),
        name="attention_backward",
        out_shape=[
            shape(3, 4, 2, 2, 128, 128),
            shape(128, 384),
            shape(16, 128),
            shape(16, 128),
            shape(2, 64, 128),
        ],
        in_specs=[smem, vmem, any_, any_, any_, vmem, any_, vmem] + [vmem] * 3,
        out_specs=[any_] + [vmem] * 4,
        scratch_shapes=[
            vm(3, 2048, 128),
            vm(2, 2048, 128),
            pltpu.VMEM((2048, 128), f32),
            vm(4, 128, 2048),
            vm(2048, 128),
            pltpu.VMEM((8, 8, 256), f32),
            pltpu.VMEM((2048, 128), f32),
            vm(16, 128, 128),
            vm(16, 2, 128, 128),
            vm(16, 2, 128, 128),
            vm(3, 16, 128, 128),
            vm(2, 16, 128, 128),
        ]
        + a_sum_scratch()
        + b_sum_scratch()
        + [vm(15, 64, 128)] * 2
        + [pltpu.SemaphoreType.DMA(k) for k in ((100,), (100,), (3, 16), (3, 16), (2, 8), (2, 8), (8,))],
        compiler_params=pltpu.CompilerParams(collective_id=2, has_side_effects=True, vmem_limit_bytes=58 * MIB),
    )(starts, grad, queries, others, att, lse, umaps, mask, a_own, b_own, two.reshape(2, 4, 4, 64, 128))


def feed_forward_kernel(
    merged, tok, gains, shifts, biases, up_down, low_up, mask, bias_all, dn, cot_own,
    w_out_in, cot_all, up, out_down_in, out_up_in, umap_in, dmap_in,
    grad_merged, grad_res, base, forth, small_out, a_out, b_out, two, mine_in, mine_cot,
    out_down, out_up, umap_all, umap, dmap, bias, w_out, residual, low_out, sa, cot, up_v, dn_v, slope, act, pre, parts, total, *refs,
):
    scratch, (send, recv, local) = refs[:-3], refs[-3:]
    place = Place()
    greet(members(place) + plane_devices(place))
    sends = Sends(send, recv)
    loads = [
        pltpu.make_async_copy(src, dst, local.at[n]) for n, (src, dst) in enumerate(
            (
                (out_down_in.at[3], out_down), (w_out_in, w_out), (out_up_in.at[3], out_up),
                (umap_in.at[:, piece(place.xl * 2 + place.c, 2048)], umap_all),
                (dmap_in.at[place.xl * 2 + place.c, :, place.xh], dmap), (up, up_v), (cot_all, cot),
            )
        )
    ]
    for copy in loads:
        copy.start()

    def dn_view(h):
        def view(fixed, half):
            cols = pl.ds(h * 1024, 1024) if half is None else pl.ds(h * 1024 + half * 512, 512)
            return dn_v.at[fixed.get("z", ALL), fixed.get("y", ALL), :, cols]

        return view

    here = {"z": place.z, "y": place.y}
    dn_v[place.z, place.y] = dn[...]
    dn_gathers = [
        ring_gather(place, sends, dn_view(h), order, dn_view(h)(here, None), Nothing(), False)
        for h, order in enumerate((("y", "z"), ("z", "y")))
    ]

    def tick(*parts):
        for part in parts:
            next(part)

    tick(*dn_gathers)
    gain, shift = gains[1:2, :], shifts[1:2, :]
    bias_out, bias_end = biases[2:3, :], biases[3:4, :]
    loads[0].wait()
    low_out[...] = (dot(merged[...], out_down[...]) * mask[...]).astype(bf16)
    loads[1].wait()
    loads[2].wait()

    def out_tile(n, _):
        cols = piece(n, 256)
        value = tok[:, cols].astype(f32) + dot(merged[...], w_out[:, cols]) + biases[2:3, cols]
        residual[:, cols] = value + dot(low_out[...], out_up[:, cols])
        return 0

    lax.fori_loop(0, 6, out_tile, 0)
    tick(*dn_gathers)
    lax.fori_loop(6, 8, out_tile, 0)
    second = layer_norm(residual[...], gain, shift).astype(bf16)
    own = sa.at[place.x, place.c]
    own[:, 0:2048] = second
    own[:, 2048:2176] = (dot(second, up_down[...]) * mask[...]).astype(bf16)
    gather = GroupGather(place, sends, sa)

    loads[3].wait()
    loads[4].wait()
    whole_bias = bias_all[:, piece(place.xl * 2 + place.c, 2048)]
    for n in range(8):
        for whole, out in ((umap_all[:, n * 256 : n * 256 + 256], umap), (whole_bias[:, n * 256 : n * 256 + 256], bias)):
            sides = [jnp.concatenate([whole[:, h : h + 64], whole[:, 128 + h : 192 + h]], axis=1) for h in (0, 64)]
            out[:, n * 128 : n * 128 + 128] = jnp.where(place.xh == 0, sides[0], sides[1])

    def rows(ref, x, start, size):
        return ref[x, :, :, pl.ds(start, size)].reshape(256, size)

    xs = places_in_turn(place)

    def hidden(k):
        x = xs[k]

        def tile(n, _):
            cols = piece(n, 256)
            value = dot(rows(sa, x, 0, 2048), up_v[:, cols]) + bias[:, cols]
            value = value + dot(rows(sa, x, 2048, 128), umap[:, cols])
            phi = 0.5 * (1.0 + lax.erf(value * 0.7071067811865476))
            act[k, :, cols] = (value * phi).astype(bf16)
            slope[k, :, cols] = phi + value * (0.3989422804014327 * jnp.exp2(value * value * (-0.5 * LOG2E)))
            return 0

        lax.fori_loop(0, 4, tile, 0)

    def grad_hidden(k):
        x = xs[k]

        def tile(n, _):
            cols = piece(n, 256)
            value = dot_nt(rows(cot, x, 0, 2048), dn_v[n].reshape(256, 2048))
            value = value + dot_nt(rows(cot, x, 2048, 128), dmap[piece(n, 4)].reshape(256, 128))
            pre[k, :, cols] = (value * slope[k, :, cols]).astype(bf16)
            return 0

        lax.fori_loop(0, 4, tile, 0)

    def backward(k, n):
        ks = pl.ds(k, n)

        def tile(t, _):
            cols = piece(t, 256)
            value = dot_nt(pre[ks].reshape(n * 256, 1024), up_v[cols, :]).astype(bf16)
            parts[ks, :, :, cols] = value.reshape(n, 2, 128, 256)
            return 0

        lax.fori_loop(0, 8, tile, 0)
        value = dot_nt(pre[ks].reshape(n * 256, 1024), umap[...]).astype(bf16)
        parts[ks, :, :, 2048:2176] = value.reshape(n, 2, 128, 128)
        value = dot(act[ks].reshape(n * 256, 1024), dmap[...].reshape(1024, 128)).astype(bf16)
        parts[ks, :, :, 2176:2304] = value.reshape(n, 2, 128, 128)

    loads[5].wait()
    gather.own()
    hidden(3)
    tick(*dn_gathers)
    gather.near()
    hidden(2)
    hidden(1)
    run_all(dn_gathers)
    loads[6].wait()
    grad_hidden(3)
    gather.far()
    grad_hidden(2)
    gather.far_done()
    hidden(0)
    grad_hidden(0)

    sums = GroupSum(place, sends, parts, scratch)
    backward(0, 1)
    sums.cross(0)
    grad_hidden(1)
    sums.merge(0)
    sums.first()
    backward(1, 1)
    sums.cross(1)
    backward(2, 2)
    sums.cross(2)
    sums.cross(3)
    sums.merge(1)
    sums.merge(2)
    sums.second()

    def small(k, _):
        x = lax.rem(place.x + jnp.where(k == 3, 0, jnp.where(k == 2, 3, 2 - k)), 4)
        one = dot_tn(act[k], rows(cot, x, 2048, 128))
        other = dot_tn(pre[k], rows(sa, x, 2048, 128))

        @pl.when(k == 0)
        def _():
            total[0] = one
            total[1] = other

        @pl.when(k > 0)
        def _():
            total[0] += one
            total[1] += other

        return 0

    lax.fori_loop(0, 4, small, 0)
    cols = piece(place.g, 256)
    mine_in[...] = sa[:, :, :, cols].reshape(1024, 256)
    mine_cot[...] = cot[:, :, :, cols].reshape(1024, 256)
    def forward(n, _):
        ks, cols = piece(n // 4, 2), piece(lax.rem(n, 4), 512)
        value = dot(act[ks].reshape(512, 1024), dn_v[:, :, :, cols].reshape(1024, 512)).astype(bf16)
        cot[ks, :, :, cols] = value.reshape(2, 2, 128, 512)
        return 0

    lax.fori_loop(0, 8, forward, 0)

    two[...] = total[...].astype(bf16)
    handed = pltpu.make_async_copy(cot.at[:, :, :, pl.ds(0, 2048)], forth, local.at[7])
    handed.start()
    summed = sums.result()
    low_up_grad = (summed[:, 2048:2176] * mask[...]).astype(bf16)
    low_down = (summed[:, 2176:2304] * mask[...]).astype(bf16)
    small_out[:, 0:128] = low_up_grad
    small_out[:, 128:256] = low_down
    grad_second = summed[:, 0:2048] + dot_nt(low_up_grad, up_down[...])
    value = cot_own[...].astype(f32) + layer_norm_back(residual[...], gain, grad_second)
    grad_res[...] = value
    branch = value.astype(bf16)
    low_grad = (dot_nt(branch, out_up[...]) * mask[...]).astype(bf16)

    def merged_tile(n, _):
        cols = piece(n, 256)
        value = dot_nt(branch, w_out[cols, :]) + dot_nt(low_grad, out_down[cols, :])
        grad_merged[:, cols] = value.astype(bf16)
        return 0

    lax.fori_loop(0, 8, merged_tile, 0)
    b_out[...] = dot_tn(low_out[...], branch).astype(bf16)
    a_out[...] = dot_tn(merged[...], low_grad).astype(bf16)
    base[...] = residual[...] + bias_end + dot(low_down, low_up[...])
    handed.wait()
    gather.finish()
    assert sends.used <= send.shape[0], sends.used


def feed_forward(*args):
    any_ = pl.BlockSpec(memory_space=pl.ANY)
    vmem = pl.BlockSpec(memory_space=pltpu.VMEM)
    vm = lambda *s: pltpu.VMEM(s, bf16)
    shape = lambda *s: jax.ShapeDtypeStruct(s, bf16)
    return pl.pallas_call(
        feed_forward_kernel,
        name="feed_forward",
        out_shape=[
            shape(128, 2048),
            jax.ShapeDtypeStruct((128, 2048), f32),
            jax.ShapeDtypeStruct((128, 2048), f32),
            shape(4, 2, 128, 2048),
            shape(128, 256),
            shape(2048, 128),
            shape(128, 2048),
            shape(2, 1024, 128),
            shape(1024, 256),
            shape(1024, 256),
        ],
        in_specs=[vmem] * 11 + [any_] * 7,
        out_specs=[vmem] * 3 + [any_] + [vmem] * 6,
        scratch_shapes=[
            vm(2048, 128),
            vm(128, 2048),
            vm(128, 2048),
            vm(128, 1024),
            vm(16, 64, 128),
            pltpu.VMEM((1, 1024), f32),
            vm(2048, 2048),
            pltpu.VMEM((128, 2048), f32),
            vm(128, 128),
            vm(4, 2, 128, 2176),
            vm(4, 2, 128, 2176),
            vm(2048, 1024),
            vm(4, 4, 64, 2048),
            pltpu.VMEM((4, 256, 1024), f32),
            vm(4, 256, 1024),
            vm(4, 256, 1024),
            vm(4, 2, 128, 2304),
            pltpu.VMEM((2, 1024, 128), f32),
        ]
        + GroupSum.scratch(2304)
        + [pltpu.SemaphoreType.DMA((k,)) for k in (40, 40, 8)],
        compiler_params=pltpu.CompilerParams(collective_id=1, has_side_effects=True, vmem_limit_bytes=63 * MIB),
    )(*args)


def both_heads(gq, p, x):
    heads = [gq[p, x, :, j].reshape(256, 128) for j in range(2)]
    return jnp.concatenate(heads, axis=1)


def tail_kernel(
    grads, qkv_w, act_all, dmaps_in, grad_res_in, forth_in, base_in, low_rank, small, tok, gain, mine_in, mine_cot, a_piece, b_piece, two_piece,
    input_grad, mixed, a_res, b_res, two_a, two_b, a_early, b_early,
    dmaps, grad_res, forth_parts, base, gq, wq, act, left, parts, lows, a_sums, b_sums, a_s, a_f, b_s, b_f, *refs,
):
    scratch, (send, recv, local) = refs[:-3], refs[-3:]
    scratch, forth_scratch = scratch[:6], scratch[6:]
    place = Place()
    greet(members(place) + plane_devices(place))
    sends = Sends(send, recv)
    loads = [
        pltpu.make_async_copy(src, dst, local.at[n])
        for n, (src, dst) in enumerate(((grads, gq), (qkv_w, wq), (act_all, act)))
    ]
    loads.append(pltpu.make_async_copy(dmaps_in.at[pl.ds(0, 3)], dmaps, local.at[44]))
    loads.append(pltpu.make_async_copy(grad_res_in, grad_res, local.at[45]))
    loads.append(pltpu.make_async_copy(forth_in, forth_parts, local.at[43]))
    loads.append(pltpu.make_async_copy(base_in, base, local.at[42]))
    for copy in loads:
        copy.start()
    own = lows.at[place.x, place.c]
    own[:, 0:384] = low_rank[...]
    own[:, 384:640] = small[...]
    spread = [sends.push(own, own, place.member(dx, 0)) for dx in (2, 1, 3)]
    passed = [sends.push(own, own, place.member(0, 1))]

    def two_view(res):
        def view(at):
            xl, xh = two_parts(at)
            return res.at[xl, place.c, at["z"], at["y"], xh]

        return view

    def b_early_view(at):
        z, y = at["z"], at["y"]
        if isinstance(y, pl.Slice):
            cols = pl.ds(y.start * 128 if z is ALL else pl.multiple_of(z * 512 + y.start * 128, 128), 256)
        elif z is ALL:
            cols = ALL
        else:
            cols = piece(z, 512) if y is ALL else piece(z * 4 + y, 128)
        return b_early.at[place.c, at["x"], :, cols]

    early = [
        give_all(place, sends, ("x", "z", "y"), two_piece.at[0], two_view(two_a), local.at[3]),
        give_all(place, sends, ("x", "y", "z"), two_piece.at[1], two_view(two_b), local.at[4]),
        give_all(
            place, sends, ("x", "y", "z"), a_piece,
            lambda at: a_early.at[place.c, at["z"], at["y"], at["x"]], local.at[5],
        ),
        give_all(place, sends, ("x", "y", "z"), b_piece, b_early_view, local.at[6]),
    ]

    def tick(*parts):
        for part in parts:
            next(part)

    tick(*early)
    def a_view(at):
        return a_res.at[:, at["x"], place.c, at["z"], at["y"]]

    def a_held(z, y):
        return a_sums.at[:, piece(z * 4 + y, 16)]

    def b_view(at):
        y = at["y"]
        if y is ALL:
            yr, yc = ALL, ALL
        elif isinstance(y, pl.Slice):
            yr, yc = pl.ds(y.start // 2, 1), ALL
        else:
            yr, yc = y // 2, lax.rem(y, 2)
        return b_res.at[:, at["x"], place.c, at["z"], yr, yc]

    def b_held(z, y):
        return b_sums.at[:, pl.ds(pl.multiple_of(z * 32 + y // 2 * 16, 16), 16), piece(lax.rem(y, 2), 128)]

    def late_part(final, held, slots, order, view, sem):
        yield from reduce_piece(place, sends, final, None, (held, slots, final), None)
        yield from give_all(place, sends, order, final, view, sem, True)

    late = [
        late_part(a_f, a_held, a_s, ("y", "x", "z"), a_view, local.at[7]),
        late_part(b_f, b_held, b_s, ("z", "x", "y"), b_view, local.at[8]),
    ]
    loads[0].wait()
    loads[1].wait()
    xs = places_in_turn(place)
    for k in range(4):
        left[k] = jnp.concatenate([both_heads(gq, p, xs[k]) for p in range(3)], axis=1)

    def partial(k, n):
        ks = pl.ds(k, n)

        def tile(t, _):
            cols = piece(t, 512)
            value = dot(left[ks].reshape(n * 256, 768), wq[:, :, cols].reshape(768, 512)).astype(bf16)
            parts[ks, :, :, cols] = value.reshape(n, 2, 128, 512)
            return 0

        lax.fori_loop(0, 4, tile, 0)

    sums = GroupSum(place, sends, parts, scratch)
    partial(0, 1)
    sums.cross(0)
    partial(1, 1)
    sums.cross(1)
    sums.merge(0)
    sums.first()
    loads[5].wait()
    forth = GroupSum(place, sends, forth_parts, forth_scratch)
    for k in range(4):
        forth.cross(k)
    loads[2].wait()
    for p in range(3):
        total = jnp.zeros((128, 256), f32)
        for x in range(4):
            left_rows = act[x, :, :, 2048 + p * 128 : 2176 + p * 128].reshape(256, 128)
            total = total + dot_tn(left_rows, both_heads(gq, p, x))
        b_sums[p] = total.astype(bf16)
    for dx, copy in zip((2, 1, 3), spread):
        copy.wait()
        came = lows.at[place.step("x", -dx), place.c]
        passed.append(sends.push(came, came, place.member(0, 1)))
    for copy in passed:
        copy.wait()
    b_sums[3] = dot_tn(lows[:, :, :, 512:640].reshape(1024, 128), mine_cot[...]).astype(bf16)
    rows = act[:, :, :, piece(place.g, 256)].reshape(1024, 256)
    for p in range(4):
        right = lows[:, :, :, p * 128 : p * 128 + 128].reshape(1024, 128)
        a_sums[p] = dot_tn(rows if p < 3 else mine_in[...], right).astype(bf16)

    tick(*late)
    partial(2, 2)
    sums.cross(2)
    sums.cross(3)
    forth.merge(0)
    forth.first()
    tick(*early)
    sums.merge(1)
    sums.merge(2)
    sums.second()
    tick(*late)
    tick(*early)
    tick(*late)
    forth.merge(1)
    forth.merge(2)
    forth.second()
    tick(*early)
    loads[3].wait()
    loads[4].wait()
    grad_first = sums.result()
    for p in range(3):
        grad_first = grad_first + dot_nt(low_rank[:, p * 128 : p * 128 + 128], dmaps[p])
    result = grad_res[...] + layer_norm_back(tok[...].astype(f32), gain[0:1, :], grad_first)
    input_grad[...] = result.astype(bf16)
    tick(*late)
    tick(*early)
    run_all(late + early)
    loads[6].wait()
    mixed[...] = (base[...] + forth.result()).astype(bf16)
    assert sends.used <= send.shape[0], sends.used


def tail(grads, qkv_w, act_all, dmaps, grad_res, forth, base, low_rank, small, tok, gain, mine_in, mine_cot, a_piece, b_piece, two_piece):
    any_ = pl.BlockSpec(memory_space=pl.ANY)
    vmem = pl.BlockSpec(memory_space=pltpu.VMEM)
    vm = lambda *s: pltpu.VMEM(s, bf16)
    shape = lambda *s: jax.ShapeDtypeStruct(s, bf16)
    a_shape, b_shape = (4, 4, 2, 4, 4, 16, 128), (4, 4, 2, 4, 2, 2, 16, 128)
    return pl.pallas_call(
        tail_kernel,
        name="tail",
        out_shape=[
            shape(128, 2048),
            shape(128, 2048),
            shape(*a_shape),
            shape(*b_shape),
            shape(2, 2, 4, 4, 2, 64, 128),
            shape(2, 2, 4, 4, 2, 64, 128),
            shape(2, 4, 4, 4, 16, 128),
            shape(2, 4, 16, 2048),
        ],
        in_specs=[any_] * 7 + [vmem] * 9,
        out_specs=[vmem] * 2 + [any_] * 6,
        scratch_shapes=[
            vm(3, 2048, 128),
            pltpu.VMEM((128, 2048), f32),
            vm(4, 2, 128, 2048),
            pltpu.VMEM((128, 2048), f32),
            vm(3, 4, 2, 2, 128, 128),
            vm(3, 256, 2048),
            vm(4, 2, 128, 2432),
            vm(4, 256, 768),
            vm(4, 2, 128, 2048),
            vm(4, 2, 128, 640),
            vm(4, 256, 128),
            vm(4, 128, 256),
            vm(15, 4, 16, 128),
            vm(4, 16, 128),
            vm(15, 4, 16, 128),
            vm(4, 16, 128),
        ]
        + GroupSum.scratch(2048) * 2
        + [pltpu.SemaphoreType.DMA((k,)) for k in (200, 200, 46)],
        compiler_params=pltpu.CompilerParams(collective_id=3, has_side_effects=True, vmem_limit_bytes=60 * MIB),
    )(
        grads, qkv_w, act_all, dmaps, grad_res, forth, base, low_rank, small, tok, gain, mine_in, mine_cot, a_piece, b_piece, two_piece
    )
def widen_kernel(a, a_one, b, b_one, hid_a, hid_b, a_out, b_out, up_out, hid_b_out, hid_a_out, down_out):
    for n in range(3):
        a_out[n] = a[n].reshape(256, 128).astype(f32)
        for yc in range(2):
            cols = pl.ds(yc * 128, 128)
            b_out[n, :, cols] = b[n, 0, 0, :, :, yc].reshape(128, 128).astype(f32)
    for yc in range(2):
        cols = pl.ds(yc * 128, 128)
        down_out[:, cols] = b[3, 0, 0, :, :, yc].reshape(128, 128).astype(f32)
    a_out[3] = a_one[...].astype(f32)
    up_out[...] = a[3].reshape(256, 128).astype(f32)
    b_out[3] = b_one[...].astype(f32)
    hid_a_out[...] = hid_a[...].astype(f32)
    hid_b_out[...] = jnp.transpose(hid_b[...].astype(f32))


def widen(a, b, hid_a, hid_b, a_one, b_one):
    out = lambda *s: jax.ShapeDtypeStruct(s, f32)
    spec = pl.BlockSpec
    return pl.pallas_call(
        widen_kernel,
        name="widen",
        grid=(8,),
        out_shape=[
            out(4, 2048, 128), out(4, 128, 2048), out(2048, 128), out(128, 8192), out(8192, 128), out(128, 2048)
        ],
        in_specs=[
            spec((4, 256, 128), lambda g: (0, g, 0)),
            spec((256, 128), lambda g: (g, 0)),
            spec((4, 1, 1, 4, 2, 2, 16, 128), lambda g: (0, g // 2, g % 2, 0, 0, 0, 0, 0)),
            spec((128, 256), lambda g: (0, g)),
            spec((1024, 128), lambda g: (g, 0)),
            spec((1024, 128), lambda g: (g, 0)),
        ],
        out_specs=[
            spec((4, 256, 128), lambda g: (0, g, 0)),
            spec((4, 128, 256), lambda g: (0, 0, g)),
            spec((256, 128), lambda g: (g, 0)),
            spec((128, 1024), lambda g: (0, g)),
            spec((1024, 128), lambda g: (g, 0)),
            spec((128, 256), lambda g: (0, g)),
        ],
        compiler_params=pltpu.CompilerParams(vmem_limit_bytes=62 * MIB),
    )(
        a.reshape(4, 2048, 128), a_one.reshape(2048, 128), b, b_one.reshape(128, 2048), hid_a.reshape(8192, 128),
        hid_b.reshape(8192, 128),
    )


def per_device(
    tokens,
    document_starts,
    document_adapter,
    layernorm_gain,
    layernorm_bias,
    projection_weight,
    output_weight,
    up_weight,
    down_weight,
    projection_bias,
    upper_bias,
    attention_down_maps,
    attention_up_maps,
    upper_down_maps,
    upper_up_maps,
    lower_down_maps,
    lower_up_maps,
    cotangent,
):
    local_rows, width = tokens.shape[1:]
    head_size = width // HEADS
    seq = local_rows * 32
    scale = head_size ** (-0.5)
    xl, c, z, y, xh = (lax.axis_index(a) for a in AXES)
    group = (xh * 2 + xl) * 2 + c
    cot = cotangent[0]
    (
        act_all, qkv_w, out_all, up_all, cot_all, by_head, across, merged, attended, lse, mask
    ) = front(
        document_starts, document_adapter, tokens[0], layernorm_gain, layernorm_bias, projection_bias, cot,
        jnp.transpose(projection_weight, (1, 0, 2)), output_weight, up_weight, attention_up_maps, attention_down_maps,
        lower_up_maps, scale,
    )
    grad_merged, grad_residual, base, forth, small, a_out, b_out, two, mine_in, mine_cot = feed_forward(
        merged, tokens[0], layernorm_gain, layernorm_bias, projection_bias, upper_down_maps, lower_up_maps, mask,
        upper_bias[None], down_weight, cot, out_all.reshape(width, width), cot_all, up_all.reshape(width, 1024),
        attention_down_maps, attention_up_maps, upper_up_maps, lower_down_maps.reshape(4, 16, 2, 64, 128),
    )
    grad_qkv, grad_adapt_qkv, a_piece, b_piece, two_piece = middle(
        document_starts, grad_merged, by_head, across, attended, lse, attention_up_maps, mask, a_out, b_out, two, scale
    )
    input_grad, mixed, *sums = tail(
        grad_qkv, qkv_w, act_all, attention_down_maps, grad_residual, forth, base, grad_adapt_qkv, small, tokens[0], layernorm_gain,
        mine_in, mine_cot, a_piece, b_piece, two_piece,
    )
    return (mixed[None], input_grad[None], *widen(*sums))


def solution(mesh):
    fine = jax.sharding.Mesh(mesh.devices.reshape(SIZES), AXES)
    by_token = P(STREAM, TOKEN, None)
    shard = AXES
    in_specs = (
        by_token,
        P(STREAM, None),
        P(STREAM, None),
        P(),
        P(),
        P(shard, None, None),
        P(shard, None),
        P(shard, None),
        P(shard, None),
        P(),
        P(),
        P(),
        P(),
        P(),
        P(),
        P(),
        P(),
        by_token,
    )
    out_specs = (by_token, by_token, P(), P(), P(), P(), P(), P())
    return jax.shard_map(per_device, mesh=fine, in_specs=in_specs, out_specs=out_specs, check_vma=False)
```

```python
import functools

import jax
import jax.numpy as jnp
from jax import lax
from jax.experimental import pallas as pl
from jax.experimental.pallas import tpu as pltpu
from jax.sharding import PartitionSpec as P

HEADS = 16
ADAPTER_RANK = 16
MESH = pl.DeviceIdType.MESH
AXES = ("xl", "c", "z", "y", "xh")
SIZES = (2, 2, 4, 4, 2)
STREAM = ("xl", "c")
TOKEN = ("z", "y", "xh")
bf16 = jnp.bfloat16
f32 = jnp.float32
LOG2E = 1.4426950408889634
MIB = 2**20
Q_TILE = 256
K_TILE = 512
F_TILE = 256
ALL = slice(None)


def layer_norm(values, gain, shift):
    center = values - jnp.mean(values, axis=-1, keepdims=True)
    spread = jnp.mean(center * center, axis=-1, keepdims=True)
    return center * lax.rsqrt(spread + 1e-05) * gain + shift


def layer_norm_back(values, gain, grad):
    center = values - jnp.mean(values, axis=-1, keepdims=True)
    scale = lax.rsqrt(jnp.mean(center * center, axis=-1, keepdims=True) + 1e-05)
    unit = center * scale
    grad = grad * gain
    along = jnp.mean(grad * unit, axis=-1, keepdims=True)
    return scale * (grad - jnp.mean(grad, axis=-1, keepdims=True) - unit * along)


def dot(left, right):
    return jnp.dot(left, right, preferred_element_type=f32)


def dot_nt(left, right):
    return lax.dot_general(left, right, (((1,), (1,)), ((), ())), preferred_element_type=f32)


def dot_tn(left, right):
    return lax.dot_general(left, right, (((0,), (0,)), ((), ())), preferred_element_type=f32)


def piece(n, size):
    return pl.ds(pl.multiple_of(n * size, size), size)


class Place:
    def __init__(self):
        self.xl, self.c, self.z, self.y, self.xh = (lax.axis_index(a) for a in AXES)
        self.x = self.xh * 2 + self.xl
        self.g = self.x * 2 + self.c

    def at(self, axis):
        return {"x": self.x, "y": self.y, "z": self.z}[axis]

    def step(self, axis, step):
        return lax.rem(self.at(axis) + (step + 4), 4)

    def toward(self, axis, step=1):
        if axis == "c":
            return {"c": 1 - self.c}
        to = self.step(axis, step)
        if axis == "x":
            return {"xl": lax.rem(to, 2), "xh": to // 2}
        return {axis: to}

    def member(self, dx, dc):
        to = {}
        if dx:
            to |= self.toward("x", dx)
        if dc:
            to |= {"c": 1 - self.c}
        return to


MEMBERS = [(dx, dc) for dx in (2, 1, 3, 0) for dc in (0, 1) if dx or dc]


class Sends:
    def __init__(self, send, recv):
        self.send, self.recv, self.used, self.open = send, recv, 0, []

    def push(self, src, dst, device):
        k = self.used
        self.used += 1
        copy = pltpu.make_async_remote_copy(
            src_ref=src,
            dst_ref=dst,
            send_sem=self.send.at[k],
            recv_sem=self.recv.at[k],
            device_id=device,
            device_id_type=MESH,
        )
        copy.start()
        self.open.append(copy)
        return copy


def greet(devices, perhaps=()):
    barrier = pltpu.get_barrier_semaphore()
    for device in devices:
        pl.semaphore_signal(barrier, inc=1, device_id=device, device_id_type=MESH)
    amount = len(devices) + len(perhaps)
    for device, myself in perhaps:
        amount = amount - myself.astype(jnp.int32)

        @pl.when(jnp.logical_not(myself))
        def _():
            pl.semaphore_signal(barrier, inc=1, device_id=device, device_id_type=MESH)

    pl.semaphore_wait(barrier, amount)


def run_all(parts):
    parts = list(parts)
    while parts:
        left = []
        for part in parts:
            try:
                next(part)
                left.append(part)
            except StopIteration:
                pass
        parts = left


def ring_gather(place, sends, view, order, chunk, landed, forward, direct=False):
    fixed = {a: place.at(a) for a in order}
    across = place.toward("c")
    later, passed = [], []

    def pass_on(block):
        if forward:
            passed.append(sends.push(view(block, None), view(block, None), across))

    if forward:
        passed.append(sends.push(chunk, view(fixed, None), across))
    for number, axis in enumerate(order):
        own = view(fixed, None)
        src = chunk if number == 0 else own
        if number == 0 or direct:
            sent = [sends.push(src, own, place.toward(axis, s)) for s in (2, 1, 3)]
            yield
            for s, copy in zip((2, 1, 3), sent):
                copy.wait_recv()
                pass_on(fixed | {axis: place.step(axis, -s)})
            if number == 0:
                landed.wait()
            later += sent
            del fixed[axis]
            continue
        up = sends.push(src, own, place.toward(axis, 1))
        down = sends.push(src, own, place.toward(axis, -1))
        yield
        before = fixed | {axis: place.step(axis, -1)}
        after = fixed | {axis: place.step(axis, 1)}
        opposite = fixed | {axis: place.step(axis, 2)}
        up.wait_recv()
        half = view(before, 0)
        up_two = sends.push(half, half, place.toward(axis, 1))
        down.wait_recv()
        half = view(after, 1)
        down_two = sends.push(half, half, place.toward(axis, -1))
        pass_on(before)
        pass_on(after)
        yield
        up_two.wait_recv()
        down_two.wait_recv()
        pass_on(opposite)
        later += [up, down, up_two, down_two]
        del fixed[axis]
    yield
    for copy in later:
        copy.wait_send()
    for copy in passed:
        copy.wait()


class Nothing:
    def wait(self):
        pass


def neighbours(place, axes):
    return [place.toward(a, s) for a in axes for s in ((1, 2, 3) if a in "xyz" else (1,))]


def members(place):
    return [place.member(*m) for m in MEMBERS]


class GroupGather:
    def __init__(self, place, sends, buf):
        self.place, self.sends, self.buf = place, sends, buf
        self.mine = buf.at[place.x, place.c]
        self.right, self.left = place.toward("x", 1), place.toward("x", -1)
        self.up = sends.push(self.mine, self.mine, self.right)
        self.down = sends.push(self.mine, self.mine, self.left)
        self.passed = [self.pass_on(self.mine)]

    def pass_on(self, ref):
        return self.sends.push(ref, ref, self.place.toward("c"))

    def own(self):
        self.passed[0].wait_recv()

    def near(self, wait=True):
        x, c = self.place.step("x", -1), self.place.c
        self.up.wait_recv()
        half = self.buf.at[x, c, pl.ds(0, 64)]
        self.up_two = self.sends.push(half, half, self.right)
        self.passed.append(self.pass_on(self.buf.at[x, c]))
        x = self.place.step("x", 1)
        self.down.wait_recv()
        half = self.buf.at[x, c, pl.ds(64, 64)]
        self.down_two = self.sends.push(half, half, self.left)
        self.passed.append(self.pass_on(self.buf.at[x, c]))
        if wait:
            self.near_done()

    def near_done(self):
        self.passed[1].wait_recv()
        self.passed[2].wait_recv()

    def far(self):
        self.up_two.wait_recv()
        self.down_two.wait_recv()
        self.passed.append(self.pass_on(self.buf.at[self.place.step("x", 2), self.place.c]))

    def far_done(self):
        self.passed[3].wait_recv()

    def finish(self):
        for copy in [self.up, self.down, self.up_two, self.down_two] + self.passed:
            copy.wait_send()


def group_gather(place, sends, buf):
    gather = GroupGather(place, sends, buf)
    yield
    gather.own()
    gather.near()
    yield
    gather.far()
    yield
    gather.far_done()
    gather.finish()


def places_in_turn(place):
    return [place.step("x", s) for s in (2, 1, -1, 0)]


class GroupSum:
    def __init__(self, place, sends, parts, scratch):
        self.place, self.sends, self.parts = place, sends, parts
        self.came, self.own, self.left_one, self.right_one, self.left_two, self.right_two = scratch
        self.right, self.left = place.toward("x", 1), place.toward("x", -1)
        self.crossed = {}

    @staticmethod
    def scratch(n):
        vm = lambda *s: pltpu.VMEM(s, bf16)
        return [vm(4, 128, n), vm(3, 128, n), vm(64, n), vm(64, n), vm(128, n), vm(128, n)]

    def cross(self, k):
        place = self.place
        self.crossed[k] = self.sends.push(
            self.parts.at[k, 1 - place.c], self.came.at[k], place.toward("c")
        )

    def merge(self, k):
        self.crossed[k].wait()
        both = self.parts[k, self.place.c].astype(f32) + self.came[k].astype(f32)
        self.own[k] = both.astype(bf16)

    def first(self):
        self.up = self.sends.push(self.own.at[0, pl.ds(0, 64)], self.left_one, self.right)
        self.down = self.sends.push(self.own.at[0, pl.ds(64, 64)], self.right_one, self.left)

    def second(self):
        self.up.wait()
        both = self.own[1, 0:64].astype(f32) + self.left_one[...].astype(f32)
        self.own[1, 0:64] = both.astype(bf16)
        self.up_two = self.sends.push(self.own.at[1], self.left_two, self.right)
        self.down.wait()
        both = self.own[2, 64:128].astype(f32) + self.right_one[...].astype(f32)
        self.own[2, 64:128] = both.astype(bf16)
        self.down_two = self.sends.push(self.own.at[2], self.right_two, self.left)

    def result(self):
        self.crossed[3].wait()
        total = self.parts[3, self.place.c].astype(f32) + self.came[3].astype(f32)
        self.up_two.wait()
        self.down_two.wait()
        return total + self.left_two[...].astype(f32) + self.right_two[...].astype(f32)


def group_sum(place, sends, parts, scratch, out):
    total = GroupSum(place, sends, parts, scratch)
    for k in range(4):
        total.cross(k)
    yield
    total.merge(0)
    total.first()
    total.merge(1)
    total.merge(2)
    yield
    total.second()
    yield
    out[...] = total.result()


def plane(place):
    steps = [(i, j) for i in (2, 1, 3, 0) for j in (2, 1, 3, 0) if i or j]
    return [(lax.rem(place.z + i, 4), lax.rem(place.y + j, 4)) for i, j in steps]


def from_plane(place):
    steps = [(i, j) for i in (2, 1, 3, 0) for j in (2, 1, 3, 0) if i or j]
    return [(lax.rem(place.z + 4 - i, 4), lax.rem(place.y + 4 - j, 4)) for i, j in steps]


def projectors(place):
    x, c = place.z, place.y // 2
    member = {"xl": lax.rem(x, 2), "xh": x // 2, "c": c}
    mine = (place.x == x) & (place.c == c)
    return [(member | {"z": z, "y": y}, None) for z, y in plane(place)] + [
        (member | {"z": place.z, "y": place.y}, mine)
    ]


def attenders(place):
    found = []
    for dx, dc in MEMBERS + [(0, 0)]:
        for j in range(2):
            z, y = place.x, 2 * place.c + j
            device = place.member(dx, dc) | {"z": z, "y": y}
            mine = None if dx or dc else (place.z == z) & (place.y == y)
            found.append((dx, dc, j, device, mine))
    return found


def head_columns(z, y):
    return pl.ds(pl.multiple_of((z * 4 + y) * 128, 128), 128)


def split_greeting(pairs):
    return [d for d, m in pairs if m is None], [(d, m) for d, m in pairs if m is not None]


def plane_devices(place):
    return [{"z": z, "y": y} for z, y in plane(place)]


class Post:
    def __init__(self, src, dst, device, myself, send_sem, recv_sem):
        self.remote = pltpu.make_async_remote_copy(
            src_ref=src, dst_ref=dst, send_sem=send_sem, recv_sem=recv_sem, device_id=device, device_id_type=MESH
        )
        self.myself = myself
        if myself is None:
            self.remote.start()
        else:
            pl.when(myself)(pltpu.make_async_copy(src, dst, recv_sem).start)
            pl.when(jnp.logical_not(myself))(self.remote.start)

    def wait_send(self):
        if self.myself is None:
            self.remote.wait_send()
        else:
            pl.when(jnp.logical_not(self.myself))(self.remote.wait_send)


def heads_out(place, sends, blocks, merged, local):
    cols = head_columns(place.z, place.y)
    keep = pltpu.make_async_copy(blocks.at[place.z * 4 + place.y], merged.at[:, cols], local)
    keep.start()
    sent = [sends.push(blocks.at[z * 4 + y], merged.at[:, cols], {"z": z, "y": y}) for z, y in plane(place)]
    yield
    for copy in sent:
        copy.wait()
    keep.wait()


def reduce_piece(place, sends, final, across, plane_step, along):
    if across:
        src, came, own, out = across
        copy = sends.push(src, came, place.toward("c"))
        yield
        copy.wait()
        out[...] = (own[...].astype(f32) + came[...].astype(f32)).astype(bf16)
    held, slots, out = plane_step
    sent = [sends.push(held(z, y), slots.at[n], {"z": z, "y": y}) for n, (z, y) in enumerate(plane(place))]
    yield
    for copy in sent:
        copy.wait()
    total = held(place.z, place.y)[...].astype(f32)
    for n in range(15):
        total = total + slots[n].astype(f32)
    out[...] = total.astype(bf16)
    if along:
        held, slots, out = along
        sent = [sends.push(held(place.step("x", d)), slots.at[d - 1], place.toward("x", d)) for d in (2, 1, 3)]
        yield
        for copy in sent:
            copy.wait()
        total = held(place.x)[...].astype(f32)
        for d in range(3):
            total = total + slots[d].astype(f32)
        out[...] = total.astype(bf16)


def give_all(place, sends, order, final, view, local, direct=False):
    here = {a: place.at(a) for a in "xyz"}
    keep = pltpu.make_async_copy(final, view(here), local)
    keep.start()

    def fixed_view(fixed, half):
        at = {a: fixed.get(a, ALL) for a in "xyz"}
        if half is not None:
            at[order[0]] = pl.ds(half * 2, 2)
        return view(at)

    return ring_gather(place, sends, fixed_view, order, final, keep, True, direct)


def a_sum_scratch():
    vm = lambda *shape: pltpu.VMEM(shape, bf16)
    return [vm(1024, 128), vm(1024, 128), vm(15, 64, 128), vm(64, 128), vm(3, 16, 128)]


def b_sum_scratch():
    vm = lambda *shape: pltpu.VMEM(shape, bf16)
    return [vm(64, 2048), vm(64, 2048), vm(15, 64, 128), vm(64, 128), vm(3, 16, 128)]


def a_sum(place, sends, a, final, scratch):
    came, half, s1, quarter, s2 = scratch
    return reduce_piece(
        place, sends, final,
        (a.at[piece(1 - place.c, 1024)], came, a.at[piece(place.c, 1024)], half),
        (lambda z, y: half.at[piece(z * 4 + y, 64)], s1, quarter),
        (lambda x: quarter.at[piece(x, 16)], s2, final),
    )


def b_sum(place, sends, b, final, scratch):
    came, half, s1, quarter, s2 = scratch
    return reduce_piece(
        place, sends, final,
        (b.at[piece(1 - place.c, 64)], came, b.at[piece(place.c, 64)], half),
        (lambda z, y: half.at[:, piece(z * 4 + y, 128)], s1, quarter),
        (lambda x: quarter.at[piece(x, 16)], s2, final),
    )


def two_parts(at):
    x = at["x"]
    if x is ALL:
        return ALL, ALL
    if isinstance(x, pl.Slice):
        return pl.ds(x.start // 2, 1), ALL
    return lax.rem(x, 2), x // 2


def positions_of(local, parity):
    return (2 * (local // 128) + parity) * 128 + lax.rem(local, 128)


def document_start(starts, positions):
    found = jnp.zeros_like(positions)
    for d in range(8):
        found = jnp.where(positions >= starts[0, d], starts[0, d], found)
    return found


def attend(t, mine, others, starts, parity, scale):
    q = mine[0, piece(t, F_TILE), :]
    q_pos = positions_of(t * F_TILE + lax.broadcasted_iota(jnp.int32, (F_TILE, 1), 0), parity)
    lo = document_start(starts, q_pos)
    ones = jnp.ones((K_TILE, 128), bf16)

    def step(kt, carry):
        top, acc = carry
        rows = piece(kt, K_TILE)
        local = kt * K_TILE + lax.broadcasted_iota(jnp.int32, (1, K_TILE), 1)
        scores = []
        for k, k_parity in ((mine[1, rows, :], parity), (others[0, rows, :], 1 - parity)):
            k_pos = positions_of(local, k_parity)
            scores.append(jnp.where((k_pos >= lo) & (k_pos <= q_pos), dot_nt(q, k), -1e30))
        new = jnp.maximum(jnp.max(scores[0], axis=1, keepdims=True), jnp.max(scores[1], axis=1, keepdims=True))
        new = jnp.maximum(top, new)
        acc = acc * jnp.exp2((top - new) * (scale * LOG2E))
        for s, v in zip(scores, (mine[2, rows, :], others[1, rows, :])):
            p = jnp.exp2((s - new) * (scale * LOG2E)).astype(bf16)
            acc = acc + dot(p, jnp.concatenate([v, ones], axis=1))
        return new, acc

    start = (jnp.full((F_TILE, 1), -1e30, f32), jnp.zeros((F_TILE, 256), f32))
    return lax.fori_loop(0, (t * F_TILE + F_TILE + K_TILE - 1) // K_TILE, step, start)


def front_kernel(
    starts, chosen, tok, gain, shift, bias, cot, wp, wo, up, umaps_in, dmaps_in, lum_in,
    act_all, qkv_w, out_all, up_all, cot_all, heads, across, merged, att, lse, mask,
    umaps, dmaps, lum, act, cotbuf, wq, up_own, rows, mine, others, low, wq_t, send, recv, a_send, a_recv, local, *, scale,
):
    place = Place()
    sends = Sends(send, recv)
    loads = [
        pltpu.make_async_copy(dmaps_in.at[pl.ds(0, 3)], dmaps, local.at[14]),
        pltpu.make_async_copy(lum_in, lum, local.at[15]),
    ]
    for copy in loads:
        copy.start()
    always, perhaps = split_greeting(projectors(place))
    greet(plane_devices(place) + members(place) + always, perhaps)
    home = (place.xl, place.c, place.z, place.y, place.xh)

    def out_view(h):
        def view(fixed, half):
            xl, xh = (ALL, ALL)
            if "x" in fixed:
                xl, xh = lax.rem(fixed["x"], 2), fixed["x"] // 2
            cols = pl.ds(h * 1024, 1024) if half is None else pl.ds(h * 1024 + half * 512, 512)
            return out_all.at[xl, place.c, fixed.get("z", ALL), fixed.get("y", ALL), xh, ALL, cols]

        return view

    def up_view(xl):
        def view(fixed, half):
            c = ALL if half is None else pl.ds(half, 1)
            return up_all.at[pl.ds(xl, 1), c, fixed.get("z", ALL), fixed.get("y", ALL)]

        return view

    def wq_view(p, xl):
        def view(fixed, half):
            c = ALL if half is None else pl.ds(half, 1)
            return wq.at[p, xl, c, fixed.get("z", ALL), fixed.get("y", ALL)]

        return view

    def index(dx, dc):
        return place.step("x", dx) * 2 + (1 - place.c if dc else place.c)

    copies = [
        pltpu.make_async_copy(
            wp.at[:, :, piece(place.g, 256)], wq.at[:, place.xl, place.c, place.z, place.y, place.xh], local.at[0]
        ),
    ]
    copies += [
        pltpu.make_async_copy(
            wo.at[:, pl.ds(h * 1024, 1024)],
            out_view(h)({a: place.at(a) for a in "xyz"}, None),
            local.at[3 + h],
        )
        for h in range(2)
    ]
    copies.append(pltpu.make_async_copy(umaps_in.at[pl.ds(0, 3), :, piece(place.g, 256)], umaps, local.at[2]))
    for copy in copies:
        copy.start()
    wq_spread = [
        sends.push(
            wp.at[:, :, piece(index(*m), 256)],
            wq.at[:, place.xl, place.c, place.z, place.y, place.xh],
            place.member(*m),
        )
        for m in MEMBERS
    ]

    values = tok[...].astype(f32)
    normed = layer_norm(values, gain[0:1, :], shift[0:1, :]).astype(bf16)
    position = ((place.z * 4 + place.y) * 2 + place.xh) * 128 + lax.broadcasted_iota(jnp.int32, (128, 1), 0)
    adapter = jnp.zeros_like(position)
    for d in range(8):
        adapter = jnp.where(position >= starts[0, d], chosen[0, d], adapter)
    column = lax.broadcasted_iota(jnp.int32, (128, 128), 1) // ADAPTER_RANK
    keep = (column == adapter).astype(f32)
    mask[...] = keep
    own = act.at[place.x, place.c]
    own[:, 0:2048] = normed
    loads[0].wait()
    for p in range(3):
        own[:, 2048 + p * 128 : 2176 + p * 128] = (dot(normed, dmaps[p]) * keep).astype(bf16)
    act_gather = GroupGather(place, sends, act)

    for lead in range(4):
        for pair in range(8):
            at = lead * 2048 + pair * 256
            one, two = up[:, at : at + 128], up[:, at + 128 : at + 256]
            for h in range(2):
                to = (h * 4 + lead) * 1024 + pair * 128
                sides = [v[:, h * 64 : h * 64 + 64] for v in (one, two)]
                up_own[:, to : to + 128] = jnp.concatenate(sides, axis=1)
    up_keep = pltpu.make_async_copy(up_own.at[:, piece(place.g, 1024)], up_all.at[home], local.at[1])
    up_keep.start()
    up_spread = [
        sends.push(up_own.at[:, piece(index(*m), 1024)], up_all.at[home], place.member(*m)) for m in MEMBERS
    ]

    copies[0].wait()
    for copy in wq_spread:
        copy.wait()
    fixed = {"z": place.z, "y": place.y}
    qkv_parts = []
    for p, xl, order in (
        (0, ALL, ("y", "z")), (1, ALL, ("z", "y")), (2, pl.ds(0, 1), ("y", "z")), (2, pl.ds(1, 1), ("z", "y"))
    ):
        view = wq_view(p, xl)
        qkv_parts.append(ring_gather(place, sends, view, order, view(fixed, None), Nothing(), False))
    up_gathers = [
        ring_gather(place, sends, up_view(n), order, up_view(n)(fixed, None), Nothing(), False)
        for n, order in enumerate((("y", "z"), ("z", "y")))
    ]
    out_gathers = [
        ring_gather(place, sends, out_view(h), order, wo.at[:, pl.ds(h * 1024, 1024)], copies[1 + h], True)
        for h, order in enumerate((("x", "y", "z"), ("z", "y", "x")))
    ]

    def tick(*parts):
        for part in parts:
            next(part)

    tick(*qkv_parts, *out_gathers)
    own = cotbuf.at[place.x, place.c]
    own[:, 0:2048] = cot[...]
    loads[1].wait()
    own[:, 2048:2176] = (dot_nt(cot[...], lum[...]) * keep).astype(bf16)
    act_gather.own()
    tick(*qkv_parts)
    act_gather.near(False)
    tick(*qkv_parts, *out_gathers)
    run_all(qkv_parts)
    kept = []
    copies[3].wait()

    def project(x):
        left = act[x, :, :, 0:2048].reshape(256, 2048)
        for p in range(3):
            low_rank = act[x, :, :, 2048 + p * 128 : 2176 + p * 128].reshape(256, 128)
            value = dot(left, wq[p].reshape(2048, 256)) + dot(low_rank, umaps[p])
            if p != 1:
                value = value + bias[p // 2 : p // 2 + 1, piece(place.g, 256)]
            for j in range(2):
                rows[p, x, :, j] = value[:, j * 128 : j * 128 + 128].astype(bf16).reshape(2, 128, 128)

    here = place.z * 4 + place.y
    kv = pl.ds(1, 2)
    posts = []

    def post(dx):
        x = place.step("x", dx)
        for n, (to, dc, j, device, myself) in enumerate(attenders(place)):
            if to == dx:
                src = rows.at[:, x, 1 - place.c if dc else place.c, j]
                posts.append(
                    Post(src, mine.at[:, piece(here, 128)], device, myself, a_send.at[0, n], a_recv.at[0, here])
                )
        for n, (to, dc, j, device, _) in enumerate(attenders(place)):
            if to == dx:
                src = rows.at[kv, x, 1 - place.c if dc else place.c, j]
                device = place.member((dx + 2) % 4, dc) | {"z": device["z"], "y": device["y"]}
                myself = None if dc or dx != 2 else (place.z == device["z"]) & (place.y == device["y"])
                posts.append(
                    Post(src, others.at[:, piece(here, 128)], device, myself, a_send.at[1, n], a_recv.at[1, here])
                )

    project(place.x)
    post(0)
    act_gather.near_done()
    project(place.step("x", -1))
    project(place.step("x", 1))
    post(1)
    post(3)
    up_keep.wait()
    for copy in up_spread:
        copy.wait()
    tick(*up_gathers, *out_gathers)
    act_gather.far()
    act_gather.far_done()
    project(place.step("x", 2))
    post(2)
    tick(*up_gathers, *out_gathers)
    kept.append(pltpu.make_async_copy(act, act_all, local.at[6]))
    kept[-1].start()
    for p in range(3):
        for n in range(4):
            wq_t[p, :, n * 512 : n * 512 + 512] = jnp.transpose(wq[p, n // 2, n % 2].reshape(512, 256))
    kept.append(pltpu.make_async_copy(wq_t, qkv_w, local.at[5]))
    kept[-1].start()
    for n in range(16):
        dst = mine.at[:, piece(n, 128)]
        pltpu.make_async_copy(dst, dst, a_recv.at[0, n]).wait()
    kept.append(pltpu.make_async_copy(mine, heads, local.at[7]))
    kept[-1].start()
    for n in range(16):
        dst = others.at[:, piece(n, 128)]
        pltpu.make_async_copy(dst, dst, a_recv.at[1, n]).wait()
    kept.append(pltpu.make_async_copy(others, across, local.at[8]))
    kept[-1].start()
    cot_gather = group_gather(place, sends, cotbuf)

    def keep_cot(n, steps):
        copies = []
        for step in steps:
            x = place.step("x", step)
            copies.append(pltpu.make_async_copy(cotbuf.at[x], cot_all.at[x], local.at[n + len(copies)]))
            copies[-1].start()
        return copies

    tick(cot_gather)

    def tile(t, _):
        peak, total = attend(t, mine, others, starts, place.xh, scale)
        weight = total[:, 128:]
        o = total[:, :128] / weight
        att[piece(t, F_TILE), :] = o
        for b in range(F_TILE // 128):
            low[t * (F_TILE // 128) + b] = o[b * 128 : (b + 1) * 128].astype(bf16)
        line = jnp.transpose(peak * (scale * LOG2E) + jnp.log2(weight))
        for n in range(F_TILE // Q_TILE):
            lse[pl.ds(t * (F_TILE // Q_TILE) + n, 1), :] = line[0:1, n * Q_TILE : n * Q_TILE + Q_TILE]
        return 0

    tiles = mine.shape[1] // F_TILE
    lax.fori_loop(0, tiles // 2, tile, 0)
    tick(*up_gathers, *out_gathers)
    lax.fori_loop(tiles // 2, tiles * 3 // 4, tile, 0)
    tick(cot_gather, *out_gathers)
    kept += keep_cot(11, (0, 1, 3))
    lax.fori_loop(tiles * 3 // 4, tiles, tile, 0)
    back = heads_out(place, sends, low, merged, local.at[9])
    tick(back)
    for copy in posts:
        copy.wait_send()
    for copy in kept:
        copy.wait()
    act_gather.finish()
    run_all([back, *up_gathers, cot_gather, *out_gathers])
    for copy in keep_cot(10, (2,)):
        copy.wait()
    assert sends.used <= send.shape[0], sends.used


def front(starts, chosen, tok, gain, shift, bias, cot, wp, wo, up, umaps, dmaps, lum, scale):
    any_ = pl.BlockSpec(memory_space=pl.ANY)
    vmem = pl.BlockSpec(memory_space=pltpu.VMEM)
    smem = pl.BlockSpec(memory_space=pltpu.SMEM)
    shape = lambda *s: jax.ShapeDtypeStruct(s, bf16)
    vm = lambda *s: pltpu.VMEM(s, bf16)
    return pl.pallas_call(
        functools.partial(front_kernel, scale=scale),
        name="front",
        out_shape=[
            shape(4, 2, 128, 2432),
            shape(3, 256, 2048),
            shape(2, 2, 4, 4, 2, 16, 2048),
            shape(2, 2, 4, 4, 2, 16, 1024),
            shape(4, 2, 128, 2176),
            shape(3, 2048, 128),
            shape(2, 2048, 128),
            shape(128, 2048),
            jax.ShapeDtypeStruct((2048, 128), f32),
            jax.ShapeDtypeStruct((8, 256), f32),
            jax.ShapeDtypeStruct((128, 128), f32),
        ],
        in_specs=[smem] * 2 + [vmem] * 8 + [any_] * 3,
        out_specs=[any_] * 8 + [vmem] * 3,
        scratch_shapes=[
            vm(3, 128, 256),
            vm(3, 2048, 128),
            vm(128, 2048),
            vm(4, 2, 128, 2432),
            vm(4, 2, 128, 2176),
            vm(3, 2, 2, 4, 4, 2, 16, 256),
            vm(16, 8192),
            vm(3, 4, 2, 2, 128, 128),
            vm(3, 2048, 128),
            vm(2, 2048, 128),
            vm(16, 128, 128),
            vm(3, 256, 2048),
        ]
        + [pltpu.SemaphoreType.DMA(n) for n in ((150,), (150,), (2, 16), (2, 16), (16,))],
        compiler_params=pltpu.CompilerParams(
            collective_id=0, has_side_effects=True, vmem_limit_bytes=56 * MIB
        ),
    )(starts, chosen, tok, gain, shift, bias, cot, wp, wo, up, umaps, dmaps, lum)


def middle_kernel(
    starts, grad, queries_in, others_in, att_in, lse, umaps_in, mask, a_own, b_own, two,
    by_member, low_rank, a_final, b_final, two_final,
    queries, others, att, umaps, do, delta, dq_acc, dq, own_low, other_low, by_head, from_other, *refs, scale,
):
    scratch, (send, recv, a_send, a_recv, s_send, s_recv, local) = list(refs[:-7]), refs[-7:]
    place = Place()
    across = [{"xh": 1 - place.xh, "z": z, "y": y} for z, y in plane(place)]
    greet(plane_devices(place) + members(place) + across)
    sends = Sends(send, recv)
    here = place.z * 4 + place.y
    parity = place.xh
    kv = pl.ds(1, 2)

    keep = pltpu.make_async_copy(grad.at[:, head_columns(place.z, place.y)], do.at[piece(here, 128)], local.at[0])
    keep.start()
    loads = [
        pltpu.make_async_copy(src, dst, local.at[1 + n])
        for n, (src, dst) in enumerate(
            ((att_in, att), (queries_in, queries), (others_in, others), (umaps_in, umaps))
        )
    ]
    for copy in loads:
        copy.start()
    grads_sent = [
        sends.push(grad.at[:, head_columns(z, y)], do.at[piece(here, 128)], {"z": z, "y": y})
        for z, y in plane(place)
    ]

    def take(n):
        got = scratch[:n]
        del scratch[:n]
        return got

    early = [
        a_sum(place, sends, a_own, a_final, take(5)),
        b_sum(place, sends, b_own, b_final, take(5)),
    ]
    early += [
        reduce_piece(
            place, sends, two_final.at[n], None,
            (lambda z, y, n=n: two.at[n, z, y], scratch[n], two_final.at[n]), None,
        )
        for n in range(2)
    ]

    def tick(*parts):
        for part in parts:
            try:
                next(part)
            except StopIteration:
                pass

    tick(*early)
    dq_acc[...] = jnp.zeros_like(dq_acc)
    keep.wait()
    for copy in grads_sent:
        copy.wait_recv()
    for copy in loads:
        copy.wait()
    ones = jnp.ones((8, 128), bf16)
    tiles, key_tiles = do.shape[0] // Q_TILE, do.shape[0] // K_TILE

    def row_dots(t, _):
        rows = piece(t, Q_TILE)
        value = do[rows, :].astype(f32) * att[rows, :]
        high = value.astype(bf16)
        low = (value - high.astype(f32)).astype(bf16)
        delta[t] = dot_nt(ones, high) + dot_nt(ones, low)
        return 0

    lax.fori_loop(0, tiles, row_dots, 0)
    tick(*early[:2])

    def keys(kt):
        rows = piece(kt, K_TILE)
        sides = ((others[0, rows, :], others[1, rows, :], 1 - parity), (queries[1, rows, :], queries[2, rows, :], parity))
        local = kt * K_TILE + lax.broadcasted_iota(jnp.int32, (K_TILE, 1), 0)

        def step(qt, carry, diagonal):
            rows = piece(qt, K_TILE)
            q = queries[0, rows, :]
            d = do[rows, :]
            q_pos = positions_of(qt * K_TILE + lax.broadcasted_iota(jnp.int32, (1, K_TILE), 1), parity)
            both = [qt * 2, qt * 2 + 1]
            lse_row = jnp.concatenate([lse[pl.ds(n, 1), :] for n in both], axis=1)
            delta_row = jnp.concatenate([delta[n, 0:1, :] for n in both], axis=1)
            lo = document_start(starts, q_pos)
            found, dq_part = [], None
            for (k, v, k_parity), (dk, dv) in zip(sides, carry):
                k_pos = positions_of(local, k_parity)
                s = dot_nt(k, q)
                allowed = k_pos >= lo
                if diagonal:
                    allowed = allowed & (k_pos <= q_pos)
                p = jnp.exp2(jnp.where(allowed, s * (scale * LOG2E) - lse_row, -1e30))
                dv = dv + dot(p.astype(bf16), d)
                ds = (p * (dot_nt(v, d) - delta_row)).astype(bf16)
                dk = dk + dot(ds, q)
                part = dot_tn(ds, k)
                dq_part = part if dq_part is None else dq_part + part
                found.append((dk, dv))
            dq_acc[rows, :] += dq_part
            return tuple(found)

        zero = jnp.zeros((K_TILE, 128), f32)
        carry = step(kt, ((zero, zero),) * 2, True)
        carry = lax.fori_loop(kt + 1, key_tiles, lambda qt, c: step(qt, c, False), carry)
        return [(dk * scale, dv) for dk, dv in carry]

    blocks = K_TILE // 128
    gone = []

    def to_token(k, n, src, dst, other, away):
        z, y = n // 4, lax.rem(n, 4)
        myself = None if other or away else (place.z == z) & (place.y == y)
        device = {"z": z, "y": y} | ({"xh": 1 - place.xh} if other else {})
        gone.append(Post(src, dst, device, myself, a_send.at[k, n], a_recv.at[k, here]))

    shared = []

    def share(turn, k, part):
        x = lax.rem(place.z + (4 - turn), 4)
        for c in range(2):
            g = x * 2 + c
            pair = piece(g, 2)
            if k:
                both = by_head[1:3, pair].astype(f32) + from_other[:, pair].astype(f32)
                by_head[1:3, pair] = both.astype(bf16)
            device = {"xl": lax.rem(x, 2), "xh": x // 2, "c": c}
            myself = (place.x == x) & (place.c == c)
            src, dst = by_head.at[part, pair], by_member.at[part, place.x, place.c]
            n = turn * 2 + c
            shared.append(Post(src, dst, device, myself, s_send.at[k, n], s_recv.at[k, place.g]))

    def heads_of(turn):
        x = lax.rem(place.z + (4 - turn), 4)
        return [x * 4 + y for y in range(4)]

    def share_keys(turn):
        for head in heads_of(turn):
            for k, dst in ((2, from_other.at[:, 0]), (1, by_head.at[kv, 0])):
                pltpu.make_async_copy(dst, dst, a_recv.at[k, head]).wait()
        share(turn, 1, kv)

    def share_queries(turn):
        for head in heads_of(turn):
            dst = by_head.at[0, 0]
            pltpu.make_async_copy(dst, dst, a_recv.at[0, head]).wait()
        share(turn, 0, 0)

    for turn in (2, 1, 3, 0):
        kt = lax.rem(place.z + turn, key_tiles)
        for k, low, (dk, dv) in zip((2, 1), (other_low, own_low), keys(kt)):
            for b in range(blocks):
                n = kt * blocks + b
                low[n, 0] = dk[b * 128 : (b + 1) * 128].astype(bf16)
                low[n, 1] = dv[b * 128 : (b + 1) * 128].astype(bf16)
                dst = from_other.at[:, here] if k == 2 else by_head.at[kv, here]
                to_token(k, n, low.at[n], dst, k == 2, turn != 0)
    for n in range(16):
        dq[n] = (dq_acc[n * 128 : (n + 1) * 128] * scale).astype(bf16)
    for turn in (2, 1, 3, 0):
        for b in range(blocks):
            n = lax.rem(place.z + turn, 4) * 4 + b
            to_token(0, n, dq.at[n], by_head.at[0, here], False, turn != 0)
    tick(*early)
    for turn in (2, 1, 3, 0):
        share_keys(turn)
    tick(*early)
    for turn in (2, 1, 3, 0):
        share_queries(turn)
    for p in range(3):
        whole = jnp.concatenate([by_head[p, n] for n in range(16)], axis=1)
        low_rank[:, p * 128 : p * 128 + 128] = (dot_nt(whole, umaps[p]) * mask[...]).astype(bf16)
    for n in range(8):
        for k, dst in ((0, by_member.at[0, 0, 0]), (1, by_member.at[kv, 0, 0])):
            pltpu.make_async_copy(dst, dst, s_recv.at[k, n]).wait()
    run_all(early)
    for copy in gone + grads_sent + shared:
        copy.wait_send()
    assert sends.used <= send.shape[0], sends.used


def middle(starts, grad, queries, others, att, lse, umaps, mask, a_own, b_own, two, scale):
    any_ = pl.BlockSpec(memory_space=pl.ANY)
    vmem = pl.BlockSpec(memory_space=pltpu.VMEM)
    smem = pl.BlockSpec(memory_space=pltpu.SMEM)
    vm = lambda *s: pltpu.VMEM(s, bf16)
    shape = lambda *s: jax.ShapeDtypeStruct(s, bf16)
    return pl.pallas_call(
        functools.partial(middle_kernel, scale=scale),
        name="attention_backward",
        out_shape=[
            shape(3, 4, 2, 2, 128, 128),
            shape(128, 384),
            shape(16, 128),
            shape(16, 128),
            shape(2, 64, 128),
        ],
        in_specs=[smem, vmem, any_, any_, any_, vmem, any_, vmem] + [vmem] * 3,
        out_specs=[any_] + [vmem] * 4,
        scratch_shapes=[
            vm(3, 2048, 128),
            vm(2, 2048, 128),
            pltpu.VMEM((2048, 128), f32),
            vm(4, 128, 2048),
            vm(2048, 128),
            pltpu.VMEM((8, 8, 256), f32),
            pltpu.VMEM((2048, 128), f32),
            vm(16, 128, 128),
            vm(16, 2, 128, 128),
            vm(16, 2, 128, 128),
            vm(3, 16, 128, 128),
            vm(2, 16, 128, 128),
        ]
        + a_sum_scratch()
        + b_sum_scratch()
        + [vm(15, 64, 128)] * 2
        + [pltpu.SemaphoreType.DMA(k) for k in ((100,), (100,), (3, 16), (3, 16), (2, 8), (2, 8), (8,))],
        compiler_params=pltpu.CompilerParams(collective_id=2, has_side_effects=True, vmem_limit_bytes=58 * MIB),
    )(starts, grad, queries, others, att, lse, umaps, mask, a_own, b_own, two.reshape(2, 4, 4, 64, 128))


def feed_forward_kernel(
    merged, tok, gains, shifts, biases, up_down, low_up, mask, bias_all, dn, cot_own,
    w_out_in, cot_all, up, out_down_in, out_up_in, umap_in, dmap_in,
    grad_merged, grad_res, base, forth, small_out, a_out, b_out, two, mine_in, mine_cot,
    out_down, out_up, umap_all, umap, dmap, bias, w_out, residual, low_out, sa, cot, up_v, dn_v, slope, act, pre, parts, total, *refs,
):
    scratch, (send, recv, local) = refs[:-3], refs[-3:]
    place = Place()
    greet(members(place) + plane_devices(place))
    sends = Sends(send, recv)
    loads = [
        pltpu.make_async_copy(src, dst, local.at[n]) for n, (src, dst) in enumerate(
            (
                (out_down_in.at[3], out_down), (w_out_in, w_out), (out_up_in.at[3], out_up),
                (umap_in.at[:, piece(place.xl * 2 + place.c, 2048)], umap_all),
                (dmap_in.at[place.xl * 2 + place.c, :, place.xh], dmap), (up, up_v), (cot_all, cot),
            )
        )
    ]
    for copy in loads:
        copy.start()

    def dn_view(h):
        def view(fixed, half):
            cols = pl.ds(h * 1024, 1024) if half is None else pl.ds(h * 1024 + half * 512, 512)
            return dn_v.at[fixed.get("z", ALL), fixed.get("y", ALL), :, cols]

        return view

    here = {"z": place.z, "y": place.y}
    dn_v[place.z, place.y] = dn[...]
    dn_gathers = [
        ring_gather(place, sends, dn_view(h), order, dn_view(h)(here, None), Nothing(), False)
        for h, order in enumerate((("y", "z"), ("z", "y")))
    ]

    def tick(*parts):
        for part in parts:
            next(part)

    tick(*dn_gathers)
    gain, shift = gains[1:2, :], shifts[1:2, :]
    bias_out, bias_end = biases[2:3, :], biases[3:4, :]
    loads[0].wait()
    low_out[...] = (dot(merged[...], out_down[...]) * mask[...]).astype(bf16)
    loads[1].wait()
    loads[2].wait()

    def out_tile(n, _):
        cols = piece(n, 256)
        value = tok[:, cols].astype(f32) + dot(merged[...], w_out[:, cols]) + biases[2:3, cols]
        residual[:, cols] = value + dot(low_out[...], out_up[:, cols])
        return 0

    lax.fori_loop(0, 8, out_tile, 0)
    second = layer_norm(residual[...], gain, shift).astype(bf16)
    own = sa.at[place.x, place.c]
    own[:, 0:2048] = second
    own[:, 2048:2176] = (dot(second, up_down[...]) * mask[...]).astype(bf16)
    gather = GroupGather(place, sends, sa)
    loads[3].wait()
    loads[4].wait()
    whole_bias = bias_all[:, piece(place.xl * 2 + place.c, 2048)]
    for n in range(8):
        for whole, out in ((umap_all[:, n * 256 : n * 256 + 256], umap), (whole_bias[:, n * 256 : n * 256 + 256], bias)):
            sides = [jnp.concatenate([whole[:, h : h + 64], whole[:, 128 + h : 192 + h]], axis=1) for h in (0, 64)]
            out[:, n * 128 : n * 128 + 128] = jnp.where(place.xh == 0, sides[0], sides[1])
    tick(*dn_gathers)

    def rows(ref, x, start, size):
        return ref[x, :, :, pl.ds(start, size)].reshape(256, size)

    xs = places_in_turn(place)

    def hidden(k):
        x = xs[k]

        def tile(n, _):
            cols = piece(n, 256)
            value = dot(rows(sa, x, 0, 2048), up_v[:, cols]) + bias[:, cols]
            value = value + dot(rows(sa, x, 2048, 128), umap[:, cols])
            phi = 0.5 * (1.0 + lax.erf(value * 0.7071067811865476))
            act[k, :, cols] = (value * phi).astype(bf16)
            slope[k, :, cols] = phi + value * (0.3989422804014327 * jnp.exp2(value * value * (-0.5 * LOG2E)))
            return 0

        lax.fori_loop(0, 4, tile, 0)

    def grad_hidden(k):
        x = xs[k]

        def tile(n, _):
            cols = piece(n, 256)
            value = dot_nt(rows(cot, x, 0, 2048), dn_v[n].reshape(256, 2048))
            value = value + dot_nt(rows(cot, x, 2048, 128), dmap[piece(n, 4)].reshape(256, 128))
            pre[k, :, cols] = (value * slope[k, :, cols]).astype(bf16)
            return 0

        lax.fori_loop(0, 4, tile, 0)

    def backward(k, n):
        ks = pl.ds(k, n)

        def tile(t, _):
            cols = piece(t, 256)
            value = dot_nt(pre[ks].reshape(n * 256, 1024), up_v[cols, :]).astype(bf16)
            parts[ks, :, :, cols] = value.reshape(n, 2, 128, 256)
            return 0

        lax.fori_loop(0, 8, tile, 0)
        value = dot_nt(pre[ks].reshape(n * 256, 1024), umap[...]).astype(bf16)
        parts[ks, :, :, 2048:2176] = value.reshape(n, 2, 128, 128)
        value = dot(act[ks].reshape(n * 256, 1024), dmap[...].reshape(1024, 128)).astype(bf16)
        parts[ks, :, :, 2176:2304] = value.reshape(n, 2, 128, 128)

    loads[5].wait()
    gather.own()
    hidden(3)
    tick(*dn_gathers)
    gather.near()
    hidden(2)
    hidden(1)
    run_all(dn_gathers)
    loads[6].wait()
    grad_hidden(3)
    gather.far()
    grad_hidden(2)
    gather.far_done()
    hidden(0)
    grad_hidden(0)

    sums = GroupSum(place, sends, parts, scratch)
    backward(0, 1)
    sums.cross(0)
    grad_hidden(1)
    sums.merge(0)
    sums.first()
    backward(1, 1)
    sums.cross(1)
    backward(2, 2)
    sums.cross(2)
    sums.cross(3)
    sums.merge(1)
    sums.merge(2)
    sums.second()

    def small(k, _):
        x = lax.rem(place.x + jnp.where(k == 3, 0, jnp.where(k == 2, 3, 2 - k)), 4)
        one = dot_tn(act[k], rows(cot, x, 2048, 128))
        other = dot_tn(pre[k], rows(sa, x, 2048, 128))

        @pl.when(k == 0)
        def _():
            total[0] = one
            total[1] = other

        @pl.when(k > 0)
        def _():
            total[0] += one
            total[1] += other

        return 0

    lax.fori_loop(0, 4, small, 0)
    cols = piece(place.g, 256)
    mine_in[...] = sa[:, :, :, cols].reshape(1024, 256)
    mine_cot[...] = cot[:, :, :, cols].reshape(1024, 256)
    def forward(n, _):
        ks, cols = piece(n // 4, 2), piece(lax.rem(n, 4), 512)
        value = dot(act[ks].reshape(512, 1024), dn_v[:, :, :, cols].reshape(1024, 512)).astype(bf16)
        cot[ks, :, :, cols] = value.reshape(2, 2, 128, 512)
        return 0

    lax.fori_loop(0, 8, forward, 0)

    two[...] = total[...].astype(bf16)
    handed = pltpu.make_async_copy(cot.at[:, :, :, pl.ds(0, 2048)], forth, local.at[7])
    handed.start()
    summed = sums.result()
    low_up_grad = (summed[:, 2048:2176] * mask[...]).astype(bf16)
    low_down = (summed[:, 2176:2304] * mask[...]).astype(bf16)
    small_out[:, 0:128] = low_up_grad
    small_out[:, 128:256] = low_down
    grad_second = summed[:, 0:2048] + dot_nt(low_up_grad, up_down[...])
    value = cot_own[...].astype(f32) + layer_norm_back(residual[...], gain, grad_second)
    grad_res[...] = value
    branch = value.astype(bf16)
    low_grad = (dot_nt(branch, out_up[...]) * mask[...]).astype(bf16)

    def merged_tile(n, _):
        cols = piece(n, 256)
        value = dot_nt(branch, w_out[cols, :]) + dot_nt(low_grad, out_down[cols, :])
        grad_merged[:, cols] = value.astype(bf16)
        return 0

    lax.fori_loop(0, 8, merged_tile, 0)
    b_out[...] = dot_tn(low_out[...], branch).astype(bf16)
    a_out[...] = dot_tn(merged[...], low_grad).astype(bf16)
    base[...] = residual[...] + bias_end + dot(low_down, low_up[...])
    handed.wait()
    gather.finish()
    assert sends.used <= send.shape[0], sends.used


def feed_forward(*args):
    any_ = pl.BlockSpec(memory_space=pl.ANY)
    vmem = pl.BlockSpec(memory_space=pltpu.VMEM)
    vm = lambda *s: pltpu.VMEM(s, bf16)
    shape = lambda *s: jax.ShapeDtypeStruct(s, bf16)
    return pl.pallas_call(
        feed_forward_kernel,
        name="feed_forward",
        out_shape=[
            shape(128, 2048),
            jax.ShapeDtypeStruct((128, 2048), f32),
            jax.ShapeDtypeStruct((128, 2048), f32),
            shape(4, 2, 128, 2048),
            shape(128, 256),
            shape(2048, 128),
            shape(128, 2048),
            shape(2, 1024, 128),
            shape(1024, 256),
            shape(1024, 256),
        ],
        in_specs=[vmem] * 11 + [any_] * 7,
        out_specs=[vmem] * 3 + [any_] + [vmem] * 6,
        scratch_shapes=[
            vm(2048, 128),
            vm(128, 2048),
            vm(128, 2048),
            vm(128, 1024),
            vm(16, 64, 128),
            pltpu.VMEM((1, 1024), f32),
            vm(2048, 2048),
            pltpu.VMEM((128, 2048), f32),
            vm(128, 128),
            vm(4, 2, 128, 2176),
            vm(4, 2, 128, 2176),
            vm(2048, 1024),
            vm(4, 4, 64, 2048),
            pltpu.VMEM((4, 256, 1024), f32),
            vm(4, 256, 1024),
            vm(4, 256, 1024),
            vm(4, 2, 128, 2304),
            pltpu.VMEM((2, 1024, 128), f32),
        ]
        + GroupSum.scratch(2304)
        + [pltpu.SemaphoreType.DMA((k,)) for k in (40, 40, 8)],
        compiler_params=pltpu.CompilerParams(collective_id=1, has_side_effects=True, vmem_limit_bytes=63 * MIB),
    )(*args)


def both_heads(gq, p, x):
    heads = [gq[p, x, :, j].reshape(256, 128) for j in range(2)]
    return jnp.concatenate(heads, axis=1)


def tail_kernel(
    grads, qkv_w, act_all, dmaps_in, grad_res_in, forth_in, base_in, low_rank, small, tok, gain, mine_in, mine_cot, a_piece, b_piece, two_piece,
    input_grad, mixed, a_res, b_res, two_a, two_b, a_early, b_early,
    dmaps, grad_res, forth_parts, base, gq, wq, act, left, parts, lows, a_sums, b_sums, a_s, a_f, b_s, b_f, *refs,
):
    scratch, (send, recv, local) = refs[:-3], refs[-3:]
    scratch, forth_scratch = scratch[:6], scratch[6:]
    place = Place()
    greet(members(place) + plane_devices(place))
    sends = Sends(send, recv)
    loads = [
        pltpu.make_async_copy(src, dst, local.at[n])
        for n, (src, dst) in enumerate(((grads, gq), (qkv_w, wq), (act_all, act)))
    ]
    loads.append(pltpu.make_async_copy(dmaps_in.at[pl.ds(0, 3)], dmaps, local.at[44]))
    loads.append(pltpu.make_async_copy(grad_res_in, grad_res, local.at[45]))
    loads.append(pltpu.make_async_copy(forth_in, forth_parts, local.at[43]))
    loads.append(pltpu.make_async_copy(base_in, base, local.at[42]))
    for copy in loads:
        copy.start()
    own = lows.at[place.x, place.c]
    own[:, 0:384] = low_rank[...]
    own[:, 384:640] = small[...]
    spread = [sends.push(own, own, place.member(dx, 0)) for dx in (2, 1, 3)]
    passed = [sends.push(own, own, place.member(0, 1))]

    def two_view(res):
        def view(at):
            xl, xh = two_parts(at)
            return res.at[xl, place.c, at["z"], at["y"], xh]

        return view

    def b_early_view(at):
        z, y = at["z"], at["y"]
        if isinstance(y, pl.Slice):
            cols = pl.ds(y.start * 128 if z is ALL else pl.multiple_of(z * 512 + y.start * 128, 128), 256)
        elif z is ALL:
            cols = ALL
        else:
            cols = piece(z, 512) if y is ALL else piece(z * 4 + y, 128)
        return b_early.at[place.c, at["x"], :, cols]

    early = [
        give_all(place, sends, ("x", "z", "y"), two_piece.at[0], two_view(two_a), local.at[3]),
        give_all(place, sends, ("x", "y", "z"), two_piece.at[1], two_view(two_b), local.at[4]),
        give_all(
            place, sends, ("x", "y", "z"), a_piece,
            lambda at: a_early.at[place.c, at["z"], at["y"], at["x"]], local.at[5],
        ),
        give_all(place, sends, ("x", "y", "z"), b_piece, b_early_view, local.at[6]),
    ]

    def tick(*parts):
        for part in parts:
            next(part)

    tick(*early)
    def a_view(at):
        return a_res.at[:, at["x"], place.c, at["z"], at["y"]]

    def a_held(z, y):
        return a_sums.at[:, piece(z * 4 + y, 16)]

    def b_view(at):
        y = at["y"]
        if y is ALL:
            yr, yc = ALL, ALL
        elif isinstance(y, pl.Slice):
            yr, yc = pl.ds(y.start // 2, 1), ALL
        else:
            yr, yc = y // 2, lax.rem(y, 2)
        return b_res.at[:, at["x"], place.c, at["z"], yr, yc]

    def b_held(z, y):
        return b_sums.at[:, pl.ds(pl.multiple_of(z * 32 + y // 2 * 16, 16), 16), piece(lax.rem(y, 2), 128)]

    def late_part(final, held, slots, order, view, sem):
        yield from reduce_piece(place, sends, final, None, (held, slots, final), None)
        yield from give_all(place, sends, order, final, view, sem, True)

    late = [
        late_part(a_f, a_held, a_s, ("y", "x", "z"), a_view, local.at[7]),
        late_part(b_f, b_held, b_s, ("z", "x", "y"), b_view, local.at[8]),
    ]
    loads[0].wait()
    loads[1].wait()
    xs = places_in_turn(place)
    for k in range(4):
        left[k] = jnp.concatenate([both_heads(gq, p, xs[k]) for p in range(3)], axis=1)

    def partial(k, n):
        ks = pl.ds(k, n)

        def tile(t, _):
            cols = piece(t, 512)
            value = dot(left[ks].reshape(n * 256, 768), wq[:, :, cols].reshape(768, 512)).astype(bf16)
            parts[ks, :, :, cols] = value.reshape(n, 2, 128, 512)
            return 0

        lax.fori_loop(0, 4, tile, 0)

    sums = GroupSum(place, sends, parts, scratch)
    partial(0, 1)
    sums.cross(0)
    partial(1, 1)
    sums.cross(1)
    sums.merge(0)
    sums.first()
    loads[5].wait()
    forth = GroupSum(place, sends, forth_parts, forth_scratch)
    for k in range(4):
        forth.cross(k)
    loads[2].wait()
    for p in range(3):
        total = jnp.zeros((128, 256), f32)
        for x in range(4):
            left_rows = act[x, :, :, 2048 + p * 128 : 2176 + p * 128].reshape(256, 128)
            total = total + dot_tn(left_rows, both_heads(gq, p, x))
        b_sums[p] = total.astype(bf16)
    for dx, copy in zip((2, 1, 3), spread):
        copy.wait()
        came = lows.at[place.step("x", -dx), place.c]
        passed.append(sends.push(came, came, place.member(0, 1)))
    for copy in passed:
        copy.wait()
    b_sums[3] = dot_tn(lows[:, :, :, 512:640].reshape(1024, 128), mine_cot[...]).astype(bf16)
    rows = act[:, :, :, piece(place.g, 256)].reshape(1024, 256)
    for p in range(4):
        right = lows[:, :, :, p * 128 : p * 128 + 128].reshape(1024, 128)
        a_sums[p] = dot_tn(rows if p < 3 else mine_in[...], right).astype(bf16)

    tick(*late)
    partial(2, 2)
    sums.cross(2)
    sums.cross(3)
    forth.merge(0)
    forth.first()
    tick(*early)
    sums.merge(1)
    sums.merge(2)
    sums.second()
    tick(*late)
    tick(*early)
    tick(*late)
    forth.merge(1)
    forth.merge(2)
    forth.second()
    tick(*early)
    loads[3].wait()
    loads[4].wait()
    grad_first = sums.result()
    for p in range(3):
        grad_first = grad_first + dot_nt(low_rank[:, p * 128 : p * 128 + 128], dmaps[p])
    result = grad_res[...] + layer_norm_back(tok[...].astype(f32), gain[0:1, :], grad_first)
    input_grad[...] = result.astype(bf16)
    tick(*late)
    tick(*early)
    run_all(late + early)
    loads[6].wait()
    mixed[...] = (base[...] + forth.result()).astype(bf16)
    assert sends.used <= send.shape[0], sends.used


def tail(grads, qkv_w, act_all, dmaps, grad_res, forth, base, low_rank, small, tok, gain, mine_in, mine_cot, a_piece, b_piece, two_piece):
    any_ = pl.BlockSpec(memory_space=pl.ANY)
    vmem = pl.BlockSpec(memory_space=pltpu.VMEM)
    vm = lambda *s: pltpu.VMEM(s, bf16)
    shape = lambda *s: jax.ShapeDtypeStruct(s, bf16)
    a_shape, b_shape = (4, 4, 2, 4, 4, 16, 128), (4, 4, 2, 4, 2, 2, 16, 128)
    return pl.pallas_call(
        tail_kernel,
        name="tail",
        out_shape=[
            shape(128, 2048),
            shape(128, 2048),
            shape(*a_shape),
            shape(*b_shape),
            shape(2, 2, 4, 4, 2, 64, 128),
            shape(2, 2, 4, 4, 2, 64, 128),
            shape(2, 4, 4, 4, 16, 128),
            shape(2, 4, 16, 2048),
        ],
        in_specs=[any_] * 7 + [vmem] * 9,
        out_specs=[vmem] * 2 + [any_] * 6,
        scratch_shapes=[
            vm(3, 2048, 128),
            pltpu.VMEM((128, 2048), f32),
            vm(4, 2, 128, 2048),
            pltpu.VMEM((128, 2048), f32),
            vm(3, 4, 2, 2, 128, 128),
            vm(3, 256, 2048),
            vm(4, 2, 128, 2432),
            vm(4, 256, 768),
            vm(4, 2, 128, 2048),
            vm(4, 2, 128, 640),
            vm(4, 256, 128),
            vm(4, 128, 256),
            vm(15, 4, 16, 128),
            vm(4, 16, 128),
            vm(15, 4, 16, 128),
            vm(4, 16, 128),
        ]
        + GroupSum.scratch(2048) * 2
        + [pltpu.SemaphoreType.DMA((k,)) for k in (200, 200, 46)],
        compiler_params=pltpu.CompilerParams(collective_id=3, has_side_effects=True, vmem_limit_bytes=60 * MIB),
    )(
        grads, qkv_w, act_all, dmaps, grad_res, forth, base, low_rank, small, tok, gain, mine_in, mine_cot, a_piece, b_piece, two_piece
    )
def widen_kernel(a, a_one, b, b_one, hid_a, hid_b, a_out, b_out, up_out, hid_b_out, hid_a_out, down_out):
    for n in range(3):
        a_out[n] = a[n].astype(f32)
    a_out[3] = a_one[...].astype(f32)
    up_out[...] = a[3].astype(f32)
    for c in range(2):
        for yc in range(2):
            cols = pl.ds(c * 256 + yc * 128, 128)
            for n in range(3):
                b_out[n, :, cols] = b[n, 0, c, :, :, yc].reshape(128, 128).astype(f32)
            down_out[:, cols] = b[3, 0, c, :, :, yc].reshape(128, 128).astype(f32)
    b_out[3] = b_one[...].astype(f32)
    hid_a_out[...] = hid_a[...].astype(f32)
    for n in range(4):
        rows = pl.ds(n * 512, 512)
        hid_b_out[:, rows] = jnp.transpose(hid_b[rows, :].astype(f32))


def widen(a, b, hid_a, hid_b, a_one, b_one):
    out = lambda *s: jax.ShapeDtypeStruct(s, f32)
    spec = pl.BlockSpec
    return pl.pallas_call(
        widen_kernel,
        name="widen",
        grid=(4,),
        out_shape=[
            out(4, 2048, 128), out(4, 128, 2048), out(2048, 128), out(128, 8192), out(8192, 128), out(128, 2048)
        ],
        in_specs=[
            spec((4, 512, 128), lambda g: (0, g, 0)),
            spec((512, 128), lambda g: (g, 0)),
            spec((4, 1, 2, 4, 2, 2, 16, 128), lambda g: (0, g, 0, 0, 0, 0, 0, 0)),
            spec((128, 512), lambda g: (0, g)),
            spec((2048, 128), lambda g: (g, 0)),
            spec((2048, 128), lambda g: (g, 0)),
        ],
        out_specs=[
            spec((4, 512, 128), lambda g: (0, g, 0)),
            spec((4, 128, 512), lambda g: (0, 0, g)),
            spec((512, 128), lambda g: (g, 0)),
            spec((128, 2048), lambda g: (0, g)),
            spec((2048, 128), lambda g: (g, 0)),
            spec((128, 512), lambda g: (0, g)),
        ],
        compiler_params=pltpu.CompilerParams(vmem_limit_bytes=62 * MIB),
    )(
        a.reshape(4, 2048, 128), a_one.reshape(2048, 128), b, b_one.reshape(128, 2048), hid_a.reshape(8192, 128),
        hid_b.reshape(8192, 128),
    )


def per_device(
    tokens,
    document_starts,
    document_adapter,
    layernorm_gain,
    layernorm_bias,
    projection_weight,
    output_weight,
    up_weight,
    down_weight,
    projection_bias,
    upper_bias,
    attention_down_maps,
    attention_up_maps,
    upper_down_maps,
    upper_up_maps,
    lower_down_maps,
    lower_up_maps,
    cotangent,
):
    local_rows, width = tokens.shape[1:]
    head_size = width // HEADS
    seq = local_rows * 32
    scale = head_size ** (-0.5)
    xl, c, z, y, xh = (lax.axis_index(a) for a in AXES)
    group = (xh * 2 + xl) * 2 + c
    cot = cotangent[0]
    (
        act_all, qkv_w, out_all, up_all, cot_all, by_head, across, merged, attended, lse, mask
    ) = front(
        document_starts, document_adapter, tokens[0], layernorm_gain, layernorm_bias, projection_bias, cot,
        jnp.transpose(projection_weight, (1, 0, 2)), output_weight, up_weight, attention_up_maps, attention_down_maps,
        lower_up_maps, scale,
    )
    grad_merged, grad_residual, base, forth, small, a_out, b_out, two, mine_in, mine_cot = feed_forward(
        merged, tokens[0], layernorm_gain, layernorm_bias, projection_bias, upper_down_maps, lower_up_maps, mask,
        upper_bias[None], down_weight, cot, out_all.reshape(width, width), cot_all, up_all.reshape(width, 1024),
        attention_down_maps, attention_up_maps, upper_up_maps, lower_down_maps.reshape(4, 16, 2, 64, 128),
    )
    grad_qkv, grad_adapt_qkv, a_piece, b_piece, two_piece = middle(
        document_starts, grad_merged, by_head, across, attended, lse, attention_up_maps, mask, a_out, b_out, two, scale
    )
    input_grad, mixed, *sums = tail(
        grad_qkv, qkv_w, act_all, attention_down_maps, grad_residual, forth, base, grad_adapt_qkv, small, tokens[0], layernorm_gain,
        mine_in, mine_cot, a_piece, b_piece, two_piece,
    )
    return (mixed[None], input_grad[None], *widen(*sums))


def solution(mesh):
    fine = jax.sharding.Mesh(mesh.devices.reshape(SIZES), AXES)
    by_token = P(STREAM, TOKEN, None)
    shard = AXES
    in_specs = (
        by_token,
        P(STREAM, None),
        P(STREAM, None),
        P(),
        P(),
        P(shard, None, None),
        P(shard, None),
        P(shard, None),
        P(shard, None),
        P(),
        P(),
        P(),
        P(),
        P(),
        P(),
        P(),
        P(),
        by_token,
    )
    out_specs = (by_token, by_token, P(), P(), P(), P(), P(), P())
    return jax.shard_map(per_device, mesh=fine, in_specs=in_specs, out_specs=out_specs, check_vma=False)
```

```python
import functools

import jax
import jax.numpy as jnp
from jax import lax
from jax.experimental import pallas as pl
from jax.experimental.pallas import tpu as pltpu
from jax.sharding import PartitionSpec as P

HEADS = 16
ADAPTER_RANK = 16
MESH = pl.DeviceIdType.MESH
AXES = ("xl", "c", "z", "y", "xh")
SIZES = (2, 2, 4, 4, 2)
STREAM = ("xl", "c")
TOKEN = ("z", "y", "xh")
bf16 = jnp.bfloat16
f32 = jnp.float32
LOG2E = 1.4426950408889634
MIB = 2**20
Q_TILE = 256
K_TILE = 512
F_TILE = 256
ALL = slice(None)


def layer_norm(values, gain, shift):
    center = values - jnp.mean(values, axis=-1, keepdims=True)
    spread = jnp.mean(center * center, axis=-1, keepdims=True)
    return center * lax.rsqrt(spread + 1e-05) * gain + shift


def layer_norm_back(values, gain, grad):
    center = values - jnp.mean(values, axis=-1, keepdims=True)
    scale = lax.rsqrt(jnp.mean(center * center, axis=-1, keepdims=True) + 1e-05)
    unit = center * scale
    grad = grad * gain
    along = jnp.mean(grad * unit, axis=-1, keepdims=True)
    return scale * (grad - jnp.mean(grad, axis=-1, keepdims=True) - unit * along)


def dot(left, right):
    return jnp.dot(left, right, preferred_element_type=f32)


def dot_nt(left, right):
    return lax.dot_general(left, right, (((1,), (1,)), ((), ())), preferred_element_type=f32)


def dot_tn(left, right):
    return lax.dot_general(left, right, (((0,), (0,)), ((), ())), preferred_element_type=f32)


def piece(n, size):
    return pl.ds(pl.multiple_of(n * size, size), size)


class Place:
    def __init__(self):
        self.xl, self.c, self.z, self.y, self.xh = (lax.axis_index(a) for a in AXES)
        self.x = self.xh * 2 + self.xl
        self.g = self.x * 2 + self.c

    def at(self, axis):
        return {"x": self.x, "y": self.y, "z": self.z}[axis]

    def step(self, axis, step):
        return lax.rem(self.at(axis) + (step + 4), 4)

    def toward(self, axis, step=1):
        if axis == "c":
            return {"c": 1 - self.c}
        to = self.step(axis, step)
        if axis == "x":
            return {"xl": lax.rem(to, 2), "xh": to // 2}
        return {axis: to}

    def member(self, dx, dc):
        to = {}
        if dx:
            to |= self.toward("x", dx)
        if dc:
            to |= {"c": 1 - self.c}
        return to


MEMBERS = [(dx, dc) for dx in (2, 1, 3, 0) for dc in (0, 1) if dx or dc]


class Sends:
    def __init__(self, send, recv):
        self.send, self.recv, self.used, self.open = send, recv, 0, []

    def push(self, src, dst, device):
        k = self.used
        self.used += 1
        copy = pltpu.make_async_remote_copy(
            src_ref=src,
            dst_ref=dst,
            send_sem=self.send.at[k],
            recv_sem=self.recv.at[k],
            device_id=device,
            device_id_type=MESH,
        )
        copy.start()
        self.open.append(copy)
        return copy


def greet(devices, perhaps=()):
    barrier = pltpu.get_barrier_semaphore()
    for device in devices:
        pl.semaphore_signal(barrier, inc=1, device_id=device, device_id_type=MESH)
    amount = len(devices) + len(perhaps)
    for device, myself in perhaps:
        amount = amount - myself.astype(jnp.int32)

        @pl.when(jnp.logical_not(myself))
        def _():
            pl.semaphore_signal(barrier, inc=1, device_id=device, device_id_type=MESH)

    pl.semaphore_wait(barrier, amount)


def run_all(parts):
    parts = list(parts)
    while parts:
        left = []
        for part in parts:
            try:
                next(part)
                left.append(part)
            except StopIteration:
                pass
        parts = left


def ring_gather(place, sends, view, order, chunk, landed, forward, direct=False):
    fixed = {a: place.at(a) for a in order}
    across = place.toward("c")
    later, passed = [], []

    def pass_on(block):
        if forward:
            passed.append(sends.push(view(block, None), view(block, None), across))

    if forward:
        passed.append(sends.push(chunk, view(fixed, None), across))
    for number, axis in enumerate(order):
        own = view(fixed, None)
        src = chunk if number == 0 else own
        if number == 0 or direct:
            sent = [sends.push(src, own, place.toward(axis, s)) for s in (2, 1, 3)]
            yield
            for s, copy in zip((2, 1, 3), sent):
                copy.wait_recv()
                pass_on(fixed | {axis: place.step(axis, -s)})
            if number == 0:
                landed.wait()
            later += sent
            del fixed[axis]
            continue
        up = sends.push(src, own, place.toward(axis, 1))
        down = sends.push(src, own, place.toward(axis, -1))
        yield
        before = fixed | {axis: place.step(axis, -1)}
        after = fixed | {axis: place.step(axis, 1)}
        opposite = fixed | {axis: place.step(axis, 2)}
        up.wait_recv()
        half = view(before, 0)
        up_two = sends.push(half, half, place.toward(axis, 1))
        down.wait_recv()
        half = view(after, 1)
        down_two = sends.push(half, half, place.toward(axis, -1))
        pass_on(before)
        pass_on(after)
        yield
        up_two.wait_recv()
        down_two.wait_recv()
        pass_on(opposite)
        later += [up, down, up_two, down_two]
        del fixed[axis]
    yield
    for copy in later:
        copy.wait_send()
    for copy in passed:
        copy.wait()


class Nothing:
    def wait(self):
        pass


def neighbours(place, axes):
    return [place.toward(a, s) for a in axes for s in ((1, 2, 3) if a in "xyz" else (1,))]


def members(place):
    return [place.member(*m) for m in MEMBERS]


class GroupGather:
    def __init__(self, place, sends, buf):
        self.place, self.sends, self.buf = place, sends, buf
        self.mine = buf.at[place.x, place.c]
        self.right, self.left = place.toward("x", 1), place.toward("x", -1)
        self.up = sends.push(self.mine, self.mine, self.right)
        self.down = sends.push(self.mine, self.mine, self.left)
        self.passed = [self.pass_on(self.mine)]

    def pass_on(self, ref):
        return self.sends.push(ref, ref, self.place.toward("c"))

    def own(self):
        self.passed[0].wait_recv()

    def near(self, wait=True):
        x, c = self.place.step("x", -1), self.place.c
        self.up.wait_recv()
        half = self.buf.at[x, c, pl.ds(0, 64)]
        self.up_two = self.sends.push(half, half, self.right)
        self.passed.append(self.pass_on(self.buf.at[x, c]))
        x = self.place.step("x", 1)
        self.down.wait_recv()
        half = self.buf.at[x, c, pl.ds(64, 64)]
        self.down_two = self.sends.push(half, half, self.left)
        self.passed.append(self.pass_on(self.buf.at[x, c]))
        if wait:
            self.near_done()

    def near_done(self):
        self.passed[1].wait_recv()
        self.passed[2].wait_recv()

    def far(self):
        self.up_two.wait_recv()
        self.down_two.wait_recv()
        self.passed.append(self.pass_on(self.buf.at[self.place.step("x", 2), self.place.c]))

    def far_done(self):
        self.passed[3].wait_recv()

    def finish(self):
        for copy in [self.up, self.down, self.up_two, self.down_two] + self.passed:
            copy.wait_send()


def group_gather(place, sends, buf):
    gather = GroupGather(place, sends, buf)
    yield
    gather.own()
    gather.near()
    yield
    gather.far()
    yield
    gather.far_done()
    gather.finish()


def places_in_turn(place):
    return [place.step("x", s) for s in (2, 1, -1, 0)]


class GroupSum:
    def __init__(self, place, sends, parts, scratch):
        self.place, self.sends, self.parts = place, sends, parts
        self.came, self.own, self.left_one, self.right_one, self.left_two, self.right_two = scratch
        self.right, self.left = place.toward("x", 1), place.toward("x", -1)
        self.crossed = {}

    @staticmethod
    def scratch(n):
        vm = lambda *s: pltpu.VMEM(s, bf16)
        return [vm(4, 128, n), vm(3, 128, n), vm(64, n), vm(64, n), vm(128, n), vm(128, n)]

    def cross(self, k):
        place = self.place
        self.crossed[k] = self.sends.push(
            self.parts.at[k, 1 - place.c], self.came.at[k], place.toward("c")
        )

    def merge(self, k):
        self.crossed[k].wait()
        both = self.parts[k, self.place.c].astype(f32) + self.came[k].astype(f32)
        self.own[k] = both.astype(bf16)

    def first(self):
        self.up = self.sends.push(self.own.at[0, pl.ds(0, 64)], self.left_one, self.right)
        self.down = self.sends.push(self.own.at[0, pl.ds(64, 64)], self.right_one, self.left)

    def second(self):
        self.up.wait()
        both = self.own[1, 0:64].astype(f32) + self.left_one[...].astype(f32)
        self.own[1, 0:64] = both.astype(bf16)
        self.up_two = self.sends.push(self.own.at[1], self.left_two, self.right)
        self.down.wait()
        both = self.own[2, 64:128].astype(f32) + self.right_one[...].astype(f32)
        self.own[2, 64:128] = both.astype(bf16)
        self.down_two = self.sends.push(self.own.at[2], self.right_two, self.left)

    def result(self):
        self.crossed[3].wait()
        total = self.parts[3, self.place.c].astype(f32) + self.came[3].astype(f32)
        self.up_two.wait()
        self.down_two.wait()
        return total + self.left_two[...].astype(f32) + self.right_two[...].astype(f32)


def group_sum(place, sends, parts, scratch, out):
    total = GroupSum(place, sends, parts, scratch)
    for k in range(4):
        total.cross(k)
    yield
    total.merge(0)
    total.first()
    total.merge(1)
    total.merge(2)
    yield
    total.second()
    yield
    out[...] = total.result()


def plane(place):
    steps = [(i, j) for i in (2, 1, 3, 0) for j in (2, 1, 3, 0) if i or j]
    return [(lax.rem(place.z + i, 4), lax.rem(place.y + j, 4)) for i, j in steps]


def from_plane(place):
    steps = [(i, j) for i in (2, 1, 3, 0) for j in (2, 1, 3, 0) if i or j]
    return [(lax.rem(place.z + 4 - i, 4), lax.rem(place.y + 4 - j, 4)) for i, j in steps]


def projectors(place):
    x, c = place.z, place.y // 2
    member = {"xl": lax.rem(x, 2), "xh": x // 2, "c": c}
    mine = (place.x == x) & (place.c == c)
    return [(member | {"z": z, "y": y}, None) for z, y in plane(place)] + [
        (member | {"z": place.z, "y": place.y}, mine)
    ]


def attenders(place):
    found = []
    for dx, dc in MEMBERS + [(0, 0)]:
        for j in range(2):
            z, y = place.x, 2 * place.c + j
            device = place.member(dx, dc) | {"z": z, "y": y}
            mine = None if dx or dc else (place.z == z) & (place.y == y)
            found.append((dx, dc, j, device, mine))
    return found


def head_columns(z, y):
    return pl.ds(pl.multiple_of((z * 4 + y) * 128, 128), 128)


def split_greeting(pairs):
    return [d for d, m in pairs if m is None], [(d, m) for d, m in pairs if m is not None]


def plane_devices(place):
    return [{"z": z, "y": y} for z, y in plane(place)]


class Post:
    def __init__(self, src, dst, device, myself, send_sem, recv_sem):
        self.remote = pltpu.make_async_remote_copy(
            src_ref=src, dst_ref=dst, send_sem=send_sem, recv_sem=recv_sem, device_id=device, device_id_type=MESH
        )
        self.myself = myself
        if myself is None:
            self.remote.start()
        else:
            pl.when(myself)(pltpu.make_async_copy(src, dst, recv_sem).start)
            pl.when(jnp.logical_not(myself))(self.remote.start)

    def wait_send(self):
        if self.myself is None:
            self.remote.wait_send()
        else:
            pl.when(jnp.logical_not(self.myself))(self.remote.wait_send)


def heads_out(place, sends, blocks, merged, local):
    cols = head_columns(place.z, place.y)
    keep = pltpu.make_async_copy(blocks.at[place.z * 4 + place.y], merged.at[:, cols], local)
    keep.start()
    sent = [sends.push(blocks.at[z * 4 + y], merged.at[:, cols], {"z": z, "y": y}) for z, y in plane(place)]
    yield
    for copy in sent:
        copy.wait()
    keep.wait()


def reduce_piece(place, sends, final, across, plane_step, along):
    if across:
        src, came, own, out = across
        copy = sends.push(src, came, place.toward("c"))
        yield
        copy.wait()
        out[...] = (own[...].astype(f32) + came[...].astype(f32)).astype(bf16)
    held, slots, out = plane_step
    sent = [sends.push(held(z, y), slots.at[n], {"z": z, "y": y}) for n, (z, y) in enumerate(plane(place))]
    yield
    for copy in sent:
        copy.wait()
    total = held(place.z, place.y)[...].astype(f32)
    for n in range(15):
        total = total + slots[n].astype(f32)
    out[...] = total.astype(bf16)
    if along:
        held, slots, out = along
        sent = [sends.push(held(place.step("x", d)), slots.at[d - 1], place.toward("x", d)) for d in (2, 1, 3)]
        yield
        for copy in sent:
            copy.wait()
        total = held(place.x)[...].astype(f32)
        for d in range(3):
            total = total + slots[d].astype(f32)
        out[...] = total.astype(bf16)


def give_all(place, sends, order, final, view, local, direct=False):
    here = {a: place.at(a) for a in "xyz"}
    keep = pltpu.make_async_copy(final, view(here), local)
    keep.start()

    def fixed_view(fixed, half):
        at = {a: fixed.get(a, ALL) for a in "xyz"}
        if half is not None:
            at[order[0]] = pl.ds(half * 2, 2)
        return view(at)

    return ring_gather(place, sends, fixed_view, order, final, keep, True, direct)


def a_sum_scratch():
    vm = lambda *shape: pltpu.VMEM(shape, bf16)
    return [vm(1024, 128), vm(1024, 128), vm(15, 64, 128), vm(64, 128), vm(3, 16, 128)]


def b_sum_scratch():
    vm = lambda *shape: pltpu.VMEM(shape, bf16)
    return [vm(64, 2048), vm(64, 2048), vm(15, 64, 128), vm(64, 128), vm(3, 16, 128)]


def a_sum(place, sends, a, final, scratch):
    came, half, s1, quarter, s2 = scratch
    return reduce_piece(
        place, sends, final,
        (a.at[piece(1 - place.c, 1024)], came, a.at[piece(place.c, 1024)], half),
        (lambda z, y: half.at[piece(z * 4 + y, 64)], s1, quarter),
        (lambda x: quarter.at[piece(x, 16)], s2, final),
    )


def b_sum(place, sends, b, final, scratch):
    came, half, s1, quarter, s2 = scratch
    return reduce_piece(
        place, sends, final,
        (b.at[piece(1 - place.c, 64)], came, b.at[piece(place.c, 64)], half),
        (lambda z, y: half.at[:, piece(z * 4 + y, 128)], s1, quarter),
        (lambda x: quarter.at[piece(x, 16)], s2, final),
    )


def two_parts(at):
    x = at["x"]
    if x is ALL:
        return ALL, ALL
    if isinstance(x, pl.Slice):
        return pl.ds(x.start // 2, 1), ALL
    return lax.rem(x, 2), x // 2


def positions_of(local, parity):
    return (2 * (local // 128) + parity) * 128 + lax.rem(local, 128)


def document_start(starts, positions):
    found = jnp.zeros_like(positions)
    for d in range(8):
        found = jnp.where(positions >= starts[0, d], starts[0, d], found)
    return found


def attend(t, mine, others, starts, parity, scale):
    q = mine[0, piece(t, F_TILE), :]
    q_pos = positions_of(t * F_TILE + lax.broadcasted_iota(jnp.int32, (F_TILE, 1), 0), parity)
    lo = document_start(starts, q_pos)
    ones = jnp.ones((K_TILE, 128), bf16)

    def step(kt, carry):
        top, acc = carry
        rows = piece(kt, K_TILE)
        local = kt * K_TILE + lax.broadcasted_iota(jnp.int32, (1, K_TILE), 1)
        scores = []
        for k, k_parity in ((mine[1, rows, :], parity), (others[0, rows, :], 1 - parity)):
            k_pos = positions_of(local, k_parity)
            scores.append(jnp.where((k_pos >= lo) & (k_pos <= q_pos), dot_nt(q, k), -1e30))
        new = jnp.maximum(jnp.max(scores[0], axis=1, keepdims=True), jnp.max(scores[1], axis=1, keepdims=True))
        new = jnp.maximum(top, new)
        acc = acc * jnp.exp2((top - new) * (scale * LOG2E))
        for s, v in zip(scores, (mine[2, rows, :], others[1, rows, :])):
            p = jnp.exp2((s - new) * (scale * LOG2E)).astype(bf16)
            acc = acc + dot(p, jnp.concatenate([v, ones], axis=1))
        return new, acc

    start = (jnp.full((F_TILE, 1), -1e30, f32), jnp.zeros((F_TILE, 256), f32))
    return lax.fori_loop(0, (t * F_TILE + F_TILE + K_TILE - 1) // K_TILE, step, start)


def front_kernel(
    starts, chosen, tok, gain, shift, bias, cot, wp, wo, up, umaps_in, dmaps_in, lum_in,
    act_all, qkv_w, out_all, up_all, cot_all, heads, across, merged, att, lse, mask,
    umaps, dmaps, lum, act, cotbuf, wq, up_own, rows, mine, others, low, wq_t, send, recv, a_send, a_recv, local, *, scale,
):
    place = Place()
    sends = Sends(send, recv)
    loads = [
        pltpu.make_async_copy(dmaps_in.at[pl.ds(0, 3)], dmaps, local.at[14]),
        pltpu.make_async_copy(lum_in, lum, local.at[15]),
    ]
    for copy in loads:
        copy.start()
    always, perhaps = split_greeting(projectors(place))
    greet(plane_devices(place) + members(place) + always, perhaps)
    home = (place.xl, place.c, place.z, place.y, place.xh)

    def out_view(h):
        def view(fixed, half):
            xl, xh = (ALL, ALL)
            if "x" in fixed:
                xl, xh = lax.rem(fixed["x"], 2), fixed["x"] // 2
            cols = pl.ds(h * 1024, 1024) if half is None else pl.ds(h * 1024 + half * 512, 512)
            return out_all.at[xl, place.c, fixed.get("z", ALL), fixed.get("y", ALL), xh, ALL, cols]

        return view

    def up_view(xl):
        def view(fixed, half):
            c = ALL if half is None else pl.ds(half, 1)
            return up_all.at[pl.ds(xl, 1), c, fixed.get("z", ALL), fixed.get("y", ALL)]

        return view

    def wq_view(p, xl):
        def view(fixed, half):
            c = ALL if half is None else pl.ds(half, 1)
            return wq.at[p, xl, c, fixed.get("z", ALL), fixed.get("y", ALL)]

        return view

    def index(dx, dc):
        return place.step("x", dx) * 2 + (1 - place.c if dc else place.c)

    copies = [
        pltpu.make_async_copy(
            wp.at[:, :, piece(place.g, 256)], wq.at[:, place.xl, place.c, place.z, place.y, place.xh], local.at[0]
        ),
    ]
    copies += [
        pltpu.make_async_copy(
            wo.at[:, pl.ds(h * 1024, 1024)],
            out_view(h)({a: place.at(a) for a in "xyz"}, None),
            local.at[3 + h],
        )
        for h in range(2)
    ]
    copies.append(pltpu.make_async_copy(umaps_in.at[pl.ds(0, 3), :, piece(place.g, 256)], umaps, local.at[2]))
    for copy in copies:
        copy.start()
    wq_spread = [
        sends.push(
            wp.at[:, :, piece(index(*m), 256)],
            wq.at[:, place.xl, place.c, place.z, place.y, place.xh],
            place.member(*m),
        )
        for m in MEMBERS
    ]

    values = tok[...].astype(f32)
    normed = layer_norm(values, gain[0:1, :], shift[0:1, :]).astype(bf16)
    position = ((place.z * 4 + place.y) * 2 + place.xh) * 128 + lax.broadcasted_iota(jnp.int32, (128, 1), 0)
    adapter = jnp.zeros_like(position)
    for d in range(8):
        adapter = jnp.where(position >= starts[0, d], chosen[0, d], adapter)
    column = lax.broadcasted_iota(jnp.int32, (128, 128), 1) // ADAPTER_RANK
    keep = (column == adapter).astype(f32)
    mask[...] = keep
    own = act.at[place.x, place.c]
    own[:, 0:2048] = normed
    loads[0].wait()
    for p in range(3):
        own[:, 2048 + p * 128 : 2176 + p * 128] = (dot(normed, dmaps[p]) * keep).astype(bf16)
    act_gather = GroupGather(place, sends, act)

    for lead in range(4):
        for pair in range(8):
            at = lead * 2048 + pair * 256
            one, two = up[:, at : at + 128], up[:, at + 128 : at + 256]
            for h in range(2):
                to = (h * 4 + lead) * 1024 + pair * 128
                sides = [v[:, h * 64 : h * 64 + 64] for v in (one, two)]
                up_own[:, to : to + 128] = jnp.concatenate(sides, axis=1)
    up_keep = pltpu.make_async_copy(up_own.at[:, piece(place.g, 1024)], up_all.at[home], local.at[1])
    up_keep.start()
    up_spread = [
        sends.push(up_own.at[:, piece(index(*m), 1024)], up_all.at[home], place.member(*m)) for m in MEMBERS
    ]

    copies[0].wait()
    for copy in wq_spread:
        copy.wait()
    fixed = {"z": place.z, "y": place.y}
    qkv_parts = []
    for p, xl, order in (
        (0, ALL, ("y", "z")), (1, ALL, ("z", "y")), (2, pl.ds(0, 1), ("y", "z")), (2, pl.ds(1, 1), ("z", "y"))
    ):
        view = wq_view(p, xl)
        qkv_parts.append(ring_gather(place, sends, view, order, view(fixed, None), Nothing(), False))
    up_gathers = [
        ring_gather(place, sends, up_view(n), order, up_view(n)(fixed, None), Nothing(), False)
        for n, order in enumerate((("y", "z"), ("z", "y")))
    ]
    out_gathers = [
        ring_gather(place, sends, out_view(h), order, wo.at[:, pl.ds(h * 1024, 1024)], copies[1 + h], True)
        for h, order in enumerate((("x", "y", "z"), ("z", "y", "x")))
    ]

    def tick(*parts):
        for part in parts:
            next(part)

    tick(*qkv_parts, *out_gathers)
    own = cotbuf.at[place.x, place.c]
    own[:, 0:2048] = cot[...]
    loads[1].wait()
    own[:, 2048:2176] = (dot_nt(cot[...], lum[...]) * keep).astype(bf16)
    act_gather.own()
    tick(*qkv_parts)
    act_gather.near(False)
    tick(*qkv_parts, *out_gathers)
    run_all(qkv_parts)
    kept = []
    copies[3].wait()

    def project(x):
        left = act[x, :, :, 0:2048].reshape(256, 2048)
        for p in range(3):
            low_rank = act[x, :, :, 2048 + p * 128 : 2176 + p * 128].reshape(256, 128)
            value = dot(left, wq[p].reshape(2048, 256)) + dot(low_rank, umaps[p])
            if p != 1:
                value = value + bias[p // 2 : p // 2 + 1, piece(place.g, 256)]
            for j in range(2):
                rows[p, x, :, j] = value[:, j * 128 : j * 128 + 128].astype(bf16).reshape(2, 128, 128)

    here = place.z * 4 + place.y
    kv = pl.ds(1, 2)
    posts = []

    def post(dx):
        x = place.step("x", dx)
        for n, (to, dc, j, device, myself) in enumerate(attenders(place)):
            if to == dx:
                src = rows.at[:, x, 1 - place.c if dc else place.c, j]
                posts.append(
                    Post(src, mine.at[:, piece(here, 128)], device, myself, a_send.at[0, n], a_recv.at[0, here])
                )
        for n, (to, dc, j, device, _) in enumerate(attenders(place)):
            if to == dx:
                src = rows.at[kv, x, 1 - place.c if dc else place.c, j]
                device = place.member((dx + 2) % 4, dc) | {"z": device["z"], "y": device["y"]}
                myself = None if dc or dx != 2 else (place.z == device["z"]) & (place.y == device["y"])
                posts.append(
                    Post(src, others.at[:, piece(here, 128)], device, myself, a_send.at[1, n], a_recv.at[1, here])
                )

    project(place.x)
    post(0)
    act_gather.near_done()
    project(place.step("x", -1))
    project(place.step("x", 1))
    post(1)
    post(3)
    up_keep.wait()
    for copy in up_spread:
        copy.wait()
    tick(*up_gathers, *out_gathers)
    act_gather.far()
    act_gather.far_done()
    project(place.step("x", 2))
    post(2)
    tick(*up_gathers, *out_gathers)
    kept.append(pltpu.make_async_copy(act, act_all, local.at[6]))
    kept[-1].start()
    for p in range(3):
        for n in range(4):
            wq_t[p, :, n * 512 : n * 512 + 512] = jnp.transpose(wq[p, n // 2, n % 2].reshape(512, 256))
    kept.append(pltpu.make_async_copy(wq_t, qkv_w, local.at[5]))
    kept[-1].start()
    for n in range(16):
        dst = mine.at[:, piece(n, 128)]
        pltpu.make_async_copy(dst, dst, a_recv.at[0, n]).wait()
    kept.append(pltpu.make_async_copy(mine, heads, local.at[7]))
    kept[-1].start()
    for n in range(16):
        dst = others.at[:, piece(n, 128)]
        pltpu.make_async_copy(dst, dst, a_recv.at[1, n]).wait()
    kept.append(pltpu.make_async_copy(others, across, local.at[8]))
    kept[-1].start()
    cot_gather = group_gather(place, sends, cotbuf)

    def keep_cot(n, steps):
        copies = []
        for step in steps:
            x = place.step("x", step)
            copies.append(pltpu.make_async_copy(cotbuf.at[x], cot_all.at[x], local.at[n + len(copies)]))
            copies[-1].start()
        return copies

    tick(cot_gather)

    def tile(t, _):
        peak, total = attend(t, mine, others, starts, place.xh, scale)
        weight = total[:, 128:]
        o = total[:, :128] / weight
        att[piece(t, F_TILE), :] = o
        for b in range(F_TILE // 128):
            low[t * (F_TILE // 128) + b] = o[b * 128 : (b + 1) * 128].astype(bf16)
        line = jnp.transpose(peak * (scale * LOG2E) + jnp.log2(weight))
        for n in range(F_TILE // Q_TILE):
            lse[pl.ds(t * (F_TILE // Q_TILE) + n, 1), :] = line[0:1, n * Q_TILE : n * Q_TILE + Q_TILE]
        return 0

    tiles = mine.shape[1] // F_TILE
    lax.fori_loop(0, tiles, tile, 0)
    back = heads_out(place, sends, low, merged, local.at[9])
    tick(back)
    tick(cot_gather, *up_gathers, *out_gathers)
    kept += keep_cot(11, (0, 1, 3))
    tick(*out_gathers)
    for copy in posts:
        copy.wait_send()
    for copy in kept:
        copy.wait()
    act_gather.finish()
    run_all([back, *up_gathers, cot_gather, *out_gathers])
    for copy in keep_cot(10, (2,)):
        copy.wait()
    assert sends.used <= send.shape[0], sends.used


def front(starts, chosen, tok, gain, shift, bias, cot, wp, wo, up, umaps, dmaps, lum, scale):
    any_ = pl.BlockSpec(memory_space=pl.ANY)
    vmem = pl.BlockSpec(memory_space=pltpu.VMEM)
    smem = pl.BlockSpec(memory_space=pltpu.SMEM)
    shape = lambda *s: jax.ShapeDtypeStruct(s, bf16)
    vm = lambda *s: pltpu.VMEM(s, bf16)
    return pl.pallas_call(
        functools.partial(front_kernel, scale=scale),
        name="front",
        out_shape=[
            shape(4, 2, 128, 2432),
            shape(3, 256, 2048),
            shape(2, 2, 4, 4, 2, 16, 2048),
            shape(2, 2, 4, 4, 2, 16, 1024),
            shape(4, 2, 128, 2176),
            shape(3, 2048, 128),
            shape(2, 2048, 128),
            shape(128, 2048),
            jax.ShapeDtypeStruct((2048, 128), f32),
            jax.ShapeDtypeStruct((8, 256), f32),
            jax.ShapeDtypeStruct((128, 128), f32),
        ],
        in_specs=[smem] * 2 + [vmem] * 8 + [any_] * 3,
        out_specs=[any_] * 8 + [vmem] * 3,
        scratch_shapes=[
            vm(3, 128, 256),
            vm(3, 2048, 128),
            vm(128, 2048),
            vm(4, 2, 128, 2432),
            vm(4, 2, 128, 2176),
            vm(3, 2, 2, 4, 4, 2, 16, 256),
            vm(16, 8192),
            vm(3, 4, 2, 2, 128, 128),
            vm(3, 2048, 128),
            vm(2, 2048, 128),
            vm(16, 128, 128),
            vm(3, 256, 2048),
        ]
        + [pltpu.SemaphoreType.DMA(n) for n in ((150,), (150,), (2, 16), (2, 16), (16,))],
        compiler_params=pltpu.CompilerParams(
            collective_id=0, has_side_effects=True, vmem_limit_bytes=56 * MIB
        ),
    )(starts, chosen, tok, gain, shift, bias, cot, wp, wo, up, umaps, dmaps, lum)


def middle_kernel(
    starts, grad, queries_in, others_in, att_in, lse, umaps_in, mask, a_own, b_own, two,
    by_member, low_rank, a_final, b_final, two_final,
    queries, others, att, umaps, do, delta, dq_acc, dq, own_low, other_low, by_head, from_other, *refs, scale,
):
    scratch, (send, recv, a_send, a_recv, s_send, s_recv, local) = list(refs[:-7]), refs[-7:]
    place = Place()
    across = [{"xh": 1 - place.xh, "z": z, "y": y} for z, y in plane(place)]
    greet(plane_devices(place) + members(place) + across)
    sends = Sends(send, recv)
    here = place.z * 4 + place.y
    parity = place.xh
    kv = pl.ds(1, 2)

    keep = pltpu.make_async_copy(grad.at[:, head_columns(place.z, place.y)], do.at[piece(here, 128)], local.at[0])
    keep.start()
    loads = [
        pltpu.make_async_copy(src, dst, local.at[1 + n])
        for n, (src, dst) in enumerate(
            ((att_in, att), (queries_in, queries), (others_in, others), (umaps_in, umaps))
        )
    ]
    for copy in loads:
        copy.start()
    grads_sent = [
        sends.push(grad.at[:, head_columns(z, y)], do.at[piece(here, 128)], {"z": z, "y": y})
        for z, y in plane(place)
    ]

    def take(n):
        got = scratch[:n]
        del scratch[:n]
        return got

    early = [
        a_sum(place, sends, a_own, a_final, take(5)),
        b_sum(place, sends, b_own, b_final, take(5)),
    ]
    early += [
        reduce_piece(
            place, sends, two_final.at[n], None,
            (lambda z, y, n=n: two.at[n, z, y], scratch[n], two_final.at[n]), None,
        )
        for n in range(2)
    ]

    def tick(*parts):
        for part in parts:
            try:
                next(part)
            except StopIteration:
                pass

    tick(*early)
    dq_acc[...] = jnp.zeros_like(dq_acc)
    keep.wait()
    for copy in grads_sent:
        copy.wait_recv()
    for copy in loads:
        copy.wait()
    ones = jnp.ones((8, 128), bf16)
    tiles, key_tiles = do.shape[0] // Q_TILE, do.shape[0] // K_TILE

    def row_dots(t, _):
        rows = piece(t, Q_TILE)
        value = do[rows, :].astype(f32) * att[rows, :]
        high = value.astype(bf16)
        low = (value - high.astype(f32)).astype(bf16)
        delta[t] = dot_nt(ones, high) + dot_nt(ones, low)
        return 0

    lax.fori_loop(0, tiles, row_dots, 0)
    tick(*early[:2])

    def keys(kt):
        rows = piece(kt, K_TILE)
        sides = ((others[0, rows, :], others[1, rows, :], 1 - parity), (queries[1, rows, :], queries[2, rows, :], parity))
        local = kt * K_TILE + lax.broadcasted_iota(jnp.int32, (K_TILE, 1), 0)

        def step(qt, carry, diagonal):
            rows = piece(qt, K_TILE)
            q = queries[0, rows, :]
            d = do[rows, :]
            q_pos = positions_of(qt * K_TILE + lax.broadcasted_iota(jnp.int32, (1, K_TILE), 1), parity)
            both = [qt * 2, qt * 2 + 1]
            lse_row = jnp.concatenate([lse[pl.ds(n, 1), :] for n in both], axis=1)
            delta_row = jnp.concatenate([delta[n, 0:1, :] for n in both], axis=1)
            lo = document_start(starts, q_pos)
            found, dq_part = [], None
            for (k, v, k_parity), (dk, dv) in zip(sides, carry):
                k_pos = positions_of(local, k_parity)
                s = dot_nt(k, q)
                allowed = k_pos >= lo
                if diagonal:
                    allowed = allowed & (k_pos <= q_pos)
                p = jnp.exp2(jnp.where(allowed, s * (scale * LOG2E) - lse_row, -1e30))
                dv = dv + dot(p.astype(bf16), d)
                ds = (p * (dot_nt(v, d) - delta_row)).astype(bf16)
                dk = dk + dot(ds, q)
                part = dot_tn(ds, k)
                dq_part = part if dq_part is None else dq_part + part
                found.append((dk, dv))
            dq_acc[rows, :] += dq_part
            return tuple(found)

        zero = jnp.zeros((K_TILE, 128), f32)
        carry = step(kt, ((zero, zero),) * 2, True)
        carry = lax.fori_loop(kt + 1, key_tiles, lambda qt, c: step(qt, c, False), carry)
        return [(dk * scale, dv) for dk, dv in carry]

    blocks = K_TILE // 128
    gone = []

    def to_token(k, n, src, dst, other, away):
        z, y = n // 4, lax.rem(n, 4)
        myself = None if other or away else (place.z == z) & (place.y == y)
        device = {"z": z, "y": y} | ({"xh": 1 - place.xh} if other else {})
        gone.append(Post(src, dst, device, myself, a_send.at[k, n], a_recv.at[k, here]))

    shared = []

    def share(turn, k, part):
        x = lax.rem(place.z + (4 - turn), 4)
        for c in range(2):
            g = x * 2 + c
            pair = piece(g, 2)
            if k:
                both = by_head[1:3, pair].astype(f32) + from_other[:, pair].astype(f32)
                by_head[1:3, pair] = both.astype(bf16)
            device = {"xl": lax.rem(x, 2), "xh": x // 2, "c": c}
            myself = (place.x == x) & (place.c == c)
            src, dst = by_head.at[part, pair], by_member.at[part, place.x, place.c]
            n = turn * 2 + c
            shared.append(Post(src, dst, device, myself, s_send.at[k, n], s_recv.at[k, place.g]))

    def heads_of(turn):
        x = lax.rem(place.z + (4 - turn), 4)
        return [x * 4 + y for y in range(4)]

    def share_keys(turn):
        for head in heads_of(turn):
            for k, dst in ((2, from_other.at[:, 0]), (1, by_head.at[kv, 0])):
                pltpu.make_async_copy(dst, dst, a_recv.at[k, head]).wait()
        share(turn, 1, kv)

    def share_queries(turn):
        for head in heads_of(turn):
            dst = by_head.at[0, 0]
            pltpu.make_async_copy(dst, dst, a_recv.at[0, head]).wait()
        share(turn, 0, 0)

    for turn in (2, 1, 3, 0):
        kt = lax.rem(place.z + turn, key_tiles)
        for k, low, (dk, dv) in zip((2, 1), (other_low, own_low), keys(kt)):
            for b in range(blocks):
                n = kt * blocks + b
                low[n, 0] = dk[b * 128 : (b + 1) * 128].astype(bf16)
                low[n, 1] = dv[b * 128 : (b + 1) * 128].astype(bf16)
                dst = from_other.at[:, here] if k == 2 else by_head.at[kv, here]
                to_token(k, n, low.at[n], dst, k == 2, turn != 0)
    for n in range(16):
        dq[n] = (dq_acc[n * 128 : (n + 1) * 128] * scale).astype(bf16)
    for turn in (2, 1, 3, 0):
        for b in range(blocks):
            n = lax.rem(place.z + turn, 4) * 4 + b
            to_token(0, n, dq.at[n], by_head.at[0, here], False, turn != 0)
    tick(*early)
    for turn in (2, 1, 3, 0):
        share_keys(turn)
    tick(*early)
    for turn in (2, 1, 3, 0):
        share_queries(turn)
    for p in range(3):
        whole = jnp.concatenate([by_head[p, n] for n in range(16)], axis=1)
        low_rank[:, p * 128 : p * 128 + 128] = (dot_nt(whole, umaps[p]) * mask[...]).astype(bf16)
    for n in range(8):
        for k, dst in ((0, by_member.at[0, 0, 0]), (1, by_member.at[kv, 0, 0])):
            pltpu.make_async_copy(dst, dst, s_recv.at[k, n]).wait()
    run_all(early)
    for copy in gone + grads_sent + shared:
        copy.wait_send()
    assert sends.used <= send.shape[0], sends.used


def middle(starts, grad, queries, others, att, lse, umaps, mask, a_own, b_own, two, scale):
    any_ = pl.BlockSpec(memory_space=pl.ANY)
    vmem = pl.BlockSpec(memory_space=pltpu.VMEM)
    smem = pl.BlockSpec(memory_space=pltpu.SMEM)
    vm = lambda *s: pltpu.VMEM(s, bf16)
    shape = lambda *s: jax.ShapeDtypeStruct(s, bf16)
    return pl.pallas_call(
        functools.partial(middle_kernel, scale=scale),
        name="attention_backward",
        out_shape=[
            shape(3, 4, 2, 2, 128, 128),
            shape(128, 384),
            shape(16, 128),
            shape(16, 128),
            shape(2, 64, 128),
        ],
        in_specs=[smem, vmem, any_, any_, any_, vmem, any_, vmem] + [vmem] * 3,
        out_specs=[any_] + [vmem] * 4,
        scratch_shapes=[
            vm(3, 2048, 128),
            vm(2, 2048, 128),
            pltpu.VMEM((2048, 128), f32),
            vm(4, 128, 2048),
            vm(2048, 128),
            pltpu.VMEM((8, 8, 256), f32),
            pltpu.VMEM((2048, 128), f32),
            vm(16, 128, 128),
            vm(16, 2, 128, 128),
            vm(16, 2, 128, 128),
            vm(3, 16, 128, 128),
            vm(2, 16, 128, 128),
        ]
        + a_sum_scratch()
        + b_sum_scratch()
        + [vm(15, 64, 128)] * 2
        + [pltpu.SemaphoreType.DMA(k) for k in ((100,), (100,), (3, 16), (3, 16), (2, 8), (2, 8), (8,))],
        compiler_params=pltpu.CompilerParams(collective_id=2, has_side_effects=True, vmem_limit_bytes=58 * MIB),
    )(starts, grad, queries, others, att, lse, umaps, mask, a_own, b_own, two.reshape(2, 4, 4, 64, 128))


def feed_forward_kernel(
    merged, tok, gains, shifts, biases, up_down, low_up, mask, bias_all, dn, cot_own,
    w_out_in, cot_all, up, out_down_in, out_up_in, umap_in, dmap_in,
    grad_merged, grad_res, base, forth, small_out, a_out, b_out, two, mine_in, mine_cot,
    out_down, out_up, umap_all, umap, dmap, bias, w_out, residual, low_out, sa, cot, up_v, dn_v, slope, act, pre, parts, total, *refs,
):
    scratch, (send, recv, local) = refs[:-3], refs[-3:]
    place = Place()
    greet(members(place) + plane_devices(place))
    sends = Sends(send, recv)
    loads = [
        pltpu.make_async_copy(src, dst, local.at[n]) for n, (src, dst) in enumerate(
            (
                (out_down_in.at[3], out_down), (w_out_in, w_out), (out_up_in.at[3], out_up),
                (umap_in.at[:, piece(place.xl * 2 + place.c, 2048)], umap_all),
                (dmap_in.at[place.xl * 2 + place.c, :, place.xh], dmap), (up, up_v), (cot_all, cot),
            )
        )
    ]
    for copy in loads:
        copy.start()

    def dn_view(h):
        def view(fixed, half):
            cols = pl.ds(h * 1024, 1024) if half is None else pl.ds(h * 1024 + half * 512, 512)
            return dn_v.at[fixed.get("z", ALL), fixed.get("y", ALL), :, cols]

        return view

    here = {"z": place.z, "y": place.y}
    dn_v[place.z, place.y] = dn[...]
    dn_gathers = [
        ring_gather(place, sends, dn_view(h), order, dn_view(h)(here, None), Nothing(), False)
        for h, order in enumerate((("y", "z"), ("z", "y")))
    ]

    def tick(*parts):
        for part in parts:
            next(part)

    tick(*dn_gathers)
    gain, shift = gains[1:2, :], shifts[1:2, :]
    bias_out, bias_end = biases[2:3, :], biases[3:4, :]
    loads[0].wait()
    low_out[...] = (dot(merged[...], out_down[...]) * mask[...]).astype(bf16)
    loads[1].wait()
    loads[2].wait()

    def out_tile(n, _):
        cols = piece(n, 256)
        value = tok[:, cols].astype(f32) + dot(merged[...], w_out[:, cols]) + biases[2:3, cols]
        residual[:, cols] = value + dot(low_out[...], out_up[:, cols])
        return 0

    lax.fori_loop(0, 8, out_tile, 0)
    second = layer_norm(residual[...], gain, shift).astype(bf16)
    own = sa.at[place.x, place.c]
    own[:, 0:2048] = second
    own[:, 2048:2176] = (dot(second, up_down[...]) * mask[...]).astype(bf16)
    gather = GroupGather(place, sends, sa)
    loads[3].wait()
    loads[4].wait()
    whole_bias = bias_all[:, piece(place.xl * 2 + place.c, 2048)]
    for n in range(8):
        for whole, out in ((umap_all[:, n * 256 : n * 256 + 256], umap), (whole_bias[:, n * 256 : n * 256 + 256], bias)):
            sides = [jnp.concatenate([whole[:, h : h + 64], whole[:, 128 + h : 192 + h]], axis=1) for h in (0, 64)]
            out[:, n * 128 : n * 128 + 128] = jnp.where(place.xh == 0, sides[0], sides[1])
    tick(*dn_gathers)

    def rows(ref, x, start, size):
        return ref[x, :, :, pl.ds(start, size)].reshape(256, size)

    xs = places_in_turn(place)

    def hidden(k):
        x = xs[k]

        def tile(n, _):
            cols = piece(n, 256)
            value = dot(rows(sa, x, 0, 2048), up_v[:, cols]) + bias[:, cols]
            value = value + dot(rows(sa, x, 2048, 128), umap[:, cols])
            phi = 0.5 * (1.0 + lax.erf(value * 0.7071067811865476))
            act[k, :, cols] = (value * phi).astype(bf16)
            slope[k, :, cols] = phi + value * (0.3989422804014327 * jnp.exp2(value * value * (-0.5 * LOG2E)))
            return 0

        lax.fori_loop(0, 4, tile, 0)

    def grad_hidden(k):
        x = xs[k]

        def tile(n, _):
            cols = piece(n, 256)
            value = dot_nt(rows(cot, x, 0, 2048), dn_v[n].reshape(256, 2048))
            value = value + dot_nt(rows(cot, x, 2048, 128), dmap[piece(n, 4)].reshape(256, 128))
            pre[k, :, cols] = (value * slope[k, :, cols]).astype(bf16)
            return 0

        lax.fori_loop(0, 4, tile, 0)

    def backward(k, n):
        ks = pl.ds(k, n)

        def tile(t, _):
            cols = piece(t, 256)
            value = dot_nt(pre[ks].reshape(n * 256, 1024), up_v[cols, :]).astype(bf16)
            parts[ks, :, :, cols] = value.reshape(n, 2, 128, 256)
            return 0

        lax.fori_loop(0, 8, tile, 0)
        value = dot_nt(pre[ks].reshape(n * 256, 1024), umap[...]).astype(bf16)
        parts[ks, :, :, 2048:2176] = value.reshape(n, 2, 128, 128)
        value = dot(act[ks].reshape(n * 256, 1024), dmap[...].reshape(1024, 128)).astype(bf16)
        parts[ks, :, :, 2176:2304] = value.reshape(n, 2, 128, 128)

    loads[5].wait()
    gather.own()
    hidden(3)
    tick(*dn_gathers)
    gather.near()
    hidden(2)
    hidden(1)
    run_all(dn_gathers)
    loads[6].wait()
    grad_hidden(3)
    gather.far()
    grad_hidden(2)
    gather.far_done()
    hidden(0)
    grad_hidden(0)

    sums = GroupSum(place, sends, parts, scratch)
    backward(0, 1)
    sums.cross(0)
    grad_hidden(1)
    sums.merge(0)
    sums.first()
    backward(1, 1)
    sums.cross(1)
    backward(2, 2)
    sums.cross(2)
    sums.cross(3)
    sums.merge(1)
    sums.merge(2)
    sums.second()

    def small(k, _):
        x = lax.rem(place.x + jnp.where(k == 3, 0, jnp.where(k == 2, 3, 2 - k)), 4)
        one = dot_tn(act[k], rows(cot, x, 2048, 128))
        other = dot_tn(pre[k], rows(sa, x, 2048, 128))

        @pl.when(k == 0)
        def _():
            total[0] = one
            total[1] = other

        @pl.when(k > 0)
        def _():
            total[0] += one
            total[1] += other

        return 0

    lax.fori_loop(0, 4, small, 0)
    cols = piece(place.g, 256)
    mine_in[...] = sa[:, :, :, cols].reshape(1024, 256)
    mine_cot[...] = cot[:, :, :, cols].reshape(1024, 256)
    def forward(n, _):
        ks, cols = piece(n // 4, 2), piece(lax.rem(n, 4), 512)
        value = dot(act[ks].reshape(512, 1024), dn_v[:, :, :, cols].reshape(1024, 512)).astype(bf16)
        cot[ks, :, :, cols] = value.reshape(2, 2, 128, 512)
        return 0

    lax.fori_loop(0, 8, forward, 0)

    two[...] = total[...].astype(bf16)
    handed = pltpu.make_async_copy(cot.at[:, :, :, pl.ds(0, 2048)], forth, local.at[7])
    handed.start()
    summed = sums.result()
    low_up_grad = (summed[:, 2048:2176] * mask[...]).astype(bf16)
    low_down = (summed[:, 2176:2304] * mask[...]).astype(bf16)
    small_out[:, 0:128] = low_up_grad
    small_out[:, 128:256] = low_down
    grad_second = summed[:, 0:2048] + dot_nt(low_up_grad, up_down[...])
    value = cot_own[...].astype(f32) + layer_norm_back(residual[...], gain, grad_second)
    grad_res[...] = value
    branch = value.astype(bf16)
    low_grad = (dot_nt(branch, out_up[...]) * mask[...]).astype(bf16)

    def merged_tile(n, _):
        cols = piece(n, 256)
        value = dot_nt(branch, w_out[cols, :]) + dot_nt(low_grad, out_down[cols, :])
        grad_merged[:, cols] = value.astype(bf16)
        return 0

    lax.fori_loop(0, 8, merged_tile, 0)
    b_out[...] = dot_tn(low_out[...], branch).astype(bf16)
    a_out[...] = dot_tn(merged[...], low_grad).astype(bf16)
    base[...] = residual[...] + bias_end + dot(low_down, low_up[...])
    handed.wait()
    gather.finish()
    assert sends.used <= send.shape[0], sends.used


def feed_forward(*args):
    any_ = pl.BlockSpec(memory_space=pl.ANY)
    vmem = pl.BlockSpec(memory_space=pltpu.VMEM)
    vm = lambda *s: pltpu.VMEM(s, bf16)
    shape = lambda *s: jax.ShapeDtypeStruct(s, bf16)
    return pl.pallas_call(
        feed_forward_kernel,
        name="feed_forward",
        out_shape=[
            shape(128, 2048),
            jax.ShapeDtypeStruct((128, 2048), f32),
            jax.ShapeDtypeStruct((128, 2048), f32),
            shape(4, 2, 128, 2048),
            shape(128, 256),
            shape(2048, 128),
            shape(128, 2048),
            shape(2, 1024, 128),
            shape(1024, 256),
            shape(1024, 256),
        ],
        in_specs=[vmem] * 11 + [any_] * 7,
        out_specs=[vmem] * 3 + [any_] + [vmem] * 6,
        scratch_shapes=[
            vm(2048, 128),
            vm(128, 2048),
            vm(128, 2048),
            vm(128, 1024),
            vm(16, 64, 128),
            pltpu.VMEM((1, 1024), f32),
            vm(2048, 2048),
            pltpu.VMEM((128, 2048), f32),
            vm(128, 128),
            vm(4, 2, 128, 2176),
            vm(4, 2, 128, 2176),
            vm(2048, 1024),
            vm(4, 4, 64, 2048),
            pltpu.VMEM((4, 256, 1024), f32),
            vm(4, 256, 1024),
            vm(4, 256, 1024),
            vm(4, 2, 128, 2304),
            pltpu.VMEM((2, 1024, 128), f32),
        ]
        + GroupSum.scratch(2304)
        + [pltpu.SemaphoreType.DMA((k,)) for k in (40, 40, 8)],
        compiler_params=pltpu.CompilerParams(collective_id=1, has_side_effects=True, vmem_limit_bytes=63 * MIB),
    )(*args)


def both_heads(gq, p, x):
    heads = [gq[p, x, :, j].reshape(256, 128) for j in range(2)]
    return jnp.concatenate(heads, axis=1)


def tail_kernel(
    grads, qkv_w, act_all, dmaps_in, grad_res_in, forth_in, base_in, low_rank, small, tok, gain, mine_in, mine_cot, a_piece, b_piece, two_piece,
    input_grad, mixed, a_res, b_res, two_a, two_b, a_early, b_early,
    dmaps, grad_res, forth_parts, base, gq, wq, act, left, parts, lows, a_sums, b_sums, a_s, a_f, b_s, b_f, *refs,
):
    scratch, (send, recv, local) = refs[:-3], refs[-3:]
    scratch, forth_scratch = scratch[:6], scratch[6:]
    place = Place()
    greet(members(place) + plane_devices(place))
    sends = Sends(send, recv)
    loads = [
        pltpu.make_async_copy(src, dst, local.at[n])
        for n, (src, dst) in enumerate(((grads, gq), (qkv_w, wq), (act_all, act)))
    ]
    loads.append(pltpu.make_async_copy(dmaps_in.at[pl.ds(0, 3)], dmaps, local.at[44]))
    loads.append(pltpu.make_async_copy(grad_res_in, grad_res, local.at[45]))
    loads.append(pltpu.make_async_copy(forth_in, forth_parts, local.at[43]))
    loads.append(pltpu.make_async_copy(base_in, base, local.at[42]))
    for copy in loads:
        copy.start()
    own = lows.at[place.x, place.c]
    own[:, 0:384] = low_rank[...]
    own[:, 384:640] = small[...]
    spread = [sends.push(own, own, place.member(dx, 0)) for dx in (2, 1, 3)]
    passed = [sends.push(own, own, place.member(0, 1))]

    def two_view(res):
        def view(at):
            xl, xh = two_parts(at)
            return res.at[xl, place.c, at["z"], at["y"], xh]

        return view

    def b_early_view(at):
        z, y = at["z"], at["y"]
        if isinstance(y, pl.Slice):
            cols = pl.ds(y.start * 128 if z is ALL else pl.multiple_of(z * 512 + y.start * 128, 128), 256)
        elif z is ALL:
            cols = ALL
        else:
            cols = piece(z, 512) if y is ALL else piece(z * 4 + y, 128)
        return b_early.at[place.c, at["x"], :, cols]

    early = [
        give_all(place, sends, ("x", "z", "y"), two_piece.at[0], two_view(two_a), local.at[3]),
        give_all(place, sends, ("x", "y", "z"), two_piece.at[1], two_view(two_b), local.at[4]),
        give_all(
            place, sends, ("x", "y", "z"), a_piece,
            lambda at: a_early.at[place.c, at["z"], at["y"], at["x"]], local.at[5],
        ),
        give_all(place, sends, ("x", "y", "z"), b_piece, b_early_view, local.at[6]),
    ]

    def tick(*parts):
        for part in parts:
            next(part)

    tick(*early)
    def a_view(at):
        return a_res.at[:, at["x"], place.c, at["z"], at["y"]]

    def a_held(z, y):
        return a_sums.at[:, piece(z * 4 + y, 16)]

    def b_view(at):
        y = at["y"]
        if y is ALL:
            yr, yc = ALL, ALL
        elif isinstance(y, pl.Slice):
            yr, yc = pl.ds(y.start // 2, 1), ALL
        else:
            yr, yc = y // 2, lax.rem(y, 2)
        return b_res.at[:, at["x"], place.c, at["z"], yr, yc]

    def b_held(z, y):
        return b_sums.at[:, pl.ds(pl.multiple_of(z * 32 + y // 2 * 16, 16), 16), piece(lax.rem(y, 2), 128)]

    def late_part(final, held, slots, order, view, sem):
        yield from reduce_piece(place, sends, final, None, (held, slots, final), None)
        yield from give_all(place, sends, order, final, view, sem, True)

    late = [
        late_part(a_f, a_held, a_s, ("y", "x", "z"), a_view, local.at[7]),
        late_part(b_f, b_held, b_s, ("z", "x", "y"), b_view, local.at[8]),
    ]
    loads[0].wait()
    loads[1].wait()
    xs = places_in_turn(place)
    for k in range(4):
        left[k] = jnp.concatenate([both_heads(gq, p, xs[k]) for p in range(3)], axis=1)

    def partial(k, n):
        ks = pl.ds(k, n)

        def tile(t, _):
            cols = piece(t, 512)
            value = dot(left[ks].reshape(n * 256, 768), wq[:, :, cols].reshape(768, 512)).astype(bf16)
            parts[ks, :, :, cols] = value.reshape(n, 2, 128, 512)
            return 0

        lax.fori_loop(0, 4, tile, 0)

    sums = GroupSum(place, sends, parts, scratch)
    partial(0, 1)
    sums.cross(0)
    partial(1, 1)
    sums.cross(1)
    sums.merge(0)
    sums.first()
    loads[5].wait()
    forth = GroupSum(place, sends, forth_parts, forth_scratch)
    for k in range(4):
        forth.cross(k)
    loads[2].wait()
    for p in range(3):
        total = jnp.zeros((128, 256), f32)
        for x in range(4):
            left_rows = act[x, :, :, 2048 + p * 128 : 2176 + p * 128].reshape(256, 128)
            total = total + dot_tn(left_rows, both_heads(gq, p, x))
        b_sums[p] = total.astype(bf16)
    for dx, copy in zip((2, 1, 3), spread):
        copy.wait()
        came = lows.at[place.step("x", -dx), place.c]
        passed.append(sends.push(came, came, place.member(0, 1)))
    for copy in passed:
        copy.wait()
    b_sums[3] = dot_tn(lows[:, :, :, 512:640].reshape(1024, 128), mine_cot[...]).astype(bf16)
    rows = act[:, :, :, piece(place.g, 256)].reshape(1024, 256)
    for p in range(4):
        right = lows[:, :, :, p * 128 : p * 128 + 128].reshape(1024, 128)
        a_sums[p] = dot_tn(rows if p < 3 else mine_in[...], right).astype(bf16)

    tick(*late)
    partial(2, 2)
    sums.cross(2)
    sums.cross(3)
    forth.merge(0)
    forth.first()
    tick(*early)
    sums.merge(1)
    sums.merge(2)
    sums.second()
    tick(*late)
    tick(*early)
    tick(*late)
    forth.merge(1)
    forth.merge(2)
    forth.second()
    tick(*early)
    loads[3].wait()
    loads[4].wait()
    grad_first = sums.result()
    for p in range(3):
        grad_first = grad_first + dot_nt(low_rank[:, p * 128 : p * 128 + 128], dmaps[p])
    result = grad_res[...] + layer_norm_back(tok[...].astype(f32), gain[0:1, :], grad_first)
    input_grad[...] = result.astype(bf16)
    tick(*late)
    tick(*early)
    run_all(late + early)
    loads[6].wait()
    mixed[...] = (base[...] + forth.result()).astype(bf16)
    assert sends.used <= send.shape[0], sends.used


def tail(grads, qkv_w, act_all, dmaps, grad_res, forth, base, low_rank, small, tok, gain, mine_in, mine_cot, a_piece, b_piece, two_piece):
    any_ = pl.BlockSpec(memory_space=pl.ANY)
    vmem = pl.BlockSpec(memory_space=pltpu.VMEM)
    vm = lambda *s: pltpu.VMEM(s, bf16)
    shape = lambda *s: jax.ShapeDtypeStruct(s, bf16)
    a_shape, b_shape = (4, 4, 2, 4, 4, 16, 128), (4, 4, 2, 4, 2, 2, 16, 128)
    return pl.pallas_call(
        tail_kernel,
        name="tail",
        out_shape=[
            shape(128, 2048),
            shape(128, 2048),
            shape(*a_shape),
            shape(*b_shape),
            shape(2, 2, 4, 4, 2, 64, 128),
            shape(2, 2, 4, 4, 2, 64, 128),
            shape(2, 4, 4, 4, 16, 128),
            shape(2, 4, 16, 2048),
        ],
        in_specs=[any_] * 7 + [vmem] * 9,
        out_specs=[vmem] * 2 + [any_] * 6,
        scratch_shapes=[
            vm(3, 2048, 128),
            pltpu.VMEM((128, 2048), f32),
            vm(4, 2, 128, 2048),
            pltpu.VMEM((128, 2048), f32),
            vm(3, 4, 2, 2, 128, 128),
            vm(3, 256, 2048),
            vm(4, 2, 128, 2432),
            vm(4, 256, 768),
            vm(4, 2, 128, 2048),
            vm(4, 2, 128, 640),
            vm(4, 256, 128),
            vm(4, 128, 256),
            vm(15, 4, 16, 128),
            vm(4, 16, 128),
            vm(15, 4, 16, 128),
            vm(4, 16, 128),
        ]
        + GroupSum.scratch(2048) * 2
        + [pltpu.SemaphoreType.DMA((k,)) for k in (200, 200, 46)],
        compiler_params=pltpu.CompilerParams(collective_id=3, has_side_effects=True, vmem_limit_bytes=60 * MIB),
    )(
        grads, qkv_w, act_all, dmaps, grad_res, forth, base, low_rank, small, tok, gain, mine_in, mine_cot, a_piece, b_piece, two_piece
    )
def widen_kernel(a, a_one, b, b_one, hid_a, hid_b, a_out, b_out, up_out, hid_b_out, hid_a_out, down_out):
    for n in range(3):
        a_out[n] = a[n].astype(f32)
    a_out[3] = a_one[...].astype(f32)
    up_out[...] = a[3].astype(f32)
    for c in range(2):
        for yc in range(2):
            cols = pl.ds(c * 256 + yc * 128, 128)
            for n in range(3):
                b_out[n, :, cols] = b[n, 0, c, :, :, yc].reshape(128, 128).astype(f32)
            down_out[:, cols] = b[3, 0, c, :, :, yc].reshape(128, 128).astype(f32)
    b_out[3] = b_one[...].astype(f32)
    hid_a_out[...] = hid_a[...].astype(f32)
    for n in range(4):
        rows = pl.ds(n * 512, 512)
        hid_b_out[:, rows] = jnp.transpose(hid_b[rows, :].astype(f32))


def widen(a, b, hid_a, hid_b, a_one, b_one):
    out = lambda *s: jax.ShapeDtypeStruct(s, f32)
    spec = pl.BlockSpec
    return pl.pallas_call(
        widen_kernel,
        name="widen",
        grid=(4,),
        out_shape=[
            out(4, 2048, 128), out(4, 128, 2048), out(2048, 128), out(128, 8192), out(8192, 128), out(128, 2048)
        ],
        in_specs=[
            spec((4, 512, 128), lambda g: (0, g, 0)),
            spec((512, 128), lambda g: (g, 0)),
            spec((4, 1, 2, 4, 2, 2, 16, 128), lambda g: (0, g, 0, 0, 0, 0, 0, 0)),
            spec((128, 512), lambda g: (0, g)),
            spec((2048, 128), lambda g: (g, 0)),
            spec((2048, 128), lambda g: (g, 0)),
        ],
        out_specs=[
            spec((4, 512, 128), lambda g: (0, g, 0)),
            spec((4, 128, 512), lambda g: (0, 0, g)),
            spec((512, 128), lambda g: (g, 0)),
            spec((128, 2048), lambda g: (0, g)),
            spec((2048, 128), lambda g: (g, 0)),
            spec((128, 512), lambda g: (0, g)),
        ],
        compiler_params=pltpu.CompilerParams(vmem_limit_bytes=62 * MIB),
    )(
        a.reshape(4, 2048, 128), a_one.reshape(2048, 128), b, b_one.reshape(128, 2048), hid_a.reshape(8192, 128),
        hid_b.reshape(8192, 128),
    )


def per_device(
    tokens,
    document_starts,
    document_adapter,
    layernorm_gain,
    layernorm_bias,
    projection_weight,
    output_weight,
    up_weight,
    down_weight,
    projection_bias,
    upper_bias,
    attention_down_maps,
    attention_up_maps,
    upper_down_maps,
    upper_up_maps,
    lower_down_maps,
    lower_up_maps,
    cotangent,
):
    local_rows, width = tokens.shape[1:]
    head_size = width // HEADS
    seq = local_rows * 32
    scale = head_size ** (-0.5)
    xl, c, z, y, xh = (lax.axis_index(a) for a in AXES)
    group = (xh * 2 + xl) * 2 + c
    cot = cotangent[0]
    (
        act_all, qkv_w, out_all, up_all, cot_all, by_head, across, merged, attended, lse, mask
    ) = front(
        document_starts, document_adapter, tokens[0], layernorm_gain, layernorm_bias, projection_bias, cot,
        jnp.transpose(projection_weight, (1, 0, 2)), output_weight, up_weight, attention_up_maps, attention_down_maps,
        lower_up_maps, scale,
    )
    grad_merged, grad_residual, base, forth, small, a_out, b_out, two, mine_in, mine_cot = feed_forward(
        merged, tokens[0], layernorm_gain, layernorm_bias, projection_bias, upper_down_maps, lower_up_maps, mask,
        upper_bias[None], down_weight, cot, out_all.reshape(width, width), cot_all, up_all.reshape(width, 1024),
        attention_down_maps, attention_up_maps, upper_up_maps, lower_down_maps.reshape(4, 16, 2, 64, 128),
    )
    grad_qkv, grad_adapt_qkv, a_piece, b_piece, two_piece = middle(
        document_starts, grad_merged, by_head, across, attended, lse, attention_up_maps, mask, a_out, b_out, two, scale
    )
    input_grad, mixed, *sums = tail(
        grad_qkv, qkv_w, act_all, attention_down_maps, grad_residual, forth, base, grad_adapt_qkv, small, tokens[0], layernorm_gain,
        mine_in, mine_cot, a_piece, b_piece, two_piece,
    )
    return (mixed[None], input_grad[None], *widen(*sums))


def solution(mesh):
    fine = jax.sharding.Mesh(mesh.devices.reshape(SIZES), AXES)
    by_token = P(STREAM, TOKEN, None)
    shard = AXES
    in_specs = (
        by_token,
        P(STREAM, None),
        P(STREAM, None),
        P(),
        P(),
        P(shard, None, None),
        P(shard, None),
        P(shard, None),
        P(shard, None),
        P(),
        P(),
        P(),
        P(),
        P(),
        P(),
        P(),
        P(),
        by_token,
    )
    out_specs = (by_token, by_token, P(), P(), P(), P(), P(), P())
    return jax.shard_map(per_device, mesh=fine, in_specs=in_specs, out_specs=out_specs, check_vma=False)
```
